32 devices in a mesh: blk: 16 (over z, y, x), grp: 2 (over core).
Axes of the slice: x: 2, y: 2, z: 4, core: 2. Of those that a mesh axis runs over, the one named last changes fastest.
Arguments:
- samples: float32 [32, 1024], P(None, ('blk', 'grp')), may hold values from 0 to 256
- bounds: int32 [2, 32, 2048], P(None, None, 'blk'), may hold values from 0 to 256, as said below
- spread: float32 [32], replicated, may hold values from 2 to 8
- counts: int32 [2048], P('blk'), may hold values from 0 to 2047
Outputs:
- log_estimate: float32 [2048], P('blk')
- spread_grad: float32 [32], replicated
The draws below stay inside these ranges and needn't reach their ends.
Inputs may be any that keep to these rules, and one draw needn't show every extreme that they name: For every query and dimension bounds[0] < bounds[1]; each query restricts exactly 3 dimensions to a width of 16 to 48 cells and has bounds 0 and 256 in all others.
All inputs are finite; a program needn't handle non-finite values.
Results may differ from the reference program's by a relative error of at most 0.0003.
Values sent between devices are 32-bit elements; how exact they have to be, the bound alone decides.
No kernel may reach another device: no remote copies, remote signals or barrier semaphores. Data moves between devices by JAX's collectives and lax.ppermute only.
A program may use at most 64 MiB of HBM per device.

```python
import math
import jax
import jax.numpy as jnp
from jax import lax

DIM = 32
GRID = 256
TABLE_ROWS = 1048576
QUERIES = 2048
SAMPLES = 1024


def draw_bounds(key, part):
    key_rank, key_width, key_start = jax.random.split(key, 3)
    scores = jax.random.randint(key_rank, (QUERIES, DIM), 0, 1 << 20) * DIM + jnp.arange(DIM, dtype=jnp.int32)[None, :]
    chosen = lax.top_k(scores, 3)[1]
    picked = jnp.any(chosen[:, :, None] == jnp.arange(DIM, dtype=jnp.int32)[None, None, :], axis=1)
    widths = jax.random.randint(key_width, (QUERIES, DIM), 16, 49)
    starts = jax.random.randint(key_start, (QUERIES, DIM), 0, GRID - widths + 1)
    lower_bound = jnp.where(picked, starts, 0)
    upper_bound = jnp.where(picked, starts + widths, GRID)
    return jnp.stack([lower_bound.T, upper_bound.T]).astype(jnp.int32)


def place_ends(values, own_key, low, high):
    place = [jax.random.randint(jax.random.fold_in(own_key, axis), (), 0, length) for axis, length in enumerate(values.shape)]
    main_axis = values.shape.index(max(values.shape))
    beside = place[:main_axis] + [(place[main_axis] + 1) % values.shape[main_axis]] + place[main_axis + 1:]
    return values.at[tuple(place)].set(low).at[tuple(beside)].set(high)


def block_levels(stream_key, extent, cuts, smallest, largest):
    level = 1.0
    for axis_at, parts in cuts:
        draws = jax.random.uniform(jax.random.fold_in(jax.random.fold_in(stream_key, 6), axis_at), (parts,), jnp.float32, smallest / len(cuts), largest / len(cuts))
        level = level * jnp.repeat(jnp.exp(draws), extent[axis_at] // parts).reshape((-1,) + (1,) * (len(extent) - 1 - axis_at))
    return level


def setup_inputs(seed: int = 0) -> dict:
    key_list = jax.random.split(jax.random.key(seed), 5)
    return {
        "samples": jnp.clip(256.0 * jax.random.uniform(key_list[0], (DIM, SAMPLES), jnp.float32) ** block_levels(key_list[0], (DIM, SAMPLES), ((1, 32),), -0.2, 0.2), 0.0, 256.0),
        "bounds": draw_bounds(jax.random.fold_in(key_list[4], 71), 0),
        "spread": jnp.clip(jnp.exp(jax.random.uniform(key_list[2], (DIM,), jnp.float32, math.log(2.0), math.log(8.0))), 2.0, 8.0),
        "counts": place_ends(jax.random.randint(key_list[3], (QUERIES,), 0, 2048), jax.random.fold_in(key_list[3], 1), 0, 2047).astype(jnp.int32),
    }


root_half = 0.7071067811865476
density_norm = 0.3989422804014327


def box_terms(lower_edge, upper_edge, points, inverse):
    upper_arg = (upper_edge - points) * inverse
    lower_arg = (lower_edge - points) * inverse
    in_box = 0.5 * (lax.erf(upper_arg * root_half) - lax.erf(lower_arg * root_half))
    slopes = density_norm * (lower_arg * jnp.exp(-0.5 * lower_arg * lower_arg) - upper_arg * jnp.exp(-0.5 * upper_arg * upper_arg))
    prefix_prod = jnp.cumprod(in_box, axis=0)
    behind = jnp.flip(jnp.cumprod(jnp.flip(in_box, 0), axis=0), 0)
    unit_row = jnp.ones_like(in_box[:1])
    before = jnp.concatenate([unit_row, prefix_prod[:-1]], 0)
    after_dims = jnp.concatenate([behind[1:], unit_row], 0)
    return prefix_prod[-1], before * after_dims * slopes


def finish(est_sum, counts_float, sample_total, query_total):
    smoothing = 1.0 / TABLE_ROWS
    estimate = est_sum / sample_total
    log_est = jnp.log(estimate + smoothing)
    target = jnp.log(counts_float / TABLE_ROWS + smoothing)
    weight = 2.0 * (log_est - target) / (query_total * (estimate + smoothing))
    return log_est, weight


def reference(samples, bounds, spread, counts):
    lower_edge = bounds[0].astype(jnp.float32)
    upper_edge = bounds[1].astype(jnp.float32)
    inverse = 1.0 / spread
    width_rows = math.gcd(SAMPLES, 64)
    blocks = samples.reshape(DIM, SAMPLES // width_rows, width_rows).transpose(1, 0, 2)

    def advance(running, points):
        totals, gradients = box_terms(lower_edge[:, None, :], upper_edge[:, None, :], points[:, :, None], inverse[:, None, None])
        return (running[0] + totals.sum(axis=0), running[1] + gradients.sum(axis=1)), None

    initial = (jnp.zeros((QUERIES,), jnp.float32), jnp.zeros((DIM, QUERIES), jnp.float32))
    est_sum, grad_sum = lax.scan(advance, initial, blocks)[0]
    log_est, weight = finish(est_sum, counts.astype(jnp.float32), SAMPLES, QUERIES)
    gradient = jnp.dot(grad_sum, weight, precision=lax.Precision.HIGHEST) / SAMPLES
    return log_est, gradient
```

```python
import functools

import jax
import jax.numpy as jnp
from jax import lax
from jax.experimental import pallas as pl
from jax.experimental.pallas import tpu as pltpu
from jax.sharding import PartitionSpec as P

TABLE_ROWS = 1048576
GRID = 256
LIMITED = 3

UNIT = 0.8493218002880191
SLOPE = 0.46971863934982566
TAIL = 0.3249638315990299
POLY = (
    0.11762449816157808,
    0.04671723593777996,
    0.3221625534171999,
    -0.31387568659162657,
    0.4408243890588848,
    -0.11345299389012899,
)


def end_terms(v):
    bell = jnp.exp2(-(v * v))
    t = pl.reciprocal(1.0 + TAIL * jnp.abs(v))
    poly = POLY[-1]
    for factor in POLY[-2::-1]:
        poly = poly * t + factor
    half = 0.5 - poly * t * bell
    return jnp.where(v < 0, -half, half), v * bell


def box_terms(low, high):
    low_erf, low_bell = end_terms(low)
    high_erf, high_bell = end_terms(high)
    return high_erf - low_erf, SLOPE * (low_bell - high_bell)


def split(x, parts):
    out = []
    for _ in range(parts - 1):
        head = x.astype(jnp.bfloat16)
        out.append(head)
        x = x - head.astype(jnp.float32)
    return out + [x.astype(jnp.bfloat16)]


def tree_sum(parts):
    while len(parts) > 1:
        parts = [a + b for a, b in zip(parts[::2], parts[1::2])]
    return parts[0]


def pack_kernel(x_ref, out_ref):
    rows, width = x_ref.shape
    out_ref[...] = jnp.concatenate(
        [x_ref[8 * j : 8 * (j + 1), :] for j in range(rows // 8)], axis=1
    )


def terms_kernel(width, *refs):
    block_refs, (bounds_ref, spread_ref, out_ref, picked, inside) = refs[:-5], refs[-5:]
    dims, queries = bounds_ref.shape[1:]
    total = len(block_refs) * width

    low, high = bounds_ref[0], bounds_ref[1]
    limited = (high - low) != GRID
    low, high = low.astype(jnp.float32), high.astype(jnp.float32)
    at = lax.broadcasted_iota(jnp.int32, (dims, queries), 0)
    first = jnp.min(jnp.where(limited, at, dims), axis=0, keepdims=True)
    last = jnp.max(jnp.where(limited, at, -1), axis=0, keepdims=True)
    is_first, is_last = at == first, at == last
    chosen = [is_first, limited & (at > first) & (at < last), is_last]

    row = lax.broadcasted_iota(jnp.int32, (dims, dims), 0)
    column = lax.broadcasted_iota(jnp.int32, (dims, dims), 1)
    spread = jnp.sum(jnp.where(row == column, spread_ref[...], 0.0), axis=1, keepdims=True)
    unit = UNIT / spread

    pick = lambda mask, values: jnp.sum(jnp.where(mask, values, 0.0), axis=0, keepdims=True)
    low_at = [pick(mask, low) for mask in chosen]
    high_at = [pick(mask, high) for mask in chosen]
    unit_at = [pick(mask, unit) for mask in chosen]

    x = jnp.concatenate(
        [
            jnp.concatenate([ref[:, width * j : width * (j + 1)] for ref in block_refs], axis=1)
            for j in range(dims // 8)
        ],
        axis=0,
    )
    full, full_slope = box_terms(-x * unit, (float(GRID) - x) * unit)
    ratio = full_slope / full
    left = jnp.concatenate(split(x, 3) + split(jnp.log(full), 3), axis=0)

    ones = [mask.astype(jnp.float32).astype(jnp.bfloat16) for mask in chosen]
    free = jnp.where(limited, 0.0, 1.0).astype(jnp.bfloat16)
    none = jnp.zeros_like(free)
    right = jnp.concatenate(
        [jnp.concatenate(ones + [none], axis=1)] * 3
        + [jnp.concatenate([none] * LIMITED + [free], axis=1)] * 3,
        axis=0,
    )
    picked[...] = lax.dot_general(
        left, right, (((0,), (0,)), ((), ())), preferred_element_type=jnp.float32
    )

    def advance(step, sums):
        rows = pl.ds(pl.multiple_of(step * 16, 16), 16)
        others = jnp.exp(picked[rows, LIMITED * queries :])
        mass, slope = [], []
        for k in range(LIMITED):
            points = picked[rows, k * queries : (k + 1) * queries]
            m, s = box_terms((low_at[k] - points) * unit_at[k], (high_at[k] - points) * unit_at[k])
            mass.append(m)
            slope.append(s)
        pair = others * mass[0]
        last_two = pair * mass[1]
        whole = last_two * mass[2]
        head, tail = split(whole, 2)
        inside[rows, :queries] = head
        inside[rows, queries:] = tail
        return (
            sums[0] + whole,
            sums[1] + others * mass[1] * mass[2] * slope[0],
            sums[2] + pair * mass[2] * slope[1],
            sums[3] + last_two * slope[2],
        )

    zero = jnp.zeros((16, queries), jnp.float32)
    sums = lax.fori_loop(0, total // 16, advance, (zero,) * 4, unroll=2)
    sums = [jnp.sum(s, axis=0, keepdims=True) for s in sums]

    ratio = jnp.concatenate(split(ratio, 2), axis=0)
    products = jnp.dot(ratio, inside[...], preferred_element_type=jnp.float32)
    deriv = products[:dims, :queries] + (products[dims:, :queries] + products[:dims, queries:])
    deriv = jnp.where(limited, 0.0, deriv)
    for mask, s in zip(chosen, sums[1:]):
        deriv = jnp.where(mask, s, deriv)
    out_ref[:dims, :] = deriv
    out_ref[dims:, :] = jnp.broadcast_to(sums[0], (8, queries))


def finish_kernel(sample_total, query_total, *refs):
    part_refs, (counts_ref, log_ref, share_ref) = refs[:-3], refs[-3:]
    whole = tree_sum([ref[...] for ref in part_refs])
    dims, queries = whole.shape[0] - 8, whole.shape[1]
    smoothing = 1.0 / TABLE_ROWS
    estimate = whole[dims : dims + 1] / sample_total
    log_est = jnp.log(estimate + smoothing)
    log_ref[...] = log_est
    target = jnp.log(counts_ref[...].astype(jnp.float32) / TABLE_ROWS + smoothing)
    weight = 2.0 * (log_est - target) / (query_total * (estimate + smoothing))
    terms = whole[:dims] * (weight / sample_total)
    terms = jnp.concatenate([terms, jnp.zeros((queries - dims, queries), jnp.float32)], axis=0)
    share_ref[...] = jnp.sum(terms.T, axis=0, keepdims=True)


def add_kernel(*refs):
    refs[-1][...] = tree_sum([ref[...] for ref in refs[:-1]])


def everyone(x, axis):
    size = lax.axis_size(axis)
    return [x] + [
        lax.ppermute(x, axis, [(i, i ^ offset) for i in range(size)]) for offset in range(1, size)
    ]


def call(kernel, args, outs, scratch=()):
    single = len(outs) == 1
    return pl.pallas_call(
        kernel,
        out_shape=outs[0] if single else outs,
        in_specs=[pl.BlockSpec(memory_space=pltpu.VMEM)] * len(args),
        out_specs=pl.BlockSpec(memory_space=pltpu.VMEM)
        if single
        else [pl.BlockSpec(memory_space=pltpu.VMEM)] * len(outs),
        scratch_shapes=list(scratch),
        compiler_params=pltpu.CompilerParams(vmem_limit_bytes=32 << 20),
    )(*args)


def shape(*sizes):
    return jax.ShapeDtypeStruct(sizes, jnp.float32)


def on_device(samples, bounds, spread, counts):
    dims, width = samples.shape
    queries = bounds.shape[2]
    blocks = lax.axis_size("blk")
    sample_total = width * blocks * lax.axis_size("grp")
    query_total = queries * blocks
    total = width * blocks

    packed = call(pack_kernel, [samples], [shape(8, dims * width // 8)])
    gathered = everyone(packed, "blk")
    part = call(
        functools.partial(terms_kernel, width),
        gathered + [bounds, spread.reshape(1, dims)],
        [shape(dims + 8, queries)],
        [
            pltpu.VMEM((total, (LIMITED + 1) * queries), jnp.float32),
            pltpu.VMEM((total, 2 * queries), jnp.bfloat16),
        ],
    )
    parts = everyone(part, "grp")
    log_est, share = call(
        functools.partial(finish_kernel, sample_total, query_total),
        parts + [counts.reshape(1, queries)],
        [shape(1, queries), shape(1, queries)],
    )
    gradient = call(add_kernel, everyone(share, "blk"), [shape(1, queries)])
    return log_est.reshape(queries), gradient[0, :dims]


def solution(mesh):
    return jax.shard_map(
        on_device,
        mesh=mesh,
        in_specs=(P(None, ("blk", "grp")), P(None, None, "blk"), P(), P("blk")),
        out_specs=(P("blk"), P()),
        check_vma=False,
    )
```

```python
import functools

import jax
import jax.numpy as jnp
from jax import lax
from jax.experimental import pallas as pl
from jax.experimental.pallas import tpu as pltpu
from jax.sharding import PartitionSpec as P

TABLE_ROWS = 1048576
GRID = 256
LIMITED = 3

UNIT = 0.8493218002880191
SLOPE = 0.46971863934982566
TAIL = 0.3249638315990299
POLY = (
    0.11762449816157808,
    0.04671723593777996,
    0.3221625534171999,
    -0.31387568659162657,
    0.4408243890588848,
    -0.11345299389012899,
)


def end_terms(v):
    bell = jnp.exp2(-(v * v))
    t = pl.reciprocal(1.0 + TAIL * jnp.abs(v))
    poly = POLY[-1]
    for factor in POLY[-2::-1]:
        poly = poly * t + factor
    half = 0.5 - poly * t * bell
    return jnp.where(v < 0, -half, half), v * bell


def box_terms(low, high):
    low_erf, low_bell = end_terms(low)
    high_erf, high_bell = end_terms(high)
    return high_erf - low_erf, SLOPE * (low_bell - high_bell)


def split(x, parts):
    out = []
    for _ in range(parts - 1):
        head = x.astype(jnp.bfloat16)
        out.append(head)
        x = x - head.astype(jnp.float32)
    return out + [x.astype(jnp.bfloat16)]


def tree_sum(parts):
    while len(parts) > 1:
        parts = [a + b for a, b in zip(parts[::2], parts[1::2])]
    return parts[0]


def pack_kernel(x_ref, out_ref):
    rows, width = x_ref.shape
    packed = jnp.concatenate([x_ref[8 * j : 8 * (j + 1), :] for j in range(rows // 8)], axis=1)
    for peer in range(out_ref.shape[0]):
        out_ref[peer] = packed


def terms_kernel(width, blocks_ref, bounds_ref, spread_ref, out_ref, picked, inside):
    dims, queries = bounds_ref.shape[1:]
    total = blocks_ref.shape[0] * width

    low, high = bounds_ref[0], bounds_ref[1]
    limited = (high - low) != GRID
    low, high = low.astype(jnp.float32), high.astype(jnp.float32)
    at = lax.broadcasted_iota(jnp.int32, (dims, queries), 0)
    first = jnp.min(jnp.where(limited, at, dims), axis=0, keepdims=True)
    last = jnp.max(jnp.where(limited, at, -1), axis=0, keepdims=True)
    is_first, is_last = at == first, at == last
    chosen = [is_first, limited & (at > first) & (at < last), is_last]

    row = lax.broadcasted_iota(jnp.int32, (dims, dims), 0)
    column = lax.broadcasted_iota(jnp.int32, (dims, dims), 1)
    spread = jnp.sum(jnp.where(row == column, spread_ref[...], 0.0), axis=1, keepdims=True)
    unit = UNIT / spread

    pick = lambda mask, values: jnp.sum(jnp.where(mask, values, 0.0), axis=0, keepdims=True)
    low_at = [pick(mask, low) for mask in chosen]
    high_at = [pick(mask, high) for mask in chosen]
    unit_at = [pick(mask, unit) for mask in chosen]

    x = jnp.concatenate(
        [
            jnp.concatenate(
                [blocks_ref[b, :, width * j : width * (j + 1)] for b in range(blocks_ref.shape[0])],
                axis=1,
            )
            for j in range(dims // 8)
        ],
        axis=0,
    )
    full, full_slope = box_terms(-x * unit, (float(GRID) - x) * unit)
    ratio = full_slope / full
    left = jnp.concatenate(split(x, 3) + split(jnp.log(full), 3), axis=0)

    ones = [mask.astype(jnp.float32).astype(jnp.bfloat16) for mask in chosen]
    free = jnp.where(limited, 0.0, 1.0).astype(jnp.bfloat16)
    none = jnp.zeros_like(free)
    right = jnp.concatenate(
        [jnp.concatenate(ones + [none], axis=1)] * 3
        + [jnp.concatenate([none] * LIMITED + [free], axis=1)] * 3,
        axis=0,
    )
    picked[...] = lax.dot_general(
        left, right, (((0,), (0,)), ((), ())), preferred_element_type=jnp.float32
    )

    def advance(step, sums):
        rows = pl.ds(pl.multiple_of(step * 16, 16), 16)
        others = jnp.exp(picked[rows, LIMITED * queries :])
        mass, slope = [], []
        for k in range(LIMITED):
            points = picked[rows, k * queries : (k + 1) * queries]
            m, s = box_terms((low_at[k] - points) * unit_at[k], (high_at[k] - points) * unit_at[k])
            mass.append(m)
            slope.append(s)
        pair = others * mass[0]
        last_two = pair * mass[1]
        whole = last_two * mass[2]
        head, tail = split(whole, 2)
        inside[rows, :queries] = head
        inside[rows, queries:] = tail
        return (
            sums[0] + whole,
            sums[1] + others * mass[1] * mass[2] * slope[0],
            sums[2] + pair * mass[2] * slope[1],
            sums[3] + last_two * slope[2],
        )

    zero = jnp.zeros((16, queries), jnp.float32)
    sums = lax.fori_loop(0, total // 16, advance, (zero,) * 4, unroll=2)
    sums = [jnp.sum(s, axis=0, keepdims=True) for s in sums]

    ratio = jnp.concatenate(split(ratio, 2), axis=0)
    products = jnp.dot(ratio, inside[...], preferred_element_type=jnp.float32)
    deriv = products[:dims, :queries] + (products[dims:, :queries] + products[:dims, queries:])
    deriv = jnp.where(limited, 0.0, deriv)
    for mask, s in zip(chosen, sums[1:]):
        deriv = jnp.where(mask, s, deriv)
    out_ref[:dims, :] = deriv
    out_ref[dims:, :] = jnp.broadcast_to(sums[0], (8, queries))


def finish_kernel(sample_total, query_total, *refs):
    part_refs, (counts_ref, log_ref, share_ref) = refs[:-3], refs[-3:]
    whole = tree_sum([ref[...] for ref in part_refs])
    dims, queries = whole.shape[0] - 8, whole.shape[1]
    smoothing = 1.0 / TABLE_ROWS
    estimate = whole[dims : dims + 1] / sample_total
    log_est = jnp.log(estimate + smoothing)
    log_ref[...] = log_est
    target = jnp.log(counts_ref[...].astype(jnp.float32) / TABLE_ROWS + smoothing)
    weight = 2.0 * (log_est - target) / (query_total * (estimate + smoothing))
    terms = whole[:dims] * (weight / sample_total)
    terms = jnp.concatenate([terms, jnp.zeros((queries - dims, queries), jnp.float32)], axis=0)
    share = jnp.sum(terms.T, axis=0, keepdims=True)
    for peer in range(share_ref.shape[0]):
        share_ref[peer] = share


def add_kernel(shares_ref, out_ref):
    out_ref[...] = tree_sum([shares_ref[peer] for peer in range(shares_ref.shape[0])])


def everyone(x, axis):
    size = lax.axis_size(axis)
    return [x] + [
        lax.ppermute(x, axis, [(i, i ^ offset) for i in range(size)]) for offset in range(1, size)
    ]


def call(kernel, args, outs, scratch=()):
    single = len(outs) == 1
    return pl.pallas_call(
        kernel,
        out_shape=outs[0] if single else outs,
        in_specs=[pl.BlockSpec(memory_space=pltpu.VMEM)] * len(args),
        out_specs=pl.BlockSpec(memory_space=pltpu.VMEM)
        if single
        else [pl.BlockSpec(memory_space=pltpu.VMEM)] * len(outs),
        scratch_shapes=list(scratch),
        compiler_params=pltpu.CompilerParams(vmem_limit_bytes=32 << 20),
    )(*args)


def shape(*sizes):
    return jax.ShapeDtypeStruct(sizes, jnp.float32)


def on_device(samples, bounds, spread, counts):
    dims, width = samples.shape
    queries = bounds.shape[2]
    blocks = lax.axis_size("blk")
    sample_total = width * blocks * lax.axis_size("grp")
    query_total = queries * blocks
    total = width * blocks

    packed = call(pack_kernel, [samples], [shape(blocks, 8, dims * width // 8)])
    gathered = lax.all_to_all(packed, "blk", 0, 0)
    part = call(
        functools.partial(terms_kernel, width),
        [gathered, bounds, spread.reshape(1, dims)],
        [shape(dims + 8, queries)],
        [
            pltpu.VMEM((total, (LIMITED + 1) * queries), jnp.float32),
            pltpu.VMEM((total, 2 * queries), jnp.bfloat16),
        ],
    )
    parts = everyone(part, "grp")
    log_est, share = call(
        functools.partial(finish_kernel, sample_total, query_total),
        parts + [counts.reshape(1, queries)],
        [shape(1, queries), shape(blocks, 1, queries)],
    )
    shares = lax.all_to_all(share, "blk", 0, 0)
    gradient = call(add_kernel, [shares], [shape(1, queries)])
    return log_est.reshape(queries), gradient[0, :dims]


def solution(mesh):
    return jax.shard_map(
        on_device,
        mesh=mesh,
        in_specs=(P(None, ("blk", "grp")), P(None, None, "blk"), P(), P("blk")),
        out_specs=(P("blk"), P()),
        check_vma=False,
    )
```

```python
import functools

import jax
import jax.numpy as jnp
from jax import lax
from jax.experimental import pallas as pl
from jax.experimental.pallas import tpu as pltpu
from jax.sharding import PartitionSpec as P

TABLE_ROWS = 1048576
GRID = 256
LIMITED = 3

UNIT = 0.8493218002880191
SLOPE = 0.46971863934982566
TAIL = 0.3249638315990299
POLY = (
    0.11762449816157808,
    0.04671723593777996,
    0.3221625534171999,
    -0.31387568659162657,
    0.4408243890588848,
    -0.11345299389012899,
)


def end_terms(v):
    bell = jnp.exp2(-(v * v))
    t = pl.reciprocal(1.0 + TAIL * jnp.abs(v))
    poly = POLY[-1]
    for factor in POLY[-2::-1]:
        poly = poly * t + factor
    half = 0.5 - poly * t * bell
    return jnp.where(v < 0, -half, half), v * bell


def box_terms(low, high):
    low_erf, low_bell = end_terms(low)
    high_erf, high_bell = end_terms(high)
    return high_erf - low_erf, SLOPE * (low_bell - high_bell)


def split(x, parts):
    out = []
    for _ in range(parts - 1):
        head = x.astype(jnp.bfloat16)
        out.append(head)
        x = x - head.astype(jnp.float32)
    return out + [x.astype(jnp.bfloat16)]


def tree_sum(parts):
    while len(parts) > 1:
        parts = [a + b for a, b in zip(parts[::2], parts[1::2])]
    return parts[0]


def pack_kernel(x_ref, out_ref):
    rows, width = x_ref.shape
    out_ref[0] = jnp.concatenate(
        [x_ref[8 * j : 8 * (j + 1), :] for j in range(rows // 8)], axis=1
    )


def join_kernel(a_ref, b_ref, out_ref):
    half = a_ref.shape[0]
    out_ref[:half] = a_ref[...]
    out_ref[half:] = b_ref[...]


def terms_kernel(width, blocks_ref, bounds_ref, spread_ref, out_ref, picked, inside):
    dims, queries = bounds_ref.shape[1:]
    total = blocks_ref.shape[0] * width

    low, high = bounds_ref[0], bounds_ref[1]
    limited = (high - low) != GRID
    low, high = low.astype(jnp.float32), high.astype(jnp.float32)
    at = lax.broadcasted_iota(jnp.int32, (dims, queries), 0)
    first = jnp.min(jnp.where(limited, at, dims), axis=0, keepdims=True)
    last = jnp.max(jnp.where(limited, at, -1), axis=0, keepdims=True)
    is_first, is_last = at == first, at == last
    chosen = [is_first, limited & (at > first) & (at < last), is_last]

    row = lax.broadcasted_iota(jnp.int32, (dims, dims), 0)
    column = lax.broadcasted_iota(jnp.int32, (dims, dims), 1)
    spread = jnp.sum(jnp.where(row == column, spread_ref[...], 0.0), axis=1, keepdims=True)
    unit = UNIT / spread

    pick = lambda mask, values: jnp.sum(jnp.where(mask, values, 0.0), axis=0, keepdims=True)
    low_at = [pick(mask, low) for mask in chosen]
    high_at = [pick(mask, high) for mask in chosen]
    unit_at = [pick(mask, unit) for mask in chosen]

    x = jnp.concatenate(
        [
            jnp.concatenate(
                [blocks_ref[b, :, width * j : width * (j + 1)] for b in range(blocks_ref.shape[0])],
                axis=1,
            )
            for j in range(dims // 8)
        ],
        axis=0,
    )
    full, full_slope = box_terms(-x * unit, (float(GRID) - x) * unit)
    ratio = full_slope / full
    left = jnp.concatenate(split(x, 3) + split(jnp.log(full), 3), axis=0)

    ones = [mask.astype(jnp.float32).astype(jnp.bfloat16) for mask in chosen]
    free = jnp.where(limited, 0.0, 1.0).astype(jnp.bfloat16)
    none = jnp.zeros_like(free)
    right = jnp.concatenate(
        [jnp.concatenate(ones + [none], axis=1)] * 3
        + [jnp.concatenate([none] * LIMITED + [free], axis=1)] * 3,
        axis=0,
    )
    picked[...] = lax.dot_general(
        left, right, (((0,), (0,)), ((), ())), preferred_element_type=jnp.float32
    )

    def advance(step, sums):
        rows = pl.ds(pl.multiple_of(step * 16, 16), 16)
        others = jnp.exp(picked[rows, LIMITED * queries :])
        mass, slope = [], []
        for k in range(LIMITED):
            points = picked[rows, k * queries : (k + 1) * queries]
            m, s = box_terms((low_at[k] - points) * unit_at[k], (high_at[k] - points) * unit_at[k])
            mass.append(m)
            slope.append(s)
        pair = others * mass[0]
        last_two = pair * mass[1]
        whole = last_two * mass[2]
        head, tail = split(whole, 2)
        inside[rows, :queries] = head
        inside[rows, queries:] = tail
        return (
            sums[0] + whole,
            sums[1] + others * mass[1] * mass[2] * slope[0],
            sums[2] + pair * mass[2] * slope[1],
            sums[3] + last_two * slope[2],
        )

    zero = jnp.zeros((16, queries), jnp.float32)
    sums = lax.fori_loop(0, total // 16, advance, (zero,) * 4, unroll=2)
    sums = [jnp.sum(s, axis=0, keepdims=True) for s in sums]

    ratio = jnp.concatenate(split(ratio, 2), axis=0)
    products = jnp.dot(ratio, inside[...], preferred_element_type=jnp.float32)
    deriv = products[:dims, :queries] + (products[dims:, :queries] + products[:dims, queries:])
    deriv = jnp.where(limited, 0.0, deriv)
    for mask, s in zip(chosen, sums[1:]):
        deriv = jnp.where(mask, s, deriv)
    out_ref[:dims, :] = deriv
    out_ref[dims:, :] = jnp.broadcast_to(sums[0], (8, queries))


def finish_kernel(sample_total, query_total, *refs):
    part_refs, (counts_ref, log_ref, share_ref) = refs[:-3], refs[-3:]
    whole = tree_sum([ref[...] for ref in part_refs])
    dims, queries = whole.shape[0] - 8, whole.shape[1]
    smoothing = 1.0 / TABLE_ROWS
    estimate = whole[dims : dims + 1] / sample_total
    log_est = jnp.log(estimate + smoothing)
    log_ref[...] = log_est
    target = jnp.log(counts_ref[...].astype(jnp.float32) / TABLE_ROWS + smoothing)
    weight = 2.0 * (log_est - target) / (query_total * (estimate + smoothing))
    terms = whole[:dims] * (weight / sample_total)
    terms = jnp.concatenate([terms, jnp.zeros((queries - dims, queries), jnp.float32)], axis=0)
    share = jnp.sum(terms.T, axis=0, keepdims=True)
    for peer in range(share_ref.shape[0]):
        share_ref[peer] = share


def add_kernel(shares_ref, out_ref):
    total = tree_sum([shares_ref[peer] for peer in range(shares_ref.shape[0])])
    for peer in range(out_ref.shape[0]):
        out_ref[peer] = total


def everyone(x, axis):
    size = lax.axis_size(axis)
    return [x] + [
        lax.ppermute(x, axis, [(i, i ^ offset) for i in range(size)]) for offset in range(1, size)
    ]


def gather(x, axis):
    size = lax.axis_size(axis)
    offset = 1
    while offset < size:
        other = lax.ppermute(x, axis, [(i, i ^ offset) for i in range(size)])
        x = call(join_kernel, [x, other], [shape(2 * x.shape[0], *x.shape[1:])])
        offset *= 2
    return x


def call(kernel, args, outs, scratch=()):
    single = len(outs) == 1
    return pl.pallas_call(
        kernel,
        out_shape=outs[0] if single else outs,
        in_specs=[pl.BlockSpec(memory_space=pltpu.VMEM)] * len(args),
        out_specs=pl.BlockSpec(memory_space=pltpu.VMEM)
        if single
        else [pl.BlockSpec(memory_space=pltpu.VMEM)] * len(outs),
        scratch_shapes=list(scratch),
        compiler_params=pltpu.CompilerParams(vmem_limit_bytes=32 << 20),
    )(*args)


def shape(*sizes):
    return jax.ShapeDtypeStruct(sizes, jnp.float32)


def on_device(samples, bounds, spread, counts):
    dims, width = samples.shape
    queries = bounds.shape[2]
    blocks = lax.axis_size("blk")
    sample_total = width * blocks * lax.axis_size("grp")
    query_total = queries * blocks
    total = width * blocks
    inner = 4
    outer = blocks // inner

    packed = call(pack_kernel, [samples], [shape(1, 8, dims * width // 8)])
    gathered = gather(packed, "blk")
    part = call(
        functools.partial(terms_kernel, width),
        [gathered, bounds, spread.reshape(1, dims)],
        [shape(dims + 8, queries)],
        [
            pltpu.VMEM((total, (LIMITED + 1) * queries), jnp.float32),
            pltpu.VMEM((total, 2 * queries), jnp.bfloat16),
        ],
    )
    parts = everyone(part, "grp")
    log_est, share = call(
        functools.partial(finish_kernel, sample_total, query_total),
        parts + [counts.reshape(1, queries)],
        [shape(1, queries), shape(inner, 1, queries)],
    )
    near = [[o * inner + i for i in range(inner)] for o in range(outer)]
    far = [[o * inner + i for o in range(outer)] for i in range(inner)]
    shares = lax.all_to_all(share, "blk", 0, 0, axis_index_groups=near)
    share = call(add_kernel, [shares], [shape(outer, 1, queries)])
    shares = lax.all_to_all(share, "blk", 0, 0, axis_index_groups=far)
    gradient = call(add_kernel, [shares], [shape(1, 1, queries)])
    return log_est.reshape(queries), gradient[0, 0, :dims]


def solution(mesh):
    return jax.shard_map(
        on_device,
        mesh=mesh,
        in_specs=(P(None, ("blk", "grp")), P(None, None, "blk"), P(), P("blk")),
        out_specs=(P("blk"), P()),
        check_vma=False,
    )
```

```python
import functools

import jax
import jax.numpy as jnp
from jax import lax
from jax.experimental import pallas as pl
from jax.experimental.pallas import tpu as pltpu
from jax.sharding import PartitionSpec as P

TABLE_ROWS = 1048576
GRID = 256
LIMITED = 3

UNIT = 0.8493218002880191
SLOPE = 0.46971863934982566
TAIL = 0.3249638315990299
POLY = (
    0.11762449816157808,
    0.04671723593777996,
    0.3221625534171999,
    -0.31387568659162657,
    0.4408243890588848,
    -0.11345299389012899,
)


def end_terms(v):
    bell = jnp.exp2(-(v * v))
    t = pl.reciprocal(1.0 + TAIL * jnp.abs(v))
    poly = POLY[-1]
    for factor in POLY[-2::-1]:
        poly = poly * t + factor
    half = 0.5 - poly * t * bell
    return jnp.where(v < 0, -half, half), v * bell


def box_terms(low, high):
    low_erf, low_bell = end_terms(low)
    high_erf, high_bell = end_terms(high)
    return high_erf - low_erf, SLOPE * (low_bell - high_bell)


def split(x, parts):
    out = []
    for _ in range(parts - 1):
        head = x.astype(jnp.bfloat16)
        out.append(head)
        x = x - head.astype(jnp.float32)
    return out + [x.astype(jnp.bfloat16)]


def tree_sum(parts):
    while len(parts) > 1:
        parts = [a + b for a, b in zip(parts[::2], parts[1::2])]
    return parts[0]


def pack_kernel(x_ref, out_ref):
    rows, width = x_ref.shape
    out_ref[...] = jnp.concatenate(
        [x_ref[8 * j : 8 * (j + 1), :] for j in range(rows // 8)], axis=1
    )


def terms_kernel(
    width, query_total, copies,
    blocks_ref, bounds_ref, spread_ref, counts_ref, log_ref, share_ref, picked, inside,
):
    dims, queries = bounds_ref.shape[1:]
    total = blocks_ref.shape[0] * width
    group = picked.shape[0] // width

    low, high = bounds_ref[0], bounds_ref[1]
    limited = (high - low) != GRID
    low, high = low.astype(jnp.float32), high.astype(jnp.float32)
    at = lax.broadcasted_iota(jnp.int32, (dims, queries), 0)
    first = jnp.min(jnp.where(limited, at, dims), axis=0, keepdims=True)
    last = jnp.max(jnp.where(limited, at, -1), axis=0, keepdims=True)
    is_first, is_last = at == first, at == last
    chosen = [is_first, limited & (at > first) & (at < last), is_last]

    row = lax.broadcasted_iota(jnp.int32, (dims, dims), 0)
    column = lax.broadcasted_iota(jnp.int32, (dims, dims), 1)
    spread = jnp.sum(jnp.where(row == column, spread_ref[...], 0.0), axis=1, keepdims=True)
    unit = UNIT / spread

    pick = lambda mask, values: jnp.sum(jnp.where(mask, values, 0.0), axis=0, keepdims=True)
    low_at = [pick(mask, low) for mask in chosen]
    high_at = [pick(mask, high) for mask in chosen]
    unit_at = [pick(mask, unit) for mask in chosen]

    ones = [mask.astype(jnp.float32).astype(jnp.bfloat16) for mask in chosen]
    free = jnp.where(limited, 0.0, 1.0).astype(jnp.bfloat16)
    none = jnp.zeros_like(free)
    right = jnp.concatenate(
        [jnp.concatenate(ones + [none], axis=1)] * 3
        + [jnp.concatenate([none] * LIMITED + [free], axis=1)] * 3,
        axis=0,
    )
    def advance(step, sums):
        rows = pl.ds(pl.multiple_of(step * 16, 16), 16)
        others = jnp.exp(picked[rows, LIMITED * queries :])
        mass, slope = [], []
        for k in range(LIMITED):
            points = picked[rows, k * queries : (k + 1) * queries]
            m, s = box_terms((low_at[k] - points) * unit_at[k], (high_at[k] - points) * unit_at[k])
            mass.append(m)
            slope.append(s)
        pair = others * mass[0]
        last_two = pair * mass[1]
        whole = last_two * mass[2]
        head, tail = split(whole, 2)
        inside[rows, :queries] = head
        inside[rows, queries:] = tail
        return (
            sums[0] + whole,
            sums[1] + others * mass[1] * mass[2] * slope[0],
            sums[2] + pair * mass[2] * slope[1],
            sums[3] + last_two * slope[2],
        )

    def chunk(number, totals):
        sums, deriv = totals[:-1], totals[-1]
        some = [blocks_ref[number * group + b] for b in range(group)]
        x = jnp.concatenate(
            [
                jnp.concatenate([block[:, width * j : width * (j + 1)] for block in some], axis=1)
                for j in range(dims // 8)
            ],
            axis=0,
        )
        full, full_slope = box_terms(-x * unit, (float(GRID) - x) * unit)
        left = jnp.concatenate(split(x, 3) + split(jnp.log(full), 3), axis=0)
        picked[...] = lax.dot_general(
            left, right, (((0,), (0,)), ((), ())), preferred_element_type=jnp.float32
        )
        sums = lax.fori_loop(0, group * width // 16, advance, sums, unroll=2)
        ratio = jnp.concatenate(split(full_slope / full, 2), axis=0)
        products = jnp.dot(ratio, inside[...], preferred_element_type=jnp.float32)
        deriv = deriv + (
            products[:dims, :queries] + (products[dims:, :queries] + products[:dims, queries:])
        )
        return (*sums, deriv)

    zero = jnp.zeros((16, queries), jnp.float32)
    totals = (zero,) * (1 + LIMITED) + (jnp.zeros((dims, queries), jnp.float32),)
    chunks = blocks_ref.shape[0] // group
    if chunks <= 2:
        for number in range(chunks):
            totals = chunk(number, totals)
    else:
        totals = lax.fori_loop(0, chunks, chunk, totals)
    sums = [jnp.sum(s, axis=0, keepdims=True) for s in totals[:-1]]
    deriv = jnp.where(limited, 0.0, totals[-1])
    for mask, s in zip(chosen, sums[1:]):
        deriv = jnp.where(mask, s, deriv)
    log_est, share = finish(
        jnp.concatenate([deriv, sums[0]], axis=0), counts_ref[...], total, query_total
    )
    log_ref[...] = log_est
    share_ref[...] = share * (1.0 / copies)


def finish(whole, counts, sample_total, query_total):
    dims, queries = whole.shape[0] - 1, whole.shape[1]
    smoothing = 1.0 / TABLE_ROWS
    estimate = whole[dims:] / sample_total
    log_est = jnp.log(estimate + smoothing)
    target = jnp.log(counts.astype(jnp.float32) / TABLE_ROWS + smoothing)
    weight = 2.0 * (log_est - target) / (query_total * (estimate + smoothing))
    terms = whole[:dims] * (weight / sample_total)
    terms = jnp.concatenate([terms, jnp.zeros((queries - dims, queries), jnp.float32)], axis=0)
    return log_est, jnp.sum(terms.T, axis=0, keepdims=True)


def call(kernel, args, outs, scratch=()):
    single = len(outs) == 1
    return pl.pallas_call(
        kernel,
        out_shape=outs[0] if single else outs,
        in_specs=[pl.BlockSpec(memory_space=pltpu.VMEM)] * len(args),
        out_specs=pl.BlockSpec(memory_space=pltpu.VMEM)
        if single
        else [pl.BlockSpec(memory_space=pltpu.VMEM)] * len(outs),
        scratch_shapes=list(scratch),
        compiler_params=pltpu.CompilerParams(vmem_limit_bytes=32 << 20),
    )(*args)


def shape(*sizes):
    return jax.ShapeDtypeStruct(sizes, jnp.float32)


def on_device(samples, bounds, spread, counts):
    dims, width = samples.shape
    queries = bounds.shape[2]
    blocks = lax.axis_size("blk")
    copies = lax.axis_size("grp")
    query_total = queries * blocks
    rows = width * min(blocks * copies, 16)

    packed = call(pack_kernel, [samples], [shape(8, dims * width // 8)])
    gathered = lax.all_gather(packed, ("blk", "grp"))
    log_est, share = call(
        functools.partial(terms_kernel, width, query_total, copies),
        [gathered, bounds, spread.reshape(1, dims), counts.reshape(1, queries)],
        [shape(1, queries), shape(1, queries)],
        [
            pltpu.VMEM((rows, (LIMITED + 1) * queries), jnp.float32),
            pltpu.VMEM((rows, 2 * queries), jnp.bfloat16),
        ],
    )
    gradient = lax.psum(share, ("blk", "grp"))
    return log_est.reshape(queries), gradient[0, :dims]


def solution(mesh):
    return jax.shard_map(
        on_device,
        mesh=mesh,
        in_specs=(P(None, ("blk", "grp")), P(None, None, "blk"), P(), P("blk")),
        out_specs=(P("blk"), P()),
        check_vma=False,
    )
```

```python
import functools

import jax
import jax.numpy as jnp
from jax import lax
from jax.experimental import pallas as pl
from jax.experimental.pallas import tpu as pltpu
from jax.sharding import PartitionSpec as P

TABLE_ROWS = 1048576
GRID = 256
LIMITED = 3

UNIT = 0.8493218002880191
SLOPE = 0.46971863934982566
ERF_UNIT = 0.8325546111576977


def end_terms(v):
    bell = jnp.exp2(-(v * v))
    return 0.5 * lax.erf(v * ERF_UNIT), v * bell


def box_terms(low, high):
    low_erf, low_bell = end_terms(low)
    high_erf, high_bell = end_terms(high)
    return high_erf - low_erf, SLOPE * (low_bell - high_bell)


def split(x, parts):
    out = []
    for _ in range(parts - 1):
        head = x.astype(jnp.bfloat16)
        out.append(head)
        x = x - head.astype(jnp.float32)
    return out + [x.astype(jnp.bfloat16)]


def tree_sum(parts):
    while len(parts) > 1:
        parts = [a + b for a, b in zip(parts[::2], parts[1::2])]
    return parts[0]


def pack_kernel(x_ref, bounds_ref, spread_ref, counts_ref, out_ref, target_ref):
    rows, width = x_ref.shape
    packed = jnp.concatenate([x_ref[8 * j : 8 * (j + 1), :] for j in range(rows // 8)], axis=1)
    for peer in range(out_ref.shape[0]):
        out_ref[peer] = packed
    smoothing = 1.0 / TABLE_ROWS
    target_ref[...] = jnp.log(counts_ref[...].astype(jnp.float32) / TABLE_ROWS + smoothing)


def terms_kernel(width, blocks_ref, bounds_ref, spread_ref, out_ref, picked, inside):
    dims, queries = bounds_ref.shape[1:]
    total = blocks_ref.shape[0] * width

    low, high = bounds_ref[0], bounds_ref[1]
    limited = (high - low) != GRID
    low, high = low.astype(jnp.float32), high.astype(jnp.float32)
    at = lax.broadcasted_iota(jnp.int32, (dims, queries), 0)
    first = jnp.min(jnp.where(limited, at, dims), axis=0, keepdims=True)
    last = jnp.max(jnp.where(limited, at, -1), axis=0, keepdims=True)
    is_first, is_last = at == first, at == last
    chosen = [is_first, limited & (at > first) & (at < last), is_last]

    row = lax.broadcasted_iota(jnp.int32, (dims, dims), 0)
    column = lax.broadcasted_iota(jnp.int32, (dims, dims), 1)
    spread = jnp.sum(jnp.where(row == column, spread_ref[...], 0.0), axis=1, keepdims=True)
    unit = UNIT / spread

    pick = lambda mask, values: jnp.sum(jnp.where(mask, values, 0.0), axis=0, keepdims=True)
    low_at = [pick(mask, low) for mask in chosen]
    high_at = [pick(mask, high) for mask in chosen]
    unit_at = [pick(mask, unit) for mask in chosen]

    x = jnp.concatenate(
        [
            jnp.concatenate(
                [blocks_ref[b, :, width * j : width * (j + 1)] for b in range(blocks_ref.shape[0])],
                axis=1,
            )
            for j in range(dims // 8)
        ],
        axis=0,
    )
    full, full_slope = box_terms(-x * unit, (float(GRID) - x) * unit)
    ratio = full_slope / full
    left = jnp.concatenate(split(x, 3) + split(jnp.log(full), 3), axis=0)

    ones = [mask.astype(jnp.float32).astype(jnp.bfloat16) for mask in chosen]
    free = jnp.where(limited, 0.0, 1.0).astype(jnp.bfloat16)
    none = jnp.zeros_like(free)
    right = jnp.concatenate(
        [jnp.concatenate(ones + [none], axis=1)] * 3
        + [jnp.concatenate([none] * LIMITED + [free], axis=1)] * 3,
        axis=0,
    )
    picked[...] = lax.dot_general(
        left, right, (((0,), (0,)), ((), ())), preferred_element_type=jnp.float32
    )

    def advance(step, sums):
        rows = pl.ds(pl.multiple_of(step * 16, 16), 16)
        others = jnp.exp(picked[rows, LIMITED * queries :])
        mass, slope = [], []
        for k in range(LIMITED):
            points = picked[rows, k * queries : (k + 1) * queries]
            m, s = box_terms((low_at[k] - points) * unit_at[k], (high_at[k] - points) * unit_at[k])
            mass.append(m)
            slope.append(s)
        pair = others * mass[0]
        last_two = pair * mass[1]
        whole = last_two * mass[2]
        head, tail = split(whole, 2)
        inside[rows, :queries] = head
        inside[rows, queries:] = tail
        return (
            sums[0] + whole,
            sums[1] + others * mass[1] * mass[2] * slope[0],
            sums[2] + pair * mass[2] * slope[1],
            sums[3] + last_two * slope[2],
        )

    zero = jnp.zeros((16, queries), jnp.float32)
    sums = lax.fori_loop(0, total // 16, advance, (zero,) * 4, unroll=2)
    sums = [jnp.sum(s, axis=0, keepdims=True) for s in sums]

    ratio = jnp.concatenate(split(ratio, 2), axis=0)
    products = jnp.dot(ratio, inside[...], preferred_element_type=jnp.float32)
    deriv = products[:dims, :queries] + (products[dims:, :queries] + products[:dims, queries:])
    deriv = jnp.where(limited, 0.0, deriv)
    for mask, s in zip(chosen, sums[1:]):
        deriv = jnp.where(mask, s, deriv)
    out_ref[:dims, :] = deriv
    out_ref[dims:, :] = jnp.broadcast_to(sums[0], (8, queries))


def finish_kernel(sample_total, query_total, *refs):
    part_refs, (target_ref, log_ref, share_ref) = refs[:-3], refs[-3:]
    whole = tree_sum([ref[...] for ref in part_refs])
    dims, queries = whole.shape[0] - 8, whole.shape[1]
    smoothing = 1.0 / TABLE_ROWS
    estimate = whole[dims : dims + 1] / sample_total
    log_est = jnp.log(estimate + smoothing)
    log_ref[...] = log_est
    weight = 2.0 * (log_est - target_ref[...]) / (query_total * (estimate + smoothing))
    terms = whole[:dims] * (weight / sample_total)
    terms = jnp.concatenate([terms, jnp.zeros((queries - dims, queries), jnp.float32)], axis=0)
    share = jnp.sum(terms.T, axis=0, keepdims=True)
    for peer in range(share_ref.shape[0]):
        share_ref[peer] = share


def add_kernel(shares_ref, out_ref):
    total = tree_sum([shares_ref[peer] for peer in range(shares_ref.shape[0])])
    out_ref[...] = total[0, : out_ref.shape[0]]


def everyone(x, axis):
    size = lax.axis_size(axis)
    return [x] + [
        lax.ppermute(x, axis, [(i, i ^ offset) for i in range(size)]) for offset in range(1, size)
    ]


def call(kernel, args, outs, scratch=()):
    single = len(outs) == 1
    return pl.pallas_call(
        kernel,
        out_shape=outs[0] if single else outs,
        in_specs=[pl.BlockSpec(memory_space=pltpu.VMEM)] * len(args),
        out_specs=pl.BlockSpec(memory_space=pltpu.VMEM)
        if single
        else [pl.BlockSpec(memory_space=pltpu.VMEM)] * len(outs),
        scratch_shapes=list(scratch),
        compiler_params=pltpu.CompilerParams(vmem_limit_bytes=32 << 20),
    )(*args)


def shape(*sizes):
    return jax.ShapeDtypeStruct(sizes, jnp.float32)


def on_device(samples, bounds, spread, counts):
    dims, width = samples.shape
    queries = bounds.shape[2]
    blocks = lax.axis_size("blk")
    sample_total = width * blocks * lax.axis_size("grp")
    query_total = queries * blocks
    total = width * blocks

    spread, counts = spread.reshape(1, dims), counts.reshape(1, queries)
    packed, target = call(
        pack_kernel,
        [samples, bounds, spread, counts],
        [shape(blocks, 8, dims * width // 8), shape(1, queries)],
    )
    gathered = lax.all_to_all(packed, "blk", 0, 0)
    part = call(
        functools.partial(terms_kernel, width),
        [gathered, bounds, spread],
        [shape(dims + 8, queries)],
        [
            pltpu.VMEM((total, (LIMITED + 1) * queries), jnp.float32),
            pltpu.VMEM((total, 2 * queries), jnp.bfloat16),
        ],
    )
    parts = everyone(part, "grp")
    log_est, share = call(
        functools.partial(finish_kernel, sample_total, query_total),
        parts + [target],
        [shape(1, queries), shape(blocks, 1, queries)],
    )
    shares = lax.all_to_all(share, "blk", 0, 0)
    gradient = call(add_kernel, [shares], [shape(dims)])
    return log_est.reshape(queries), gradient


def solution(mesh):
    return jax.shard_map(
        on_device,
        mesh=mesh,
        in_specs=(P(None, ("blk", "grp")), P(None, None, "blk"), P(), P("blk")),
        out_specs=(P("blk"), P()),
        check_vma=False,
    )
```

```python
import functools
import math

import jax
import jax.numpy as jnp
from jax import lax
from jax.experimental import pallas as pl
from jax.experimental.pallas import tpu as pltpu
from jax.sharding import PartitionSpec as P

TABLE_ROWS = 1048576
GRID = 256
LIMITED = 3

UNIT = 0.8493218002880191
SLOPE = 0.46971863934982566
ERF_UNIT = 0.8325546111576977


def end_terms(v):
    bell = jnp.exp2(-(v * v))
    return 0.5 * lax.erf(v * ERF_UNIT), v * bell


def box_terms(low, high):
    low_erf, low_bell = end_terms(low)
    high_erf, high_bell = end_terms(high)
    return high_erf - low_erf, SLOPE * (low_bell - high_bell)


def split(x, parts):
    out = []
    for _ in range(parts - 1):
        head = x.astype(jnp.bfloat16)
        out.append(head)
        x = x - head.astype(jnp.float32)
    return out + [x.astype(jnp.bfloat16)]


def load_kernel(
    x_ref, bounds_ref, spread_ref, counts_ref,
    out_ref, held_bounds, held_spread, target_ref,
    held_x, held_counts, sems,
):
    sources = (x_ref, bounds_ref, spread_ref, counts_ref)
    targets = (held_x, held_bounds, held_spread, held_counts)
    copies = [
        pltpu.make_async_copy(source, target, sems.at[i])
        for i, (source, target) in enumerate(zip(sources, targets))
    ]
    for copy in copies:
        copy.start()
    copies[0].wait()
    rows = held_x.shape[0]
    packed = jnp.concatenate([held_x[8 * j : 8 * (j + 1), :] for j in range(rows // 8)], axis=1)
    for peer in range(out_ref.shape[0]):
        out_ref[peer] = packed
    for copy in copies[1:]:
        copy.wait()
    smoothing = 1.0 / TABLE_ROWS
    target_ref[...] = jnp.log(held_counts[...].astype(jnp.float32) / TABLE_ROWS + smoothing)


def terms_kernel(width, blocks_ref, bounds_ref, spread_ref, out_ref, picked, inside):
    dims, queries = bounds_ref.shape[1:]
    total = blocks_ref.shape[0] * width

    low, high = bounds_ref[0], bounds_ref[1]
    limited = (high - low) != GRID
    low, high = low.astype(jnp.float32), high.astype(jnp.float32)
    at = lax.broadcasted_iota(jnp.int32, (dims, queries), 0)
    first = jnp.min(jnp.where(limited, at, dims), axis=0, keepdims=True)
    last = jnp.max(jnp.where(limited, at, -1), axis=0, keepdims=True)
    is_first, is_last = at == first, at == last
    chosen = [is_first, limited & (at > first) & (at < last), is_last]

    row = lax.broadcasted_iota(jnp.int32, (dims, dims), 0)
    column = lax.broadcasted_iota(jnp.int32, (dims, dims), 1)
    spread = jnp.sum(jnp.where(row == column, spread_ref[...], 0.0), axis=1, keepdims=True)
    unit = UNIT / spread

    pick = lambda mask, values: jnp.sum(jnp.where(mask, values, 0.0), axis=0, keepdims=True)
    low_at = [pick(mask, low) for mask in chosen]
    high_at = [pick(mask, high) for mask in chosen]
    unit_at = [pick(mask, unit) for mask in chosen]

    x = jnp.concatenate(
        [
            jnp.concatenate(
                [blocks_ref[b, :, width * j : width * (j + 1)] for b in range(blocks_ref.shape[0])],
                axis=1,
            )
            for j in range(dims // 8)
        ],
        axis=0,
    )
    full, full_slope = box_terms(-x * unit, (float(GRID) - x) * unit)
    ratio = full_slope / full
    left = jnp.concatenate(split(x, 3) + split(jnp.log(full), 3), axis=0)

    ones = [mask.astype(jnp.float32).astype(jnp.bfloat16) for mask in chosen]
    free = jnp.where(limited, 0.0, 1.0).astype(jnp.bfloat16)
    none = jnp.zeros_like(free)
    right = jnp.concatenate(
        [jnp.concatenate(ones + [none], axis=1)] * 3
        + [jnp.concatenate([none] * LIMITED + [free], axis=1)] * 3,
        axis=0,
    )
    picked[...] = lax.dot_general(
        left, right, (((0,), (0,)), ((), ())), preferred_element_type=jnp.float32
    )

    def advance(step, sums):
        rows = pl.ds(pl.multiple_of(step * 16, 16), 16)
        others = jnp.exp(picked[rows, LIMITED * queries :])
        mass, slope = [], []
        for k in range(LIMITED):
            points = picked[rows, k * queries : (k + 1) * queries]
            m, s = box_terms((low_at[k] - points) * unit_at[k], (high_at[k] - points) * unit_at[k])
            mass.append(m)
            slope.append(s)
        pair = others * mass[0]
        last_two = pair * mass[1]
        whole = last_two * mass[2]
        head, tail = split(whole, 2)
        inside[rows, :queries] = head
        inside[rows, queries:] = tail
        return (
            sums[0] + whole,
            sums[1] + others * mass[1] * mass[2] * slope[0],
            sums[2] + pair * mass[2] * slope[1],
            sums[3] + last_two * slope[2],
        )

    zero = jnp.zeros((16, queries), jnp.float32)
    sums = lax.fori_loop(0, total // 16, advance, (zero,) * 4, unroll=2)
    sums = [jnp.sum(s, axis=0, keepdims=True) for s in sums]

    ratio = jnp.concatenate(split(ratio, 2), axis=0)
    products = jnp.dot(ratio, inside[...], preferred_element_type=jnp.float32)
    deriv = products[:dims, :queries] + (products[dims:, :queries] + products[:dims, queries:])
    deriv = jnp.where(limited, 0.0, deriv)
    for mask, s in zip(chosen, sums[1:]):
        deriv = jnp.where(mask, s, deriv)
    out_ref[:dims, :] = deriv
    out_ref[dims:, :] = jnp.broadcast_to(sums[0], (8, queries))


def finish_kernel(sample_total, query_total, *refs):
    part_refs, (target_ref, log_ref, share_ref) = refs[:-3], refs[-3:]
    whole = total_of(part_refs)
    dims, queries = whole.shape[0] - 8, whole.shape[1]
    smoothing = 1.0 / TABLE_ROWS
    estimate = whole[dims : dims + 1] / sample_total
    log_est = jnp.log(estimate + smoothing)
    leads = lax.axis_index("grp") == lax.axis_size("grp") - 1
    log_ref[...] = jnp.where(leads, log_est, 0.0)
    weight = 2.0 * (log_est - target_ref[...]) / (query_total * (estimate + smoothing))
    terms = whole[:dims] * (weight / sample_total)
    terms = jnp.concatenate([terms, jnp.zeros((queries - dims, queries), jnp.float32)], axis=0)
    share_ref[...] = jnp.sum(terms.T, axis=0, keepdims=True)


def total_of(refs):
    total = refs[0][...]
    for ref in refs[1:]:
        total = total + ref[...]
    return total


def sum_kernel(*refs):
    refs[-1][...] = total_of(refs[:-1])


def root_kernel(*refs):
    *shares, log_ref, total_ref, both_ref = refs
    leads = lax.axis_index("grp") == lax.axis_size("grp") - 1
    root = leads & (lax.axis_index("blk") == 0)
    total = jnp.where(root, total_of(shares), 0.0)
    total_ref[...] = total
    both_ref[:1, :] = total
    both_ref[1:, :] = log_ref[...]


def spread_kernel(*refs):
    *shares, pair_ref, total_ref, held_ref = refs
    total_ref[...] = total_of(shares)
    held_ref[...] = pair_ref[...]


def pair_kernel(*refs):
    *shares, log_ref, both_ref = refs
    both_ref[:1, :] = total_of(shares)
    both_ref[1:, :] = log_ref[...]


def last_kernel(*refs):
    *both, log_ref, gradient_ref = refs
    total = total_of(both)
    log_ref[...] = total[1]
    gradient_ref[...] = total[0, : gradient_ref.shape[0]]


def call(kernel, args, outs, scratch=(), placed=pltpu.VMEM):
    single = len(outs) == 1
    return pl.pallas_call(
        kernel,
        out_shape=outs[0] if single else outs,
        in_specs=[pl.BlockSpec(memory_space=placed)] * len(args),
        out_specs=pl.BlockSpec(memory_space=pltpu.VMEM)
        if single
        else [pl.BlockSpec(memory_space=pltpu.VMEM)] * len(outs),
        scratch_shapes=list(scratch),
        compiler_params=pltpu.CompilerParams(vmem_limit_bytes=32 << 20),
    )(*args)


def shape(*sizes):
    return jax.ShapeDtypeStruct(sizes, jnp.float32)


def on_device(samples, bounds, spread, counts):
    dims, width = samples.shape
    queries = bounds.shape[2]
    blocks, copies = lax.axis_size("blk"), lax.axis_size("grp")
    sample_total = width * blocks * copies
    query_total = queries * blocks
    total = width * blocks

    both = ("blk", "grp")
    lead = lambda block: block * copies + copies - 1
    send = lambda x, pairs: lax.ppermute(x, both, pairs)
    size = math.isqrt(blocks)
    groups = [list(range(b, min(b + size, blocks))) for b in range(1, blocks, size)]
    followers = [[(g[0], g[m]) for g in groups if len(g) > m] for m in range(1, size)]

    counts_vector = pltpu.VMEM((1, queries), jnp.int32)
    packed, bounds, spread, target = call(
        load_kernel,
        [
            pltpu.with_memory_space_constraint(array, pltpu.HBM)
            for array in (samples, bounds, spread.reshape(1, dims), counts.reshape(1, queries))
        ],
        [
            pltpu.VMEM((blocks, 8, dims * width // 8), jnp.float32),
            pltpu.VMEM(bounds.shape, bounds.dtype),
            pltpu.VMEM((1, dims), jnp.float32),
            pltpu.VMEM((1, queries), jnp.float32),
        ],
        [pltpu.VMEM((dims, width), jnp.float32), counts_vector, pltpu.SemaphoreType.DMA((4,))],
        placed=pl.ANY,
    )
    gathered = lax.all_to_all(packed, "blk", 0, 0)
    part = call(
        functools.partial(terms_kernel, width),
        [gathered, bounds, spread],
        [shape(dims + 8, queries)],
        [
            pltpu.VMEM((total, (LIMITED + 1) * queries), jnp.float32),
            pltpu.VMEM((total, 2 * queries), jnp.bfloat16),
        ],
    )
    parts = [part] + [
        send(part, [(b * copies + c, lead(b)) for b in range(blocks)]) for c in range(copies - 1)
    ]
    log_est, share = call(
        functools.partial(finish_kernel, sample_total, query_total),
        parts + [target],
        [shape(1, queries), shape(1, queries)],
    )

    row = shape(1, queries)
    shares = [share] + [
        send(share, [(lead(follower), lead(leader)) for leader, follower in pairs])
        for pairs in followers
    ]
    share = call(sum_kernel, shares, [row])
    shares = [share] + [send(share, [(lead(g[0]), lead(0))]) for g in groups]
    share, pair = call(root_kernel, shares + [log_est], [row, shape(2, queries)])
    shares = [share] + [send(share, [(lead(0), lead(g[0]))]) for g in groups]
    at_root = functools.reduce(
        jnp.add, [send(pair, [(lead(0), c)]) for c in range(copies - 1)]
    )
    share, at_root = call(spread_kernel, shares + [at_root], [row, shape(2, queries)])
    shares = [share] + [
        send(share, [(lead(leader), lead(follower)) for leader, follower in pairs])
        for pairs in followers
    ]
    pair = call(pair_kernel, shares + [log_est], [shape(2, queries)])
    elsewhere = [
        send(pair, [(lead(b), b * copies + c) for b in range(1, blocks)]) for c in range(copies - 1)
    ]
    log_est, gradient = call(last_kernel, [pair, at_root] + elsewhere, [shape(queries), shape(dims)])
    return log_est, gradient


def solution(mesh):
    return jax.shard_map(
        on_device,
        mesh=mesh,
        in_specs=(P(None, ("blk", "grp")), P(None, None, "blk"), P(), P("blk")),
        out_specs=(P("blk"), P()),
        check_vma=False,
    )
```

```python
import functools

import jax
import jax.numpy as jnp
from jax import lax
from jax.experimental import pallas as pl
from jax.experimental.pallas import tpu as pltpu
from jax.sharding import PartitionSpec as P

TABLE_ROWS = 1048576
GRID = 256
LIMITED = 3

UNIT = 0.8493218002880191
SLOPE = 0.46971863934982566
ERF_UNIT = 0.8325546111576977


def end_terms(v):
    bell = jnp.exp2(-(v * v))
    return 0.5 * lax.erf(v * ERF_UNIT), v * bell


def box_terms(low, high):
    low_erf, low_bell = end_terms(low)
    high_erf, high_bell = end_terms(high)
    return high_erf - low_erf, SLOPE * (low_bell - high_bell)


def split(x, parts):
    out = []
    for _ in range(parts - 1):
        head = x.astype(jnp.bfloat16)
        out.append(head)
        x = x - head.astype(jnp.float32)
    return out + [x.astype(jnp.bfloat16)]


def tree_sum(parts):
    while len(parts) > 1:
        parts = [a + b for a, b in zip(parts[::2], parts[1::2])]
    return parts[0]


def load_kernel(
    x_ref, bounds_ref, spread_ref, counts_ref,
    out_ref, held_bounds, held_spread, target_ref,
    held_x, held_counts, sems,
):
    sources = (x_ref, bounds_ref, spread_ref, counts_ref)
    targets = (held_x, held_bounds, held_spread, held_counts)
    copies = [
        pltpu.make_async_copy(source, target, sems.at[i])
        for i, (source, target) in enumerate(zip(sources, targets))
    ]
    for copy in copies:
        copy.start()
    copies[0].wait()
    rows = held_x.shape[0]
    packed = jnp.concatenate([held_x[8 * j : 8 * (j + 1), :] for j in range(rows // 8)], axis=1)
    for peer in range(out_ref.shape[0]):
        out_ref[peer] = packed
    for copy in copies[1:]:
        copy.wait()
    smoothing = 1.0 / TABLE_ROWS
    target_ref[...] = jnp.log(held_counts[...].astype(jnp.float32) / TABLE_ROWS + smoothing)


def terms_kernel(width, blocks_ref, bounds_ref, spread_ref, out_ref, picked, inside):
    dims, queries = bounds_ref.shape[1:]
    total = blocks_ref.shape[0] * width

    low, high = bounds_ref[0], bounds_ref[1]
    limited = (high - low) != GRID
    low, high = low.astype(jnp.float32), high.astype(jnp.float32)
    at = lax.broadcasted_iota(jnp.int32, (dims, queries), 0)
    first = jnp.min(jnp.where(limited, at, dims), axis=0, keepdims=True)
    last = jnp.max(jnp.where(limited, at, -1), axis=0, keepdims=True)
    is_first, is_last = at == first, at == last
    chosen = [is_first, limited & (at > first) & (at < last), is_last]

    row = lax.broadcasted_iota(jnp.int32, (dims, dims), 0)
    column = lax.broadcasted_iota(jnp.int32, (dims, dims), 1)
    spread = jnp.sum(jnp.where(row == column, spread_ref[...], 0.0), axis=1, keepdims=True)
    unit = UNIT / spread

    pick = lambda mask, values: jnp.sum(jnp.where(mask, values, 0.0), axis=0, keepdims=True)
    low_at = [pick(mask, low) for mask in chosen]
    high_at = [pick(mask, high) for mask in chosen]
    unit_at = [pick(mask, unit) for mask in chosen]

    x = jnp.concatenate(
        [
            jnp.concatenate(
                [blocks_ref[b, :, width * j : width * (j + 1)] for b in range(blocks_ref.shape[0])],
                axis=1,
            )
            for j in range(dims // 8)
        ],
        axis=0,
    )
    full, full_slope = box_terms(-x * unit, (float(GRID) - x) * unit)
    ratio = full_slope / full
    left = jnp.concatenate(split(x, 3) + split(jnp.log(full), 3), axis=0)

    ones = [mask.astype(jnp.float32).astype(jnp.bfloat16) for mask in chosen]
    free = jnp.where(limited, 0.0, 1.0).astype(jnp.bfloat16)
    none = jnp.zeros_like(free)
    right = jnp.concatenate(
        [jnp.concatenate(ones + [none], axis=1)] * 3
        + [jnp.concatenate([none] * LIMITED + [free], axis=1)] * 3,
        axis=0,
    )
    picked[...] = lax.dot_general(
        left, right, (((0,), (0,)), ((), ())), preferred_element_type=jnp.float32
    )

    def advance(step, sums):
        rows = pl.ds(pl.multiple_of(step * 16, 16), 16)
        others = jnp.exp(picked[rows, LIMITED * queries :])
        mass, slope = [], []
        for k in range(LIMITED):
            points = picked[rows, k * queries : (k + 1) * queries]
            m, s = box_terms((low_at[k] - points) * unit_at[k], (high_at[k] - points) * unit_at[k])
            mass.append(m)
            slope.append(s)
        pair = others * mass[0]
        last_two = pair * mass[1]
        whole = last_two * mass[2]
        head, tail = split(whole, 2)
        inside[rows, :queries] = head
        inside[rows, queries:] = tail
        return (
            sums[0] + whole,
            sums[1] + others * mass[1] * mass[2] * slope[0],
            sums[2] + pair * mass[2] * slope[1],
            sums[3] + last_two * slope[2],
        )

    zero = jnp.zeros((16, queries), jnp.float32)
    sums = lax.fori_loop(0, total // 16, advance, (zero,) * 4, unroll=2)
    sums = [jnp.sum(s, axis=0, keepdims=True) for s in sums]

    ratio = jnp.concatenate(split(ratio, 2), axis=0)
    products = jnp.dot(ratio, inside[...], preferred_element_type=jnp.float32)
    deriv = products[:dims, :queries] + (products[dims:, :queries] + products[:dims, queries:])
    deriv = jnp.where(limited, 0.0, deriv)
    for mask, s in zip(chosen, sums[1:]):
        deriv = jnp.where(mask, s, deriv)
    out_ref[:dims, :] = deriv
    out_ref[dims:, :] = jnp.broadcast_to(sums[0], (8, queries))


def finish_kernel(sample_total, query_total, *refs):
    part_refs, (target_ref, log_ref, share_ref) = refs[:-3], refs[-3:]
    whole = tree_sum([ref[...] for ref in part_refs])
    dims, queries = whole.shape[0] - 8, whole.shape[1]
    smoothing = 1.0 / TABLE_ROWS
    estimate = whole[dims : dims + 1] / sample_total
    log_est = jnp.log(estimate + smoothing)
    log_ref[...] = log_est
    weight = 2.0 * (log_est - target_ref[...]) / (query_total * (estimate + smoothing))
    terms = whole[:dims] * (weight / sample_total)
    terms = jnp.concatenate([terms, jnp.zeros((queries - dims, queries), jnp.float32)], axis=0)
    share = jnp.sum(terms.T, axis=0, keepdims=True)
    for peer in range(share_ref.shape[0]):
        share_ref[peer] = share


def last_kernel(shares_ref, held_log_ref, log_ref, gradient_ref):
    total = tree_sum([shares_ref[peer] for peer in range(shares_ref.shape[0])])
    log_ref[...] = held_log_ref[0]
    gradient_ref[...] = total[0, : gradient_ref.shape[0]]


def everyone(x, axis):
    size = lax.axis_size(axis)
    return [x] + [
        lax.ppermute(x, axis, [(i, i ^ offset) for i in range(size)]) for offset in range(1, size)
    ]


def call(kernel, args, outs, scratch=(), placed=pltpu.VMEM):
    single = len(outs) == 1
    return pl.pallas_call(
        kernel,
        out_shape=outs[0] if single else outs,
        in_specs=[pl.BlockSpec(memory_space=placed)] * len(args),
        out_specs=pl.BlockSpec(memory_space=pltpu.VMEM)
        if single
        else [pl.BlockSpec(memory_space=pltpu.VMEM)] * len(outs),
        scratch_shapes=list(scratch),
        compiler_params=pltpu.CompilerParams(vmem_limit_bytes=32 << 20),
    )(*args)


def shape(*sizes):
    return jax.ShapeDtypeStruct(sizes, jnp.float32)


def on_device(samples, bounds, spread, counts):
    dims, width = samples.shape
    queries = bounds.shape[2]
    blocks, copies = lax.axis_size("blk"), lax.axis_size("grp")
    sample_total = width * blocks * copies
    query_total = queries * blocks
    total = width * blocks

    counts_vector = pltpu.VMEM((1, queries), jnp.int32)
    packed, bounds, spread, target = call(
        load_kernel,
        [
            pltpu.with_memory_space_constraint(array, pltpu.HBM)
            for array in (samples, bounds, spread.reshape(1, dims), counts.reshape(1, queries))
        ],
        [
            pltpu.VMEM((blocks, 8, dims * width // 8), jnp.float32),
            pltpu.VMEM(bounds.shape, bounds.dtype),
            pltpu.VMEM((1, dims), jnp.float32),
            pltpu.VMEM((1, queries), jnp.float32),
        ],
        [pltpu.VMEM((dims, width), jnp.float32), counts_vector, pltpu.SemaphoreType.DMA((4,))],
        placed=pl.ANY,
    )
    gathered = lax.all_to_all(
        packed, "blk", 0, 0, axis_index_groups=[list(reversed(range(blocks)))]
    )
    part = call(
        functools.partial(terms_kernel, width),
        [gathered, bounds, spread],
        [shape(dims + 8, queries)],
        [
            pltpu.VMEM((total, (LIMITED + 1) * queries), jnp.float32),
            pltpu.VMEM((total, 2 * queries), jnp.bfloat16),
        ],
    )
    log_est, share = call(
        functools.partial(finish_kernel, sample_total, query_total),
        everyone(part, "grp") + [target],
        [shape(1, queries), shape(blocks, 1, queries)],
    )
    shares = lax.all_to_all(share, "blk", 0, 0)
    return call(last_kernel, [shares, log_est], [shape(queries), shape(dims)])


def solution(mesh):
    return jax.shard_map(
        on_device,
        mesh=mesh,
        in_specs=(P(None, ("blk", "grp")), P(None, None, "blk"), P(), P("blk")),
        out_specs=(P("blk"), P()),
        check_vma=False,
    )
```

```python
import functools

import jax
import jax.numpy as jnp
from jax import lax
from jax.experimental import pallas as pl
from jax.experimental.pallas import tpu as pltpu
from jax.sharding import PartitionSpec as P

TABLE_ROWS = 1048576
GRID = 256
LIMITED = 3

UNIT = 0.8493218002880191
SLOPE = 0.46971863934982566
ERF_UNIT = 0.8325546111576977


def end_terms(v):
    bell = jnp.exp2(-(v * v))
    return 0.5 * lax.erf(v * ERF_UNIT), v * bell


def box_terms(low, high):
    low_erf, low_bell = end_terms(low)
    high_erf, high_bell = end_terms(high)
    return high_erf - low_erf, SLOPE * (low_bell - high_bell)


def split(x, parts):
    out = []
    for _ in range(parts - 1):
        head = x.astype(jnp.bfloat16)
        out.append(head)
        x = x - head.astype(jnp.float32)
    return out + [x.astype(jnp.bfloat16)]


def tree_sum(parts):
    while len(parts) > 1:
        parts = [a + b for a, b in zip(parts[::2], parts[1::2])]
    return parts[0]


def load_kernel(
    x_ref, bounds_ref, spread_ref, counts_ref,
    out_ref, held_bounds, held_spread, target_ref,
    held_x, held_counts, sems,
):
    sources = (x_ref, bounds_ref, spread_ref, counts_ref)
    targets = (held_x, held_bounds, held_spread, held_counts)
    copies = [
        pltpu.make_async_copy(source, target, sems.at[i])
        for i, (source, target) in enumerate(zip(sources, targets))
    ]
    for copy in copies:
        copy.start()
    copies[0].wait()
    rows = held_x.shape[0]
    packed = jnp.concatenate([held_x[8 * j : 8 * (j + 1), :] for j in range(rows // 8)], axis=1)
    for peer in range(out_ref.shape[0]):
        out_ref[peer] = packed
    for copy in copies[1:]:
        copy.wait()
    smoothing = 1.0 / TABLE_ROWS
    target_ref[...] = jnp.log(held_counts[...].astype(jnp.float32) / TABLE_ROWS + smoothing)


def terms_kernel(width, blocks_ref, bounds_ref, spread_ref, out_ref, picked, inside):
    dims, queries = bounds_ref.shape[1:]
    total = blocks_ref.shape[0] * width

    low, high = bounds_ref[0], bounds_ref[1]
    limited = (high - low) != GRID
    low, high = low.astype(jnp.float32), high.astype(jnp.float32)
    at = lax.broadcasted_iota(jnp.int32, (dims, queries), 0)
    first = jnp.min(jnp.where(limited, at, dims), axis=0, keepdims=True)
    last = jnp.max(jnp.where(limited, at, -1), axis=0, keepdims=True)
    is_first, is_last = at == first, at == last
    chosen = [is_first, limited & (at > first) & (at < last), is_last]

    row = lax.broadcasted_iota(jnp.int32, (dims, dims), 0)
    column = lax.broadcasted_iota(jnp.int32, (dims, dims), 1)
    spread = jnp.sum(jnp.where(row == column, spread_ref[...], 0.0), axis=1, keepdims=True)
    unit = UNIT / spread

    pick = lambda mask, values: jnp.sum(jnp.where(mask, values, 0.0), axis=0, keepdims=True)
    low_at = [pick(mask, low) for mask in chosen]
    high_at = [pick(mask, high) for mask in chosen]
    unit_at = [pick(mask, unit) for mask in chosen]

    x = jnp.concatenate(
        [
            jnp.concatenate(
                [blocks_ref[b, :, width * j : width * (j + 1)] for b in range(blocks_ref.shape[0])],
                axis=1,
            )
            for j in range(dims // 8)
        ],
        axis=0,
    )
    full, full_slope = box_terms(-x * unit, (float(GRID) - x) * unit)
    ratio = full_slope / full
    left = jnp.concatenate(split(x, 3) + split(jnp.log(full), 3), axis=0)

    ones = [mask.astype(jnp.float32).astype(jnp.bfloat16) for mask in chosen]
    free = jnp.where(limited, 0.0, 1.0).astype(jnp.bfloat16)
    none = jnp.zeros_like(free)
    right = jnp.concatenate(
        [jnp.concatenate(ones + [none], axis=1)] * 3
        + [jnp.concatenate([none] * LIMITED + [free], axis=1)] * 3,
        axis=0,
    )
    picked[...] = lax.dot_general(
        left, right, (((0,), (0,)), ((), ())), preferred_element_type=jnp.float32
    )

    def advance(step, sums):
        rows = pl.ds(pl.multiple_of(step * 16, 16), 16)
        others = jnp.exp(picked[rows, LIMITED * queries :])
        mass, slope = [], []
        for k in range(LIMITED):
            points = picked[rows, k * queries : (k + 1) * queries]
            m, s = box_terms((low_at[k] - points) * unit_at[k], (high_at[k] - points) * unit_at[k])
            mass.append(m)
            slope.append(s)
        pair = others * mass[0]
        last_two = pair * mass[1]
        whole = last_two * mass[2]
        head, tail = split(whole, 2)
        inside[rows, :queries] = head
        inside[rows, queries:] = tail
        return (
            sums[0] + whole,
            sums[1] + others * mass[1] * mass[2] * slope[0],
            sums[2] + pair * mass[2] * slope[1],
            sums[3] + last_two * slope[2],
        )

    zero = jnp.zeros((16, queries), jnp.float32)
    sums = lax.fori_loop(0, total // 16, advance, (zero,) * 4, unroll=2)
    sums = [jnp.sum(s, axis=0, keepdims=True) for s in sums]

    ratio = jnp.concatenate(split(ratio, 2), axis=0)
    products = jnp.dot(ratio, inside[...], preferred_element_type=jnp.float32)
    deriv = products[:dims, :queries] + (products[dims:, :queries] + products[:dims, queries:])
    deriv = jnp.where(limited, 0.0, deriv)
    for mask, s in zip(chosen, sums[1:]):
        deriv = jnp.where(mask, s, deriv)
    out_ref[:dims, :] = deriv
    out_ref[dims:, :] = jnp.broadcast_to(sums[0], (8, queries))


def finish_kernel(sample_total, query_total, *refs):
    part_refs, (target_ref, log_ref, share_ref) = refs[:-3], refs[-3:]
    whole = tree_sum([ref[...] for ref in part_refs])
    dims, queries = whole.shape[0] - 8, whole.shape[1]
    smoothing = 1.0 / TABLE_ROWS
    estimate = whole[dims : dims + 1] / sample_total
    log_est = jnp.log(estimate + smoothing)
    log_ref[...] = log_est
    weight = 2.0 * (log_est - target_ref[...]) / (query_total * (estimate + smoothing))
    terms = whole[:dims] * (weight / sample_total)
    terms = jnp.concatenate([terms, jnp.zeros((queries - dims, queries), jnp.float32)], axis=0)
    share = jnp.sum(terms.T, axis=0, keepdims=True)
    for peer in range(share_ref.shape[0]):
        share_ref[peer] = share


def last_kernel(shares_ref, held_log_ref, log_ref, gradient_ref):
    total = tree_sum([shares_ref[peer] for peer in range(shares_ref.shape[0])])
    log_ref[...] = held_log_ref[0]
    gradient_ref[...] = total[0, : gradient_ref.shape[0]]


def everyone(x, axis):
    size = lax.axis_size(axis)
    return [x] + [
        lax.ppermute(x, axis, [(i, i ^ offset) for i in range(size)]) for offset in range(1, size)
    ]


def call(kernel, args, outs, scratch=(), placed=pltpu.VMEM):
    single = len(outs) == 1
    return pl.pallas_call(
        kernel,
        out_shape=outs[0] if single else outs,
        in_specs=[pl.BlockSpec(memory_space=placed)] * len(args),
        out_specs=pl.BlockSpec(memory_space=pltpu.VMEM)
        if single
        else [pl.BlockSpec(memory_space=pltpu.VMEM)] * len(outs),
        scratch_shapes=list(scratch),
        compiler_params=pltpu.CompilerParams(vmem_limit_bytes=32 << 20),
    )(*args)


def shape(*sizes):
    return jax.ShapeDtypeStruct(sizes, jnp.float32)


def on_device(samples, bounds, spread, counts):
    dims, width = samples.shape
    queries = bounds.shape[2]
    blocks, copies = lax.axis_size("blk"), lax.axis_size("grp")
    sample_total = width * blocks * copies
    query_total = queries * blocks
    total = width * blocks

    counts_vector = pltpu.VMEM((1, queries), jnp.int32)
    packed, bounds, spread, target = call(
        load_kernel,
        [
            pltpu.with_memory_space_constraint(array, pltpu.HBM)
            for array in (samples, bounds, spread.reshape(1, dims), counts.reshape(1, queries))
        ],
        [
            pltpu.VMEM((blocks, 8, dims * width // 8), jnp.float32),
            pltpu.VMEM(bounds.shape, bounds.dtype),
            pltpu.VMEM((1, dims), jnp.float32),
            pltpu.VMEM((1, queries), jnp.float32),
        ],
        [pltpu.VMEM((dims, width), jnp.float32), counts_vector, pltpu.SemaphoreType.DMA((4,))],
        placed=pl.ANY,
    )
    order = [list(reversed(range(blocks)))]
    gathered = lax.all_to_all(packed, "blk", 0, 0, axis_index_groups=order)
    part = call(
        functools.partial(terms_kernel, width),
        [gathered, bounds, spread],
        [shape(dims + 8, queries)],
        [
            pltpu.VMEM((total, (LIMITED + 1) * queries), jnp.float32),
            pltpu.VMEM((total, 2 * queries), jnp.bfloat16),
        ],
    )
    log_est, share = call(
        functools.partial(finish_kernel, sample_total, query_total),
        everyone(part, "grp") + [target],
        [shape(1, queries), shape(blocks, 1, queries)],
    )
    shares = lax.all_to_all(share, "blk", 0, 0, axis_index_groups=order)
    return call(last_kernel, [shares, log_est], [shape(queries), shape(dims)])


def solution(mesh):
    return jax.shard_map(
        on_device,
        mesh=mesh,
        in_specs=(P(None, ("blk", "grp")), P(None, None, "blk"), P(), P("blk")),
        out_specs=(P("blk"), P()),
        check_vma=False,
    )
```

```python
import functools

import jax
import jax.numpy as jnp
from jax import lax
from jax.experimental import pallas as pl
from jax.experimental.pallas import tpu as pltpu
from jax.sharding import PartitionSpec as P

TABLE_ROWS = 1048576
GRID = 256
LIMITED = 3

ROOT_HALF = 0.7071067811865476
LOG2_E = 1.4426950408889634
SLOPE = 0.5641895835477563


def box_terms(low, high):
    low_bell = jnp.exp2((low * low) * -LOG2_E)
    high_bell = jnp.exp2((high * high) * -LOG2_E)
    return lax.erf(high) - lax.erf(low), low * low_bell - high * high_bell


def split(x, parts):
    out = []
    for _ in range(parts - 1):
        head = x.astype(jnp.bfloat16)
        out.append(head)
        x = x - head.astype(jnp.float32)
    return out + [x.astype(jnp.bfloat16)]


def tree_sum(parts):
    while len(parts) > 1:
        parts = [a + b for a, b in zip(parts[::2], parts[1::2])]
    return parts[0]


def load_kernel(
    x_ref, bounds_ref, spread_ref, counts_ref,
    out_ref, held_bounds, held_spread, target_ref,
    held_x, held_counts, sems,
):
    sources = (x_ref, bounds_ref, spread_ref, counts_ref)
    targets = (held_x, held_bounds, held_spread, held_counts)
    copies = [
        pltpu.make_async_copy(source, target, sems.at[i])
        for i, (source, target) in enumerate(zip(sources, targets))
    ]
    for copy in copies:
        copy.start()
    copies[0].wait()
    rows = held_x.shape[0]
    packed = jnp.concatenate([held_x[8 * j : 8 * (j + 1), :] for j in range(rows // 8)], axis=1)
    for peer in range(out_ref.shape[0]):
        out_ref[peer] = packed
    for copy in copies[1:]:
        copy.wait()
    smoothing = 1.0 / TABLE_ROWS
    target_ref[...] = jnp.log(held_counts[...].astype(jnp.float32) / TABLE_ROWS + smoothing)


def terms_kernel(width, blocks_ref, bounds_ref, spread_ref, out_ref):
    dims, queries = bounds_ref.shape[1:]
    count = blocks_ref.shape[0]
    per_piece = 128 // width
    group = min(count, 4 * per_piece)

    low, high = bounds_ref[0], bounds_ref[1]
    limited = (high - low) != GRID
    at = lax.broadcasted_iota(jnp.int32, (dims, queries), 0)
    first = jnp.min(jnp.where(limited, at, dims), axis=0, keepdims=True)
    last = jnp.max(jnp.where(limited, at, -1), axis=0, keepdims=True)
    chosen = [at == first, limited & (at > first) & (at < last), at == last]

    row = lax.broadcasted_iota(jnp.int32, (dims, dims), 0)
    column = lax.broadcasted_iota(jnp.int32, (dims, dims), 1)
    spread = jnp.sum(jnp.where(row == column, spread_ref[...], 0.0), axis=1, keepdims=True)
    unit = ROOT_HALF / spread

    pick = lambda mask, values: jnp.sum(jnp.where(mask, values, 0.0), axis=0, keepdims=True)
    low = low.astype(jnp.float32) * unit
    high = high.astype(jnp.float32) * unit
    low_at = [pick(mask, low) for mask in chosen]
    high_at = [pick(mask, high) for mask in chosen]

    ones = [mask.astype(jnp.float32).astype(jnp.bfloat16) for mask in chosen]
    free = jnp.where(limited, 0.0, 1.0).astype(jnp.bfloat16)
    none = jnp.zeros_like(free)
    right = jnp.concatenate(
        [jnp.concatenate(ones + [none], axis=1)] * 3
        + [jnp.concatenate([none] * LIMITED + [free], axis=1)] * 3,
        axis=0,
    )

    def step(picked, sums):
        others = jnp.exp2(picked[:, LIMITED * queries :])
        mass, slope = [], []
        for k in range(LIMITED):
            points = picked[:, k * queries : (k + 1) * queries]
            m, s = box_terms(low_at[k] - points, high_at[k] - points)
            mass.append(m)
            slope.append(s)
        pair = others * mass[0]
        last_two = pair * mass[1]
        whole = last_two * mass[2]
        return whole, (
            sums[0] + whole,
            sums[1] + (others * mass[1]) * (mass[2] * slope[0]),
            sums[2] + pair * (mass[2] * slope[1]),
            sums[3] + last_two * slope[2],
        )

    def piece(start, totals):
        sums, products = totals[:-1], totals[-1]
        some = [blocks_ref[start + b] for b in range(per_piece)]
        x = unit * jnp.concatenate(
            [
                jnp.concatenate([block[:, width * j : width * (j + 1)] for block in some], axis=1)
                for j in range(dims // 8)
            ],
            axis=0,
        )
        full, slope = box_terms(-x, float(GRID) * unit - x)
        ratio = jnp.concatenate(split(slope / full, 2), axis=0)
        left = jnp.concatenate(split(x, 3) + split(jnp.log(0.5 * full) * LOG2_E, 3), axis=0)
        picked = lax.dot_general(
            left, right, (((0,), (0,)), ((), ())), preferred_element_type=jnp.float32
        )
        inside = []
        for at_row in range(0, per_piece * width, 16):
            whole, sums = step(picked[at_row : at_row + 16], sums)
            inside.append(jnp.concatenate(split(whole, 2), axis=1))
        inside = jnp.concatenate(inside, axis=0)
        products = products + jnp.dot(ratio, inside, preferred_element_type=jnp.float32)
        return (*sums, products)

    def pieces(number, totals):
        for start in range(0, group, per_piece):
            totals = piece(number * group + start, totals)
        return totals

    zero = jnp.zeros((16, queries), jnp.float32)
    totals = (zero,) * (1 + LIMITED) + (jnp.zeros((2 * dims, 2 * queries), jnp.float32),)
    if count == group:
        totals = pieces(0, totals)
    else:
        totals = lax.fori_loop(0, count // group, pieces, totals)
    sums = [jnp.sum(s, axis=0, keepdims=True) for s in totals[:-1]]
    products = totals[-1]
    deriv = products[:dims, :queries] + (products[dims:, :queries] + products[:dims, queries:])
    deriv = jnp.where(limited, 0.0, deriv * (SLOPE / 4))
    for mask, s in zip(chosen, sums[1:]):
        deriv = jnp.where(mask, s * (SLOPE / 4), deriv)
    out_ref[:dims, :] = deriv
    out_ref[dims:, :] = jnp.broadcast_to(sums[0] * 0.125, (8, queries))


def finish_kernel(sample_total, query_total, *refs):
    part_refs, (target_ref, log_ref, share_ref) = refs[:-3], refs[-3:]
    whole = tree_sum([ref[...] for ref in part_refs])
    dims, queries = whole.shape[0] - 8, whole.shape[1]
    smoothing = 1.0 / TABLE_ROWS
    estimate = whole[dims : dims + 1] / sample_total
    log_est = jnp.log(estimate + smoothing)
    log_ref[...] = log_est
    weight = 2.0 * (log_est - target_ref[...]) / (query_total * (estimate + smoothing))
    terms = whole[:dims] * (weight / sample_total)
    terms = jnp.concatenate([terms, jnp.zeros((queries - dims, queries), jnp.float32)], axis=0)
    share = jnp.sum(terms.T, axis=0, keepdims=True)
    for peer in range(share_ref.shape[0]):
        share_ref[peer] = share


def last_kernel(shares_ref, held_log_ref, log_ref, gradient_ref):
    total = tree_sum([shares_ref[peer] for peer in range(shares_ref.shape[0])])
    log_ref[...] = held_log_ref[0]
    gradient_ref[...] = total[0, : gradient_ref.shape[0]]


def everyone(x, axis):
    size = lax.axis_size(axis)
    return [x] + [
        lax.ppermute(x, axis, [(i, i ^ offset) for i in range(size)]) for offset in range(1, size)
    ]


def call(kernel, args, outs, scratch=(), placed=pltpu.VMEM):
    single = len(outs) == 1
    return pl.pallas_call(
        kernel,
        out_shape=outs[0] if single else outs,
        in_specs=[pl.BlockSpec(memory_space=placed)] * len(args),
        out_specs=pl.BlockSpec(memory_space=pltpu.VMEM)
        if single
        else [pl.BlockSpec(memory_space=pltpu.VMEM)] * len(outs),
        scratch_shapes=list(scratch),
        compiler_params=pltpu.CompilerParams(vmem_limit_bytes=32 << 20),
    )(*args)


def shape(*sizes):
    return jax.ShapeDtypeStruct(sizes, jnp.float32)


def on_device(samples, bounds, spread, counts):
    dims, width = samples.shape
    queries = bounds.shape[2]
    blocks, copies = lax.axis_size("blk"), lax.axis_size("grp")
    sample_total = width * blocks * copies
    query_total = queries * blocks

    counts_vector = pltpu.VMEM((1, queries), jnp.int32)
    packed, bounds, spread, target = call(
        load_kernel,
        [
            pltpu.with_memory_space_constraint(array, pltpu.HBM)
            for array in (samples, bounds, spread.reshape(1, dims), counts.reshape(1, queries))
        ],
        [
            pltpu.VMEM((blocks, 8, dims * width // 8), jnp.float32),
            pltpu.VMEM(bounds.shape, bounds.dtype),
            pltpu.VMEM((1, dims), jnp.float32),
            pltpu.VMEM((1, queries), jnp.float32),
        ],
        [pltpu.VMEM((dims, width), jnp.float32), counts_vector, pltpu.SemaphoreType.DMA((4,))],
        placed=pl.ANY,
    )
    order = [list(reversed(range(blocks)))]
    gathered = lax.all_to_all(packed, "blk", 0, 0, axis_index_groups=order)
    part = call(
        functools.partial(terms_kernel, width),
        [gathered, bounds, spread],
        [shape(dims + 8, queries)],
    )
    log_est, share = call(
        functools.partial(finish_kernel, sample_total, query_total),
        everyone(part, "grp") + [target],
        [shape(1, queries), shape(blocks, 1, queries)],
    )
    shares = lax.all_to_all(share, "blk", 0, 0, axis_index_groups=order)
    return call(last_kernel, [shares, log_est], [shape(queries), shape(dims)])


def solution(mesh):
    return jax.shard_map(
        on_device,
        mesh=mesh,
        in_specs=(P(None, ("blk", "grp")), P(None, None, "blk"), P(), P("blk")),
        out_specs=(P("blk"), P()),
        check_vma=False,
    )
```

```python
import functools

import jax
import jax.numpy as jnp
from jax import lax
from jax.experimental import pallas as pl
from jax.experimental.pallas import tpu as pltpu
from jax.sharding import PartitionSpec as P

TABLE_ROWS = 1048576
GRID = 256
LIMITED = 3

ROOT_HALF = 0.7071067811865476
LOG2_E = 1.4426950408889634
SLOPE = 0.5641895835477563


def box_terms(low, high):
    low_bell = jnp.exp2((low * low) * -LOG2_E)
    high_bell = jnp.exp2((high * high) * -LOG2_E)
    return lax.erf(high) - lax.erf(low), low * low_bell - high * high_bell


def split(x, parts):
    out = []
    for _ in range(parts - 1):
        head = x.astype(jnp.bfloat16)
        out.append(head)
        x = x - head.astype(jnp.float32)
    return out + [x.astype(jnp.bfloat16)]


def tree_sum(parts):
    while len(parts) > 1:
        parts = [a + b for a, b in zip(parts[::2], parts[1::2])]
    return parts[0]


def load_kernel(
    x_ref, bounds_ref, spread_ref, counts_ref,
    out_ref, held_bounds, held_spread, target_ref,
    held_x, held_counts, sems,
):
    sources = (x_ref, bounds_ref, spread_ref, counts_ref)
    targets = (held_x, held_bounds, held_spread, held_counts)
    copies = [
        pltpu.make_async_copy(source, target, sems.at[i])
        for i, (source, target) in enumerate(zip(sources, targets))
    ]
    for copy in copies:
        copy.start()
    copies[0].wait()
    rows = held_x.shape[0]
    packed = jnp.concatenate([held_x[8 * j : 8 * (j + 1), :] for j in range(rows // 8)], axis=1)
    for peer in range(out_ref.shape[0]):
        out_ref[peer] = packed
    for copy in copies[1:]:
        copy.wait()
    smoothing = 1.0 / TABLE_ROWS
    target_ref[...] = jnp.log(held_counts[...].astype(jnp.float32) / TABLE_ROWS + smoothing)


def terms_kernel(width, blocks_ref, bounds_ref, spread_ref, out_ref):
    dims, queries = bounds_ref.shape[1:]
    count = blocks_ref.shape[0]
    per_piece = 128 // width
    group = min(count, 4 * per_piece)

    low, high = bounds_ref[0], bounds_ref[1]
    limited = (high - low) != GRID
    at = lax.broadcasted_iota(jnp.int32, (dims, queries), 0)
    first = jnp.min(jnp.where(limited, at, dims), axis=0, keepdims=True)
    last = jnp.max(jnp.where(limited, at, -1), axis=0, keepdims=True)
    chosen = [at == first, limited & (at > first) & (at < last), at == last]

    row = lax.broadcasted_iota(jnp.int32, (dims, dims), 0)
    column = lax.broadcasted_iota(jnp.int32, (dims, dims), 1)
    spread = jnp.sum(jnp.where(row == column, spread_ref[...], 0.0), axis=1, keepdims=True)
    unit = ROOT_HALF / spread

    pick = lambda mask, values: jnp.sum(jnp.where(mask, values, 0.0), axis=0, keepdims=True)
    low = low.astype(jnp.float32) * unit
    high = high.astype(jnp.float32) * unit
    low_at = [pick(mask, low) for mask in chosen]
    high_at = [pick(mask, high) for mask in chosen]

    ones = [mask.astype(jnp.float32).astype(jnp.bfloat16) for mask in chosen]
    free = jnp.where(limited, 0.0, 1.0).astype(jnp.bfloat16)
    none = jnp.zeros_like(free)
    right = jnp.concatenate(
        [jnp.concatenate(ones + [none], axis=1)] * 3
        + [jnp.concatenate([none] * LIMITED + [free], axis=1)] * 3,
        axis=0,
    )

    def step(picked, sums):
        others = jnp.exp2(picked[:, LIMITED * queries :])
        mass, slope = [], []
        for k in range(LIMITED):
            points = picked[:, k * queries : (k + 1) * queries]
            m, s = box_terms(low_at[k] - points, high_at[k] - points)
            mass.append(m)
            slope.append(s)
        pair = others * mass[0]
        last_two = pair * mass[1]
        whole = last_two * mass[2]
        return whole, (
            sums[0] + whole,
            sums[1] + (others * mass[1]) * (mass[2] * slope[0]),
            sums[2] + pair * (mass[2] * slope[1]),
            sums[3] + last_two * slope[2],
        )

    def piece(start, totals):
        sums, products = totals[:-1], totals[-1]
        some = [blocks_ref[start + b] for b in range(per_piece)]
        x = unit * jnp.concatenate(
            [
                jnp.concatenate([block[:, width * j : width * (j + 1)] for block in some], axis=1)
                for j in range(dims // 8)
            ],
            axis=0,
        )
        full, slope = box_terms(-x, float(GRID) * unit - x)
        ratio = jnp.concatenate(split(slope / full, 2), axis=0)
        left = jnp.concatenate(split(x, 3) + split(jnp.log(0.5 * full) * LOG2_E, 3), axis=0)
        picked = lax.dot_general(
            left, right, (((0,), (0,)), ((), ())), preferred_element_type=jnp.float32
        )
        inside = []
        for at_row in range(0, per_piece * width, 16):
            whole, sums = step(picked[at_row : at_row + 16], sums)
            inside.append(jnp.concatenate(split(whole, 2), axis=1))
        inside = jnp.concatenate(inside, axis=0)
        products = products + jnp.dot(ratio, inside, preferred_element_type=jnp.float32)
        return (*sums, products)

    def pieces(number, totals):
        for start in range(0, group, per_piece):
            totals = piece(number * group + start, totals)
        return totals

    zero = jnp.zeros((16, queries), jnp.float32)
    totals = (zero,) * (1 + LIMITED) + (jnp.zeros((2 * dims, 2 * queries), jnp.float32),)
    if count == group:
        totals = pieces(0, totals)
    else:
        totals = lax.fori_loop(0, count // group, pieces, totals)
    sums = [jnp.sum(s, axis=0, keepdims=True) for s in totals[:-1]]
    products = totals[-1]
    deriv = products[:dims, :queries] + (products[dims:, :queries] + products[:dims, queries:])
    deriv = jnp.where(limited, 0.0, deriv * (SLOPE / 4))
    for mask, s in zip(chosen, sums[1:]):
        deriv = jnp.where(mask, s * (SLOPE / 4), deriv)
    out_ref[:dims, :] = deriv
    out_ref[dims:, :] = jnp.broadcast_to(sums[0] * 0.125, (8, queries))


def finish_kernel(sample_total, query_total, *refs):
    part_refs, (target_ref, log_ref, share_ref) = refs[:-3], refs[-3:]
    whole = tree_sum([ref[...] for ref in part_refs])
    dims, queries = whole.shape[0] - 8, whole.shape[1]
    smoothing = 1.0 / TABLE_ROWS
    estimate = whole[dims : dims + 1] / sample_total
    log_est = jnp.log(estimate + smoothing)
    log_ref[...] = log_est
    weight = 2.0 * (log_est - target_ref[...]) / (query_total * (estimate + smoothing))
    terms = whole[:dims] * (weight / sample_total)
    terms = jnp.concatenate([terms, jnp.zeros((queries - dims, queries), jnp.float32)], axis=0)
    share = jnp.sum(terms.T, axis=0, keepdims=True)
    for peer in range(share_ref.shape[0]):
        share_ref[peer] = share


def last_kernel(shares_ref, held_log_ref, log_ref, gradient_ref):
    total = tree_sum([shares_ref[peer] for peer in range(shares_ref.shape[0])])
    log_ref[...] = held_log_ref[0]
    gradient_ref[...] = total[0, : gradient_ref.shape[0]]


def everyone(x, axis):
    size = lax.axis_size(axis)
    return [x] + [
        lax.ppermute(x, axis, [(i, i ^ offset) for i in range(size)]) for offset in range(1, size)
    ]


def call(kernel, args, outs, scratch=(), placed=pltpu.VMEM):
    single = len(outs) == 1
    return pl.pallas_call(
        kernel,
        out_shape=outs[0] if single else outs,
        in_specs=[pl.BlockSpec(memory_space=placed)] * len(args),
        out_specs=pl.BlockSpec(memory_space=pltpu.VMEM)
        if single
        else [pl.BlockSpec(memory_space=pltpu.VMEM)] * len(outs),
        scratch_shapes=list(scratch),
        compiler_params=pltpu.CompilerParams(vmem_limit_bytes=32 << 20),
    )(*args)


def shape(*sizes):
    return jax.ShapeDtypeStruct(sizes, jnp.float32)


def on_device(samples, bounds, spread, counts):
    dims, width = samples.shape
    queries = bounds.shape[2]
    blocks, copies = lax.axis_size("blk"), lax.axis_size("grp")
    sample_total = width * blocks * copies
    query_total = queries * blocks

    counts_vector = pltpu.VMEM((1, queries), jnp.int32)
    packed, bounds, spread, target = call(
        load_kernel,
        [
            pltpu.with_memory_space_constraint(array, pltpu.HBM)
            for array in (samples, bounds, spread.reshape(1, dims), counts.reshape(1, queries))
        ],
        [
            pltpu.VMEM((blocks, 8, dims * width // 8), jnp.float32),
            pltpu.VMEM(bounds.shape, bounds.dtype),
            pltpu.VMEM((1, dims), jnp.float32),
            pltpu.VMEM((1, queries), jnp.float32),
        ],
        [pltpu.VMEM((dims, width), jnp.float32), counts_vector, pltpu.SemaphoreType.DMA((4,))],
        placed=pl.ANY,
    )
    turned = [1] + [0] * (blocks - 1)
    groups = [
        [b * copies + (c + turned[b]) % copies for b in reversed(range(blocks))]
        for c in range(copies)
    ]
    exchange = lambda x: lax.all_to_all(x, ("blk", "grp"), 0, 0, axis_index_groups=groups)
    gathered = exchange(packed)
    part = call(
        functools.partial(terms_kernel, width),
        [gathered, bounds, spread],
        [shape(dims + 8, queries)],
    )
    log_est, share = call(
        functools.partial(finish_kernel, sample_total, query_total),
        everyone(part, "grp") + [target],
        [shape(1, queries), shape(blocks, 1, queries)],
    )
    shares = exchange(share)
    return call(last_kernel, [shares, log_est], [shape(queries), shape(dims)])


def solution(mesh):
    return jax.shard_map(
        on_device,
        mesh=mesh,
        in_specs=(P(None, ("blk", "grp")), P(None, None, "blk"), P(), P("blk")),
        out_specs=(P("blk"), P()),
        check_vma=False,
    )
```

```python
import functools

import jax
import jax.numpy as jnp
from jax import lax
from jax.experimental import pallas as pl
from jax.experimental.pallas import tpu as pltpu
from jax.sharding import PartitionSpec as P

TABLE_ROWS = 1048576
GRID = 256
LIMITED = 3

ROOT_HALF = 0.7071067811865476
LOG2_E = 1.4426950408889634
SLOPE = 0.5641895835477563


def box_terms(low, high):
    low_bell = jnp.exp2((low * low) * -LOG2_E)
    high_bell = jnp.exp2((high * high) * -LOG2_E)
    return lax.erf(high) - lax.erf(low), low * low_bell - high * high_bell


def split(x, parts):
    out = []
    for _ in range(parts - 1):
        head = x.astype(jnp.bfloat16)
        out.append(head)
        x = x - head.astype(jnp.float32)
    return out + [x.astype(jnp.bfloat16)]


def tree_sum(parts):
    while len(parts) > 1:
        parts = [a + b for a, b in zip(parts[::2], parts[1::2])]
    return parts[0]


def load_kernel(
    x_ref, bounds_ref, spread_ref, counts_ref,
    out_ref, held_bounds, held_spread, target_ref,
    held_x, held_counts, sems,
):
    sources = (x_ref, bounds_ref, spread_ref, counts_ref)
    targets = (held_x, held_bounds, held_spread, held_counts)
    copies = [
        pltpu.make_async_copy(source, target, sems.at[i])
        for i, (source, target) in enumerate(zip(sources, targets))
    ]
    for copy in copies:
        copy.start()
    copies[0].wait()
    rows = held_x.shape[0]
    packed = jnp.concatenate([held_x[8 * j : 8 * (j + 1), :] for j in range(rows // 8)], axis=1)
    for peer in range(out_ref.shape[0]):
        out_ref[peer] = packed
    for copy in copies[1:]:
        copy.wait()
    smoothing = 1.0 / TABLE_ROWS
    target_ref[...] = jnp.log(held_counts[...].astype(jnp.float32) / TABLE_ROWS + smoothing)


def limits(bounds_ref):
    low, high = bounds_ref[0], bounds_ref[1]
    limited = (high - low) != GRID
    at = lax.broadcasted_iota(jnp.int32, low.shape, 0)
    first = jnp.min(jnp.where(limited, at, low.shape[0]), axis=0, keepdims=True)
    last = jnp.max(jnp.where(limited, at, -1), axis=0, keepdims=True)
    return limited, [at == first, limited & (at > first) & (at < last), at == last]


def select(masks, bounds_ref, spread_ref):
    limited, chosen = masks
    dims, queries = limited.shape
    row = lax.broadcasted_iota(jnp.int32, (dims, dims), 0)
    column = lax.broadcasted_iota(jnp.int32, (dims, dims), 1)
    spread = jnp.sum(jnp.where(row == column, spread_ref[...], 0.0), axis=1, keepdims=True)
    unit = ROOT_HALF / spread

    pick = lambda mask, values: jnp.sum(jnp.where(mask, values, 0.0), axis=0, keepdims=True)
    low = bounds_ref[0].astype(jnp.float32) * unit
    high = bounds_ref[1].astype(jnp.float32) * unit
    ends = [pick(mask, low) for mask in chosen] + [pick(mask, high) for mask in chosen]

    ones = [mask.astype(jnp.float32).astype(jnp.bfloat16) for mask in chosen]
    free = jnp.where(limited, 0.0, 1.0).astype(jnp.bfloat16)
    none = jnp.zeros_like(free)
    right = jnp.concatenate(
        [jnp.concatenate(ones + [none], axis=1)] * 3
        + [jnp.concatenate([none] * LIMITED + [free], axis=1)] * 3,
        axis=0,
    )
    return right, ends, unit


def terms(width, blocks_ref, masks, right, ends, unit):
    limited, chosen = masks
    dims, queries = limited.shape
    count = blocks_ref.shape[0]
    per_piece = 128 // width
    group = min(count, 4 * per_piece)
    low_at, high_at = ends[:LIMITED], ends[LIMITED:]

    def step(picked, sums):
        others = jnp.exp2(picked[:, LIMITED * queries :])
        mass, slope = [], []
        for k in range(LIMITED):
            points = picked[:, k * queries : (k + 1) * queries]
            m, s = box_terms(low_at[k] - points, high_at[k] - points)
            mass.append(m)
            slope.append(s)
        pair = others * mass[0]
        last_two = pair * mass[1]
        whole = last_two * mass[2]
        return whole, (
            sums[0] + whole,
            sums[1] + (others * mass[1]) * (mass[2] * slope[0]),
            sums[2] + pair * (mass[2] * slope[1]),
            sums[3] + last_two * slope[2],
        )

    def piece(start, totals):
        sums, products = totals[:-1], totals[-1]
        some = [blocks_ref[start + b] for b in range(per_piece)]
        x = unit * jnp.concatenate(
            [
                jnp.concatenate([block[:, width * j : width * (j + 1)] for block in some], axis=1)
                for j in range(dims // 8)
            ],
            axis=0,
        )
        full, slope = box_terms(-x, float(GRID) * unit - x)
        ratio = jnp.concatenate(split(slope / full, 2), axis=0)
        left = jnp.concatenate(split(x, 3) + split(jnp.log(0.5 * full) * LOG2_E, 3), axis=0)
        picked = lax.dot_general(
            left, right, (((0,), (0,)), ((), ())), preferred_element_type=jnp.float32
        )
        inside = []
        for at_row in range(0, per_piece * width, 16):
            whole, sums = step(picked[at_row : at_row + 16], sums)
            inside.append(jnp.concatenate(split(whole, 2), axis=1))
        inside = jnp.concatenate(inside, axis=0)
        products = products + jnp.dot(ratio, inside, preferred_element_type=jnp.float32)
        return (*sums, products)

    def pieces(number, totals):
        for start in range(0, group, per_piece):
            totals = piece(number * group + start, totals)
        return totals

    zero = jnp.zeros((16, queries), jnp.float32)
    totals = (zero,) * (1 + LIMITED) + (jnp.zeros((2 * dims, 2 * queries), jnp.float32),)
    if count == group:
        totals = pieces(0, totals)
    else:
        totals = lax.fori_loop(0, count // group, pieces, totals)
    sums = [jnp.sum(s, axis=0, keepdims=True) for s in totals[:-1]]
    products = totals[-1]
    deriv = products[:dims, :queries] + (products[dims:, :queries] + products[:dims, queries:])
    deriv = jnp.where(limited, 0.0, deriv * (SLOPE / 4))
    for mask, s in zip(chosen, sums[1:]):
        deriv = jnp.where(mask, s * (SLOPE / 4), deriv)
    return jnp.concatenate([deriv, jnp.broadcast_to(sums[0] * 0.125, (8, queries))], axis=0)


def own_kernel(width, blocks_ref, bounds_ref, spread_ref, part_ref, right_ref, ends_ref, unit_ref):
    masks = limits(bounds_ref)
    right, ends, unit = select(masks, bounds_ref, spread_ref)
    part_ref[...] = terms(width, blocks_ref, masks, right, ends, unit)
    right_ref[...] = right
    for i, end in enumerate(ends):
        ends_ref[i : i + 1, :] = end
    unit_ref[...] = jnp.broadcast_to(unit, unit_ref.shape)


def other_kernel(width, sample_total, query_total, *refs):
    blocks_refs = refs[:-8]
    part_ref, right_ref, ends_ref, unit_ref, bounds_ref, target_ref, log_ref, share_ref = refs[-8:]
    masks = limits(bounds_ref)
    right, unit = right_ref[...], unit_ref[:, :1]
    ends = [ends_ref[i : i + 1, :] for i in range(2 * LIMITED)]
    parts = [part_ref[...]]
    parts += [terms(width, blocks_ref, masks, right, ends, unit) for blocks_ref in blocks_refs]
    whole = tree_sum(parts)
    dims, queries = masks[0].shape
    smoothing = 1.0 / TABLE_ROWS
    estimate = whole[dims : dims + 1] / sample_total
    log_est = jnp.log(estimate + smoothing)
    log_ref[...] = log_est
    weight = 2.0 * (log_est - target_ref[...]) / (query_total * (estimate + smoothing))
    terms_at = whole[:dims] * (weight / sample_total)
    terms_at = jnp.concatenate([terms_at, jnp.zeros((queries - dims, queries), jnp.float32)], axis=0)
    share = jnp.sum(terms_at.T, axis=0, keepdims=True)
    for peer in range(share_ref.shape[0]):
        share_ref[peer] = share


def last_kernel(shares_ref, held_log_ref, log_ref, gradient_ref):
    total = tree_sum([shares_ref[peer] for peer in range(shares_ref.shape[0])])
    log_ref[...] = held_log_ref[0]
    gradient_ref[...] = total[0, : gradient_ref.shape[0]]


def everyone(x, axis):
    size = lax.axis_size(axis)
    return [x] + [
        lax.ppermute(x, axis, [(i, i ^ offset) for i in range(size)]) for offset in range(1, size)
    ]


def call(kernel, args, outs, scratch=(), placed=pltpu.VMEM, cost=None):
    single = len(outs) == 1
    return pl.pallas_call(
        kernel,
        out_shape=outs[0] if single else outs,
        in_specs=[pl.BlockSpec(memory_space=placed)] * len(args),
        out_specs=pl.BlockSpec(memory_space=pltpu.VMEM)
        if single
        else [pl.BlockSpec(memory_space=pltpu.VMEM)] * len(outs),
        scratch_shapes=list(scratch),
        cost_estimate=cost,
        compiler_params=pltpu.CompilerParams(vmem_limit_bytes=32 << 20),
    )(*args)


def shape(*sizes):
    return jax.ShapeDtypeStruct(sizes, jnp.float32)


def on_device(samples, bounds, spread, counts):
    dims, width = samples.shape
    queries = bounds.shape[2]
    blocks, copies = lax.axis_size("blk"), lax.axis_size("grp")
    sample_total = width * blocks * copies
    query_total = queries * blocks

    counts_vector = pltpu.VMEM((1, queries), jnp.int32)
    packed, bounds, spread, target = call(
        load_kernel,
        [
            pltpu.with_memory_space_constraint(array, pltpu.HBM)
            for array in (samples, bounds, spread.reshape(1, dims), counts.reshape(1, queries))
        ],
        [
            pltpu.VMEM((blocks, 8, dims * width // 8), jnp.float32),
            pltpu.VMEM(bounds.shape, bounds.dtype),
            pltpu.VMEM((1, dims), jnp.float32),
            pltpu.VMEM((1, queries), jnp.float32),
        ],
        [pltpu.VMEM((dims, width), jnp.float32), counts_vector, pltpu.SemaphoreType.DMA((4,))],
        placed=pl.ANY,
    )
    turned = [1] + [0] * (blocks - 1)
    groups = [
        [b * copies + (c + turned[b]) % copies for b in reversed(range(blocks))]
        for c in range(copies)
    ]
    exchange = lambda x: lax.all_to_all(x, ("blk", "grp"), 0, 0, axis_index_groups=groups)
    gathered = exchange(packed)
    others = everyone(gathered, "grp")[1:]
    elements = LIMITED * gathered.shape[0] * width * queries
    part, right, ends, unit = call(
        functools.partial(own_kernel, width),
        [gathered, bounds, spread],
        [
            shape(dims + 8, queries),
            jax.ShapeDtypeStruct((6 * dims, (LIMITED + 1) * queries), jnp.bfloat16),
            shape(8, queries),
            shape(dims, queries),
        ],
        cost=pl.CostEstimate(
            flops=100 * elements, bytes_accessed=64 * elements, transcendentals=4 * elements
        ),
    )
    log_est, share = call(
        functools.partial(other_kernel, width, sample_total, query_total),
        others + [part, right, ends, unit, bounds, target],
        [shape(1, queries), shape(blocks, 1, queries)],
    )
    shares = exchange(share)
    return call(last_kernel, [shares, log_est], [shape(queries), shape(dims)])


def solution(mesh):
    return jax.shard_map(
        on_device,
        mesh=mesh,
        in_specs=(P(None, ("blk", "grp")), P(None, None, "blk"), P(), P("blk")),
        out_specs=(P("blk"), P()),
        check_vma=False,
    )
```

```python
import functools

import jax
import jax.numpy as jnp
from jax import lax
from jax.experimental import pallas as pl
from jax.experimental.pallas import tpu as pltpu
from jax.sharding import PartitionSpec as P

TABLE_ROWS = 1048576
GRID = 256
LIMITED = 3

ROOT_HALF = 0.7071067811865476
LOG2_E = 1.4426950408889634
SLOPE = 0.5641895835477563


def box_terms(low, high):
    low_bell = jnp.exp2((low * low) * -LOG2_E)
    high_bell = jnp.exp2((high * high) * -LOG2_E)
    return lax.erf(high) - lax.erf(low), low * low_bell - high * high_bell


def split(x, parts):
    out = []
    for _ in range(parts - 1):
        head = x.astype(jnp.bfloat16)
        out.append(head)
        x = x - head.astype(jnp.float32)
    return out + [x.astype(jnp.bfloat16)]


def tree_sum(parts):
    while len(parts) > 1:
        parts = [a + b for a, b in zip(parts[::2], parts[1::2])]
    return parts[0]


def load_kernel(
    x_ref, bounds_ref, spread_ref, counts_ref,
    out_ref, held_bounds, held_spread, target_ref,
    held_x, held_counts, sems,
):
    sources = (x_ref, bounds_ref, spread_ref, counts_ref)
    targets = (held_x, held_bounds, held_spread, held_counts)
    copies = [
        pltpu.make_async_copy(source, target, sems.at[i])
        for i, (source, target) in enumerate(zip(sources, targets))
    ]
    for copy in copies:
        copy.start()
    copies[0].wait()
    rows = held_x.shape[0]
    packed = jnp.concatenate([held_x[8 * j : 8 * (j + 1), :] for j in range(rows // 8)], axis=1)
    for peer in range(out_ref.shape[0]):
        out_ref[peer] = packed
    for copy in copies[1:]:
        copy.wait()
    smoothing = 1.0 / TABLE_ROWS
    target_ref[...] = jnp.log(held_counts[...].astype(jnp.float32) / TABLE_ROWS + smoothing)


def terms_kernel(width, blocks_ref, bounds_ref, spread_ref, out_ref):
    dims, queries = bounds_ref.shape[1:]
    count = blocks_ref.shape[0]
    per_piece = 128 // width
    group = min(count, 4 * per_piece)

    low, high = bounds_ref[0], bounds_ref[1]
    limited = (high - low) != GRID
    at = lax.broadcasted_iota(jnp.int32, (dims, queries), 0)
    first = jnp.min(jnp.where(limited, at, dims), axis=0, keepdims=True)
    last = jnp.max(jnp.where(limited, at, -1), axis=0, keepdims=True)
    chosen = [at == first, limited & (at > first) & (at < last), at == last]

    row = lax.broadcasted_iota(jnp.int32, (dims, dims), 0)
    column = lax.broadcasted_iota(jnp.int32, (dims, dims), 1)
    spread = jnp.sum(jnp.where(row == column, spread_ref[...], 0.0), axis=1, keepdims=True)
    unit = ROOT_HALF / spread

    pick = lambda mask, values: jnp.sum(jnp.where(mask, values, 0.0), axis=0, keepdims=True)
    low = low.astype(jnp.float32) * unit
    high = high.astype(jnp.float32) * unit
    low_at = [pick(mask, low) for mask in chosen]
    high_at = [pick(mask, high) for mask in chosen]

    ones = [mask.astype(jnp.float32).astype(jnp.bfloat16) for mask in chosen]
    free = jnp.where(limited, 0.0, 1.0).astype(jnp.bfloat16)
    none = jnp.zeros_like(free)
    right = jnp.concatenate(
        [jnp.concatenate(ones + [none], axis=1)] * 3
        + [jnp.concatenate([none] * LIMITED + [free], axis=1)] * 3,
        axis=0,
    )

    def step(picked, sums):
        others = jnp.exp2(picked[:, LIMITED * queries :])
        mass, slope = [], []
        for k in range(LIMITED):
            points = picked[:, k * queries : (k + 1) * queries]
            m, s = box_terms(low_at[k] - points, high_at[k] - points)
            mass.append(m)
            slope.append(s)
        pair = others * mass[0]
        last_two = pair * mass[1]
        whole = last_two * mass[2]
        return whole, (
            sums[0] + whole,
            sums[1] + (others * mass[1]) * (mass[2] * slope[0]),
            sums[2] + pair * (mass[2] * slope[1]),
            sums[3] + last_two * slope[2],
        )

    def piece(start, totals):
        sums, products = totals[:-1], totals[-1]
        some = [blocks_ref[start + b] for b in range(per_piece)]
        x = unit * jnp.concatenate(
            [
                jnp.concatenate([block[:, width * j : width * (j + 1)] for block in some], axis=1)
                for j in range(dims // 8)
            ],
            axis=0,
        )
        full, slope = box_terms(-x, float(GRID) * unit - x)
        ratio = jnp.concatenate(split(slope / full, 2), axis=0)
        left = jnp.concatenate(split(x, 3) + split(jnp.log(0.5 * full) * LOG2_E, 3), axis=0)
        picked = lax.dot_general(
            left, right, (((0,), (0,)), ((), ())), preferred_element_type=jnp.float32
        )
        inside = []
        for at_row in range(0, per_piece * width, 16):
            whole, sums = step(picked[at_row : at_row + 16], sums)
            inside.append(jnp.concatenate(split(whole, 2), axis=1))
        inside = jnp.concatenate(inside, axis=0)
        products = products + jnp.dot(ratio, inside, preferred_element_type=jnp.float32)
        return (*sums, products)

    def pieces(number, totals):
        for start in range(0, group, per_piece):
            totals = piece(number * group + start, totals)
        return totals

    zero = jnp.zeros((16, queries), jnp.float32)
    totals = (zero,) * (1 + LIMITED) + (jnp.zeros((2 * dims, 2 * queries), jnp.float32),)
    if count == group:
        totals = pieces(0, totals)
    else:
        totals = lax.fori_loop(0, count // group, pieces, totals)
    sums = [jnp.sum(s, axis=0, keepdims=True) for s in totals[:-1]]
    products = totals[-1]
    deriv = products[:dims, :queries] + (products[dims:, :queries] + products[:dims, queries:])
    deriv = jnp.where(limited, 0.0, deriv * (SLOPE / 4))
    for mask, s in zip(chosen, sums[1:]):
        deriv = jnp.where(mask, s * (SLOPE / 4), deriv)
    out_ref[:dims, :] = deriv
    out_ref[dims:, :] = jnp.broadcast_to(sums[0] * 0.125, (8, queries))


def finish_kernel(sample_total, query_total, *refs):
    part_refs, (target_ref, log_ref, share_ref) = refs[:-3], refs[-3:]
    whole = tree_sum([ref[...] for ref in part_refs])
    dims, queries = whole.shape[0] - 8, whole.shape[1]
    smoothing = 1.0 / TABLE_ROWS
    estimate = whole[dims : dims + 1] / sample_total
    log_est = jnp.log(estimate + smoothing)
    log_ref[...] = log_est
    weight = 2.0 * (log_est - target_ref[...]) / (query_total * (estimate + smoothing))
    terms = whole[:dims] * (weight / sample_total)
    terms = jnp.concatenate([terms, jnp.zeros((queries - dims, queries), jnp.float32)], axis=0)
    share = jnp.sum(terms.T, axis=0, keepdims=True)
    for peer in range(share_ref.shape[0]):
        share_ref[peer] = share


def last_kernel(shares_ref, held_log_ref, log_ref, gradient_ref):
    total = tree_sum([shares_ref[peer] for peer in range(shares_ref.shape[0])])
    log_ref[...] = held_log_ref[0]
    gradient_ref[...] = total[0, : gradient_ref.shape[0]]


def everyone(x, axis):
    size = lax.axis_size(axis)
    return [x] + [
        lax.ppermute(x, axis, [(i, i ^ offset) for i in range(size)]) for offset in range(1, size)
    ]


def call(kernel, args, outs, scratch=(), placed=pltpu.VMEM):
    single = len(outs) == 1
    return pl.pallas_call(
        kernel,
        out_shape=outs[0] if single else outs,
        in_specs=[pl.BlockSpec(memory_space=placed)] * len(args),
        out_specs=pl.BlockSpec(memory_space=pltpu.VMEM)
        if single
        else [pl.BlockSpec(memory_space=pltpu.VMEM)] * len(outs),
        scratch_shapes=list(scratch),
        compiler_params=pltpu.CompilerParams(vmem_limit_bytes=32 << 20),
    )(*args)


def shape(*sizes):
    return jax.ShapeDtypeStruct(sizes, jnp.float32)


def on_device(samples, bounds, spread, counts):
    dims, width = samples.shape
    queries = bounds.shape[2]
    blocks, copies = lax.axis_size("blk"), lax.axis_size("grp")
    sample_total = width * blocks * copies
    query_total = queries * blocks

    counts_vector = pltpu.VMEM((1, queries), jnp.int32)
    packed, bounds, spread, target = call(
        load_kernel,
        [
            pltpu.with_memory_space_constraint(array, pltpu.HBM)
            for array in (samples, bounds, spread.reshape(1, dims), counts.reshape(1, queries))
        ],
        [
            pltpu.VMEM((blocks, 8, dims * width // 8), jnp.float32),
            pltpu.VMEM(bounds.shape, bounds.dtype),
            pltpu.VMEM((1, dims), jnp.float32),
            pltpu.VMEM((1, queries), jnp.float32),
        ],
        [pltpu.VMEM((dims, width), jnp.float32), counts_vector, pltpu.SemaphoreType.DMA((4,))],
        placed=pl.ANY,
    )
    def exchange(x, turned, lasts):
        groups = []
        for c in range(copies):
            blocks_of = [b for b in reversed(range(blocks)) if b != lasts[c]] + [lasts[c]]
            groups.append([b * copies + (c + (b == turned)) % copies for b in blocks_of])
        return lax.all_to_all(x, ("blk", "grp"), 0, 0, axis_index_groups=groups)

    middle = blocks // 3
    gathered = exchange(packed, middle, [middle] * (copies - 1) + [middle + 1])
    part = call(
        functools.partial(terms_kernel, width),
        [gathered, bounds, spread],
        [shape(dims + 8, queries)],
    )
    log_est, share = call(
        functools.partial(finish_kernel, sample_total, query_total),
        everyone(part, "grp") + [target],
        [shape(1, queries), shape(blocks, 1, queries)],
    )
    shares = exchange(share, 0, [0] * copies)
    return call(last_kernel, [shares, log_est], [shape(queries), shape(dims)])


def solution(mesh):
    return jax.shard_map(
        on_device,
        mesh=mesh,
        in_specs=(P(None, ("blk", "grp")), P(None, None, "blk"), P(), P("blk")),
        out_specs=(P("blk"), P()),
        check_vma=False,
    )
```

```python
import functools

import jax
import jax.numpy as jnp
from jax import lax
from jax.experimental import pallas as pl
from jax.experimental.pallas import tpu as pltpu
from jax.sharding import PartitionSpec as P

TABLE_ROWS = 1048576
GRID = 256
LIMITED = 3

ROOT_HALF = 0.7071067811865476
LOG2_E = 1.4426950408889634
SLOPE = 0.5641895835477563


def box_terms(low, high):
    low_bell = jnp.exp2((low * low) * -LOG2_E)
    high_bell = jnp.exp2((high * high) * -LOG2_E)
    return lax.erf(high) - lax.erf(low), low * low_bell - high * high_bell


def split(x, parts):
    out = []
    for _ in range(parts - 1):
        head = x.astype(jnp.bfloat16)
        out.append(head)
        x = x - head.astype(jnp.float32)
    return out + [x.astype(jnp.bfloat16)]


def tree_sum(parts):
    while len(parts) > 1:
        parts = [a + b for a, b in zip(parts[::2], parts[1::2])]
    return parts[0]


def load_kernel(
    x_ref, bounds_ref, spread_ref, counts_ref,
    out_ref, held_bounds, held_spread, target_ref,
    held_x, held_counts, sems,
):
    sources = (x_ref, bounds_ref, spread_ref, counts_ref)
    targets = (held_x, held_bounds, held_spread, held_counts)
    copies = [
        pltpu.make_async_copy(source, target, sems.at[i])
        for i, (source, target) in enumerate(zip(sources, targets))
    ]
    for copy in copies:
        copy.start()
    copies[0].wait()
    rows = held_x.shape[0]
    packed = jnp.concatenate([held_x[8 * j : 8 * (j + 1), :] for j in range(rows // 8)], axis=1)
    for peer in range(out_ref.shape[0]):
        out_ref[peer] = packed
    for copy in copies[1:]:
        copy.wait()
    smoothing = 1.0 / TABLE_ROWS
    target_ref[...] = jnp.log(held_counts[...].astype(jnp.float32) / TABLE_ROWS + smoothing)


def terms_kernel(width, blocks_ref, bounds_ref, spread_ref, out_ref):
    dims, queries = bounds_ref.shape[1:]
    count = blocks_ref.shape[0]
    per_piece = 128 // width
    group = min(count, 4 * per_piece)

    low, high = bounds_ref[0], bounds_ref[1]
    limited = (high - low) != GRID
    at = lax.broadcasted_iota(jnp.int32, (dims, queries), 0)
    first = jnp.min(jnp.where(limited, at, dims), axis=0, keepdims=True)
    last = jnp.max(jnp.where(limited, at, -1), axis=0, keepdims=True)
    chosen = [at == first, limited & (at > first) & (at < last), at == last]

    row = lax.broadcasted_iota(jnp.int32, (dims, dims), 0)
    column = lax.broadcasted_iota(jnp.int32, (dims, dims), 1)
    spread = jnp.sum(jnp.where(row == column, spread_ref[...], 0.0), axis=1, keepdims=True)
    unit = ROOT_HALF / spread

    pick = lambda mask, values: jnp.sum(jnp.where(mask, values, 0.0), axis=0, keepdims=True)
    low = low.astype(jnp.float32) * unit
    high = high.astype(jnp.float32) * unit
    low_at = [pick(mask, low) for mask in chosen]
    high_at = [pick(mask, high) for mask in chosen]

    ones = [mask.astype(jnp.float32).astype(jnp.bfloat16) for mask in chosen]
    free = jnp.where(limited, 0.0, 1.0).astype(jnp.bfloat16)
    none = jnp.zeros_like(free)
    right = jnp.concatenate(
        [jnp.concatenate(ones + [none], axis=1)] * 3
        + [jnp.concatenate([none] * LIMITED + [free], axis=1)] * 3,
        axis=0,
    )

    def step(picked, sums):
        others = jnp.exp2(picked[:, LIMITED * queries :])
        mass, slope = [], []
        for k in range(LIMITED):
            points = picked[:, k * queries : (k + 1) * queries]
            m, s = box_terms(low_at[k] - points, high_at[k] - points)
            mass.append(m)
            slope.append(s)
        pair = others * mass[0]
        last_two = pair * mass[1]
        whole = last_two * mass[2]
        return whole, (
            sums[0] + whole,
            sums[1] + (others * mass[1]) * (mass[2] * slope[0]),
            sums[2] + pair * (mass[2] * slope[1]),
            sums[3] + last_two * slope[2],
        )

    def piece(start, totals):
        sums, products = totals[:-1], totals[-1]
        some = [blocks_ref[start + b] for b in range(per_piece)]
        x = unit * jnp.concatenate(
            [
                jnp.concatenate([block[:, width * j : width * (j + 1)] for block in some], axis=1)
                for j in range(dims // 8)
            ],
            axis=0,
        )
        full, slope = box_terms(-x, float(GRID) * unit - x)
        ratio = jnp.concatenate(split(slope / full, 2), axis=0)
        left = jnp.concatenate(split(x, 3) + split(jnp.log(0.5 * full) * LOG2_E, 3), axis=0)
        picked = lax.dot_general(
            left, right, (((0,), (0,)), ((), ())), preferred_element_type=jnp.float32
        )
        inside = []
        for at_row in range(0, per_piece * width, 16):
            whole, sums = step(picked[at_row : at_row + 16], sums)
            inside.append(jnp.concatenate(split(whole, 2), axis=1))
        inside = jnp.concatenate(inside, axis=0)
        products = products + jnp.dot(ratio, inside, preferred_element_type=jnp.float32)
        return (*sums, products)

    def pieces(number, totals):
        for start in range(0, group, per_piece):
            totals = piece(number * group + start, totals)
        return totals

    zero = jnp.zeros((16, queries), jnp.float32)
    totals = (zero,) * (1 + LIMITED) + (jnp.zeros((2 * dims, 2 * queries), jnp.float32),)
    if count == group:
        totals = pieces(0, totals)
    else:
        totals = lax.fori_loop(0, count // group, pieces, totals)
    sums = [jnp.sum(s, axis=0, keepdims=True) for s in totals[:-1]]
    products = totals[-1]
    deriv = products[:dims, :queries] + (products[dims:, :queries] + products[:dims, queries:])
    deriv = jnp.where(limited, 0.0, deriv * (SLOPE / 4))
    for mask, s in zip(chosen, sums[1:]):
        deriv = jnp.where(mask, s * (SLOPE / 4), deriv)
    out_ref[:dims, :] = deriv
    out_ref[dims:, :] = jnp.broadcast_to(sums[0] * 0.125, (8, queries))


def finish_kernel(sample_total, query_total, *refs):
    part_refs, (target_ref, log_ref, share_ref) = refs[:-3], refs[-3:]
    whole = tree_sum([ref[...] for ref in part_refs])
    dims, queries = whole.shape[0] - 8, whole.shape[1]
    smoothing = 1.0 / TABLE_ROWS
    estimate = whole[dims : dims + 1] / sample_total
    log_est = jnp.log(estimate + smoothing)
    log_ref[...] = log_est
    weight = 2.0 * (log_est - target_ref[...]) / (query_total * (estimate + smoothing))
    terms = whole[:dims] * (weight / sample_total)
    terms = jnp.concatenate([terms, jnp.zeros((queries - dims, queries), jnp.float32)], axis=0)
    share = jnp.sum(terms.T, axis=0, keepdims=True)
    for peer in range(share_ref.shape[0]):
        share_ref[peer] = share


def last_kernel(shares_ref, held_log_ref, log_ref, gradient_ref):
    total = tree_sum([shares_ref[peer] for peer in range(shares_ref.shape[0])])
    log_ref[...] = held_log_ref[0]
    gradient_ref[...] = total[0, : gradient_ref.shape[0]]


def everyone(x, axis):
    size = lax.axis_size(axis)
    return [x] + [
        lax.ppermute(x, axis, [(i, i ^ offset) for i in range(size)]) for offset in range(1, size)
    ]


def call(kernel, args, outs, scratch=(), placed=pltpu.VMEM):
    single = len(outs) == 1
    return pl.pallas_call(
        kernel,
        out_shape=outs[0] if single else outs,
        in_specs=[pl.BlockSpec(memory_space=placed)] * len(args),
        out_specs=pl.BlockSpec(memory_space=pltpu.VMEM)
        if single
        else [pl.BlockSpec(memory_space=pltpu.VMEM)] * len(outs),
        scratch_shapes=list(scratch),
        compiler_params=pltpu.CompilerParams(vmem_limit_bytes=32 << 20),
    )(*args)


def shape(*sizes):
    return jax.ShapeDtypeStruct(sizes, jnp.float32)


def on_device(samples, bounds, spread, counts):
    dims, width = samples.shape
    queries = bounds.shape[2]
    blocks, copies = lax.axis_size("blk"), lax.axis_size("grp")
    sample_total = width * blocks * copies
    query_total = queries * blocks

    counts_vector = pltpu.VMEM((1, queries), jnp.int32)
    packed, bounds, spread, target = call(
        load_kernel,
        [
            pltpu.with_memory_space_constraint(array, pltpu.HBM)
            for array in (samples, bounds, spread.reshape(1, dims), counts.reshape(1, queries))
        ],
        [
            pltpu.VMEM((blocks, 8, dims * width // 8), jnp.float32),
            pltpu.VMEM(bounds.shape, bounds.dtype),
            pltpu.VMEM((1, dims), jnp.float32),
            pltpu.VMEM((1, queries), jnp.float32),
        ],
        [pltpu.VMEM((dims, width), jnp.float32), counts_vector, pltpu.SemaphoreType.DMA((4,))],
        placed=pl.ANY,
    )
    turned = [1] + [0] * (blocks - 1)

    def exchange(x, order):
        groups = [
            [b * copies + (c + turned[b]) % copies for b in order] for c in range(copies)
        ]
        return lax.all_to_all(x, ("blk", "grp"), 0, 0, axis_index_groups=groups)

    gathered = exchange(packed, range(blocks))
    part = call(
        functools.partial(terms_kernel, width),
        [gathered, bounds, spread],
        [shape(dims + 8, queries)],
    )
    log_est, share = call(
        functools.partial(finish_kernel, sample_total, query_total),
        everyone(part, "grp") + [target],
        [shape(1, queries), shape(blocks, 1, queries)],
    )
    shares = exchange(share, range(blocks - 1, -1, -1))
    return call(last_kernel, [shares, log_est], [shape(queries), shape(dims)])


def solution(mesh):
    return jax.shard_map(
        on_device,
        mesh=mesh,
        in_specs=(P(None, ("blk", "grp")), P(None, None, "blk"), P(), P("blk")),
        out_specs=(P("blk"), P()),
        check_vma=False,
    )
```

```python
import functools

import jax
import jax.numpy as jnp
from jax import lax
from jax.experimental import pallas as pl
from jax.experimental.pallas import tpu as pltpu
from jax.sharding import PartitionSpec as P

TABLE_ROWS = 1048576
GRID = 256
LIMITED = 3

ROOT_HALF = 0.7071067811865476
LOG2_E = 1.4426950408889634
SLOPE = 0.5641895835477563


def box_terms(low, high):
    low_bell = jnp.exp2((low * low) * -LOG2_E)
    high_bell = jnp.exp2((high * high) * -LOG2_E)
    return lax.erf(high) - lax.erf(low), low * low_bell - high * high_bell


def split(x, parts):
    out = []
    for _ in range(parts - 1):
        head = x.astype(jnp.bfloat16)
        out.append(head)
        x = x - head.astype(jnp.float32)
    return out + [x.astype(jnp.bfloat16)]


def tree_sum(parts):
    while len(parts) > 1:
        parts = [a + b for a, b in zip(parts[::2], parts[1::2])]
    return parts[0]


def load_kernel(
    x_ref, bounds_ref, spread_ref, counts_ref,
    out_ref, held_bounds, held_spread, target_ref,
    held_x, held_counts, sems,
):
    sources = (x_ref, bounds_ref, spread_ref, counts_ref)
    targets = (held_x, held_bounds, held_spread, held_counts)
    copies = [
        pltpu.make_async_copy(source, target, sems.at[i])
        for i, (source, target) in enumerate(zip(sources, targets))
    ]
    for copy in copies:
        copy.start()
    copies[0].wait()
    rows = held_x.shape[1]
    turned = held_x[...].T
    packed = jnp.concatenate([turned[8 * j : 8 * (j + 1), :] for j in range(rows // 8)], axis=1)
    for peer in range(out_ref.shape[0]):
        out_ref[peer] = packed
    for copy in copies[1:]:
        copy.wait()
    smoothing = 1.0 / TABLE_ROWS
    target_ref[...] = jnp.log(held_counts[...].astype(jnp.float32) / TABLE_ROWS + smoothing)


def terms_kernel(blocks_ref, bounds_ref, spread_ref, out_ref):
    dims, queries = bounds_ref.shape[1:]
    lanes = blocks_ref.shape[2]
    pieces = lanes // dims
    group = 128 // blocks_ref.shape[1]

    low, high = bounds_ref[0], bounds_ref[1]
    limited = (high - low) != GRID
    at = lax.broadcasted_iota(jnp.int32, (dims, queries), 0)
    first = jnp.min(jnp.where(limited, at, dims), axis=0, keepdims=True)
    last = jnp.max(jnp.where(limited, at, -1), axis=0, keepdims=True)
    chosen = [at == first, limited & (at > first) & (at < last), at == last]

    unit_row = ROOT_HALF / spread_ref[...]
    row = lax.broadcasted_iota(jnp.int32, (dims, dims), 0)
    column = lax.broadcasted_iota(jnp.int32, (dims, dims), 1)
    unit = jnp.sum(jnp.where(row == column, unit_row, 0.0), axis=1, keepdims=True)
    unit_row = jnp.concatenate([unit_row] * pieces, axis=1)

    pick = lambda mask, values: jnp.sum(jnp.where(mask, values, 0.0), axis=0, keepdims=True)
    low = low.astype(jnp.float32) * unit
    high = high.astype(jnp.float32) * unit
    low_at = [pick(mask, low) for mask in chosen]
    high_at = [pick(mask, high) for mask in chosen]

    as_ones = lambda mask: jnp.where(mask, 1.0, 0.0).astype(jnp.bfloat16)
    one_hot = jnp.concatenate([as_ones(mask) for mask in chosen], axis=1)
    one_hot = jnp.concatenate([one_hot] * pieces, axis=0)
    free = jnp.concatenate([as_ones(jnp.logical_not(limited))] * pieces, axis=0)

    def step(boxes, others, sums):
        others = jnp.exp2(others)
        mass, slope = [], []
        for k in range(LIMITED):
            points = boxes[:, k * queries : (k + 1) * queries]
            m, s = box_terms(low_at[k] - points, high_at[k] - points)
            mass.append(m)
            slope.append(s)
        pair = others * mass[0]
        last_two = pair * mass[1]
        whole = last_two * mass[2]
        return whole, (
            sums[0] + whole,
            sums[1] + (others * mass[1]) * (mass[2] * slope[0]),
            sums[2] + pair * (mass[2] * slope[1]),
            sums[3] + last_two * slope[2],
        )

    place = lax.broadcasted_iota(jnp.int32, (1, lanes), 1) // dims

    def thirds(x):
        head = x.astype(jnp.bfloat16).astype(jnp.float32)
        rest = x - head
        tail = rest - rest.astype(jnp.bfloat16).astype(jnp.float32)
        return [x, pltpu.roll(rest, dims, 1), pltpu.roll(tail, 2 * dims, 1)]

    def left(parts, j):
        x = jnp.zeros_like(parts[0])
        for p, part in enumerate(parts):
            x = jnp.where(place == (j + p) % pieces, part, x)
        return x.astype(jnp.bfloat16)

    def chunk(number, totals):
        sums, products = totals[:-1], totals[-1]
        x = blocks_ref[pl.ds(number * group, group)].reshape(128, lanes) * unit_row
        points = thirds(x)
        full, slope = box_terms(-x, float(GRID) * unit_row - x)
        logs = thirds(jnp.log(0.5 * full) * LOG2_E)
        ratio = split((slope / full).T, 2)
        for j in range(pieces):
            boxes = jnp.dot(left(points, j), one_hot, preferred_element_type=jnp.float32)
            others = jnp.dot(left(logs, j), free, preferred_element_type=jnp.float32)
            inside = []
            for r in range(0, 128, 16):
                whole, sums = step(boxes[r : r + 16], others[r : r + 16], sums)
                inside.append(jnp.concatenate(split(whole, 2), axis=1))
            ratio_at = jnp.concatenate([part[j * dims : (j + 1) * dims] for part in ratio], axis=0)
            products = products + jnp.dot(
                ratio_at, jnp.concatenate(inside, axis=0), preferred_element_type=jnp.float32
            )
        return (*sums, products)

    zero = jnp.zeros((16, queries), jnp.float32)
    totals = (zero,) * (1 + LIMITED) + (jnp.zeros((2 * dims, 2 * queries), jnp.float32),)
    chunks = blocks_ref.shape[0] // group
    totals = chunk(0, totals) if chunks == 1 else lax.fori_loop(0, chunks, chunk, totals)
    sums = [jnp.sum(s, axis=0, keepdims=True) for s in totals[:-1]]
    products = totals[-1]
    deriv = products[:dims, :queries] + (products[dims:, :queries] + products[:dims, queries:])
    deriv = jnp.where(limited, 0.0, deriv * (SLOPE / 4))
    for mask, s in zip(chosen, sums[1:]):
        deriv = jnp.where(mask, s * (SLOPE / 4), deriv)
    out_ref[:dims, :] = deriv
    out_ref[dims:, :] = jnp.broadcast_to(sums[0] * 0.125, (8, queries))


def finish_kernel(sample_total, query_total, *refs):
    part_refs, (target_ref, log_ref, share_ref) = refs[:-3], refs[-3:]
    whole = tree_sum([ref[...] for ref in part_refs])
    dims, queries = whole.shape[0] - 8, whole.shape[1]
    smoothing = 1.0 / TABLE_ROWS
    estimate = whole[dims : dims + 1] / sample_total
    log_est = jnp.log(estimate + smoothing)
    log_ref[...] = log_est
    weight = 2.0 * (log_est - target_ref[...]) / (query_total * (estimate + smoothing))
    terms = whole[:dims] * (weight / sample_total)
    terms = jnp.concatenate([terms, jnp.zeros((queries - dims, queries), jnp.float32)], axis=0)
    share = jnp.sum(terms.T, axis=0, keepdims=True)
    for peer in range(share_ref.shape[0]):
        share_ref[peer] = share


def last_kernel(shares_ref, held_log_ref, log_ref, gradient_ref):
    total = tree_sum([shares_ref[peer] for peer in range(shares_ref.shape[0])])
    log_ref[...] = held_log_ref[0]
    gradient_ref[...] = total[0, : gradient_ref.shape[0]]


def everyone(x, axis):
    size = lax.axis_size(axis)
    return [x] + [
        lax.ppermute(x, axis, [(i, i ^ offset) for i in range(size)]) for offset in range(1, size)
    ]


def call(kernel, args, outs, scratch=(), placed=pltpu.VMEM):
    single = len(outs) == 1
    return pl.pallas_call(
        kernel,
        out_shape=outs[0] if single else outs,
        in_specs=[pl.BlockSpec(memory_space=placed)] * len(args),
        out_specs=pl.BlockSpec(memory_space=pltpu.VMEM)
        if single
        else [pl.BlockSpec(memory_space=pltpu.VMEM)] * len(outs),
        scratch_shapes=list(scratch),
        compiler_params=pltpu.CompilerParams(vmem_limit_bytes=32 << 20),
    )(*args)


def shape(*sizes):
    return jax.ShapeDtypeStruct(sizes, jnp.float32)


def on_device(samples, bounds, spread, counts):
    dims, width = samples.shape
    queries = bounds.shape[2]
    blocks, copies = lax.axis_size("blk"), lax.axis_size("grp")
    sample_total = width * blocks * copies
    query_total = queries * blocks

    counts_vector = pltpu.VMEM((1, queries), jnp.int32)
    packed, bounds, spread, target = call(
        load_kernel,
        [
            pltpu.with_memory_space_constraint(array, pltpu.HBM)
            for array in (samples, bounds, spread.reshape(1, dims), counts.reshape(1, queries))
        ],
        [
            pltpu.VMEM((blocks, 8, dims * width // 8), jnp.float32),
            pltpu.VMEM(bounds.shape, bounds.dtype),
            pltpu.VMEM((1, dims), jnp.float32),
            pltpu.VMEM((1, queries), jnp.float32),
        ],
        [pltpu.VMEM((dims, width), jnp.float32), counts_vector, pltpu.SemaphoreType.DMA((4,))],
        placed=pl.ANY,
    )
    turned = [1] + [0] * (blocks - 1)
    groups = [
        [b * copies + (c + turned[b]) % copies for b in reversed(range(blocks))]
        for c in range(copies)
    ]
    exchange = lambda x: lax.all_to_all(x, ("blk", "grp"), 0, 0, axis_index_groups=groups)
    gathered = exchange(packed)
    part = call(
        terms_kernel,
        [gathered, bounds, spread],
        [shape(dims + 8, queries)],
    )
    log_est, share = call(
        functools.partial(finish_kernel, sample_total, query_total),
        everyone(part, "grp") + [target],
        [shape(1, queries), shape(blocks, 1, queries)],
    )
    shares = exchange(share)
    return call(last_kernel, [shares, log_est], [shape(queries), shape(dims)])


def solution(mesh):
    return jax.shard_map(
        on_device,
        mesh=mesh,
        in_specs=(P(None, ("blk", "grp")), P(None, None, "blk"), P(), P("blk")),
        out_specs=(P("blk"), P()),
        check_vma=False,
    )
```

```python
import functools

import jax
import jax.numpy as jnp
from jax import lax
from jax.experimental import pallas as pl
from jax.experimental.pallas import tpu as pltpu
from jax.sharding import PartitionSpec as P

TABLE_ROWS = 1048576
GRID = 256
LIMITED = 3

ROOT_HALF = 0.7071067811865476
LOG2_E = 1.4426950408889634
SLOPE = 0.5641895835477563


def box_terms(low, high):
    low_bell = jnp.exp2((low * low) * -LOG2_E)
    high_bell = jnp.exp2((high * high) * -LOG2_E)
    return lax.erf(high) - lax.erf(low), low * low_bell - high * high_bell


def split(x, parts):
    out = []
    for _ in range(parts - 1):
        head = x.astype(jnp.bfloat16)
        out.append(head)
        x = x - head.astype(jnp.float32)
    return out + [x.astype(jnp.bfloat16)]


def tree_sum(parts):
    while len(parts) > 1:
        parts = [a + b for a, b in zip(parts[::2], parts[1::2])]
    return parts[0]


def load_kernel(
    x_ref, bounds_ref, spread_ref, counts_ref,
    out_ref, held_bounds, held_spread, target_ref,
    held_x, held_counts, sems,
):
    sources = (x_ref, bounds_ref, spread_ref, counts_ref)
    targets = (held_x, held_bounds, held_spread, held_counts)
    copies = [
        pltpu.make_async_copy(source, target, sems.at[i])
        for i, (source, target) in enumerate(zip(sources, targets))
    ]
    for copy in copies:
        copy.start()
    copies[0].wait()
    rows = held_x.shape[0]
    packed = jnp.concatenate([held_x[8 * j : 8 * (j + 1), :] for j in range(rows // 8)], axis=1)
    for peer in range(out_ref.shape[0]):
        out_ref[peer] = packed
    for copy in copies[1:]:
        copy.wait()
    smoothing = 1.0 / TABLE_ROWS
    target_ref[...] = jnp.log(held_counts[...].astype(jnp.float32) / TABLE_ROWS + smoothing)


def terms_kernel(width, blocks_ref, bounds_ref, spread_ref, out_ref):
    dims, queries = bounds_ref.shape[1:]
    count = blocks_ref.shape[0]
    group = min(count, 512 // width)

    low, high = bounds_ref[0], bounds_ref[1]
    limited = (high - low) != GRID
    at = lax.broadcasted_iota(jnp.int32, (dims, queries), 0)
    first = jnp.min(jnp.where(limited, at, dims), axis=0, keepdims=True)
    last = jnp.max(jnp.where(limited, at, -1), axis=0, keepdims=True)
    chosen = [at == first, limited & (at > first) & (at < last), at == last]

    row = lax.broadcasted_iota(jnp.int32, (dims, dims), 0)
    column = lax.broadcasted_iota(jnp.int32, (dims, dims), 1)
    spread = jnp.sum(jnp.where(row == column, spread_ref[...], 0.0), axis=1, keepdims=True)
    unit = ROOT_HALF / spread

    pick = lambda mask, values: jnp.sum(jnp.where(mask, values, 0.0), axis=0, keepdims=True)
    low = low.astype(jnp.float32) * unit
    high = high.astype(jnp.float32) * unit
    low_at = [pick(mask, low) for mask in chosen]
    high_at = [pick(mask, high) for mask in chosen]

    ones = [mask.astype(jnp.float32).astype(jnp.bfloat16) for mask in chosen]
    free = jnp.where(limited, 0.0, 1.0).astype(jnp.bfloat16)
    none = jnp.zeros_like(free)
    right = jnp.concatenate(
        [jnp.concatenate(ones + [none], axis=1)] * 3
        + [jnp.concatenate([none] * LIMITED + [free], axis=1)] * 3,
        axis=0,
    )

    def step(picked, sums):
        others = jnp.exp2(picked[:, LIMITED * queries :])
        mass, slope = [], []
        for k in range(LIMITED):
            points = picked[:, k * queries : (k + 1) * queries]
            m, s = box_terms(low_at[k] - points, high_at[k] - points)
            mass.append(m)
            slope.append(s)
        pair = others * mass[0]
        last_two = pair * mass[1]
        whole = last_two * mass[2]
        return whole, (
            sums[0] + whole,
            sums[1] + (others * mass[1]) * (mass[2] * slope[0]),
            sums[2] + pair * (mass[2] * slope[1]),
            sums[3] + last_two * slope[2],
        )

    def chunk(number, totals):
        sums, products = totals[:-1], totals[-1]
        some = [blocks_ref[number * group + b] for b in range(group)]
        x = unit * jnp.concatenate(
            [
                jnp.concatenate([block[:, width * j : width * (j + 1)] for block in some], axis=1)
                for j in range(dims // 8)
            ],
            axis=0,
        )
        full, slope = box_terms(-x, float(GRID) * unit - x)
        ratio = jnp.concatenate(split(slope / full, 2), axis=0)
        left = jnp.concatenate(split(x, 3) + split(jnp.log(0.5 * full) * LOG2_E, 3), axis=0)
        picked = lax.dot_general(
            left, right, (((0,), (0,)), ((), ())), preferred_element_type=jnp.float32
        )
        samples = group * width
        for start in range(0, samples, 256):
            inside = []
            for at_row in range(start, start + 256, 16):
                whole, sums = step(picked[at_row : at_row + 16], sums)
                inside.append(jnp.concatenate(split(whole, 2), axis=1))
            products = products + jnp.dot(
                ratio[:, start : start + 256],
                jnp.concatenate(inside, axis=0),
                preferred_element_type=jnp.float32,
            )
        return (*sums, products)

    zero = jnp.zeros((16, queries), jnp.float32)
    totals = (zero,) * (1 + LIMITED) + (jnp.zeros((2 * dims, 2 * queries), jnp.float32),)
    if count == group:
        totals = chunk(0, totals)
    else:
        totals = lax.fori_loop(0, count // group, chunk, totals)
    sums = [jnp.sum(s, axis=0, keepdims=True) for s in totals[:-1]]
    products = totals[-1]
    deriv = products[:dims, :queries] + (products[dims:, :queries] + products[:dims, queries:])
    deriv = jnp.where(limited, 0.0, deriv * (SLOPE / 4))
    for mask, s in zip(chosen, sums[1:]):
        deriv = jnp.where(mask, s * (SLOPE / 4), deriv)
    out_ref[:dims, :] = deriv
    out_ref[dims:, :] = jnp.broadcast_to(sums[0] * 0.125, (8, queries))


def finish_kernel(sample_total, query_total, *refs):
    part_refs, (target_ref, log_ref, share_ref) = refs[:-3], refs[-3:]
    whole = tree_sum([ref[...] for ref in part_refs])
    dims, queries = whole.shape[0] - 8, whole.shape[1]
    smoothing = 1.0 / TABLE_ROWS
    estimate = whole[dims : dims + 1] / sample_total
    log_est = jnp.log(estimate + smoothing)
    log_ref[...] = log_est
    weight = 2.0 * (log_est - target_ref[...]) / (query_total * (estimate + smoothing))
    terms = whole[:dims] * (weight / sample_total)
    terms = jnp.concatenate([terms, jnp.zeros((queries - dims, queries), jnp.float32)], axis=0)
    share = jnp.sum(terms.T, axis=0, keepdims=True)
    for peer in range(share_ref.shape[0]):
        share_ref[peer] = share


def last_kernel(shares_ref, held_log_ref, log_ref, gradient_ref):
    total = tree_sum([shares_ref[peer] for peer in range(shares_ref.shape[0])])
    log_ref[...] = held_log_ref[0]
    gradient_ref[...] = total[0, : gradient_ref.shape[0]]


def everyone(x, axis):
    size = lax.axis_size(axis)
    return [x] + [
        lax.ppermute(x, axis, [(i, i ^ offset) for i in range(size)]) for offset in range(1, size)
    ]


def call(kernel, args, outs, scratch=(), placed=pltpu.VMEM):
    single = len(outs) == 1
    return pl.pallas_call(
        kernel,
        out_shape=outs[0] if single else outs,
        in_specs=[pl.BlockSpec(memory_space=placed)] * len(args),
        out_specs=pl.BlockSpec(memory_space=pltpu.VMEM)
        if single
        else [pl.BlockSpec(memory_space=pltpu.VMEM)] * len(outs),
        scratch_shapes=list(scratch),
        compiler_params=pltpu.CompilerParams(vmem_limit_bytes=32 << 20),
    )(*args)


def shape(*sizes):
    return jax.ShapeDtypeStruct(sizes, jnp.float32)


def on_device(samples, bounds, spread, counts):
    dims, width = samples.shape
    queries = bounds.shape[2]
    blocks, copies = lax.axis_size("blk"), lax.axis_size("grp")
    sample_total = width * blocks * copies
    query_total = queries * blocks

    counts_vector = pltpu.VMEM((1, queries), jnp.int32)
    packed, bounds, spread, target = call(
        load_kernel,
        [
            pltpu.with_memory_space_constraint(array, pltpu.HBM)
            for array in (samples, bounds, spread.reshape(1, dims), counts.reshape(1, queries))
        ],
        [
            pltpu.VMEM((blocks, 8, dims * width // 8), jnp.float32),
            pltpu.VMEM(bounds.shape, bounds.dtype),
            pltpu.VMEM((1, dims), jnp.float32),
            pltpu.VMEM((1, queries), jnp.float32),
        ],
        [pltpu.VMEM((dims, width), jnp.float32), counts_vector, pltpu.SemaphoreType.DMA((4,))],
        placed=pl.ANY,
    )
    turned = [1] + [0] * (blocks - 1)
    groups = [
        [b * copies + (c + turned[b]) % copies for b in reversed(range(blocks))]
        for c in range(copies)
    ]
    exchange = lambda x: lax.all_to_all(x, ("blk", "grp"), 0, 0, axis_index_groups=groups)
    gathered = exchange(packed)
    part = call(
        functools.partial(terms_kernel, width),
        [gathered, bounds, spread],
        [shape(dims + 8, queries)],
    )
    log_est, share = call(
        functools.partial(finish_kernel, sample_total, query_total),
        everyone(part, "grp") + [target],
        [shape(1, queries), shape(blocks, 1, queries)],
    )
    shares = exchange(share)
    return call(last_kernel, [shares, log_est], [shape(queries), shape(dims)])


def solution(mesh):
    return jax.shard_map(
        on_device,
        mesh=mesh,
        in_specs=(P(None, ("blk", "grp")), P(None, None, "blk"), P(), P("blk")),
        out_specs=(P("blk"), P()),
        check_vma=False,
    )
```

```python
import functools

import jax
import jax.numpy as jnp
from jax import lax
from jax.experimental import pallas as pl
from jax.experimental.pallas import tpu as pltpu
from jax.sharding import PartitionSpec as P

TABLE_ROWS = 1048576
GRID = 256
LIMITED = 3

ROOT_HALF = 0.7071067811865476
LOG2_E = 1.4426950408889634
SLOPE = 0.5641895835477563


def box_terms(low, high):
    low_bell = jnp.exp2((low * low) * -LOG2_E)
    high_bell = jnp.exp2((high * high) * -LOG2_E)
    return lax.erf(high) - lax.erf(low), low * low_bell - high * high_bell


def split(x, parts):
    out = []
    for _ in range(parts - 1):
        head = x.astype(jnp.bfloat16)
        out.append(head)
        x = x - head.astype(jnp.float32)
    return out + [x.astype(jnp.bfloat16)]


def tree_sum(parts):
    while len(parts) > 1:
        parts = [a + b for a, b in zip(parts[::2], parts[1::2])]
    return parts[0]


def load_kernel(
    x_ref, bounds_ref, spread_ref, counts_ref,
    out_ref, held_bounds, held_spread, target_ref,
    held_x, held_counts, sems,
):
    sources = (x_ref, bounds_ref, spread_ref, counts_ref)
    targets = (held_x, held_bounds, held_spread, held_counts)
    copies = [
        pltpu.make_async_copy(source, target, sems.at[i])
        for i, (source, target) in enumerate(zip(sources, targets))
    ]
    for copy in copies:
        copy.start()
    copies[0].wait()
    rows = held_x.shape[0]
    packed = jnp.concatenate([held_x[8 * j : 8 * (j + 1), :] for j in range(rows // 8)], axis=1)
    for peer in range(out_ref.shape[0]):
        out_ref[peer] = packed
    for copy in copies[1:]:
        copy.wait()
    smoothing = 1.0 / TABLE_ROWS
    target_ref[...] = jnp.log(held_counts[...].astype(jnp.float32) / TABLE_ROWS + smoothing)


def terms_kernel(width, blocks_ref, bounds_ref, spread_ref, out_ref):
    dims, queries = bounds_ref.shape[1:]
    count = blocks_ref.shape[0]
    per_piece = 128 // width
    group = min(count, 4 * per_piece)

    low, high = bounds_ref[0], bounds_ref[1]
    limited = (high - low) != GRID
    at = lax.broadcasted_iota(jnp.int32, (dims, queries), 0)
    first = jnp.min(jnp.where(limited, at, dims), axis=0, keepdims=True)
    last = jnp.max(jnp.where(limited, at, -1), axis=0, keepdims=True)
    chosen = [at == first, limited & (at > first) & (at < last), at == last]

    row = lax.broadcasted_iota(jnp.int32, (dims, dims), 0)
    column = lax.broadcasted_iota(jnp.int32, (dims, dims), 1)
    spread = jnp.sum(jnp.where(row == column, spread_ref[...], 0.0), axis=1, keepdims=True)
    unit = ROOT_HALF / spread

    pick = lambda mask, values: jnp.sum(jnp.where(mask, values, 0.0), axis=0, keepdims=True)
    low = low.astype(jnp.float32) * unit
    high = high.astype(jnp.float32) * unit
    low_at = [pick(mask, low) for mask in chosen]
    high_at = [pick(mask, high) for mask in chosen]

    ones = [mask.astype(jnp.float32).astype(jnp.bfloat16) for mask in chosen]
    free = jnp.where(limited, 0.0, 1.0).astype(jnp.bfloat16)
    none = jnp.zeros_like(free)
    right = jnp.concatenate(
        [jnp.concatenate(ones + [none], axis=1)] * 3
        + [jnp.concatenate([none] * LIMITED + [free], axis=1)] * 3,
        axis=0,
    )

    def step(picked, sums):
        others = jnp.exp2(picked[:, LIMITED * queries :])
        mass, slope = [], []
        for k in range(LIMITED):
            points = picked[:, k * queries : (k + 1) * queries]
            m, s = box_terms(low_at[k] - points, high_at[k] - points)
            mass.append(m)
            slope.append(s)
        pair = others * mass[0]
        last_two = pair * mass[1]
        whole = last_two * mass[2]
        return whole, (
            sums[0] + whole,
            sums[1] + (others * mass[1]) * (mass[2] * slope[0]),
            sums[2] + pair * (mass[2] * slope[1]),
            sums[3] + last_two * slope[2],
        )

    def piece(start, totals):
        sums, products = totals[:-1], totals[-1]
        some = [blocks_ref[start + b] for b in range(per_piece)]
        x = unit * jnp.concatenate(
            [
                jnp.concatenate([block[:, width * j : width * (j + 1)] for block in some], axis=1)
                for j in range(dims // 8)
            ],
            axis=0,
        )
        full, slope = box_terms(-x, float(GRID) * unit - x)
        ratio = jnp.concatenate(split(slope / full, 2), axis=0)
        left = jnp.concatenate(split(x, 3) + split(jnp.log(0.5 * full) * LOG2_E, 3), axis=0)
        picked = lax.dot_general(
            left, right, (((0,), (0,)), ((), ())), preferred_element_type=jnp.float32
        )
        inside = []
        for at_row in range(0, per_piece * width, 16):
            whole, sums = step(picked[at_row : at_row + 16], sums)
            inside.append(jnp.concatenate(split(whole, 2), axis=1))
        inside = jnp.concatenate(inside, axis=0)
        products = products + jnp.dot(ratio, inside, preferred_element_type=jnp.float32)
        return (*sums, products)

    def pieces(number, totals):
        for start in range(0, group, per_piece):
            totals = piece(number * group + start, totals)
        return totals

    zero = jnp.zeros((16, queries), jnp.float32)
    totals = (zero,) * (1 + LIMITED) + (jnp.zeros((2 * dims, 2 * queries), jnp.float32),)
    if count == group:
        totals = pieces(0, totals)
    else:
        totals = lax.fori_loop(0, count // group, pieces, totals)
    sums = [jnp.sum(s, axis=0, keepdims=True) for s in totals[:-1]]
    products = totals[-1]
    deriv = products[:dims, :queries] + (products[dims:, :queries] + products[:dims, queries:])
    deriv = jnp.where(limited, 0.0, deriv * (SLOPE / 4))
    for mask, s in zip(chosen, sums[1:]):
        deriv = jnp.where(mask, s * (SLOPE / 4), deriv)
    out_ref[:dims, :] = deriv
    out_ref[dims:, :] = jnp.broadcast_to(sums[0] * 0.125, (8, queries))


def finish_kernel(sample_total, query_total, *refs):
    part_refs, (target_ref, log_ref, share_ref) = refs[:-3], refs[-3:]
    whole = tree_sum([ref[...] for ref in part_refs])
    dims, queries = whole.shape[0] - 8, whole.shape[1]
    smoothing = 1.0 / TABLE_ROWS
    estimate = whole[dims : dims + 1] / sample_total
    log_est = jnp.log(estimate + smoothing)
    log_ref[...] = log_est
    weight = 2.0 * (log_est - target_ref[...]) / (query_total * (estimate + smoothing))
    terms = whole[:dims] * (weight / sample_total)
    terms = jnp.concatenate([terms, jnp.zeros((queries - dims, queries), jnp.float32)], axis=0)
    share = jnp.sum(terms.T, axis=0, keepdims=True)
    for peer in range(share_ref.shape[0]):
        share_ref[peer] = share


def last_kernel(shares_ref, held_log_ref, log_ref, gradient_ref):
    total = tree_sum([shares_ref[peer] for peer in range(shares_ref.shape[0])])
    log_ref[...] = held_log_ref[0]
    gradient_ref[...] = total[0, : gradient_ref.shape[0]]


def everyone(x, axis):
    size = lax.axis_size(axis)
    return [x] + [
        lax.ppermute(x, axis, [(i, i ^ offset) for i in range(size)]) for offset in range(1, size)
    ]


def call(kernel, args, outs, scratch=(), placed=pltpu.VMEM):
    single = len(outs) == 1
    return pl.pallas_call(
        kernel,
        out_shape=outs[0] if single else outs,
        in_specs=[pl.BlockSpec(memory_space=placed)] * len(args),
        out_specs=pl.BlockSpec(memory_space=pltpu.VMEM)
        if single
        else [pl.BlockSpec(memory_space=pltpu.VMEM)] * len(outs),
        scratch_shapes=list(scratch),
        compiler_params=pltpu.CompilerParams(vmem_limit_bytes=32 << 20),
    )(*args)


def shape(*sizes):
    return jax.ShapeDtypeStruct(sizes, jnp.float32)


def on_device(samples, bounds, spread, counts):
    dims, width = samples.shape
    queries = bounds.shape[2]
    blocks, copies = lax.axis_size("blk"), lax.axis_size("grp")
    sample_total = width * blocks * copies
    query_total = queries * blocks

    counts_vector = pltpu.VMEM((1, queries), jnp.int32)
    packed, bounds, spread, target = call(
        load_kernel,
        [
            pltpu.with_memory_space_constraint(array, pltpu.HBM)
            for array in (samples, bounds, spread.reshape(1, dims), counts.reshape(1, queries))
        ],
        [
            pltpu.VMEM((blocks, 8, dims * width // 8), jnp.float32),
            pltpu.VMEM(bounds.shape, bounds.dtype),
            pltpu.VMEM((1, dims), jnp.float32),
            pltpu.VMEM((1, queries), jnp.float32),
        ],
        [pltpu.VMEM((dims, width), jnp.float32), counts_vector, pltpu.SemaphoreType.DMA((4,))],
        placed=pl.ANY,
    )
    turned = [1] + [0] * (blocks - 1)

    def exchange(x, order):
        groups = [
            [b * copies + (c + turned[b]) % copies for b in order] for c in range(copies)
        ]
        return lax.all_to_all(x, ("blk", "grp"), 0, 0, axis_index_groups=groups)

    falling = list(reversed(range(blocks)))
    far = blocks // 5
    near = blocks // 4
    gather_order = falling[far : blocks - 1 - near] + falling[blocks - 1 - near : -1]
    gather_order += falling[:far][::-1] + [0]
    gathered = exchange(packed, gather_order)
    part = call(
        functools.partial(terms_kernel, width),
        [gathered, bounds, spread],
        [shape(dims + 8, queries)],
    )
    log_est, share = call(
        functools.partial(finish_kernel, sample_total, query_total),
        everyone(part, "grp") + [target],
        [shape(1, queries), shape(blocks, 1, queries)],
    )
    shares = exchange(share, falling)
    return call(last_kernel, [shares, log_est], [shape(queries), shape(dims)])


def solution(mesh):
    return jax.shard_map(
        on_device,
        mesh=mesh,
        in_specs=(P(None, ("blk", "grp")), P(None, None, "blk"), P(), P("blk")),
        out_specs=(P("blk"), P()),
        check_vma=False,
    )
```

```python
import functools

import jax
import jax.numpy as jnp
from jax import lax
from jax.experimental import pallas as pl
from jax.experimental.pallas import tpu as pltpu
from jax.sharding import PartitionSpec as P

TABLE_ROWS = 1048576
GRID = 256
LIMITED = 3

ROOT_HALF = 0.7071067811865476
LOG2_E = 1.4426950408889634
SLOPE = 0.5641895835477563


def box_terms(low, high):
    low_bell = jnp.exp2((low * low) * -LOG2_E)
    high_bell = jnp.exp2((high * high) * -LOG2_E)
    return lax.erf(high) - lax.erf(low), low * low_bell - high * high_bell


def split(x, parts):
    out = []
    for _ in range(parts - 1):
        head = x.astype(jnp.bfloat16)
        out.append(head)
        x = x - head.astype(jnp.float32)
    return out + [x.astype(jnp.bfloat16)]


def tree_sum(parts):
    while len(parts) > 1:
        parts = [a + b for a, b in zip(parts[::2], parts[1::2])]
    return parts[0]


def load_kernel(
    x_ref, bounds_ref, spread_ref, counts_ref,
    out_ref, held_bounds, held_spread, target_ref,
    held_x, held_counts, sems,
):
    sources = (x_ref, bounds_ref, spread_ref, counts_ref)
    targets = (held_x, held_bounds, held_spread, held_counts)
    copies = [
        pltpu.make_async_copy(source, target, sems.at[i])
        for i, (source, target) in enumerate(zip(sources, targets))
    ]
    for copy in copies:
        copy.start()
    copies[0].wait()
    rows = held_x.shape[0]
    packed = jnp.concatenate([held_x[8 * j : 8 * (j + 1), :] for j in range(rows // 8)], axis=1)
    for peer in range(out_ref.shape[0]):
        out_ref[peer] = packed
    for copy in copies[1:]:
        copy.wait()
    smoothing = 1.0 / TABLE_ROWS
    target_ref[...] = jnp.log(held_counts[...].astype(jnp.float32) / TABLE_ROWS + smoothing)


def terms_kernel(width, blocks_ref, bounds_ref, spread_ref, out_ref):
    dims, queries = bounds_ref.shape[1:]
    count = blocks_ref.shape[0]
    per_piece = 128 // width
    group = min(count, 4 * per_piece)

    low, high = bounds_ref[0], bounds_ref[1]
    limited = (high - low) != GRID
    at = lax.broadcasted_iota(jnp.int32, (dims, queries), 0)
    first = jnp.min(jnp.where(limited, at, dims), axis=0, keepdims=True)
    last = jnp.max(jnp.where(limited, at, -1), axis=0, keepdims=True)
    chosen = [at == first, limited & (at > first) & (at < last), at == last]

    row = lax.broadcasted_iota(jnp.int32, (dims, dims), 0)
    column = lax.broadcasted_iota(jnp.int32, (dims, dims), 1)
    spread = jnp.sum(jnp.where(row == column, spread_ref[...], 0.0), axis=1, keepdims=True)
    unit = ROOT_HALF / spread

    pick = lambda mask, values: jnp.sum(jnp.where(mask, values, 0.0), axis=0, keepdims=True)
    low = low.astype(jnp.float32) * unit
    high = high.astype(jnp.float32) * unit
    low_at = [pick(mask, low) for mask in chosen]
    high_at = [pick(mask, high) for mask in chosen]

    ones = [mask.astype(jnp.float32).astype(jnp.bfloat16) for mask in chosen]
    free = jnp.where(limited, 0.0, 1.0).astype(jnp.bfloat16)
    none = jnp.zeros_like(free)
    right = jnp.concatenate(
        [jnp.concatenate(ones + [none], axis=1)] * 3
        + [jnp.concatenate([none] * LIMITED + [free], axis=1)] * 3,
        axis=0,
    )

    def step(picked, sums):
        others = jnp.exp2(picked[:, LIMITED * queries :])
        mass, slope = [], []
        for k in range(LIMITED):
            points = picked[:, k * queries : (k + 1) * queries]
            m, s = box_terms(low_at[k] - points, high_at[k] - points)
            mass.append(m)
            slope.append(s)
        pair = others * mass[0]
        last_two = pair * mass[1]
        whole = last_two * mass[2]
        return whole, (
            sums[0] + whole,
            sums[1] + (others * mass[1]) * (mass[2] * slope[0]),
            sums[2] + pair * (mass[2] * slope[1]),
            sums[3] + last_two * slope[2],
        )

    def piece(start, totals):
        sums, products = totals[:-1], totals[-1]
        some = [blocks_ref[start + b] for b in range(per_piece)]
        x = unit * jnp.concatenate(
            [
                jnp.concatenate([block[:, width * j : width * (j + 1)] for block in some], axis=1)
                for j in range(dims // 8)
            ],
            axis=0,
        )
        full, slope = box_terms(-x, float(GRID) * unit - x)
        ratio = jnp.concatenate(split(slope / full, 2), axis=0)
        left = jnp.concatenate(split(x, 3) + split(jnp.log(0.5 * full) * LOG2_E, 3), axis=0)
        picked = lax.dot_general(
            left, right, (((0,), (0,)), ((), ())), preferred_element_type=jnp.float32
        )
        inside = []
        for at_row in range(0, per_piece * width, 16):
            whole, sums = step(picked[at_row : at_row + 16], sums)
            inside.append(jnp.concatenate(split(whole, 2), axis=1))
        inside = jnp.concatenate(inside, axis=0)
        products = products + jnp.dot(ratio, inside, preferred_element_type=jnp.float32)
        return (*sums, products)

    def pieces(number, totals):
        for start in range(0, group, per_piece):
            totals = piece(number * group + start, totals)
        return totals

    zero = jnp.zeros((16, queries), jnp.float32)
    totals = (zero,) * (1 + LIMITED) + (jnp.zeros((2 * dims, 2 * queries), jnp.float32),)
    if count == group:
        totals = pieces(0, totals)
    else:
        totals = lax.fori_loop(0, count // group, pieces, totals)
    sums = [jnp.sum(s, axis=0, keepdims=True) for s in totals[:-1]]
    products = totals[-1]
    deriv = products[:dims, :queries] + (products[dims:, :queries] + products[:dims, queries:])
    deriv = jnp.where(limited, 0.0, deriv * (SLOPE / 4))
    for mask, s in zip(chosen, sums[1:]):
        deriv = jnp.where(mask, s * (SLOPE / 4), deriv)
    out_ref[:dims, :] = deriv
    out_ref[dims:, :] = jnp.broadcast_to(sums[0] * 0.125, (8, queries))


def finish_kernel(sample_total, query_total, *refs):
    part_refs, (target_ref, log_ref, share_ref) = refs[:-3], refs[-3:]
    whole = tree_sum([ref[...] for ref in part_refs])
    dims, queries = whole.shape[0] - 8, whole.shape[1]
    smoothing = 1.0 / TABLE_ROWS
    estimate = whole[dims : dims + 1] / sample_total
    log_est = jnp.log(estimate + smoothing)
    log_ref[...] = log_est
    weight = 2.0 * (log_est - target_ref[...]) / (query_total * (estimate + smoothing))
    terms = whole[:dims] * (weight / sample_total)
    terms = jnp.concatenate([terms, jnp.zeros((queries - dims, queries), jnp.float32)], axis=0)
    share = jnp.sum(terms.T, axis=0, keepdims=True)
    for peer in range(share_ref.shape[0]):
        share_ref[peer] = share


def last_kernel(shares_ref, held_log_ref, log_ref, gradient_ref):
    total = tree_sum([shares_ref[peer] for peer in range(shares_ref.shape[0])])
    log_ref[...] = held_log_ref[0]
    gradient_ref[...] = total[0, : gradient_ref.shape[0]]


def everyone(x, axis):
    size = lax.axis_size(axis)
    return [x] + [
        lax.ppermute(x, axis, [(i, i ^ offset) for i in range(size)]) for offset in range(1, size)
    ]


def call(kernel, args, outs, scratch=(), placed=pltpu.VMEM):
    single = len(outs) == 1
    return pl.pallas_call(
        kernel,
        out_shape=outs[0] if single else outs,
        in_specs=[pl.BlockSpec(memory_space=placed)] * len(args),
        out_specs=pl.BlockSpec(memory_space=pltpu.VMEM)
        if single
        else [pl.BlockSpec(memory_space=pltpu.VMEM)] * len(outs),
        scratch_shapes=list(scratch),
        compiler_params=pltpu.CompilerParams(vmem_limit_bytes=32 << 20),
    )(*args)


def shape(*sizes):
    return jax.ShapeDtypeStruct(sizes, jnp.float32)


def on_device(samples, bounds, spread, counts):
    dims, width = samples.shape
    queries = bounds.shape[2]
    blocks, copies = lax.axis_size("blk"), lax.axis_size("grp")
    sample_total = width * blocks * copies
    query_total = queries * blocks

    counts_vector = pltpu.VMEM((1, queries), jnp.int32)
    packed, bounds, spread, target = call(
        load_kernel,
        [
            pltpu.with_memory_space_constraint(array, pltpu.HBM)
            for array in (samples, bounds, spread.reshape(1, dims), counts.reshape(1, queries))
        ],
        [
            pltpu.VMEM((blocks, 8, dims * width // 8), jnp.float32),
            pltpu.VMEM(bounds.shape, bounds.dtype),
            pltpu.VMEM((1, dims), jnp.float32),
            pltpu.VMEM((1, queries), jnp.float32),
        ],
        [pltpu.VMEM((dims, width), jnp.float32), counts_vector, pltpu.SemaphoreType.DMA((4,))],
        placed=pl.ANY,
    )
    def exchange(x, turned):
        groups = [
            [b * copies + (c + turned(b)) % copies for b in reversed(range(blocks))]
            for c in range(copies)
        ]
        return lax.all_to_all(x, ("blk", "grp"), 0, 0, axis_index_groups=groups)

    gathered = exchange(packed, lambda b: 1 - (b & 7).bit_count() % 2)
    part = call(
        functools.partial(terms_kernel, width),
        [gathered, bounds, spread],
        [shape(dims + 8, queries)],
    )
    log_est, share = call(
        functools.partial(finish_kernel, sample_total, query_total),
        everyone(part, "grp") + [target],
        [shape(1, queries), shape(blocks, 1, queries)],
    )
    shares = exchange(share, lambda b: int(b == 0))
    return call(last_kernel, [shares, log_est], [shape(queries), shape(dims)])


def solution(mesh):
    return jax.shard_map(
        on_device,
        mesh=mesh,
        in_specs=(P(None, ("blk", "grp")), P(None, None, "blk"), P(), P("blk")),
        out_specs=(P("blk"), P()),
        check_vma=False,
    )
```

```python
import functools

import jax
import jax.numpy as jnp
from jax import lax
from jax.experimental import pallas as pl
from jax.experimental.pallas import tpu as pltpu
from jax.sharding import PartitionSpec as P

TABLE_ROWS = 1048576
GRID = 256
LIMITED = 3

ROOT_HALF = 0.7071067811865476
LOG2_E = 1.4426950408889634
SLOPE = 0.5641895835477563


def box_terms(low, high):
    low_bell = jnp.exp2((low * low) * -LOG2_E)
    high_bell = jnp.exp2((high * high) * -LOG2_E)
    return lax.erf(high) - lax.erf(low), low * low_bell - high * high_bell


def split(x, parts):
    out = []
    for _ in range(parts - 1):
        head = x.astype(jnp.bfloat16)
        out.append(head)
        x = x - head.astype(jnp.float32)
    return out + [x.astype(jnp.bfloat16)]


def tree_sum(parts):
    while len(parts) > 1:
        parts = [a + b for a, b in zip(parts[::2], parts[1::2])]
    return parts[0]


def load_kernel(
    x_ref, bounds_ref, spread_ref, counts_ref,
    out_ref, held_bounds, held_spread, target_ref,
    held_x, held_counts, sems,
):
    sources = (x_ref, bounds_ref, spread_ref, counts_ref)
    targets = (held_x, held_bounds, held_spread, held_counts)
    copies = [
        pltpu.make_async_copy(source, target, sems.at[i])
        for i, (source, target) in enumerate(zip(sources, targets))
    ]
    for copy in copies:
        copy.start()
    copies[0].wait()
    rows = held_x.shape[0]
    packed = jnp.concatenate([held_x[8 * j : 8 * (j + 1), :] for j in range(rows // 8)], axis=1)
    for peer in range(out_ref.shape[0]):
        out_ref[peer] = packed
    for copy in copies[1:]:
        copy.wait()
    smoothing = 1.0 / TABLE_ROWS
    target_ref[...] = jnp.log(held_counts[...].astype(jnp.float32) / TABLE_ROWS + smoothing)


def terms_kernel(width, blocks_ref, bounds_ref, spread_ref, out_ref):
    dims, queries = bounds_ref.shape[1:]
    count = blocks_ref.shape[0]
    per_piece = 128 // width
    group = min(count, 4 * per_piece)

    low, high = bounds_ref[0], bounds_ref[1]
    limited = (high - low) != GRID
    at = lax.broadcasted_iota(jnp.int32, (dims, queries), 0)
    first = jnp.min(jnp.where(limited, at, dims), axis=0, keepdims=True)
    last = jnp.max(jnp.where(limited, at, -1), axis=0, keepdims=True)
    chosen = [at == first, limited & (at > first) & (at < last), at == last]

    row = lax.broadcasted_iota(jnp.int32, (dims, dims), 0)
    column = lax.broadcasted_iota(jnp.int32, (dims, dims), 1)
    spread = jnp.sum(jnp.where(row == column, spread_ref[...], 0.0), axis=1, keepdims=True)
    unit = ROOT_HALF / spread

    pick = lambda mask, values: jnp.sum(jnp.where(mask, values, 0.0), axis=0, keepdims=True)
    low = low.astype(jnp.float32) * unit
    high = high.astype(jnp.float32) * unit
    ends = [pick(mask, low) for mask in chosen] + [pick(mask, high) for mask in chosen]

    minus = jnp.concatenate([jnp.where(mask, -1.0, 0.0) for mask in chosen] * 2, axis=1)
    minus = jnp.concatenate([minus, jnp.zeros((dims, queries), jnp.float32)], axis=1)
    free = jnp.concatenate(
        [jnp.zeros((dims, 2 * LIMITED * queries), jnp.float32), jnp.where(limited, 0.0, 1.0)],
        axis=1,
    )
    wide = jnp.concatenate(ends + [jnp.zeros((1, queries), jnp.float32)], axis=1)
    end_rows = jnp.zeros((16, wide.shape[1]), jnp.float32)
    place = lax.broadcasted_iota(jnp.int32, (16, 1), 0)
    for p, part in enumerate(split(wide, 3)):
        end_rows = jnp.where(place == p, part.astype(jnp.float32), end_rows)
    right = jnp.concatenate(
        [minus.astype(jnp.bfloat16)] * 3
        + [end_rows.astype(jnp.bfloat16)]
        + [free.astype(jnp.bfloat16)] * 3,
        axis=0,
    )
    ones = jnp.ones((16, per_piece * width), jnp.bfloat16)

    def step(picked, sums):
        at_block = lambda i: picked[:, i * queries : (i + 1) * queries]
        others = jnp.exp2(at_block(2 * LIMITED))
        mass, slope = zip(*[box_terms(at_block(k), at_block(LIMITED + k)) for k in range(LIMITED)])
        pair = others * mass[0]
        both = mass[1] * mass[2]
        return pair * both, (
            sums[0] + (others * slope[0]) * both,
            sums[1] + pair * (mass[2] * slope[1]),
            sums[2] + pair * (mass[1] * slope[2]),
        )

    def piece(start, totals):
        sums, products = totals[:-1], totals[-1]
        some = [blocks_ref[start + b] for b in range(per_piece)]
        x = unit * jnp.concatenate(
            [
                jnp.concatenate([block[:, width * j : width * (j + 1)] for block in some], axis=1)
                for j in range(dims // 8)
            ],
            axis=0,
        )
        rest = float(GRID) * unit - x
        full = lax.erf(rest) + lax.erf(x)
        slope = x * jnp.exp2((x * x) * -LOG2_E) + rest * jnp.exp2((rest * rest) * -LOG2_E)
        ratio = jnp.concatenate(split(-slope / full, 2) + [ones], axis=0)
        logs = jnp.log(0.5 * full) * LOG2_E
        left = jnp.concatenate(split(x, 3) + [ones] + split(logs, 3), axis=0)
        picked = lax.dot_general(
            left, right, (((0,), (0,)), ((), ())), preferred_element_type=jnp.float32
        )
        inside = []
        for at_row in range(0, per_piece * width, 16):
            whole, sums = step(picked[at_row : at_row + 16], sums)
            inside.append(jnp.concatenate(split(whole, 2), axis=1))
        inside = jnp.concatenate(inside, axis=0)
        products = products + jnp.dot(ratio, inside, preferred_element_type=jnp.float32)
        return (*sums, products)

    def pieces(number, totals):
        for start in range(0, group, per_piece):
            totals = piece(number * group + start, totals)
        return totals

    zero = jnp.zeros((16, queries), jnp.float32)
    totals = (zero,) * LIMITED + (jnp.zeros((2 * dims + 16, 2 * queries), jnp.float32),)
    if count == group:
        totals = pieces(0, totals)
    else:
        totals = lax.fori_loop(0, count // group, pieces, totals)
    sums = [jnp.sum(s, axis=0, keepdims=True) for s in totals[:-1]]
    products = totals[-1]
    deriv = products[:dims, :queries]
    deriv = deriv + (products[dims : 2 * dims, :queries] + products[:dims, queries:])
    total = products[2 * dims : 2 * dims + 8, :queries] + products[2 * dims : 2 * dims + 8, queries:]
    deriv = jnp.where(limited, 0.0, deriv * (SLOPE / 4))
    for mask, s in zip(chosen, sums):
        deriv = jnp.where(mask, s * (SLOPE / 4), deriv)
    out_ref[:dims, :] = deriv
    out_ref[dims:, :] = total * 0.125


def finish_kernel(sample_total, query_total, *refs):
    part_refs, (target_ref, log_ref, share_ref) = refs[:-3], refs[-3:]
    whole = tree_sum([ref[...] for ref in part_refs])
    dims, queries = whole.shape[0] - 8, whole.shape[1]
    smoothing = 1.0 / TABLE_ROWS
    estimate = whole[dims : dims + 1] / sample_total
    log_est = jnp.log(estimate + smoothing)
    log_ref[...] = log_est
    weight = 2.0 * (log_est - target_ref[...]) / (query_total * (estimate + smoothing))
    terms = whole[:dims] * (weight / sample_total)
    terms = jnp.concatenate([terms, jnp.zeros((queries - dims, queries), jnp.float32)], axis=0)
    share = jnp.sum(terms.T, axis=0, keepdims=True)
    for peer in range(share_ref.shape[0]):
        share_ref[peer] = share


def last_kernel(shares_ref, held_log_ref, log_ref, gradient_ref):
    total = tree_sum([shares_ref[peer] for peer in range(shares_ref.shape[0])])
    log_ref[...] = held_log_ref[0]
    gradient_ref[...] = total[0, : gradient_ref.shape[0]]


def everyone(x, axis):
    size = lax.axis_size(axis)
    return [x] + [
        lax.ppermute(x, axis, [(i, i ^ offset) for i in range(size)]) for offset in range(1, size)
    ]


def call(kernel, args, outs, scratch=(), placed=pltpu.VMEM):
    single = len(outs) == 1
    return pl.pallas_call(
        kernel,
        out_shape=outs[0] if single else outs,
        in_specs=[pl.BlockSpec(memory_space=placed)] * len(args),
        out_specs=pl.BlockSpec(memory_space=pltpu.VMEM)
        if single
        else [pl.BlockSpec(memory_space=pltpu.VMEM)] * len(outs),
        scratch_shapes=list(scratch),
        compiler_params=pltpu.CompilerParams(vmem_limit_bytes=32 << 20),
    )(*args)


def shape(*sizes):
    return jax.ShapeDtypeStruct(sizes, jnp.float32)


def on_device(samples, bounds, spread, counts):
    dims, width = samples.shape
    queries = bounds.shape[2]
    blocks, copies = lax.axis_size("blk"), lax.axis_size("grp")
    sample_total = width * blocks * copies
    query_total = queries * blocks

    counts_vector = pltpu.VMEM((1, queries), jnp.int32)
    packed, bounds, spread, target = call(
        load_kernel,
        [
            pltpu.with_memory_space_constraint(array, pltpu.HBM)
            for array in (samples, bounds, spread.reshape(1, dims), counts.reshape(1, queries))
        ],
        [
            pltpu.VMEM((blocks, 8, dims * width // 8), jnp.float32),
            pltpu.VMEM(bounds.shape, bounds.dtype),
            pltpu.VMEM((1, dims), jnp.float32),
            pltpu.VMEM((1, queries), jnp.float32),
        ],
        [pltpu.VMEM((dims, width), jnp.float32), counts_vector, pltpu.SemaphoreType.DMA((4,))],
        placed=pl.ANY,
    )
    turned = [1] + [0] * (blocks - 1)
    groups = [
        [b * copies + (c + turned[b]) % copies for b in reversed(range(blocks))]
        for c in range(copies)
    ]
    exchange = lambda x: lax.all_to_all(x, ("blk", "grp"), 0, 0, axis_index_groups=groups)
    gathered = exchange(packed)
    part = call(
        functools.partial(terms_kernel, width),
        [gathered, bounds, spread],
        [shape(dims + 8, queries)],
    )
    log_est, share = call(
        functools.partial(finish_kernel, sample_total, query_total),
        everyone(part, "grp") + [target],
        [shape(1, queries), shape(blocks, 1, queries)],
    )
    shares = exchange(share)
    return call(last_kernel, [shares, log_est], [shape(queries), shape(dims)])


def solution(mesh):
    return jax.shard_map(
        on_device,
        mesh=mesh,
        in_specs=(P(None, ("blk", "grp")), P(None, None, "blk"), P(), P("blk")),
        out_specs=(P("blk"), P()),
        check_vma=False,
    )
```

```python
import functools

import jax
import jax.numpy as jnp
from jax import lax
from jax.experimental import pallas as pl
from jax.experimental.pallas import tpu as pltpu
from jax.sharding import PartitionSpec as P

TABLE_ROWS = 1048576
GRID = 256
LIMITED = 3

ROOT_HALF = 0.7071067811865476
LOG2_E = 1.4426950408889634
SLOPE = 0.5641895835477563


def box_terms(low, high):
    low_bell = jnp.exp2((low * low) * -LOG2_E)
    high_bell = jnp.exp2((high * high) * -LOG2_E)
    return lax.erf(high) - lax.erf(low), low * low_bell - high * high_bell


def split(x, parts):
    out = []
    for _ in range(parts - 1):
        head = x.astype(jnp.bfloat16)
        out.append(head)
        x = x - head.astype(jnp.float32)
    return out + [x.astype(jnp.bfloat16)]


def tree_sum(parts):
    while len(parts) > 1:
        parts = [a + b for a, b in zip(parts[::2], parts[1::2])]
    return parts[0]


def load_kernel(
    x_ref, bounds_ref, spread_ref, counts_ref,
    out_ref, held_bounds, held_spread, target_ref,
    held_x, held_counts, sems,
):
    sources = (x_ref, bounds_ref, spread_ref, counts_ref)
    targets = (held_x, held_bounds, held_spread, held_counts)
    copies = [
        pltpu.make_async_copy(source, target, sems.at[i])
        for i, (source, target) in enumerate(zip(sources, targets))
    ]
    for copy in copies:
        copy.start()
    copies[0].wait()
    rows = held_x.shape[0]
    packed = jnp.concatenate([held_x[8 * j : 8 * (j + 1), :] for j in range(rows // 8)], axis=1)
    for peer in range(out_ref.shape[0]):
        out_ref[peer] = packed
    for copy in copies[1:]:
        copy.wait()
    smoothing = 1.0 / TABLE_ROWS
    target_ref[...] = jnp.log(held_counts[...].astype(jnp.float32) / TABLE_ROWS + smoothing)


def terms_kernel(width, blocks_ref, bounds_ref, spread_ref, out_ref):
    dims, queries = bounds_ref.shape[1:]
    count = blocks_ref.shape[0]
    per_piece = 128 // width
    group = min(count, 4 * per_piece)

    low, high = bounds_ref[0], bounds_ref[1]
    limited = (high - low) != GRID
    at = lax.broadcasted_iota(jnp.int32, (dims, queries), 0)
    first = jnp.min(jnp.where(limited, at, dims), axis=0, keepdims=True)
    last = jnp.max(jnp.where(limited, at, -1), axis=0, keepdims=True)
    chosen = [at == first, limited & (at > first) & (at < last), at == last]

    row = lax.broadcasted_iota(jnp.int32, (dims, dims), 0)
    column = lax.broadcasted_iota(jnp.int32, (dims, dims), 1)
    spread = jnp.sum(jnp.where(row == column, spread_ref[...], 0.0), axis=1, keepdims=True)
    unit = ROOT_HALF / spread

    pick = lambda mask, values: jnp.sum(jnp.where(mask, values, 0.0), axis=0, keepdims=True)
    low = low.astype(jnp.float32) * unit
    high = high.astype(jnp.float32) * unit
    low_at = [pick(mask, low) for mask in chosen]
    high_at = [pick(mask, high) for mask in chosen]

    ones = [mask.astype(jnp.float32).astype(jnp.bfloat16) for mask in chosen]
    free = jnp.where(limited, 0.0, 1.0).astype(jnp.bfloat16)
    none = jnp.zeros_like(free)
    right = jnp.concatenate(
        [jnp.concatenate(ones + [none], axis=1)] * 3
        + [jnp.concatenate([none] * LIMITED + [free], axis=1)] * 3,
        axis=0,
    )

    def step(picked, sums):
        others = jnp.exp2(picked[:, LIMITED * queries :])
        mass, slope = [], []
        for k in range(LIMITED):
            points = picked[:, k * queries : (k + 1) * queries]
            m, s = box_terms(low_at[k] - points, high_at[k] - points)
            mass.append(m)
            slope.append(s)
        pair = others * mass[0]
        last_two = pair * mass[1]
        whole = last_two * mass[2]
        return whole, (
            sums[0] + whole,
            sums[1] + (others * mass[1]) * (mass[2] * slope[0]),
            sums[2] + pair * (mass[2] * slope[1]),
            sums[3] + last_two * slope[2],
        )

    def selection(start):
        some = [blocks_ref[start + b] for b in range(per_piece)]
        x = unit * jnp.concatenate(
            [
                jnp.concatenate([block[:, width * j : width * (j + 1)] for block in some], axis=1)
                for j in range(dims // 8)
            ],
            axis=0,
        )
        full, slope = box_terms(-x, float(GRID) * unit - x)
        ratio = jnp.concatenate(split(slope / full, 2), axis=0)
        left = jnp.concatenate(split(x, 3) + split(jnp.log(0.5 * full) * LOG2_E, 3), axis=0)
        picked = lax.dot_general(
            left, right, (((0,), (0,)), ((), ())), preferred_element_type=jnp.float32
        )
        return picked, ratio

    def pieces(number, totals):
        sums, products = totals[:-1], totals[-1]
        starts = [number * group + start for start in range(0, group, per_piece)]
        ahead, behind = selection(starts[0]), None
        for i in range(len(starts)):
            picked, ratio = ahead
            if i + 1 < len(starts):
                ahead = selection(starts[i + 1])
            if behind is not None:
                products = products + jnp.dot(*behind, preferred_element_type=jnp.float32)
            inside = []
            for at_row in range(0, per_piece * width, 16):
                whole, sums = step(picked[at_row : at_row + 16], sums)
                inside.append(jnp.concatenate(split(whole, 2), axis=1))
            behind = ratio, jnp.concatenate(inside, axis=0)
        products = products + jnp.dot(*behind, preferred_element_type=jnp.float32)
        return (*sums, products)

    zero = jnp.zeros((16, queries), jnp.float32)
    totals = (zero,) * (1 + LIMITED) + (jnp.zeros((2 * dims, 2 * queries), jnp.float32),)
    if count == group:
        totals = pieces(0, totals)
    else:
        totals = lax.fori_loop(0, count // group, pieces, totals)
    sums = [jnp.sum(s, axis=0, keepdims=True) for s in totals[:-1]]
    products = totals[-1]
    deriv = products[:dims, :queries] + (products[dims:, :queries] + products[:dims, queries:])
    deriv = jnp.where(limited, 0.0, deriv * (SLOPE / 4))
    for mask, s in zip(chosen, sums[1:]):
        deriv = jnp.where(mask, s * (SLOPE / 4), deriv)
    out_ref[:dims, :] = deriv
    out_ref[dims:, :] = jnp.broadcast_to(sums[0] * 0.125, (8, queries))


def finish_kernel(sample_total, query_total, *refs):
    part_refs, (target_ref, log_ref, share_ref) = refs[:-3], refs[-3:]
    whole = tree_sum([ref[...] for ref in part_refs])
    dims, queries = whole.shape[0] - 8, whole.shape[1]
    smoothing = 1.0 / TABLE_ROWS
    estimate = whole[dims : dims + 1] / sample_total
    log_est = jnp.log(estimate + smoothing)
    log_ref[...] = log_est
    weight = 2.0 * (log_est - target_ref[...]) / (query_total * (estimate + smoothing))
    terms = whole[:dims] * (weight / sample_total)
    terms = jnp.concatenate([terms, jnp.zeros((queries - dims, queries), jnp.float32)], axis=0)
    share = jnp.sum(terms.T, axis=0, keepdims=True)
    for peer in range(share_ref.shape[0]):
        share_ref[peer] = share


def last_kernel(shares_ref, held_log_ref, log_ref, gradient_ref):
    total = tree_sum([shares_ref[peer] for peer in range(shares_ref.shape[0])])
    log_ref[...] = held_log_ref[0]
    gradient_ref[...] = total[0, : gradient_ref.shape[0]]


def everyone(x, axis):
    size = lax.axis_size(axis)
    return [x] + [
        lax.ppermute(x, axis, [(i, i ^ offset) for i in range(size)]) for offset in range(1, size)
    ]


def call(kernel, args, outs, scratch=(), placed=pltpu.VMEM):
    single = len(outs) == 1
    return pl.pallas_call(
        kernel,
        out_shape=outs[0] if single else outs,
        in_specs=[pl.BlockSpec(memory_space=placed)] * len(args),
        out_specs=pl.BlockSpec(memory_space=pltpu.VMEM)
        if single
        else [pl.BlockSpec(memory_space=pltpu.VMEM)] * len(outs),
        scratch_shapes=list(scratch),
        compiler_params=pltpu.CompilerParams(vmem_limit_bytes=32 << 20),
    )(*args)


def shape(*sizes):
    return jax.ShapeDtypeStruct(sizes, jnp.float32)


def on_device(samples, bounds, spread, counts):
    dims, width = samples.shape
    queries = bounds.shape[2]
    blocks, copies = lax.axis_size("blk"), lax.axis_size("grp")
    sample_total = width * blocks * copies
    query_total = queries * blocks

    counts_vector = pltpu.VMEM((1, queries), jnp.int32)
    packed, bounds, spread, target = call(
        load_kernel,
        [
            pltpu.with_memory_space_constraint(array, pltpu.HBM)
            for array in (samples, bounds, spread.reshape(1, dims), counts.reshape(1, queries))
        ],
        [
            pltpu.VMEM((blocks, 8, dims * width // 8), jnp.float32),
            pltpu.VMEM(bounds.shape, bounds.dtype),
            pltpu.VMEM((1, dims), jnp.float32),
            pltpu.VMEM((1, queries), jnp.float32),
        ],
        [pltpu.VMEM((dims, width), jnp.float32), counts_vector, pltpu.SemaphoreType.DMA((4,))],
        placed=pl.ANY,
    )
    turned = [1] + [0] * (blocks - 1)
    groups = [
        [b * copies + (c + turned[b]) % copies for b in reversed(range(blocks))]
        for c in range(copies)
    ]
    exchange = lambda x: lax.all_to_all(x, ("blk", "grp"), 0, 0, axis_index_groups=groups)
    gathered = exchange(packed)
    part = call(
        functools.partial(terms_kernel, width),
        [gathered, bounds, spread],
        [shape(dims + 8, queries)],
    )
    log_est, share = call(
        functools.partial(finish_kernel, sample_total, query_total),
        everyone(part, "grp") + [target],
        [shape(1, queries), shape(blocks, 1, queries)],
    )
    shares = exchange(share)
    return call(last_kernel, [shares, log_est], [shape(queries), shape(dims)])


def solution(mesh):
    return jax.shard_map(
        on_device,
        mesh=mesh,
        in_specs=(P(None, ("blk", "grp")), P(None, None, "blk"), P(), P("blk")),
        out_specs=(P("blk"), P()),
        check_vma=False,
    )
```

```python
import functools

import jax
import jax.numpy as jnp
from jax import lax
from jax.experimental import pallas as pl
from jax.experimental.pallas import tpu as pltpu
from jax.sharding import PartitionSpec as P

TABLE_ROWS = 1048576
GRID = 256
LIMITED = 3

ROOT_HALF = 0.7071067811865476
LOG2_E = 1.4426950408889634
SLOPE = 0.5641895835477563


def box_terms(low, high):
    low_bell = jnp.exp2((low * low) * -LOG2_E)
    high_bell = jnp.exp2((high * high) * -LOG2_E)
    return lax.erf(high) - lax.erf(low), low * low_bell - high * high_bell


def split(x, parts):
    out = []
    for _ in range(parts - 1):
        head = x.astype(jnp.bfloat16)
        out.append(head)
        x = x - head.astype(jnp.float32)
    return out + [x.astype(jnp.bfloat16)]


def tree_sum(parts):
    while len(parts) > 1:
        parts = [a + b for a, b in zip(parts[::2], parts[1::2])]
    return parts[0]


def load_kernel(
    x_ref, bounds_ref, spread_ref, counts_ref,
    out_ref, held_bounds, held_spread, target_ref,
    held_x, held_counts, sems,
):
    sources = (x_ref, bounds_ref, spread_ref, counts_ref)
    targets = (held_x, held_bounds, held_spread, held_counts)
    copies = [
        pltpu.make_async_copy(source, target, sems.at[i])
        for i, (source, target) in enumerate(zip(sources, targets))
    ]
    for copy in copies:
        copy.start()
    copies[0].wait()
    rows = held_x.shape[1]
    turned = held_x[...].T
    packed = jnp.concatenate([turned[8 * j : 8 * (j + 1), :] for j in range(rows // 8)], axis=1)
    for peer in range(out_ref.shape[0]):
        out_ref[peer] = packed
    for copy in copies[1:]:
        copy.wait()
    smoothing = 1.0 / TABLE_ROWS
    target_ref[...] = jnp.log(held_counts[...].astype(jnp.float32) / TABLE_ROWS + smoothing)


def terms_kernel(blocks_ref, bounds_ref, spread_ref, out_ref):
    dims, queries = bounds_ref.shape[1:]
    lanes = blocks_ref.shape[2]
    pieces = lanes // dims
    group = 128 // blocks_ref.shape[1]

    low, high = bounds_ref[0], bounds_ref[1]
    limited = (high - low) != GRID
    at = lax.broadcasted_iota(jnp.int32, (dims, queries), 0)
    first = jnp.min(jnp.where(limited, at, dims), axis=0, keepdims=True)
    last = jnp.max(jnp.where(limited, at, -1), axis=0, keepdims=True)
    chosen = [at == first, limited & (at > first) & (at < last), at == last]

    unit_row = ROOT_HALF / spread_ref[...]
    row = lax.broadcasted_iota(jnp.int32, (dims, dims), 0)
    column = lax.broadcasted_iota(jnp.int32, (dims, dims), 1)
    unit = jnp.sum(jnp.where(row == column, unit_row, 0.0), axis=1, keepdims=True)
    unit_row = jnp.concatenate([unit_row] * pieces, axis=1)

    pick = lambda mask, values: jnp.sum(jnp.where(mask, values, 0.0), axis=0, keepdims=True)
    low = low.astype(jnp.float32) * unit
    high = high.astype(jnp.float32) * unit
    low_at = [pick(mask, low) for mask in chosen]
    high_at = [pick(mask, high) for mask in chosen]
    second = jnp.sum(jnp.where(chosen[1], at, 0), axis=0, keepdims=True)
    lane_of = [
        [jnp.broadcast_to(dim + dims * j, (16, queries)) for dim in (first, second, last)]
        for j in range(pieces)
    ]
    place = lambda axis: lax.broadcasted_iota(jnp.int32, (lanes, lanes), axis) // dims
    same = jnp.where(place(0) == place(1), 1.0, 0.0).astype(jnp.bfloat16)

    def step(x, minus_log, rest_log, lane_at, sums):
        take = lambda values, k: jnp.take_along_axis(
            values, lane_at[k], axis=1, mode="promise_in_bounds"
        )
        others = jnp.exp2(take(minus_log, 0) + take(minus_log, 1) + take(rest_log, 2))
        mass, slope = [], []
        for k in range(LIMITED):
            points = take(x, k)
            m, s = box_terms(low_at[k] - points, high_at[k] - points)
            mass.append(m)
            slope.append(s)
        pair = others * mass[0]
        last_two = pair * mass[1]
        whole = last_two * mass[2]
        return whole, (
            sums[0] + whole,
            sums[1] + (others * mass[1]) * (mass[2] * slope[0]),
            sums[2] + pair * (mass[2] * slope[1]),
            sums[3] + last_two * slope[2],
        )

    def chunk(number, totals):
        sums, products = totals[:-1], totals[-1]
        x = blocks_ref[pl.ds(number * group, group)].reshape(128, lanes) * unit_row
        full, slope = box_terms(-x, float(GRID) * unit_row - x)
        logs = jnp.log(0.5 * full) * LOG2_E
        every = jnp.dot(
            jnp.concatenate(split(logs, 3), axis=1),
            jnp.concatenate([same] * 3, axis=0),
            preferred_element_type=jnp.float32,
        )
        rest_log = every - logs
        ratio = split((slope / full).T, 2)
        for j in range(pieces):
            inside = []
            for r in range(0, 128, 16):
                rows = slice(r, r + 16)
                whole, sums = step(x[rows], -logs[rows], rest_log[rows], lane_of[j], sums)
                inside.append(jnp.concatenate(split(whole, 2), axis=1))
            ratio_at = jnp.concatenate([part[j * dims : (j + 1) * dims] for part in ratio], axis=0)
            products = products + jnp.dot(
                ratio_at, jnp.concatenate(inside, axis=0), preferred_element_type=jnp.float32
            )
        return (*sums, products)

    zero = jnp.zeros((16, queries), jnp.float32)
    totals = (zero,) * (1 + LIMITED) + (jnp.zeros((2 * dims, 2 * queries), jnp.float32),)
    chunks = blocks_ref.shape[0] // group
    totals = chunk(0, totals) if chunks == 1 else lax.fori_loop(0, chunks, chunk, totals)
    sums = [jnp.sum(s, axis=0, keepdims=True) for s in totals[:-1]]
    products = totals[-1]
    deriv = products[:dims, :queries] + (products[dims:, :queries] + products[:dims, queries:])
    deriv = jnp.where(limited, 0.0, deriv * (SLOPE / 4))
    for mask, s in zip(chosen, sums[1:]):
        deriv = jnp.where(mask, s * (SLOPE / 4), deriv)
    out_ref[:dims, :] = deriv
    out_ref[dims:, :] = jnp.broadcast_to(sums[0] * 0.125, (8, queries))


def finish_kernel(sample_total, query_total, *refs):
    part_refs, (target_ref, log_ref, share_ref) = refs[:-3], refs[-3:]
    whole = tree_sum([ref[...] for ref in part_refs])
    dims, queries = whole.shape[0] - 8, whole.shape[1]
    smoothing = 1.0 / TABLE_ROWS
    estimate = whole[dims : dims + 1] / sample_total
    log_est = jnp.log(estimate + smoothing)
    log_ref[...] = log_est
    weight = 2.0 * (log_est - target_ref[...]) / (query_total * (estimate + smoothing))
    terms = whole[:dims] * (weight / sample_total)
    terms = jnp.concatenate([terms, jnp.zeros((queries - dims, queries), jnp.float32)], axis=0)
    share = jnp.sum(terms.T, axis=0, keepdims=True)
    for peer in range(share_ref.shape[0]):
        share_ref[peer] = share


def last_kernel(shares_ref, held_log_ref, log_ref, gradient_ref):
    total = tree_sum([shares_ref[peer] for peer in range(shares_ref.shape[0])])
    log_ref[...] = held_log_ref[0]
    gradient_ref[...] = total[0, : gradient_ref.shape[0]]


def everyone(x, axis):
    size = lax.axis_size(axis)
    return [x] + [
        lax.ppermute(x, axis, [(i, i ^ offset) for i in range(size)]) for offset in range(1, size)
    ]


def call(kernel, args, outs, scratch=(), placed=pltpu.VMEM):
    single = len(outs) == 1
    return pl.pallas_call(
        kernel,
        out_shape=outs[0] if single else outs,
        in_specs=[pl.BlockSpec(memory_space=placed)] * len(args),
        out_specs=pl.BlockSpec(memory_space=pltpu.VMEM)
        if single
        else [pl.BlockSpec(memory_space=pltpu.VMEM)] * len(outs),
        scratch_shapes=list(scratch),
        compiler_params=pltpu.CompilerParams(vmem_limit_bytes=32 << 20),
    )(*args)


def shape(*sizes):
    return jax.ShapeDtypeStruct(sizes, jnp.float32)


def on_device(samples, bounds, spread, counts):
    dims, width = samples.shape
    queries = bounds.shape[2]
    blocks, copies = lax.axis_size("blk"), lax.axis_size("grp")
    sample_total = width * blocks * copies
    query_total = queries * blocks

    counts_vector = pltpu.VMEM((1, queries), jnp.int32)
    packed, bounds, spread, target = call(
        load_kernel,
        [
            pltpu.with_memory_space_constraint(array, pltpu.HBM)
            for array in (samples, bounds, spread.reshape(1, dims), counts.reshape(1, queries))
        ],
        [
            pltpu.VMEM((blocks, 8, dims * width // 8), jnp.float32),
            pltpu.VMEM(bounds.shape, bounds.dtype),
            pltpu.VMEM((1, dims), jnp.float32),
            pltpu.VMEM((1, queries), jnp.float32),
        ],
        [pltpu.VMEM((dims, width), jnp.float32), counts_vector, pltpu.SemaphoreType.DMA((4,))],
        placed=pl.ANY,
    )
    turned = [1] + [0] * (blocks - 1)
    groups = [
        [b * copies + (c + turned[b]) % copies for b in reversed(range(blocks))]
        for c in range(copies)
    ]
    exchange = lambda x: lax.all_to_all(x, ("blk", "grp"), 0, 0, axis_index_groups=groups)
    gathered = exchange(packed)
    part = call(
        terms_kernel,
        [gathered, bounds, spread],
        [shape(dims + 8, queries)],
    )
    log_est, share = call(
        functools.partial(finish_kernel, sample_total, query_total),
        everyone(part, "grp") + [target],
        [shape(1, queries), shape(blocks, 1, queries)],
    )
    shares = exchange(share)
    return call(last_kernel, [shares, log_est], [shape(queries), shape(dims)])


def solution(mesh):
    return jax.shard_map(
        on_device,
        mesh=mesh,
        in_specs=(P(None, ("blk", "grp")), P(None, None, "blk"), P(), P("blk")),
        out_specs=(P("blk"), P()),
        check_vma=False,
    )
```

```python
import functools

import jax
import jax.numpy as jnp
from jax import lax
from jax.experimental import pallas as pl
from jax.experimental.pallas import tpu as pltpu
from jax.sharding import PartitionSpec as P

TABLE_ROWS = 1048576
GRID = 256
LIMITED = 3

ROOT_HALF = 0.7071067811865476
LOG2_E = 1.4426950408889634
SLOPE = 0.5641895835477563


def box_terms(low, high):
    low_bell = jnp.exp2((low * low) * -LOG2_E)
    high_bell = jnp.exp2((high * high) * -LOG2_E)
    return lax.erf(high) - lax.erf(low), low * low_bell - high * high_bell


def split(x, parts):
    out = []
    for _ in range(parts - 1):
        head = x.astype(jnp.bfloat16)
        out.append(head)
        x = x - head.astype(jnp.float32)
    return out + [x.astype(jnp.bfloat16)]


def tree_sum(parts):
    while len(parts) > 1:
        parts = [a + b for a, b in zip(parts[::2], parts[1::2])]
    return parts[0]


def load_kernel(
    x_ref, bounds_ref, spread_ref, counts_ref,
    out_ref, held_bounds, held_spread, target_ref,
    held_x, held_counts, sems,
):
    sources = (x_ref, bounds_ref, spread_ref, counts_ref)
    targets = (held_x, held_bounds, held_spread, held_counts)
    copies = [
        pltpu.make_async_copy(source, target, sems.at[i])
        for i, (source, target) in enumerate(zip(sources, targets))
    ]
    for copy in copies:
        copy.start()
    copies[0].wait()
    rows = held_x.shape[0]
    packed = jnp.concatenate([held_x[8 * j : 8 * (j + 1), :] for j in range(rows // 8)], axis=1)
    for peer in range(out_ref.shape[0]):
        out_ref[peer] = packed
    for copy in copies[1:]:
        copy.wait()
    smoothing = 1.0 / TABLE_ROWS
    target_ref[...] = jnp.log(held_counts[...].astype(jnp.float32) / TABLE_ROWS + smoothing)


def terms_kernel(width, blocks_ref, bounds_ref, spread_ref, out_ref):
    dims, queries = bounds_ref.shape[1:]
    count = blocks_ref.shape[0]
    per_piece = 128 // width
    group = min(count, 4 * per_piece)

    low, high = bounds_ref[0], bounds_ref[1]
    limited = (high - low) != GRID
    at = lax.broadcasted_iota(jnp.int32, (dims, queries), 0)
    first = jnp.min(jnp.where(limited, at, dims), axis=0, keepdims=True)
    last = jnp.max(jnp.where(limited, at, -1), axis=0, keepdims=True)
    chosen = [at == first, limited & (at > first) & (at < last), at == last]

    row = lax.broadcasted_iota(jnp.int32, (dims, dims), 0)
    column = lax.broadcasted_iota(jnp.int32, (dims, dims), 1)
    spread = jnp.sum(jnp.where(row == column, spread_ref[...], 0.0), axis=1, keepdims=True)
    unit = ROOT_HALF / spread

    pick = lambda mask, values: jnp.sum(jnp.where(mask, values, 0.0), axis=0, keepdims=True)
    low = low.astype(jnp.float32) * unit
    high = high.astype(jnp.float32) * unit
    low_at = [pick(mask, low) for mask in chosen]
    high_at = [pick(mask, high) for mask in chosen]

    ones = [mask.astype(jnp.float32).astype(jnp.bfloat16) for mask in chosen]
    free = jnp.where(limited, 0.0, 1.0).astype(jnp.bfloat16)
    none = jnp.zeros_like(free)
    right = jnp.concatenate(
        [jnp.concatenate(ones + [none], axis=1)] * 3
        + [jnp.concatenate([none] * LIMITED + [free], axis=1)] * 3,
        axis=0,
    )

    def step(picked, sums):
        others = jnp.exp2(picked[:, LIMITED * queries :])
        mass, slope = [], []
        for k in range(LIMITED):
            points = picked[:, k * queries : (k + 1) * queries]
            m, s = box_terms(low_at[k] - points, high_at[k] - points)
            mass.append(m)
            slope.append(s)
        pair = others * mass[0]
        last_two = pair * mass[1]
        whole = last_two * mass[2]
        return whole, (
            sums[0] + whole,
            sums[1] + (others * mass[1]) * (mass[2] * slope[0]),
            sums[2] + pair * (mass[2] * slope[1]),
            sums[3] + last_two * slope[2],
        )

    def piece(start, totals):
        sums, products = totals[:-1], totals[-1]
        some = [blocks_ref[start + b] for b in range(per_piece)]
        x = unit * jnp.concatenate(
            [
                jnp.concatenate([block[:, width * j : width * (j + 1)] for block in some], axis=1)
                for j in range(dims // 8)
            ],
            axis=0,
        )
        full, slope = box_terms(-x, float(GRID) * unit - x)
        ratio = jnp.concatenate(split(slope / full, 2), axis=0)
        left = jnp.concatenate(split(x, 3) + split(jnp.log(0.5 * full) * LOG2_E, 3), axis=0)
        picked = lax.dot_general(
            left, right, (((0,), (0,)), ((), ())), preferred_element_type=jnp.float32
        )
        inside = []
        for at_row in range(0, per_piece * width, 16):
            whole, sums = step(picked[at_row : at_row + 16], sums)
            inside.append(jnp.concatenate(split(whole, 2), axis=1))
        inside = jnp.concatenate(inside, axis=0)
        products = products + jnp.dot(ratio, inside, preferred_element_type=jnp.float32)
        return (*sums, products)

    def pieces(number, totals):
        for start in range(0, group, per_piece):
            totals = piece(number * group + start, totals)
        return totals

    zero = jnp.zeros((16, queries), jnp.float32)
    totals = (zero,) * (1 + LIMITED) + (jnp.zeros((2 * dims, 2 * queries), jnp.float32),)
    if count == group:
        totals = pieces(0, totals)
    else:
        totals = lax.fori_loop(0, count // group, pieces, totals)
    sums = [jnp.sum(s, axis=0, keepdims=True) for s in totals[:-1]]
    products = totals[-1]
    deriv = products[:dims, :queries] + (products[dims:, :queries] + products[:dims, queries:])
    deriv = jnp.where(limited, 0.0, deriv * (SLOPE / 4))
    for mask, s in zip(chosen, sums[1:]):
        deriv = jnp.where(mask, s * (SLOPE / 4), deriv)
    out_ref[:dims, :] = deriv
    out_ref[dims:, :] = jnp.broadcast_to(sums[0] * 0.125, (8, queries))


def finish_kernel(sample_total, query_total, *refs):
    part_refs, (target_ref, log_ref, share_ref) = refs[:-3], refs[-3:]
    whole = tree_sum([ref[...] for ref in part_refs])
    dims, queries = whole.shape[0] - 8, whole.shape[1]
    smoothing = 1.0 / TABLE_ROWS
    estimate = whole[dims : dims + 1] / sample_total
    log_est = jnp.log(estimate + smoothing)
    log_ref[...] = log_est
    weight = 2.0 * (log_est - target_ref[...]) / (query_total * (estimate + smoothing))
    terms = whole[:dims] * (weight / sample_total)
    terms = jnp.concatenate([terms, jnp.zeros((queries - dims, queries), jnp.float32)], axis=0)
    share = jnp.sum(terms.T, axis=0, keepdims=True)
    for peer in range(share_ref.shape[0]):
        share_ref[peer] = share


def last_kernel(shares_ref, held_log_ref, log_ref, gradient_ref):
    total = tree_sum([shares_ref[peer] for peer in range(shares_ref.shape[0])])
    log_ref[...] = held_log_ref[0]
    gradient_ref[...] = total[0, : gradient_ref.shape[0]]


def everyone(x, axis):
    size = lax.axis_size(axis)
    return [x] + [
        lax.ppermute(x, axis, [(i, i ^ offset) for i in range(size)]) for offset in range(1, size)
    ]


def call(kernel, args, outs, scratch=(), placed=pltpu.VMEM):
    single = len(outs) == 1
    return pl.pallas_call(
        kernel,
        out_shape=outs[0] if single else outs,
        in_specs=[pl.BlockSpec(memory_space=placed)] * len(args),
        out_specs=pl.BlockSpec(memory_space=pltpu.VMEM)
        if single
        else [pl.BlockSpec(memory_space=pltpu.VMEM)] * len(outs),
        scratch_shapes=list(scratch),
        compiler_params=pltpu.CompilerParams(vmem_limit_bytes=32 << 20),
    )(*args)


def shape(*sizes):
    return jax.ShapeDtypeStruct(sizes, jnp.float32)


def on_device(samples, bounds, spread, counts):
    dims, width = samples.shape
    queries = bounds.shape[2]
    blocks, copies = lax.axis_size("blk"), lax.axis_size("grp")
    sample_total = width * blocks * copies
    query_total = queries * blocks

    counts_vector = pltpu.VMEM((1, queries), jnp.int32)
    packed, bounds, spread, target = call(
        load_kernel,
        [
            pltpu.with_memory_space_constraint(array, pltpu.HBM)
            for array in (samples, bounds, spread.reshape(1, dims), counts.reshape(1, queries))
        ],
        [
            pltpu.VMEM((blocks, 8, dims * width // 8), jnp.float32),
            pltpu.VMEM(bounds.shape, bounds.dtype),
            pltpu.VMEM((1, dims), jnp.float32),
            pltpu.VMEM((1, queries), jnp.float32),
        ],
        [pltpu.VMEM((dims, width), jnp.float32), counts_vector, pltpu.SemaphoreType.DMA((4,))],
        placed=pl.ANY,
    )
    def exchange(x, turned, orders):
        groups = [
            [b * copies + (c + (b in turned)) % copies for b in orders[c]] for c in range(copies)
        ]
        return lax.all_to_all(x, ("blk", "grp"), 0, 0, axis_index_groups=groups)

    falling = list(reversed(range(blocks)))
    far = blocks // 5
    far_early = falling[far:-1] + falling[:far][::-1] + [0]
    gathered = exchange(
        packed, [0] + falling[1 : 1 + far], [falling] * (copies - 1) + [far_early]
    )
    part = call(
        functools.partial(terms_kernel, width),
        [gathered, bounds, spread],
        [shape(dims + 8, queries)],
    )
    log_est, share = call(
        functools.partial(finish_kernel, sample_total, query_total),
        everyone(part, "grp") + [target],
        [shape(1, queries), shape(blocks, 1, queries)],
    )
    shares = exchange(share, [0], [falling] * copies)
    return call(last_kernel, [shares, log_est], [shape(queries), shape(dims)])


def solution(mesh):
    return jax.shard_map(
        on_device,
        mesh=mesh,
        in_specs=(P(None, ("blk", "grp")), P(None, None, "blk"), P(), P("blk")),
        out_specs=(P("blk"), P()),
        check_vma=False,
    )
```

```python
import functools

import jax
import jax.numpy as jnp
from jax import lax
from jax.experimental import pallas as pl
from jax.experimental.pallas import tpu as pltpu
from jax.sharding import PartitionSpec as P

TABLE_ROWS = 1048576
GRID = 256
LIMITED = 3

ROOT_HALF = 0.7071067811865476
LOG2_E = 1.4426950408889634
SLOPE = 0.5641895835477563


def box_terms(low, high):
    low_bell = jnp.exp2((low * low) * -LOG2_E)
    high_bell = jnp.exp2((high * high) * -LOG2_E)
    return lax.erf(high) - lax.erf(low), low * low_bell - high * high_bell


def split(x, parts):
    out = []
    for _ in range(parts - 1):
        head = x.astype(jnp.bfloat16)
        out.append(head)
        x = x - head.astype(jnp.float32)
    return out + [x.astype(jnp.bfloat16)]


def tree_sum(parts):
    while len(parts) > 1:
        parts = [a + b for a, b in zip(parts[::2], parts[1::2])]
    return parts[0]


def load_kernel(
    x_ref, bounds_ref, spread_ref, counts_ref,
    out_ref, held_bounds, held_spread, target_ref,
    held_x, held_counts, sems,
):
    sources = (x_ref, bounds_ref, spread_ref, counts_ref)
    targets = (held_x, held_bounds, held_spread, held_counts)
    copies = [
        pltpu.make_async_copy(source, target, sems.at[i])
        for i, (source, target) in enumerate(zip(sources, targets))
    ]
    for copy in copies:
        copy.start()
    copies[0].wait()
    rows = held_x.shape[0]
    packed = jnp.concatenate([held_x[8 * j : 8 * (j + 1), :] for j in range(rows // 8)], axis=1)
    for peer in range(out_ref.shape[0]):
        out_ref[peer] = packed
    for copy in copies[1:]:
        copy.wait()
    smoothing = 1.0 / TABLE_ROWS
    target_ref[...] = jnp.log(held_counts[...].astype(jnp.float32) / TABLE_ROWS + smoothing)


def limits(bounds_ref):
    low, high = bounds_ref[0], bounds_ref[1]
    limited = (high - low) != GRID
    at = lax.broadcasted_iota(jnp.int32, low.shape, 0)
    first = jnp.min(jnp.where(limited, at, low.shape[0]), axis=0, keepdims=True)
    last = jnp.max(jnp.where(limited, at, -1), axis=0, keepdims=True)
    return limited, [at == first, limited & (at > first) & (at < last), at == last]


def select(masks, bounds_ref, spread_ref):
    limited, chosen = masks
    dims, queries = limited.shape
    row = lax.broadcasted_iota(jnp.int32, (dims, dims), 0)
    column = lax.broadcasted_iota(jnp.int32, (dims, dims), 1)
    spread = jnp.sum(jnp.where(row == column, spread_ref[...], 0.0), axis=1, keepdims=True)
    unit = ROOT_HALF / spread

    pick = lambda mask, values: jnp.sum(jnp.where(mask, values, 0.0), axis=0, keepdims=True)
    low = bounds_ref[0].astype(jnp.float32) * unit
    high = bounds_ref[1].astype(jnp.float32) * unit
    ends = [pick(mask, low) for mask in chosen] + [pick(mask, high) for mask in chosen]

    ones = [mask.astype(jnp.float32).astype(jnp.bfloat16) for mask in chosen]
    free = jnp.where(limited, 0.0, 1.0).astype(jnp.bfloat16)
    none = jnp.zeros_like(free)
    right = jnp.concatenate(
        [jnp.concatenate(ones + [none], axis=1)] * 3
        + [jnp.concatenate([none] * LIMITED + [free], axis=1)] * 3,
        axis=0,
    )
    return right, ends, unit


def terms(width, blocks_ref, masks, right, ends, unit):
    limited, chosen = masks
    dims, queries = limited.shape
    count = blocks_ref.shape[0]
    per_piece = 128 // width
    group = min(count, 4 * per_piece)
    low_at, high_at = ends[:LIMITED], ends[LIMITED:]
    unit = jnp.broadcast_to(unit, (dims, per_piece * width))

    def step(picked, sums):
        others = jnp.exp2(picked[:, LIMITED * queries :])
        mass, slope = [], []
        for k in range(LIMITED):
            points = picked[:, k * queries : (k + 1) * queries]
            m, s = box_terms(low_at[k] - points, high_at[k] - points)
            mass.append(m)
            slope.append(s)
        pair = others * mass[0]
        last_two = pair * mass[1]
        whole = last_two * mass[2]
        return whole, (
            sums[0] + whole,
            sums[1] + (others * mass[1]) * (mass[2] * slope[0]),
            sums[2] + pair * (mass[2] * slope[1]),
            sums[3] + last_two * slope[2],
        )

    def piece(start, totals):
        sums, products = totals[:-1], totals[-1]
        some = [blocks_ref[start + b] for b in range(per_piece)]
        x = unit * jnp.concatenate(
            [
                jnp.concatenate([block[:, width * j : width * (j + 1)] for block in some], axis=1)
                for j in range(dims // 8)
            ],
            axis=0,
        )
        full, slope = box_terms(-x, float(GRID) * unit - x)
        ratio = jnp.concatenate(split(slope / full, 2), axis=0)
        left = jnp.concatenate(split(x, 3) + split(jnp.log(0.5 * full) * LOG2_E, 3), axis=0)
        picked = lax.dot_general(
            left, right, (((0,), (0,)), ((), ())), preferred_element_type=jnp.float32
        )
        inside = []
        for at_row in range(0, per_piece * width, 16):
            whole, sums = step(picked[at_row : at_row + 16], sums)
            inside.append(jnp.concatenate(split(whole, 2), axis=1))
        inside = jnp.concatenate(inside, axis=0)
        products = products + jnp.dot(ratio, inside, preferred_element_type=jnp.float32)
        return (*sums, products)

    def pieces(number, totals):
        for start in range(0, group, per_piece):
            totals = piece(number * group + start, totals)
        return totals

    zero = jnp.zeros((16, queries), jnp.float32)
    totals = (zero,) * (1 + LIMITED) + (jnp.zeros((2 * dims, 2 * queries), jnp.float32),)
    if count == group:
        totals = pieces(0, totals)
    else:
        totals = lax.fori_loop(0, count // group, pieces, totals)
    sums = [jnp.sum(s, axis=0, keepdims=True) for s in totals[:-1]]
    products = totals[-1]
    deriv = products[:dims, :queries] + (products[dims:, :queries] + products[:dims, queries:])
    deriv = jnp.where(limited, 0.0, deriv * (SLOPE / 4))
    for mask, s in zip(chosen, sums[1:]):
        deriv = jnp.where(mask, s * (SLOPE / 4), deriv)
    return jnp.concatenate([deriv, jnp.broadcast_to(sums[0] * 0.125, (8, queries))], axis=0)


def own_kernel(
    width, blocks_ref, bounds_ref, spread_ref, part_ref, right_ref, ends_ref, unit_ref, masks_ref
):
    masks = limits(bounds_ref)
    right, ends, unit = select(masks, bounds_ref, spread_ref)
    right_ref[...] = right
    for i, end in enumerate(ends):
        ends_ref[i : i + 1, :] = end
    unit_ref[...] = jnp.broadcast_to(unit, unit_ref.shape)
    for i, mask in enumerate([masks[0]] + masks[1]):
        masks_ref[i] = jnp.where(mask, 1.0, 0.0)
    part_ref[...] = terms(width, blocks_ref, masks, right, ends, unit)


def other_kernel(width, blocks_ref, right_ref, ends_ref, unit_ref, masks_ref, part_ref):
    masks = [masks_ref[i] > 0.0 for i in range(1 + LIMITED)]
    ends = [ends_ref[i : i + 1, :] for i in range(2 * LIMITED)]
    part_ref[...] = terms(
        width, blocks_ref, (masks[0], masks[1:]), right_ref[...], ends, unit_ref[...]
    )


def finish_kernel(sample_total, query_total, *refs):
    part_refs, (target_ref, log_ref, share_ref) = refs[:-3], refs[-3:]
    whole = tree_sum([ref[...] for ref in part_refs])
    dims, queries = whole.shape[0] - 8, whole.shape[1]
    smoothing = 1.0 / TABLE_ROWS
    estimate = whole[dims : dims + 1] / sample_total
    log_est = jnp.log(estimate + smoothing)
    log_ref[...] = log_est
    weight = 2.0 * (log_est - target_ref[...]) / (query_total * (estimate + smoothing))
    terms = whole[:dims] * (weight / sample_total)
    terms = jnp.concatenate([terms, jnp.zeros((queries - dims, queries), jnp.float32)], axis=0)
    share = jnp.sum(terms.T, axis=0, keepdims=True)
    for peer in range(share_ref.shape[0]):
        share_ref[peer] = share


def last_kernel(shares_ref, held_log_ref, log_ref, gradient_ref):
    total = tree_sum([shares_ref[peer] for peer in range(shares_ref.shape[0])])
    log_ref[...] = held_log_ref[0]
    gradient_ref[...] = total[0, : gradient_ref.shape[0]]


def everyone(x, axis):
    size = lax.axis_size(axis)
    return [x] + [
        lax.ppermute(x, axis, [(i, i ^ offset) for i in range(size)]) for offset in range(1, size)
    ]


def call(kernel, args, outs, scratch=(), placed=pltpu.VMEM, cost=None):
    single = len(outs) == 1
    return pl.pallas_call(
        kernel,
        out_shape=outs[0] if single else outs,
        in_specs=[pl.BlockSpec(memory_space=placed)] * len(args),
        out_specs=pl.BlockSpec(memory_space=pltpu.VMEM)
        if single
        else [pl.BlockSpec(memory_space=pltpu.VMEM)] * len(outs),
        scratch_shapes=list(scratch),
        cost_estimate=cost,
        compiler_params=pltpu.CompilerParams(vmem_limit_bytes=32 << 20),
    )(*args)


def shape(*sizes):
    return jax.ShapeDtypeStruct(sizes, jnp.float32)


def on_device(samples, bounds, spread, counts):
    dims, width = samples.shape
    queries = bounds.shape[2]
    blocks, copies = lax.axis_size("blk"), lax.axis_size("grp")
    sample_total = width * blocks * copies
    query_total = queries * blocks

    counts_vector = pltpu.VMEM((1, queries), jnp.int32)
    packed, bounds, spread, target = call(
        load_kernel,
        [
            pltpu.with_memory_space_constraint(array, pltpu.HBM)
            for array in (samples, bounds, spread.reshape(1, dims), counts.reshape(1, queries))
        ],
        [
            pltpu.VMEM((blocks, 8, dims * width // 8), jnp.float32),
            pltpu.VMEM(bounds.shape, bounds.dtype),
            pltpu.VMEM((1, dims), jnp.float32),
            pltpu.VMEM((1, queries), jnp.float32),
        ],
        [pltpu.VMEM((dims, width), jnp.float32), counts_vector, pltpu.SemaphoreType.DMA((4,))],
        placed=pl.ANY,
    )
    turned = [1] + [0] * (blocks - 1)
    groups = [
        [b * copies + (c + turned[b]) % copies for b in reversed(range(blocks))]
        for c in range(copies)
    ]
    exchange = lambda x: lax.all_to_all(x, ("blk", "grp"), 0, 0, axis_index_groups=groups)
    gathered = exchange(packed)
    others = everyone(gathered, "grp")[1:]
    elements = LIMITED * gathered.shape[0] * width * queries
    part, right, ends, unit, masks = call(
        functools.partial(own_kernel, width),
        [gathered, bounds, spread],
        [
            shape(dims + 8, queries),
            jax.ShapeDtypeStruct((6 * dims, (LIMITED + 1) * queries), jnp.bfloat16),
            shape(8, queries),
            shape(dims, queries),
            shape(1 + LIMITED, dims, queries),
        ],
        cost=pl.CostEstimate(
            flops=100 * elements, bytes_accessed=64 * elements, transcendentals=4 * elements
        ),
    )
    parts = [part] + [
        call(
            functools.partial(other_kernel, width),
            [other, right, ends, unit, masks],
            [shape(dims + 8, queries)],
        )
        for other in others
    ]
    log_est, share = call(
        functools.partial(finish_kernel, sample_total, query_total),
        parts + [target],
        [shape(1, queries), shape(blocks, 1, queries)],
    )
    shares = exchange(share)
    return call(last_kernel, [shares, log_est], [shape(queries), shape(dims)])


def solution(mesh):
    return jax.shard_map(
        on_device,
        mesh=mesh,
        in_specs=(P(None, ("blk", "grp")), P(None, None, "blk"), P(), P("blk")),
        out_specs=(P("blk"), P()),
        check_vma=False,
    )
```

```python
import functools

import jax
import jax.numpy as jnp
from jax import lax
from jax.experimental import pallas as pl
from jax.experimental.pallas import tpu as pltpu
from jax.sharding import PartitionSpec as P

TABLE_ROWS = 1048576
GRID = 256
LIMITED = 3

ROOT_HALF = 0.7071067811865476
LOG2_E = 1.4426950408889634
SLOPE = 0.5641895835477563


def box_terms(low, high):
    low_bell = jnp.exp2((low * low) * -LOG2_E)
    high_bell = jnp.exp2((high * high) * -LOG2_E)
    return lax.erf(high) - lax.erf(low), low * low_bell - high * high_bell


def split(x, parts):
    out = []
    for _ in range(parts - 1):
        head = x.astype(jnp.bfloat16)
        out.append(head)
        x = x - head.astype(jnp.float32)
    return out + [x.astype(jnp.bfloat16)]


def tree_sum(parts):
    while len(parts) > 1:
        parts = [a + b for a, b in zip(parts[::2], parts[1::2])]
    return parts[0]


def load_kernel(
    x_ref, bounds_ref, spread_ref, counts_ref,
    out_ref, held_bounds, held_spread, target_ref,
    held_x, held_counts, sems,
):
    sources = (x_ref, bounds_ref, spread_ref, counts_ref)
    targets = (held_x, held_bounds, held_spread, held_counts)
    copies = [
        pltpu.make_async_copy(source, target, sems.at[i])
        for i, (source, target) in enumerate(zip(sources, targets))
    ]
    for copy in copies:
        copy.start()
    copies[0].wait()
    rows = held_x.shape[0]
    packed = jnp.concatenate([held_x[8 * j : 8 * (j + 1), :] for j in range(rows // 8)], axis=1)
    for peer in range(out_ref.shape[0]):
        out_ref[peer] = packed
    for copy in copies[1:]:
        copy.wait()
    smoothing = 1.0 / TABLE_ROWS
    target_ref[...] = jnp.log(held_counts[...].astype(jnp.float32) / TABLE_ROWS + smoothing)


def terms_kernel(width, blocks_ref, bounds_ref, spread_ref, out_ref, picked, inside):
    dims, queries = bounds_ref.shape[1:]
    count = blocks_ref.shape[0]
    samples = picked.shape[0]
    group = samples // width

    low, high = bounds_ref[0], bounds_ref[1]
    limited = (high - low) != GRID
    at = lax.broadcasted_iota(jnp.int32, (dims, queries), 0)
    first = jnp.min(jnp.where(limited, at, dims), axis=0, keepdims=True)
    last = jnp.max(jnp.where(limited, at, -1), axis=0, keepdims=True)
    chosen = [at == first, limited & (at > first) & (at < last), at == last]

    row = lax.broadcasted_iota(jnp.int32, (dims, dims), 0)
    column = lax.broadcasted_iota(jnp.int32, (dims, dims), 1)
    spread = jnp.sum(jnp.where(row == column, spread_ref[...], 0.0), axis=1, keepdims=True)
    unit = ROOT_HALF / spread

    pick = lambda mask, values: jnp.sum(jnp.where(mask, values, 0.0), axis=0, keepdims=True)
    low = low.astype(jnp.float32) * unit
    high = high.astype(jnp.float32) * unit
    low_at = [pick(mask, low) for mask in chosen]
    high_at = [pick(mask, high) for mask in chosen]

    ones = [mask.astype(jnp.float32).astype(jnp.bfloat16) for mask in chosen]
    free = jnp.where(limited, 0.0, 1.0).astype(jnp.bfloat16)
    none = jnp.zeros_like(free)
    right = jnp.concatenate(
        [jnp.concatenate(ones + [none], axis=1)] * 3
        + [jnp.concatenate([none] * LIMITED + [free], axis=1)] * 3,
        axis=0,
    )

    def step(picked, sums):
        others = jnp.exp2(picked[:, LIMITED * queries :])
        mass, slope = [], []
        for k in range(LIMITED):
            points = picked[:, k * queries : (k + 1) * queries]
            m, s = box_terms(low_at[k] - points, high_at[k] - points)
            mass.append(m)
            slope.append(s)
        pair = others * mass[0]
        last_two = pair * mass[1]
        whole = last_two * mass[2]
        return whole, (
            sums[0] + whole,
            sums[1] + (others * mass[1]) * (mass[2] * slope[0]),
            sums[2] + pair * (mass[2] * slope[1]),
            sums[3] + last_two * slope[2],
        )

    def chunk(number, totals):
        sums, products = totals[:-1], totals[-1]
        some = [blocks_ref[number * group + b] for b in range(group)]
        x = unit * jnp.concatenate(
            [
                jnp.concatenate([block[:, width * j : width * (j + 1)] for block in some], axis=1)
                for j in range(dims // 8)
            ],
            axis=0,
        )
        full, slope = box_terms(-x, float(GRID) * unit - x)
        ratio = jnp.concatenate(split(slope / full, 2), axis=0)
        left = jnp.concatenate(split(x, 3) + split(jnp.log(0.5 * full) * LOG2_E, 3), axis=0)
        picked[...] = lax.dot_general(
            left, right, (((0,), (0,)), ((), ())), preferred_element_type=jnp.float32
        )

        def turn(number, sums):
            for at_row in range(0, 128, 16):
                rows = pl.ds(pl.multiple_of(number * 128 + at_row, 16), 16)
                whole, sums = step(picked[rows, :], sums)
                head, tail = split(whole, 2)
                inside[rows, :queries] = head
                inside[rows, queries:] = tail
            return sums

        sums = lax.fori_loop(0, samples // 128, turn, sums)
        products = products + jnp.dot(ratio, inside[...], preferred_element_type=jnp.float32)
        return (*sums, products)

    zero = jnp.zeros((16, queries), jnp.float32)
    totals = (zero,) * (1 + LIMITED) + (jnp.zeros((2 * dims, 2 * queries), jnp.float32),)
    if count == group:
        totals = chunk(0, totals)
    else:
        totals = lax.fori_loop(0, count // group, chunk, totals)
    sums = [jnp.sum(s, axis=0, keepdims=True) for s in totals[:-1]]
    products = totals[-1]
    deriv = products[:dims, :queries] + (products[dims:, :queries] + products[:dims, queries:])
    deriv = jnp.where(limited, 0.0, deriv * (SLOPE / 4))
    for mask, s in zip(chosen, sums[1:]):
        deriv = jnp.where(mask, s * (SLOPE / 4), deriv)
    out_ref[:dims, :] = deriv
    out_ref[dims:, :] = jnp.broadcast_to(sums[0] * 0.125, (8, queries))


def finish_kernel(sample_total, query_total, *refs):
    part_refs, (target_ref, log_ref, share_ref) = refs[:-3], refs[-3:]
    whole = tree_sum([ref[...] for ref in part_refs])
    dims, queries = whole.shape[0] - 8, whole.shape[1]
    smoothing = 1.0 / TABLE_ROWS
    estimate = whole[dims : dims + 1] / sample_total
    log_est = jnp.log(estimate + smoothing)
    log_ref[...] = log_est
    weight = 2.0 * (log_est - target_ref[...]) / (query_total * (estimate + smoothing))
    terms = whole[:dims] * (weight / sample_total)
    terms = jnp.concatenate([terms, jnp.zeros((queries - dims, queries), jnp.float32)], axis=0)
    share = jnp.sum(terms.T, axis=0, keepdims=True)
    for peer in range(share_ref.shape[0]):
        share_ref[peer] = share


def last_kernel(shares_ref, held_log_ref, log_ref, gradient_ref):
    total = tree_sum([shares_ref[peer] for peer in range(shares_ref.shape[0])])
    log_ref[...] = held_log_ref[0]
    gradient_ref[...] = total[0, : gradient_ref.shape[0]]


def everyone(x, axis):
    size = lax.axis_size(axis)
    return [x] + [
        lax.ppermute(x, axis, [(i, i ^ offset) for i in range(size)]) for offset in range(1, size)
    ]


def call(kernel, args, outs, scratch=(), placed=pltpu.VMEM):
    single = len(outs) == 1
    return pl.pallas_call(
        kernel,
        out_shape=outs[0] if single else outs,
        in_specs=[pl.BlockSpec(memory_space=placed)] * len(args),
        out_specs=pl.BlockSpec(memory_space=pltpu.VMEM)
        if single
        else [pl.BlockSpec(memory_space=pltpu.VMEM)] * len(outs),
        scratch_shapes=list(scratch),
        compiler_params=pltpu.CompilerParams(vmem_limit_bytes=32 << 20),
    )(*args)


def shape(*sizes):
    return jax.ShapeDtypeStruct(sizes, jnp.float32)


def on_device(samples, bounds, spread, counts):
    dims, width = samples.shape
    queries = bounds.shape[2]
    blocks, copies = lax.axis_size("blk"), lax.axis_size("grp")
    sample_total = width * blocks * copies
    query_total = queries * blocks

    counts_vector = pltpu.VMEM((1, queries), jnp.int32)
    packed, bounds, spread, target = call(
        load_kernel,
        [
            pltpu.with_memory_space_constraint(array, pltpu.HBM)
            for array in (samples, bounds, spread.reshape(1, dims), counts.reshape(1, queries))
        ],
        [
            pltpu.VMEM((blocks, 8, dims * width // 8), jnp.float32),
            pltpu.VMEM(bounds.shape, bounds.dtype),
            pltpu.VMEM((1, dims), jnp.float32),
            pltpu.VMEM((1, queries), jnp.float32),
        ],
        [pltpu.VMEM((dims, width), jnp.float32), counts_vector, pltpu.SemaphoreType.DMA((4,))],
        placed=pl.ANY,
    )
    turned = [1] + [0] * (blocks - 1)
    groups = [
        [b * copies + (c + turned[b]) % copies for b in reversed(range(blocks))]
        for c in range(copies)
    ]
    exchange = lambda x: lax.all_to_all(x, ("blk", "grp"), 0, 0, axis_index_groups=groups)
    gathered = exchange(packed)
    rows = min(width * blocks, 512)
    part = call(
        functools.partial(terms_kernel, width),
        [gathered, bounds, spread],
        [shape(dims + 8, queries)],
        [
            pltpu.VMEM((rows, (LIMITED + 1) * queries), jnp.float32),
            pltpu.VMEM((rows, 2 * queries), jnp.bfloat16),
        ],
    )
    log_est, share = call(
        functools.partial(finish_kernel, sample_total, query_total),
        everyone(part, "grp") + [target],
        [shape(1, queries), shape(blocks, 1, queries)],
    )
    shares = exchange(share)
    return call(last_kernel, [shares, log_est], [shape(queries), shape(dims)])


def solution(mesh):
    return jax.shard_map(
        on_device,
        mesh=mesh,
        in_specs=(P(None, ("blk", "grp")), P(None, None, "blk"), P(), P("blk")),
        out_specs=(P("blk"), P()),
        check_vma=False,
    )
```

```python
import functools

import jax
import jax.numpy as jnp
from jax import lax
from jax.experimental import pallas as pl
from jax.experimental.pallas import tpu as pltpu
from jax.sharding import PartitionSpec as P

TABLE_ROWS = 1048576
GRID = 256
LIMITED = 3

ROOT_HALF = 0.7071067811865476
LOG2_E = 1.4426950408889634
SLOPE = 0.5641895835477563


def box_terms(low, high):
    low_bell = jnp.exp2((low * low) * -LOG2_E)
    high_bell = jnp.exp2((high * high) * -LOG2_E)
    return lax.erf(high) - lax.erf(low), low * low_bell - high * high_bell


def split(x, parts):
    out = []
    for _ in range(parts - 1):
        head = x.astype(jnp.bfloat16)
        out.append(head)
        x = x - head.astype(jnp.float32)
    return out + [x.astype(jnp.bfloat16)]


def tree_sum(parts):
    while len(parts) > 1:
        parts = [a + b for a, b in zip(parts[::2], parts[1::2])]
    return parts[0]


def load_kernel(
    x_ref, bounds_ref, spread_ref, counts_ref,
    out_ref, held_bounds, held_spread, target_ref,
    held_x, held_counts, sems,
):
    sources = (x_ref, bounds_ref, spread_ref, counts_ref)
    targets = (held_x, held_bounds, held_spread, held_counts)
    copies = [
        pltpu.make_async_copy(source, target, sems.at[i])
        for i, (source, target) in enumerate(zip(sources, targets))
    ]
    for copy in copies:
        copy.start()
    copies[0].wait()
    rows = held_x.shape[0]
    packed = jnp.concatenate([held_x[8 * j : 8 * (j + 1), :] for j in range(rows // 8)], axis=1)
    for peer in range(out_ref.shape[0]):
        out_ref[peer] = packed
    for copy in copies[1:]:
        copy.wait()
    smoothing = 1.0 / TABLE_ROWS
    target_ref[...] = jnp.log(held_counts[...].astype(jnp.float32) / TABLE_ROWS + smoothing)


def terms_kernel(width, blocks_ref, bounds_ref, spread_ref, out_ref):
    dims, queries = bounds_ref.shape[1:]
    count = blocks_ref.shape[0]
    per_piece = 128 // width
    group = min(count, 4 * per_piece)

    low, high = bounds_ref[0], bounds_ref[1]
    limited = (high - low) != GRID
    at = lax.broadcasted_iota(jnp.int32, (dims, queries), 0)
    first = jnp.min(jnp.where(limited, at, dims), axis=0, keepdims=True)
    last = jnp.max(jnp.where(limited, at, -1), axis=0, keepdims=True)
    chosen = [at == first, limited & (at > first) & (at < last), at == last]

    row = lax.broadcasted_iota(jnp.int32, (dims, dims), 0)
    column = lax.broadcasted_iota(jnp.int32, (dims, dims), 1)
    spread = jnp.sum(jnp.where(row == column, spread_ref[...], 0.0), axis=1, keepdims=True)
    unit = ROOT_HALF / spread

    pick = lambda mask, values: jnp.sum(jnp.where(mask, values, 0.0), axis=0, keepdims=True)
    low = low.astype(jnp.float32) * unit
    high = high.astype(jnp.float32) * unit
    low_at = [pick(mask, low) for mask in chosen]
    high_at = [pick(mask, high) for mask in chosen]

    ones = [mask.astype(jnp.float32).astype(jnp.bfloat16) for mask in chosen]
    free = jnp.where(limited, 0.0, 1.0).astype(jnp.bfloat16)
    none = jnp.zeros_like(free)
    right = jnp.concatenate(
        [jnp.concatenate(ones + [none], axis=1)] * 3
        + [jnp.concatenate([none] * LIMITED + [free], axis=1)] * 3,
        axis=0,
    )

    def step(picked, sums):
        others = jnp.exp2(picked[:, LIMITED * queries :])
        mass, slope = [], []
        for k in range(LIMITED):
            points = picked[:, k * queries : (k + 1) * queries]
            m, s = box_terms(low_at[k] - points, high_at[k] - points)
            mass.append(m)
            slope.append(s)
        pair = others * mass[0]
        last_two = pair * mass[1]
        whole = last_two * mass[2]
        return whole, (
            sums[0] + whole,
            sums[1] + (others * mass[1]) * (mass[2] * slope[0]),
            sums[2] + pair * (mass[2] * slope[1]),
            sums[3] + last_two * slope[2],
        )

    def piece(start, totals):
        sums, products = totals[:-1], totals[-1]
        some = [blocks_ref[start + b] for b in range(per_piece)]
        x = unit * jnp.concatenate(
            [
                jnp.concatenate([block[:, width * j : width * (j + 1)] for block in some], axis=1)
                for j in range(dims // 8)
            ],
            axis=0,
        )
        full, slope = box_terms(-x, float(GRID) * unit - x)
        ratio = jnp.concatenate(split(slope / full, 2), axis=0)
        left = jnp.concatenate(split(x, 3) + split(jnp.log(0.5 * full) * LOG2_E, 3), axis=0)
        picked = lax.dot_general(
            left, right, (((0,), (0,)), ((), ())), preferred_element_type=jnp.float32
        )
        inside = []
        for at_row in range(0, per_piece * width, 16):
            whole, sums = step(picked[at_row : at_row + 16], sums)
            inside.append(jnp.concatenate(split(whole, 2), axis=1))
        inside = jnp.concatenate(inside, axis=0)
        products = products + jnp.dot(ratio, inside, preferred_element_type=jnp.float32)
        return (*sums, products)

    def pieces(number, totals):
        for start in range(0, group, per_piece):
            totals = piece(number * group + start, totals)
        return totals

    zero = jnp.zeros((16, queries), jnp.float32)
    totals = (zero,) * (1 + LIMITED) + (jnp.zeros((2 * dims, 2 * queries), jnp.float32),)
    if count == group:
        totals = pieces(0, totals)
    else:
        totals = lax.fori_loop(0, count // group, pieces, totals)
    sums = [jnp.sum(s, axis=0, keepdims=True) for s in totals[:-1]]
    products = totals[-1]
    deriv = products[:dims, :queries] + (products[dims:, :queries] + products[:dims, queries:])
    deriv = jnp.where(limited, 0.0, deriv * (SLOPE / 4))
    for mask, s in zip(chosen, sums[1:]):
        deriv = jnp.where(mask, s * (SLOPE / 4), deriv)
    out_ref[:dims, :] = deriv
    out_ref[dims:, :] = jnp.broadcast_to(sums[0] * 0.125, (8, queries))


def finish_kernel(sample_total, query_total, *refs):
    part_refs, (target_ref, log_ref, share_ref) = refs[:-3], refs[-3:]
    whole = tree_sum([ref[...] for ref in part_refs])
    dims, queries = whole.shape[0] - 8, whole.shape[1]
    smoothing = 1.0 / TABLE_ROWS
    estimate = whole[dims : dims + 1] / sample_total
    log_est = jnp.log(estimate + smoothing)
    log_ref[...] = log_est
    weight = 2.0 * (log_est - target_ref[...]) / (query_total * (estimate + smoothing))
    terms = whole[:dims] * (weight / sample_total)
    terms = jnp.concatenate([terms, jnp.zeros((queries - dims, queries), jnp.float32)], axis=0)
    share = jnp.sum(terms.T, axis=0, keepdims=True)
    for peer in range(share_ref.shape[0]):
        share_ref[peer] = share


def last_kernel(shares_ref, held_log_ref, log_ref, gradient_ref):
    total = tree_sum([shares_ref[peer] for peer in range(shares_ref.shape[0])])
    log_ref[...] = held_log_ref[0]
    gradient_ref[...] = total[0, : gradient_ref.shape[0]]


def everyone(x, axis):
    size = lax.axis_size(axis)
    return [x] + [
        lax.ppermute(x, axis, [(i, i ^ offset) for i in range(size)]) for offset in range(1, size)
    ]


def call(kernel, args, outs, scratch=(), placed=pltpu.VMEM):
    single = len(outs) == 1
    return pl.pallas_call(
        kernel,
        out_shape=outs[0] if single else outs,
        in_specs=[pl.BlockSpec(memory_space=placed)] * len(args),
        out_specs=pl.BlockSpec(memory_space=pltpu.VMEM)
        if single
        else [pl.BlockSpec(memory_space=pltpu.VMEM)] * len(outs),
        scratch_shapes=list(scratch),
        compiler_params=pltpu.CompilerParams(vmem_limit_bytes=32 << 20),
    )(*args)


def shape(*sizes):
    return jax.ShapeDtypeStruct(sizes, jnp.float32)


def on_device(samples, bounds, spread, counts):
    dims, width = samples.shape
    queries = bounds.shape[2]
    blocks, copies = lax.axis_size("blk"), lax.axis_size("grp")
    sample_total = width * blocks * copies
    query_total = queries * blocks

    counts_vector = pltpu.VMEM((1, queries), jnp.int32)
    packed, bounds, spread, target = call(
        load_kernel,
        [
            pltpu.with_memory_space_constraint(array, pltpu.HBM)
            for array in (samples, bounds, spread.reshape(1, dims), counts.reshape(1, queries))
        ],
        [
            pltpu.VMEM((blocks, 8, dims * width // 8), jnp.float32),
            pltpu.VMEM(bounds.shape, bounds.dtype),
            pltpu.VMEM((1, dims), jnp.float32),
            pltpu.VMEM((1, queries), jnp.float32),
        ],
        [pltpu.VMEM((dims, width), jnp.float32), counts_vector, pltpu.SemaphoreType.DMA((4,))],
        placed=pl.ANY,
    )
    def exchange(x, turned):
        groups = [
            [b * copies + (c + (b in turned)) % copies for b in falling] for c in range(copies)
        ]
        return lax.all_to_all(x, ("blk", "grp"), 0, 0, axis_index_groups=groups)

    falling = list(reversed(range(blocks)))
    far = blocks // 5
    gathered = exchange(packed, [0] + falling[1 : 1 + far])
    part = call(
        functools.partial(terms_kernel, width),
        [gathered, bounds, spread],
        [shape(dims + 8, queries)],
    )
    log_est, share = call(
        functools.partial(finish_kernel, sample_total, query_total),
        everyone(part, "grp") + [target],
        [shape(1, queries), shape(blocks, 1, queries)],
    )
    shares = exchange(share, [0])
    return call(last_kernel, [shares, log_est], [shape(queries), shape(dims)])


def solution(mesh):
    return jax.shard_map(
        on_device,
        mesh=mesh,
        in_specs=(P(None, ("blk", "grp")), P(None, None, "blk"), P(), P("blk")),
        out_specs=(P("blk"), P()),
        check_vma=False,
    )
```

```python
import functools

import jax
import jax.numpy as jnp
from jax import lax
from jax.experimental import pallas as pl
from jax.experimental.pallas import tpu as pltpu
from jax.sharding import PartitionSpec as P

TABLE_ROWS = 1048576
GRID = 256
LIMITED = 3

ROOT_HALF = 0.7071067811865476
LOG2_E = 1.4426950408889634
SLOPE = 0.5641895835477563


def box_terms(low, high):
    low_bell = jnp.exp2((low * low) * -LOG2_E)
    high_bell = jnp.exp2((high * high) * -LOG2_E)
    return lax.erf(high) - lax.erf(low), low * low_bell - high * high_bell


def split(x, parts):
    out = []
    for _ in range(parts - 1):
        head = x.astype(jnp.bfloat16)
        out.append(head)
        x = x - head.astype(jnp.float32)
    return out + [x.astype(jnp.bfloat16)]


def tree_sum(parts):
    while len(parts) > 1:
        parts = [a + b for a, b in zip(parts[::2], parts[1::2])]
    return parts[0]


def load_kernel(
    x_ref, bounds_ref, spread_ref, counts_ref,
    out_ref, held_bounds, held_spread, target_ref,
    held_x, held_counts, sems,
):
    sources = (x_ref, bounds_ref, spread_ref, counts_ref)
    targets = (held_x, held_bounds, held_spread, held_counts)
    copies = [
        pltpu.make_async_copy(source, target, sems.at[i])
        for i, (source, target) in enumerate(zip(sources, targets))
    ]
    for copy in copies:
        copy.start()
    copies[0].wait()
    rows = held_x.shape[0]
    packed = jnp.concatenate([held_x[8 * j : 8 * (j + 1), :] for j in range(rows // 8)], axis=1)
    for peer in range(out_ref.shape[0]):
        out_ref[peer] = packed
    for copy in copies[1:]:
        copy.wait()
    smoothing = 1.0 / TABLE_ROWS
    target_ref[...] = jnp.log(held_counts[...].astype(jnp.float32) / TABLE_ROWS + smoothing)


def terms_kernel(width, blocks_ref, bounds_ref, spread_ref, out_ref):
    dims, queries = bounds_ref.shape[1:]
    count = blocks_ref.shape[0]
    per_piece = 128 // width
    group = min(count, 4 * per_piece)

    low, high = bounds_ref[0], bounds_ref[1]
    limited = (high - low) != GRID
    at = lax.broadcasted_iota(jnp.int32, (dims, queries), 0)
    first = jnp.min(jnp.where(limited, at, dims), axis=0, keepdims=True)
    last = jnp.max(jnp.where(limited, at, -1), axis=0, keepdims=True)
    chosen = [at == first, limited & (at > first) & (at < last), at == last]

    row = lax.broadcasted_iota(jnp.int32, (dims, dims), 0)
    column = lax.broadcasted_iota(jnp.int32, (dims, dims), 1)
    spread = jnp.sum(jnp.where(row == column, spread_ref[...], 0.0), axis=1, keepdims=True)
    unit = ROOT_HALF / spread

    pick = lambda mask, values: jnp.sum(jnp.where(mask, values, 0.0), axis=0, keepdims=True)
    low = low.astype(jnp.float32) * unit
    high = high.astype(jnp.float32) * unit
    low_at = [pick(mask, low) for mask in chosen]
    high_at = [pick(mask, high) for mask in chosen]

    ones = [mask.astype(jnp.float32).astype(jnp.bfloat16) for mask in chosen]
    free = jnp.where(limited, 0.0, 1.0).astype(jnp.bfloat16)
    none = jnp.zeros_like(free)
    right = jnp.concatenate(
        [jnp.concatenate(ones + [none], axis=1)] * 3
        + [jnp.concatenate([none] * LIMITED + [free], axis=1)] * 3,
        axis=0,
    )

    def step(picked, sums):
        others = jnp.exp2(picked[:, LIMITED * queries :])
        mass, slope = [], []
        for k in range(LIMITED):
            points = picked[:, k * queries : (k + 1) * queries]
            m, s = box_terms(low_at[k] - points, high_at[k] - points)
            mass.append(m)
            slope.append(s)
        pair = others * mass[0]
        last_two = pair * mass[1]
        whole = last_two * mass[2]
        return whole, (
            sums[0] + whole,
            sums[1] + (others * mass[1]) * (mass[2] * slope[0]),
            sums[2] + pair * (mass[2] * slope[1]),
            sums[3] + last_two * slope[2],
        )

    def piece(start, totals):
        sums, products = totals[:-1], totals[-1]
        some = [blocks_ref[start + b] for b in range(per_piece)]
        x = unit * jnp.concatenate(
            [
                jnp.concatenate([block[:, width * j : width * (j + 1)] for block in some], axis=1)
                for j in range(dims // 8)
            ],
            axis=0,
        )
        full, slope = box_terms(-x, float(GRID) * unit - x)
        ratio = jnp.concatenate(split(slope / full, 2), axis=0)
        left = jnp.concatenate(split(x, 3) + split(jnp.log(0.5 * full) * LOG2_E, 3), axis=0)
        picked = lax.dot_general(
            left, right, (((0,), (0,)), ((), ())), preferred_element_type=jnp.float32
        )
        inside = []
        for at_row in range(0, per_piece * width, 16):
            whole, sums = step(picked[at_row : at_row + 16], sums)
            inside.append(jnp.concatenate(split(whole, 2), axis=1))
        inside = jnp.concatenate(inside, axis=0)
        products = products + jnp.dot(ratio, inside, preferred_element_type=jnp.float32)
        return (*sums, products)

    def pieces(number, totals):
        for start in range(0, group, per_piece):
            totals = piece(number * group + start, totals)
        return totals

    zero = jnp.zeros((16, queries), jnp.float32)
    totals = (zero,) * (1 + LIMITED) + (jnp.zeros((2 * dims, 2 * queries), jnp.float32),)
    if count == group:
        totals = pieces(0, totals)
    else:
        totals = lax.fori_loop(0, count // group, pieces, totals)
    sums = [jnp.sum(s, axis=0, keepdims=True) for s in totals[:-1]]
    products = totals[-1]
    deriv = products[:dims, :queries] + (products[dims:, :queries] + products[:dims, queries:])
    deriv = jnp.where(limited, 0.0, deriv * (SLOPE / 4))
    for mask, s in zip(chosen, sums[1:]):
        deriv = jnp.where(mask, s * (SLOPE / 4), deriv)
    out_ref[:dims, :] = deriv
    out_ref[dims:, :] = jnp.broadcast_to(sums[0] * 0.125, (8, queries))


def finish_kernel(sample_total, query_total, *refs):
    part_refs, (target_ref, log_ref, share_ref) = refs[:-3], refs[-3:]
    whole = tree_sum([ref[...] for ref in part_refs])
    dims, queries = whole.shape[0] - 8, whole.shape[1]
    smoothing = 1.0 / TABLE_ROWS
    estimate = whole[dims : dims + 1] / sample_total
    log_est = jnp.log(estimate + smoothing)
    log_ref[...] = log_est
    weight = 2.0 * (log_est - target_ref[...]) / (query_total * (estimate + smoothing))
    terms = whole[:dims] * (weight / sample_total)
    terms = jnp.concatenate([terms, jnp.zeros((queries - dims, queries), jnp.float32)], axis=0)
    share = jnp.sum(terms.T, axis=0, keepdims=True)
    for peer in range(share_ref.shape[0]):
        share_ref[peer] = share


def last_kernel(shares_ref, held_log_ref, log_ref, gradient_ref):
    total = tree_sum([shares_ref[peer] for peer in range(shares_ref.shape[0])])
    log_ref[...] = held_log_ref[0]
    gradient_ref[...] = total[0, : gradient_ref.shape[0]]


def everyone(x, axis):
    size = lax.axis_size(axis)
    return [x] + [
        lax.ppermute(x, axis, [(i, i ^ offset) for i in range(size)]) for offset in range(1, size)
    ]


def call(kernel, args, outs, scratch=(), placed=pltpu.VMEM):
    single = len(outs) == 1
    return pl.pallas_call(
        kernel,
        out_shape=outs[0] if single else outs,
        in_specs=[pl.BlockSpec(memory_space=placed)] * len(args),
        out_specs=pl.BlockSpec(memory_space=pltpu.VMEM)
        if single
        else [pl.BlockSpec(memory_space=pltpu.VMEM)] * len(outs),
        scratch_shapes=list(scratch),
        compiler_params=pltpu.CompilerParams(vmem_limit_bytes=32 << 20),
    )(*args)


def shape(*sizes):
    return jax.ShapeDtypeStruct(sizes, jnp.float32)


def on_device(samples, bounds, spread, counts):
    dims, width = samples.shape
    queries = bounds.shape[2]
    blocks, copies = lax.axis_size("blk"), lax.axis_size("grp")
    sample_total = width * blocks * copies
    query_total = queries * blocks

    counts_vector = pltpu.VMEM((1, queries), jnp.int32)
    packed, bounds, spread, target = call(
        load_kernel,
        [
            pltpu.with_memory_space_constraint(array, pltpu.HBM)
            for array in (samples, bounds, spread.reshape(1, dims), counts.reshape(1, queries))
        ],
        [
            pltpu.VMEM((blocks, 8, dims * width // 8), jnp.float32),
            pltpu.VMEM(bounds.shape, bounds.dtype),
            pltpu.VMEM((1, dims), jnp.float32),
            pltpu.VMEM((1, queries), jnp.float32),
        ],
        [pltpu.VMEM((dims, width), jnp.float32), counts_vector, pltpu.SemaphoreType.DMA((4,))],
        placed=pl.ANY,
    )
    def exchange(x, turned, order):
        groups = [
            [b * copies + (c + (b in turned)) % copies for b in order] for c in range(copies)
        ]
        return lax.all_to_all(x, ("blk", "grp"), 0, 0, axis_index_groups=groups)

    falling = list(reversed(range(blocks)))
    far = blocks // 5
    half = blocks // 2
    far_between = falling[far:half] + falling[:far][::-1] + falling[half:]
    gathered = exchange(packed, [0] + falling[1 : 1 + far], far_between)
    part = call(
        functools.partial(terms_kernel, width),
        [gathered, bounds, spread],
        [shape(dims + 8, queries)],
    )
    log_est, share = call(
        functools.partial(finish_kernel, sample_total, query_total),
        everyone(part, "grp") + [target],
        [shape(1, queries), shape(blocks, 1, queries)],
    )
    shares = exchange(share, [0], falling)
    return call(last_kernel, [shares, log_est], [shape(queries), shape(dims)])


def solution(mesh):
    return jax.shard_map(
        on_device,
        mesh=mesh,
        in_specs=(P(None, ("blk", "grp")), P(None, None, "blk"), P(), P("blk")),
        out_specs=(P("blk"), P()),
        check_vma=False,
    )
```

```python
import functools

import jax
import jax.numpy as jnp
from jax import lax
from jax.experimental import pallas as pl
from jax.experimental.pallas import tpu as pltpu
from jax.sharding import PartitionSpec as P

TABLE_ROWS = 1048576
GRID = 256
LIMITED = 3

ROOT_HALF = 0.7071067811865476
LOG2_E = 1.4426950408889634
SLOPE = 0.5641895835477563


def box_terms(low, high):
    low_bell = jnp.exp2((low * low) * -LOG2_E)
    high_bell = jnp.exp2((high * high) * -LOG2_E)
    return lax.erf(high) - lax.erf(low), low * low_bell - high * high_bell


def split(x, parts):
    out = []
    for _ in range(parts - 1):
        head = x.astype(jnp.bfloat16)
        out.append(head)
        x = x - head.astype(jnp.float32)
    return out + [x.astype(jnp.bfloat16)]


def tree_sum(parts):
    while len(parts) > 1:
        parts = [a + b for a, b in zip(parts[::2], parts[1::2])]
    return parts[0]


def load_kernel(
    x_ref, bounds_ref, spread_ref, counts_ref,
    out_ref, held_bounds, held_spread, held_counts,
    held_x, sems,
):
    sources = (x_ref, bounds_ref, spread_ref, counts_ref)
    targets = (held_x, held_bounds, held_spread, held_counts)
    copies = [
        pltpu.make_async_copy(source, target, sems.at[i])
        for i, (source, target) in enumerate(zip(sources, targets))
    ]
    for copy in copies:
        copy.start()
    copies[0].wait()
    rows = held_x.shape[0]
    packed = jnp.concatenate([held_x[8 * j : 8 * (j + 1), :] for j in range(rows // 8)], axis=1)
    for peer in range(out_ref.shape[0]):
        out_ref[peer] = packed
    for copy in copies[1:]:
        copy.wait()


def terms_kernel(width, blocks_ref, bounds_ref, spread_ref, out_ref):
    dims, queries = bounds_ref.shape[1:]
    count = blocks_ref.shape[0]
    per_piece = 128 // width
    group = min(count, 4 * per_piece)

    low, high = bounds_ref[0], bounds_ref[1]
    limited = (high - low) != GRID
    at = lax.broadcasted_iota(jnp.int32, (dims, queries), 0)
    first = jnp.min(jnp.where(limited, at, dims), axis=0, keepdims=True)
    last = jnp.max(jnp.where(limited, at, -1), axis=0, keepdims=True)
    chosen = [at == first, limited & (at > first) & (at < last), at == last]

    row = lax.broadcasted_iota(jnp.int32, (dims, dims), 0)
    column = lax.broadcasted_iota(jnp.int32, (dims, dims), 1)
    spread = jnp.sum(jnp.where(row == column, spread_ref[...], 0.0), axis=1, keepdims=True)
    unit = ROOT_HALF / spread

    pick = lambda mask, values: jnp.sum(jnp.where(mask, values, 0.0), axis=0, keepdims=True)
    low = low.astype(jnp.float32) * unit
    high = high.astype(jnp.float32) * unit
    low_at = [pick(mask, low) for mask in chosen]
    high_at = [pick(mask, high) for mask in chosen]

    ones = [mask.astype(jnp.float32).astype(jnp.bfloat16) for mask in chosen]
    free = jnp.where(limited, 0.0, 1.0).astype(jnp.bfloat16)
    none = jnp.zeros_like(free)
    right = jnp.concatenate(
        [jnp.concatenate(ones + [none], axis=1)] * 3
        + [jnp.concatenate([none] * LIMITED + [free], axis=1)] * 3,
        axis=0,
    )

    ones = jnp.ones((16, per_piece * width), jnp.bfloat16)

    def step(picked, sums):
        others = jnp.exp2(picked[:, LIMITED * queries :])
        mass, slope = [], []
        for k in range(LIMITED):
            points = picked[:, k * queries : (k + 1) * queries]
            m, s = box_terms(low_at[k] - points, high_at[k] - points)
            mass.append(m)
            slope.append(s)
        pair = others * mass[0]
        last_two = pair * mass[1]
        whole = last_two * mass[2]
        return whole, (
            sums[0] + (others * mass[1]) * (mass[2] * slope[0]),
            sums[1] + pair * (mass[2] * slope[1]),
            sums[2] + last_two * slope[2],
        )

    def piece(start, totals):
        sums, products = totals[:-1], totals[-1]
        some = [blocks_ref[start + b] for b in range(per_piece)]
        x = unit * jnp.concatenate(
            [
                jnp.concatenate([block[:, width * j : width * (j + 1)] for block in some], axis=1)
                for j in range(dims // 8)
            ],
            axis=0,
        )
        rest = float(GRID) * unit - x
        full = lax.erf(rest) + lax.erf(x)
        slope = x * jnp.exp2((x * x) * -LOG2_E) + rest * jnp.exp2((rest * rest) * -LOG2_E)
        ratio = jnp.concatenate(split(-slope / full, 2) + [ones], axis=0)
        left = jnp.concatenate(split(x, 3) + split(jnp.log(0.5 * full) * LOG2_E, 3), axis=0)
        picked = lax.dot_general(
            left, right, (((0,), (0,)), ((), ())), preferred_element_type=jnp.float32
        )
        inside = []
        for at_row in range(0, per_piece * width, 16):
            whole, sums = step(picked[at_row : at_row + 16], sums)
            inside.append(jnp.concatenate(split(whole, 2), axis=1))
        inside = jnp.concatenate(inside, axis=0)
        products = products + jnp.dot(ratio, inside, preferred_element_type=jnp.float32)
        return (*sums, products)

    def pieces(number, totals):
        for start in range(0, group, per_piece):
            totals = piece(number * group + start, totals)
        return totals

    zero = jnp.zeros((16, queries), jnp.float32)
    totals = (zero,) * LIMITED + (jnp.zeros((2 * dims + 16, 2 * queries), jnp.float32),)
    if count == group:
        totals = pieces(0, totals)
    else:
        totals = lax.fori_loop(0, count // group, pieces, totals)
    sums = [jnp.sum(s, axis=0, keepdims=True) for s in totals[:-1]]
    products = totals[-1]
    deriv = products[dims : 2 * dims, :queries] + products[:dims, queries:]
    deriv = products[:dims, :queries] + deriv
    total = products[2 * dims : 2 * dims + 8, :queries] + products[2 * dims : 2 * dims + 8, queries:]
    deriv = jnp.where(limited, 0.0, deriv * (SLOPE / 4))
    for mask, s in zip(chosen, sums):
        deriv = jnp.where(mask, s * (SLOPE / 4), deriv)
    out_ref[:dims, :] = deriv
    out_ref[dims:, :] = total * 0.125


def finish_kernel(sample_total, query_total, *refs):
    part_refs, (counts_ref, log_ref, share_ref) = refs[:-3], refs[-3:]
    whole = tree_sum([ref[...] for ref in part_refs])
    dims, queries = whole.shape[0] - 8, whole.shape[1]
    smoothing = 1.0 / TABLE_ROWS
    estimate = whole[dims : dims + 1] / sample_total
    log_est = jnp.log(estimate + smoothing)
    log_ref[...] = log_est
    target = jnp.log(counts_ref[...].astype(jnp.float32) / TABLE_ROWS + smoothing)
    weight = 2.0 * (log_est - target) / (query_total * (estimate + smoothing))
    terms = whole[:dims] * (weight / sample_total)
    terms = jnp.concatenate([terms, jnp.zeros((queries - dims, queries), jnp.float32)], axis=0)
    share = jnp.sum(terms.T, axis=0, keepdims=True)
    for peer in range(share_ref.shape[0]):
        share_ref[peer] = share


def last_kernel(shares_ref, held_log_ref, log_ref, gradient_ref):
    total = tree_sum([shares_ref[peer] for peer in range(shares_ref.shape[0])])
    log_ref[...] = held_log_ref[0]
    gradient_ref[...] = total[0, : gradient_ref.shape[0]]


def everyone(x, axis):
    size = lax.axis_size(axis)
    return [x] + [
        lax.ppermute(x, axis, [(i, i ^ offset) for i in range(size)]) for offset in range(1, size)
    ]


def call(kernel, args, outs, scratch=(), placed=pltpu.VMEM):
    single = len(outs) == 1
    return pl.pallas_call(
        kernel,
        out_shape=outs[0] if single else outs,
        in_specs=[pl.BlockSpec(memory_space=placed)] * len(args),
        out_specs=pl.BlockSpec(memory_space=pltpu.VMEM)
        if single
        else [pl.BlockSpec(memory_space=pltpu.VMEM)] * len(outs),
        scratch_shapes=list(scratch),
        compiler_params=pltpu.CompilerParams(vmem_limit_bytes=32 << 20),
    )(*args)


def shape(*sizes):
    return jax.ShapeDtypeStruct(sizes, jnp.float32)


def on_device(samples, bounds, spread, counts):
    dims, width = samples.shape
    queries = bounds.shape[2]
    blocks, copies = lax.axis_size("blk"), lax.axis_size("grp")
    sample_total = width * blocks * copies
    query_total = queries * blocks

    packed, bounds, spread, counts = call(
        load_kernel,
        [
            pltpu.with_memory_space_constraint(array, pltpu.HBM)
            for array in (samples, bounds, spread.reshape(1, dims), counts.reshape(1, queries))
        ],
        [
            pltpu.VMEM((blocks, 8, dims * width // 8), jnp.float32),
            pltpu.VMEM(bounds.shape, bounds.dtype),
            pltpu.VMEM((1, dims), jnp.float32),
            pltpu.VMEM((1, queries), jnp.int32),
        ],
        [pltpu.VMEM((dims, width), jnp.float32), pltpu.SemaphoreType.DMA((4,))],
        placed=pl.ANY,
    )
    turned = [1] + [0] * (blocks - 1)
    groups = [
        [b * copies + (c + turned[b]) % copies for b in reversed(range(blocks))]
        for c in range(copies)
    ]
    exchange = lambda x: lax.all_to_all(x, ("blk", "grp"), 0, 0, axis_index_groups=groups)
    gathered = exchange(packed)
    part = call(
        functools.partial(terms_kernel, width),
        [gathered, bounds, spread],
        [shape(dims + 8, queries)],
    )
    log_est, share = call(
        functools.partial(finish_kernel, sample_total, query_total),
        everyone(part, "grp") + [counts],
        [shape(1, queries), shape(blocks, 1, queries)],
    )
    shares = exchange(share)
    return call(last_kernel, [shares, log_est], [shape(queries), shape(dims)])


def solution(mesh):
    return jax.shard_map(
        on_device,
        mesh=mesh,
        in_specs=(P(None, ("blk", "grp")), P(None, None, "blk"), P(), P("blk")),
        out_specs=(P("blk"), P()),
        check_vma=False,
    )
```

```python
import functools

import jax
import jax.numpy as jnp
from jax import lax
from jax.experimental import pallas as pl
from jax.experimental.pallas import tpu as pltpu
from jax.sharding import PartitionSpec as P

TABLE_ROWS = 1048576
GRID = 256
LIMITED = 3

ROOT_HALF = 0.7071067811865476
LOG2_E = 1.4426950408889634
SLOPE = 0.5641895835477563


def box_terms(low, high):
    low_bell = jnp.exp2((low * low) * -LOG2_E)
    high_bell = jnp.exp2((high * high) * -LOG2_E)
    return lax.erf(high) - lax.erf(low), low * low_bell - high * high_bell


def split(x, parts):
    out = []
    for _ in range(parts - 1):
        head = x.astype(jnp.bfloat16)
        out.append(head)
        x = x - head.astype(jnp.float32)
    return out + [x.astype(jnp.bfloat16)]


def tree_sum(parts):
    while len(parts) > 1:
        parts = [a + b for a, b in zip(parts[::2], parts[1::2])]
    return parts[0]


def load_kernel(
    x_ref, bounds_ref, spread_ref, counts_ref,
    out_ref, held_bounds, held_spread, held_counts,
    held_x, sems,
):
    sources = (x_ref, bounds_ref, spread_ref, counts_ref)
    targets = (held_x, held_bounds, held_spread, held_counts)
    copies = [
        pltpu.make_async_copy(source, target, sems.at[i])
        for i, (source, target) in enumerate(zip(sources, targets))
    ]
    for copy in copies:
        copy.start()
    copies[0].wait()
    rows = held_x.shape[0]
    packed = jnp.concatenate([held_x[8 * j : 8 * (j + 1), :] for j in range(rows // 8)], axis=1)
    for peer in range(out_ref.shape[0]):
        out_ref[peer] = packed
    for copy in copies[1:]:
        copy.wait()


def terms_kernel(width, blocks_ref, bounds_ref, spread_ref, out_ref):
    dims, queries = bounds_ref.shape[1:]
    count = blocks_ref.shape[0]
    per_piece = 128 // width
    group = min(count, 4 * per_piece)

    low, high = bounds_ref[0], bounds_ref[1]
    limited = (high - low) != GRID
    at = lax.broadcasted_iota(jnp.int32, (dims, queries), 0)
    first = jnp.min(jnp.where(limited, at, dims), axis=0, keepdims=True)
    last = jnp.max(jnp.where(limited, at, -1), axis=0, keepdims=True)
    chosen = [at == first, limited & (at > first) & (at < last), at == last]

    row = lax.broadcasted_iota(jnp.int32, (dims, dims), 0)
    column = lax.broadcasted_iota(jnp.int32, (dims, dims), 1)
    spread = jnp.sum(jnp.where(row == column, spread_ref[...], 0.0), axis=1, keepdims=True)
    unit = ROOT_HALF / spread

    pick = lambda mask, values: jnp.sum(jnp.where(mask, values, 0.0), axis=0, keepdims=True)
    low = low.astype(jnp.float32) * unit
    high = high.astype(jnp.float32) * unit
    low_at = [pick(mask, low) for mask in chosen]
    high_at = [pick(mask, high) for mask in chosen]

    ones = [mask.astype(jnp.float32).astype(jnp.bfloat16) for mask in chosen]
    free = jnp.where(limited, 0.0, 1.0).astype(jnp.bfloat16)
    none = jnp.zeros_like(free)
    right = jnp.concatenate(
        [jnp.concatenate(ones + [none], axis=1)] * 3
        + [jnp.concatenate([none] * LIMITED + [free], axis=1)] * 3,
        axis=0,
    )

    ones = jnp.ones((16, per_piece * width), jnp.bfloat16)

    def step(picked, sums):
        others = jnp.exp2(picked[:, LIMITED * queries :])
        mass, slope = [], []
        for k in range(LIMITED):
            points = picked[:, k * queries : (k + 1) * queries]
            m, s = box_terms(low_at[k] - points, high_at[k] - points)
            mass.append(m)
            slope.append(s)
        pair = others * mass[0]
        last_two = pair * mass[1]
        whole = last_two * mass[2]
        return whole, (
            sums[0] + (others * mass[1]) * (mass[2] * slope[0]),
            sums[1] + pair * (mass[2] * slope[1]),
            sums[2] + last_two * slope[2],
        )

    def piece(start, totals):
        sums, products = totals[:-1], totals[-1]
        some = [blocks_ref[start + b] for b in range(per_piece)]
        x = unit * jnp.concatenate(
            [
                jnp.concatenate([block[:, width * j : width * (j + 1)] for block in some], axis=1)
                for j in range(dims // 8)
            ],
            axis=0,
        )
        rest = float(GRID) * unit - x
        full = lax.erf(rest) + lax.erf(x)
        slope = x * jnp.exp2((x * x) * -LOG2_E) + rest * jnp.exp2((rest * rest) * -LOG2_E)
        ratio = jnp.concatenate(split(-slope / full, 2) + [ones], axis=0)
        left = jnp.concatenate(split(x, 3) + split(jnp.log(0.5 * full) * LOG2_E, 3), axis=0)
        picked = lax.dot_general(
            left, right, (((0,), (0,)), ((), ())), preferred_element_type=jnp.float32
        )
        inside = []
        for at_row in range(0, per_piece * width, 16):
            whole, sums = step(picked[at_row : at_row + 16], sums)
            inside.append(jnp.concatenate(split(whole, 2), axis=1))
        inside = jnp.concatenate(inside, axis=0)
        products = products + jnp.dot(ratio, inside, preferred_element_type=jnp.float32)
        return (*sums, products)

    def pieces(number, totals):
        for start in range(0, group, per_piece):
            totals = piece(number * group + start, totals)
        return totals

    zero = jnp.zeros((16, queries), jnp.float32)
    totals = (zero,) * LIMITED + (jnp.zeros((2 * dims + 16, 2 * queries), jnp.float32),)
    if count == group:
        totals = pieces(0, totals)
    else:
        totals = lax.fori_loop(0, count // group, pieces, totals)
    sums = [jnp.sum(s, axis=0, keepdims=True) for s in totals[:-1]]
    products = totals[-1]
    deriv = products[dims : 2 * dims, :queries] + products[:dims, queries:]
    deriv = products[:dims, :queries] + deriv
    total = products[2 * dims : 2 * dims + 8, :queries] + products[2 * dims : 2 * dims + 8, queries:]
    deriv = jnp.where(limited, 0.0, deriv * (SLOPE / 4))
    for mask, s in zip(chosen, sums):
        deriv = jnp.where(mask, s * (SLOPE / 4), deriv)
    out_ref[:dims, :] = deriv
    out_ref[dims:, :] = total * 0.125


def finish_kernel(sample_total, query_total, *refs):
    part_refs, (counts_ref, log_ref, share_ref) = refs[:-3], refs[-3:]
    whole = tree_sum([ref[...] for ref in part_refs])
    dims, queries = whole.shape[0] - 8, whole.shape[1]
    smoothing = 1.0 / TABLE_ROWS
    estimate = whole[dims : dims + 1] / sample_total
    log_est = jnp.log(estimate + smoothing)
    log_ref[...] = log_est
    target = jnp.log(counts_ref[...].astype(jnp.float32) / TABLE_ROWS + smoothing)
    weight = 2.0 * (log_est - target) / (query_total * (estimate + smoothing))
    terms = whole[:dims] * (weight / sample_total)
    terms = jnp.concatenate([terms, jnp.zeros((queries - dims, queries), jnp.float32)], axis=0)
    share = jnp.sum(terms.T, axis=0, keepdims=True)
    for peer in range(share_ref.shape[0]):
        share_ref[peer] = share


def last_kernel(shares_ref, held_log_ref, log_ref, gradient_ref):
    total = tree_sum([shares_ref[peer] for peer in range(shares_ref.shape[0])])
    log_ref[...] = held_log_ref[0]
    gradient_ref[...] = total[0, : gradient_ref.shape[0]]


def everyone(x, axis):
    size = lax.axis_size(axis)
    return [x] + [
        lax.ppermute(x, axis, [(i, i ^ offset) for i in range(size)]) for offset in range(1, size)
    ]


def call(kernel, args, outs, scratch=(), placed=pltpu.VMEM):
    single = len(outs) == 1
    return pl.pallas_call(
        kernel,
        out_shape=outs[0] if single else outs,
        in_specs=[pl.BlockSpec(memory_space=placed)] * len(args),
        out_specs=pl.BlockSpec(memory_space=pltpu.VMEM)
        if single
        else [pl.BlockSpec(memory_space=pltpu.VMEM)] * len(outs),
        scratch_shapes=list(scratch),
        compiler_params=pltpu.CompilerParams(vmem_limit_bytes=32 << 20),
    )(*args)


def shape(*sizes):
    return jax.ShapeDtypeStruct(sizes, jnp.float32)


def on_device(samples, bounds, spread, counts):
    dims, width = samples.shape
    queries = bounds.shape[2]
    blocks, copies = lax.axis_size("blk"), lax.axis_size("grp")
    sample_total = width * blocks * copies
    query_total = queries * blocks

    packed, bounds, spread, counts = call(
        load_kernel,
        [
            pltpu.with_memory_space_constraint(array, pltpu.HBM)
            for array in (samples, bounds, spread.reshape(1, dims), counts.reshape(1, queries))
        ],
        [
            pltpu.VMEM((blocks, 8, dims * width // 8), jnp.float32),
            pltpu.VMEM(bounds.shape, bounds.dtype),
            pltpu.VMEM((1, dims), jnp.float32),
            pltpu.VMEM((1, queries), jnp.int32),
        ],
        [pltpu.VMEM((dims, width), jnp.float32), pltpu.SemaphoreType.DMA((4,))],
        placed=pl.ANY,
    )
    def exchange(x, turned):
        groups = [
            [b * copies + (c + (b in turned)) % copies for b in reversed(range(blocks))]
            for c in range(copies)
        ]
        return lax.all_to_all(x, ("blk", "grp"), 0, 0, axis_index_groups=groups)

    gathered = exchange(packed, [0, blocks - 1])
    part = call(
        functools.partial(terms_kernel, width),
        [gathered, bounds, spread],
        [shape(dims + 8, queries)],
    )
    log_est, share = call(
        functools.partial(finish_kernel, sample_total, query_total),
        everyone(part, "grp") + [counts],
        [shape(1, queries), shape(blocks, 1, queries)],
    )
    shares = exchange(share, [0])
    return call(last_kernel, [shares, log_est], [shape(queries), shape(dims)])


def solution(mesh):
    return jax.shard_map(
        on_device,
        mesh=mesh,
        in_specs=(P(None, ("blk", "grp")), P(None, None, "blk"), P(), P("blk")),
        out_specs=(P("blk"), P()),
        check_vma=False,
    )
```

```python
import functools

import jax
import jax.numpy as jnp
from jax import lax
from jax.experimental import pallas as pl
from jax.experimental.pallas import tpu as pltpu
from jax.sharding import PartitionSpec as P

TABLE_ROWS = 1048576
GRID = 256
LIMITED = 3

ROOT_HALF = 0.7071067811865476
LOG2_E = 1.4426950408889634
SLOPE = 0.5641895835477563


def box_terms(low, high):
    low_bell = jnp.exp2((low * low) * -LOG2_E)
    high_bell = jnp.exp2((high * high) * -LOG2_E)
    return lax.erf(high) - lax.erf(low), low * low_bell - high * high_bell


def split(x, parts):
    out = []
    for _ in range(parts - 1):
        head = x.astype(jnp.bfloat16)
        out.append(head)
        x = x - head.astype(jnp.float32)
    return out + [x.astype(jnp.bfloat16)]


def tree_sum(parts):
    while len(parts) > 1:
        parts = [a + b for a, b in zip(parts[::2], parts[1::2])]
    return parts[0]


def load_kernel(
    x_ref, bounds_ref, spread_ref, counts_ref,
    out_ref, held_bounds, held_spread, held_counts,
    held_x, sems,
):
    sources = (x_ref, bounds_ref, spread_ref, counts_ref)
    targets = (held_x, held_bounds, held_spread, held_counts)
    copies = [
        pltpu.make_async_copy(source, target, sems.at[i])
        for i, (source, target) in enumerate(zip(sources, targets))
    ]
    for copy in copies:
        copy.start()
    copies[0].wait()
    rows = held_x.shape[0]
    packed = jnp.concatenate([held_x[8 * j : 8 * (j + 1), :] for j in range(rows // 8)], axis=1)
    for peer in range(out_ref.shape[0]):
        out_ref[peer] = packed
    for copy in copies[1:]:
        copy.wait()


def terms_kernel(width, begin, count, blocks_ref, bounds_ref, spread_ref, out_ref):
    dims, queries = bounds_ref.shape[1:]
    per_piece = 128 // width
    group = min(count, 4 * per_piece)

    low, high = bounds_ref[0], bounds_ref[1]
    limited = (high - low) != GRID
    at = lax.broadcasted_iota(jnp.int32, (dims, queries), 0)
    first = jnp.min(jnp.where(limited, at, dims), axis=0, keepdims=True)
    last = jnp.max(jnp.where(limited, at, -1), axis=0, keepdims=True)
    chosen = [at == first, limited & (at > first) & (at < last), at == last]

    row = lax.broadcasted_iota(jnp.int32, (dims, dims), 0)
    column = lax.broadcasted_iota(jnp.int32, (dims, dims), 1)
    spread = jnp.sum(jnp.where(row == column, spread_ref[...], 0.0), axis=1, keepdims=True)
    unit = ROOT_HALF / spread

    pick = lambda mask, values: jnp.sum(jnp.where(mask, values, 0.0), axis=0, keepdims=True)
    low = low.astype(jnp.float32) * unit
    high = high.astype(jnp.float32) * unit
    low_at = [pick(mask, low) for mask in chosen]
    high_at = [pick(mask, high) for mask in chosen]

    ones = [mask.astype(jnp.float32).astype(jnp.bfloat16) for mask in chosen]
    free = jnp.where(limited, 0.0, 1.0).astype(jnp.bfloat16)
    none = jnp.zeros_like(free)
    right = jnp.concatenate(
        [jnp.concatenate(ones + [none], axis=1)] * 3
        + [jnp.concatenate([none] * LIMITED + [free], axis=1)] * 3,
        axis=0,
    )

    ones = jnp.ones((16, per_piece * width), jnp.bfloat16)

    def step(picked, sums):
        others = jnp.exp2(picked[:, LIMITED * queries :])
        mass, slope = [], []
        for k in range(LIMITED):
            points = picked[:, k * queries : (k + 1) * queries]
            m, s = box_terms(low_at[k] - points, high_at[k] - points)
            mass.append(m)
            slope.append(s)
        pair = others * mass[0]
        last_two = pair * mass[1]
        whole = last_two * mass[2]
        return whole, (
            sums[0] + (others * mass[1]) * (mass[2] * slope[0]),
            sums[1] + pair * (mass[2] * slope[1]),
            sums[2] + last_two * slope[2],
        )

    def piece(start, totals):
        sums, products = totals[:-1], totals[-1]
        some = [blocks_ref[start + b] for b in range(per_piece)]
        x = unit * jnp.concatenate(
            [
                jnp.concatenate([block[:, width * j : width * (j + 1)] for block in some], axis=1)
                for j in range(dims // 8)
            ],
            axis=0,
        )
        rest = float(GRID) * unit - x
        full = lax.erf(rest) + lax.erf(x)
        slope = x * jnp.exp2((x * x) * -LOG2_E) + rest * jnp.exp2((rest * rest) * -LOG2_E)
        ratio = jnp.concatenate(split(-slope / full, 2) + [ones], axis=0)
        left = jnp.concatenate(split(x, 3) + split(jnp.log(0.5 * full) * LOG2_E, 3), axis=0)
        picked = lax.dot_general(
            left, right, (((0,), (0,)), ((), ())), preferred_element_type=jnp.float32
        )
        inside = []
        for at_row in range(0, per_piece * width, 16):
            whole, sums = step(picked[at_row : at_row + 16], sums)
            inside.append(jnp.concatenate(split(whole, 2), axis=1))
        inside = jnp.concatenate(inside, axis=0)
        products = products + jnp.dot(ratio, inside, preferred_element_type=jnp.float32)
        return (*sums, products)

    def pieces(number, totals):
        for start in range(0, group, per_piece):
            totals = piece(begin + number * group + start, totals)
        return totals

    zero = jnp.zeros((16, queries), jnp.float32)
    totals = (zero,) * LIMITED + (jnp.zeros((2 * dims + 16, 2 * queries), jnp.float32),)
    if count == group:
        totals = pieces(0, totals)
    else:
        totals = lax.fori_loop(0, count // group, pieces, totals)
    sums = [jnp.sum(s, axis=0, keepdims=True) for s in totals[:-1]]
    products = totals[-1]
    deriv = products[dims : 2 * dims, :queries] + products[:dims, queries:]
    deriv = products[:dims, :queries] + deriv
    total = products[2 * dims : 2 * dims + 8, :queries] + products[2 * dims : 2 * dims + 8, queries:]
    deriv = jnp.where(limited, 0.0, deriv * (SLOPE / 4))
    for mask, s in zip(chosen, sums):
        deriv = jnp.where(mask, s * (SLOPE / 4), deriv)
    out_ref[:dims, :] = deriv
    out_ref[dims:, :] = total * 0.125


def finish_kernel(sample_total, query_total, *refs):
    part_refs, (counts_ref, log_ref, share_ref) = refs[:-3], refs[-3:]
    halves = len(part_refs) // 2
    whole = [tree_sum([ref[...] for ref in refs]) for refs in (part_refs[:halves], part_refs[halves:])]
    whole = whole[0] + whole[1]
    dims, queries = whole.shape[0] - 8, whole.shape[1]
    smoothing = 1.0 / TABLE_ROWS
    estimate = whole[dims : dims + 1] / sample_total
    log_est = jnp.log(estimate + smoothing)
    log_ref[...] = log_est
    target = jnp.log(counts_ref[...].astype(jnp.float32) / TABLE_ROWS + smoothing)
    weight = 2.0 * (log_est - target) / (query_total * (estimate + smoothing))
    terms = whole[:dims] * (weight / sample_total)
    terms = jnp.concatenate([terms, jnp.zeros((queries - dims, queries), jnp.float32)], axis=0)
    share = jnp.sum(terms.T, axis=0, keepdims=True)
    for peer in range(share_ref.shape[0]):
        share_ref[peer] = share


def last_kernel(shares_ref, held_log_ref, log_ref, gradient_ref):
    total = tree_sum([shares_ref[peer] for peer in range(shares_ref.shape[0])])
    log_ref[...] = held_log_ref[0]
    gradient_ref[...] = total[0, : gradient_ref.shape[0]]


def everyone(x, axis):
    size = lax.axis_size(axis)
    return [x] + [
        lax.ppermute(x, axis, [(i, i ^ offset) for i in range(size)]) for offset in range(1, size)
    ]


def call(kernel, args, outs, scratch=(), placed=pltpu.VMEM, cost=None):
    single = len(outs) == 1
    return pl.pallas_call(
        kernel,
        out_shape=outs[0] if single else outs,
        in_specs=[pl.BlockSpec(memory_space=placed)] * len(args),
        out_specs=pl.BlockSpec(memory_space=pltpu.VMEM)
        if single
        else [pl.BlockSpec(memory_space=pltpu.VMEM)] * len(outs),
        scratch_shapes=list(scratch),
        cost_estimate=cost,
        compiler_params=pltpu.CompilerParams(vmem_limit_bytes=32 << 20),
    )(*args)


def shape(*sizes):
    return jax.ShapeDtypeStruct(sizes, jnp.float32)


def on_device(samples, bounds, spread, counts):
    dims, width = samples.shape
    queries = bounds.shape[2]
    blocks, copies = lax.axis_size("blk"), lax.axis_size("grp")
    sample_total = width * blocks * copies
    query_total = queries * blocks

    packed, bounds, spread, counts = call(
        load_kernel,
        [
            pltpu.with_memory_space_constraint(array, pltpu.HBM)
            for array in (samples, bounds, spread.reshape(1, dims), counts.reshape(1, queries))
        ],
        [
            pltpu.VMEM((blocks, 8, dims * width // 8), jnp.float32),
            pltpu.VMEM(bounds.shape, bounds.dtype),
            pltpu.VMEM((1, dims), jnp.float32),
            pltpu.VMEM((1, queries), jnp.int32),
        ],
        [pltpu.VMEM((dims, width), jnp.float32), pltpu.SemaphoreType.DMA((4,))],
        placed=pl.ANY,
    )
    turned = [1] + [0] * (blocks - 1)
    groups = [
        [b * copies + (c + turned[b]) % copies for b in reversed(range(blocks))]
        for c in range(copies)
    ]
    exchange = lambda x: lax.all_to_all(x, ("blk", "grp"), 0, 0, axis_index_groups=groups)
    gathered = exchange(packed)
    half = blocks // 2
    elements = LIMITED * half * width * queries

    def terms_of(tiles, begin):
        return call(
            functools.partial(terms_kernel, width, begin, half),
            [tiles, bounds, spread],
            [shape(dims + 8, queries)],
            cost=pl.CostEstimate(
                flops=100 * elements, bytes_accessed=64 * elements, transcendentals=4 * elements
            ),
        )

    tiles = everyone(gathered, "grp")
    parts = everyone(terms_of(gathered, 0), "grp")
    parts += [terms_of(other, half) for other in tiles]
    log_est, share = call(
        functools.partial(finish_kernel, sample_total, query_total),
        parts + [counts],
        [shape(1, queries), shape(blocks, 1, queries)],
    )
    shares = exchange(share)
    return call(last_kernel, [shares, log_est], [shape(queries), shape(dims)])


def solution(mesh):
    return jax.shard_map(
        on_device,
        mesh=mesh,
        in_specs=(P(None, ("blk", "grp")), P(None, None, "blk"), P(), P("blk")),
        out_specs=(P("blk"), P()),
        check_vma=False,
    )
```

```python
import functools

import jax
import jax.numpy as jnp
from jax import lax
from jax.experimental import pallas as pl
from jax.experimental.pallas import tpu as pltpu
from jax.sharding import PartitionSpec as P

TABLE_ROWS = 1048576
GRID = 256
LIMITED = 3

ROOT_HALF = 0.7071067811865476
LOG2_E = 1.4426950408889634
SLOPE = 0.5641895835477563


def box_terms(low, high):
    low_bell = jnp.exp2((low * low) * -LOG2_E)
    high_bell = jnp.exp2((high * high) * -LOG2_E)
    return lax.erf(high) - lax.erf(low), low * low_bell - high * high_bell


def split(x, parts):
    out = []
    for _ in range(parts - 1):
        head = x.astype(jnp.bfloat16)
        out.append(head)
        x = x - head.astype(jnp.float32)
    return out + [x.astype(jnp.bfloat16)]


def tree_sum(parts):
    while len(parts) > 1:
        parts = [a + b for a, b in zip(parts[::2], parts[1::2])]
    return parts[0]


def load_kernel(
    x_ref, bounds_ref, spread_ref, counts_ref,
    out_ref, held_bounds, unit_ref, held_counts,
    held_x, held_spread, sems,
):
    sources = (x_ref, bounds_ref, spread_ref, counts_ref)
    targets = (held_x, held_bounds, held_spread, held_counts)
    copies = [
        pltpu.make_async_copy(source, target, sems.at[i])
        for i, (source, target) in enumerate(zip(sources, targets))
    ]
    for copy in copies:
        copy.start()
    copies[0].wait()
    rows = held_x.shape[0]
    packed = jnp.concatenate([held_x[8 * j : 8 * (j + 1), :] for j in range(rows // 8)], axis=1)
    for peer in range(out_ref.shape[0]):
        out_ref[peer] = packed
    for copy in copies[1:]:
        copy.wait()
    dims = held_spread.shape[1]
    row = lax.broadcasted_iota(jnp.int32, (dims, dims), 0)
    column = lax.broadcasted_iota(jnp.int32, (dims, dims), 1)
    unit = jnp.where(row == column, ROOT_HALF / held_spread[...], 0.0)
    unit_ref[...] = jnp.broadcast_to(jnp.sum(unit, axis=1, keepdims=True), unit_ref.shape)


def terms_kernel(width, blocks_ref, bounds_ref, unit_ref, out_ref):
    dims, queries = bounds_ref.shape[1:]
    count = blocks_ref.shape[0]
    per_piece = 128 // width
    group = min(count, 4 * per_piece)

    low, high = bounds_ref[0], bounds_ref[1]
    limited = (high - low) != GRID
    at = lax.broadcasted_iota(jnp.int32, (dims, queries), 0)
    first = jnp.min(jnp.where(limited, at, dims), axis=0, keepdims=True)
    last = jnp.max(jnp.where(limited, at, -1), axis=0, keepdims=True)
    chosen = [at == first, limited & (at > first) & (at < last), at == last]

    unit = unit_ref[...]

    pick = lambda mask, values: jnp.sum(jnp.where(mask, values, 0.0), axis=0, keepdims=True)
    low = low.astype(jnp.float32) * unit
    high = high.astype(jnp.float32) * unit
    low_at = [pick(mask, low) for mask in chosen]
    high_at = [pick(mask, high) for mask in chosen]

    ones = [mask.astype(jnp.float32).astype(jnp.bfloat16) for mask in chosen]
    free = jnp.where(limited, 0.0, 1.0).astype(jnp.bfloat16)
    none = jnp.zeros_like(free)
    right = jnp.concatenate(
        [jnp.concatenate(ones + [none], axis=1)] * 3
        + [jnp.concatenate([none] * LIMITED + [free], axis=1)] * 3,
        axis=0,
    )

    ones = jnp.ones((16, per_piece * width), jnp.bfloat16)

    def step(picked, sums):
        others = jnp.exp2(picked[:, LIMITED * queries :])
        mass, slope = [], []
        for k in range(LIMITED):
            points = picked[:, k * queries : (k + 1) * queries]
            m, s = box_terms(low_at[k] - points, high_at[k] - points)
            mass.append(m)
            slope.append(s)
        pair = others * mass[0]
        last_two = pair * mass[1]
        whole = last_two * mass[2]
        return whole, (
            sums[0] + (others * mass[1]) * (mass[2] * slope[0]),
            sums[1] + pair * (mass[2] * slope[1]),
            sums[2] + last_two * slope[2],
        )

    def piece(start, totals):
        sums, products = totals[:-1], totals[-1]
        some = [blocks_ref[start + b] for b in range(per_piece)]
        x = unit * jnp.concatenate(
            [
                jnp.concatenate([block[:, width * j : width * (j + 1)] for block in some], axis=1)
                for j in range(dims // 8)
            ],
            axis=0,
        )
        rest = float(GRID) * unit - x
        full = lax.erf(rest) + lax.erf(x)
        slope = x * jnp.exp2((x * x) * -LOG2_E) + rest * jnp.exp2((rest * rest) * -LOG2_E)
        ratio = jnp.concatenate(split(-slope / full, 2) + [ones], axis=0)
        left = jnp.concatenate(split(x, 3) + split(jnp.log(0.5 * full) * LOG2_E, 3), axis=0)
        picked = lax.dot_general(
            left, right, (((0,), (0,)), ((), ())), preferred_element_type=jnp.float32
        )
        inside = []
        for at_row in range(0, per_piece * width, 16):
            whole, sums = step(picked[at_row : at_row + 16], sums)
            inside.append(jnp.concatenate(split(whole, 2), axis=1))
        inside = jnp.concatenate(inside, axis=0)
        products = products + jnp.dot(ratio, inside, preferred_element_type=jnp.float32)
        return (*sums, products)

    def pieces(number, totals):
        for start in range(0, group, per_piece):
            totals = piece(number * group + start, totals)
        return totals

    zero = jnp.zeros((16, queries), jnp.float32)
    totals = (zero,) * LIMITED + (jnp.zeros((2 * dims + 16, 2 * queries), jnp.float32),)
    if count == group:
        totals = pieces(0, totals)
    else:
        totals = lax.fori_loop(0, count // group, pieces, totals)
    sums = [jnp.sum(s, axis=0, keepdims=True) for s in totals[:-1]]
    products = totals[-1]
    deriv = products[dims : 2 * dims, :queries] + products[:dims, queries:]
    deriv = products[:dims, :queries] + deriv
    total = products[2 * dims : 2 * dims + 8, :queries] + products[2 * dims : 2 * dims + 8, queries:]
    deriv = jnp.where(limited, 0.0, deriv * (SLOPE / 4))
    for mask, s in zip(chosen, sums):
        deriv = jnp.where(mask, s * (SLOPE / 4), deriv)
    out_ref[:dims, :] = deriv
    out_ref[dims:, :] = total * 0.125


def finish_kernel(sample_total, query_total, *refs):
    part_refs, (counts_ref, log_ref, share_ref) = refs[:-3], refs[-3:]
    whole = tree_sum([ref[...] for ref in part_refs])
    dims, queries = whole.shape[0] - 8, whole.shape[1]
    smoothing = 1.0 / TABLE_ROWS
    estimate = whole[dims : dims + 1] / sample_total
    log_est = jnp.log(estimate + smoothing)
    log_ref[...] = log_est
    target = jnp.log(counts_ref[...].astype(jnp.float32) / TABLE_ROWS + smoothing)
    weight = 2.0 * (log_est - target) / (query_total * (estimate + smoothing))
    terms = whole[:dims] * (weight / sample_total)
    terms = jnp.concatenate([terms, jnp.zeros((queries - dims, queries), jnp.float32)], axis=0)
    share = jnp.sum(terms.T, axis=0, keepdims=True)
    for peer in range(share_ref.shape[0]):
        share_ref[peer] = share


def last_kernel(shares_ref, held_log_ref, log_ref, gradient_ref):
    total = tree_sum([shares_ref[peer] for peer in range(shares_ref.shape[0])])
    log_ref[...] = held_log_ref[0]
    gradient_ref[...] = total[0, : gradient_ref.shape[0]]


def everyone(x, axis):
    size = lax.axis_size(axis)
    return [x] + [
        lax.ppermute(x, axis, [(i, i ^ offset) for i in range(size)]) for offset in range(1, size)
    ]


def call(kernel, args, outs, scratch=(), placed=pltpu.VMEM):
    single = len(outs) == 1
    return pl.pallas_call(
        kernel,
        out_shape=outs[0] if single else outs,
        in_specs=[pl.BlockSpec(memory_space=placed)] * len(args),
        out_specs=pl.BlockSpec(memory_space=pltpu.VMEM)
        if single
        else [pl.BlockSpec(memory_space=pltpu.VMEM)] * len(outs),
        scratch_shapes=list(scratch),
        compiler_params=pltpu.CompilerParams(vmem_limit_bytes=32 << 20),
    )(*args)


def shape(*sizes):
    return jax.ShapeDtypeStruct(sizes, jnp.float32)


def on_device(samples, bounds, spread, counts):
    dims, width = samples.shape
    queries = bounds.shape[2]
    blocks, copies = lax.axis_size("blk"), lax.axis_size("grp")
    sample_total = width * blocks * copies
    query_total = queries * blocks

    packed, bounds, unit, counts = call(
        load_kernel,
        [
            pltpu.with_memory_space_constraint(array, pltpu.HBM)
            for array in (samples, bounds, spread.reshape(1, dims), counts.reshape(1, queries))
        ],
        [
            pltpu.VMEM((blocks, 8, dims * width // 8), jnp.float32),
            pltpu.VMEM(bounds.shape, bounds.dtype),
            pltpu.VMEM((dims, queries), jnp.float32),
            pltpu.VMEM((1, queries), jnp.int32),
        ],
        [
            pltpu.VMEM((dims, width), jnp.float32),
            pltpu.VMEM((1, dims), jnp.float32),
            pltpu.SemaphoreType.DMA((4,)),
        ],
        placed=pl.ANY,
    )
    turned = [1] + [0] * (blocks - 1)
    groups = [
        [b * copies + (c + turned[b]) % copies for b in reversed(range(blocks))]
        for c in range(copies)
    ]
    exchange = lambda x: lax.all_to_all(x, ("blk", "grp"), 0, 0, axis_index_groups=groups)
    gathered = exchange(packed)
    part = call(
        functools.partial(terms_kernel, width),
        [gathered, bounds, unit],
        [shape(dims + 8, queries)],
    )
    log_est, share = call(
        functools.partial(finish_kernel, sample_total, query_total),
        everyone(part, "grp") + [counts],
        [shape(1, queries), shape(blocks, 1, queries)],
    )
    shares = exchange(share)
    return call(last_kernel, [shares, log_est], [shape(queries), shape(dims)])


def solution(mesh):
    return jax.shard_map(
        on_device,
        mesh=mesh,
        in_specs=(P(None, ("blk", "grp")), P(None, None, "blk"), P(), P("blk")),
        out_specs=(P("blk"), P()),
        check_vma=False,
    )
```

```python
import functools

import jax
import jax.numpy as jnp
from jax import lax
from jax.experimental import pallas as pl
from jax.experimental.pallas import tpu as pltpu
from jax.sharding import PartitionSpec as P

TABLE_ROWS = 1048576
GRID = 256
LIMITED = 3

ROOT_HALF = 0.7071067811865476
LOG2_E = 1.4426950408889634
SLOPE = 0.5641895835477563


def box_terms(low, high):
    low_bell = jnp.exp2((low * low) * -LOG2_E)
    high_bell = jnp.exp2((high * high) * -LOG2_E)
    return lax.erf(high) - lax.erf(low), low * low_bell - high * high_bell


def split(x, parts):
    out = []
    for _ in range(parts - 1):
        head = x.astype(jnp.bfloat16)
        out.append(head)
        x = x - head.astype(jnp.float32)
    return out + [x.astype(jnp.bfloat16)]


def tree_sum(parts):
    while len(parts) > 1:
        parts = [a + b for a, b in zip(parts[::2], parts[1::2])]
    return parts[0]


def load_kernel(
    x_ref, bounds_ref, spread_ref, counts_ref,
    out_ref, held_bounds, held_spread, target_ref,
    held_x, held_counts, sems,
):
    sources = (x_ref, bounds_ref, spread_ref, counts_ref)
    targets = (held_x, held_bounds, held_spread, held_counts)
    copies = [
        pltpu.make_async_copy(source, target, sems.at[i])
        for i, (source, target) in enumerate(zip(sources, targets))
    ]
    for copy in copies:
        copy.start()
    copies[0].wait()
    rows = held_x.shape[0]
    packed = jnp.concatenate([held_x[8 * j : 8 * (j + 1), :] for j in range(rows // 8)], axis=1)
    for peer in range(out_ref.shape[0]):
        out_ref[peer] = packed
    for copy in copies[1:]:
        copy.wait()
    smoothing = 1.0 / TABLE_ROWS
    target_ref[...] = jnp.log(held_counts[...].astype(jnp.float32) / TABLE_ROWS + smoothing)


def terms_kernel(width, blocks_ref, bounds_ref, spread_ref, out_ref):
    dims, queries = bounds_ref.shape[1:]
    count = blocks_ref.shape[0]
    per_piece = 128 // width
    group = min(count, 4 * per_piece)

    low, high = bounds_ref[0], bounds_ref[1]
    limited = (high - low) != GRID
    at = lax.broadcasted_iota(jnp.int32, (dims, queries), 0)
    first = jnp.min(jnp.where(limited, at, dims), axis=0, keepdims=True)
    last = jnp.max(jnp.where(limited, at, -1), axis=0, keepdims=True)
    chosen = [at == first, limited & (at > first) & (at < last), at == last]

    row = lax.broadcasted_iota(jnp.int32, (dims, dims), 0)
    column = lax.broadcasted_iota(jnp.int32, (dims, dims), 1)
    spread = jnp.sum(jnp.where(row == column, spread_ref[...], 0.0), axis=1, keepdims=True)
    unit = ROOT_HALF / spread

    pick = lambda mask, values: jnp.sum(jnp.where(mask, values, 0.0), axis=0, keepdims=True)
    low = low.astype(jnp.float32) * unit
    high = high.astype(jnp.float32) * unit
    low_at = [pick(mask, low) for mask in chosen]
    high_at = [pick(mask, high) for mask in chosen]

    ones = [mask.astype(jnp.float32).astype(jnp.bfloat16) for mask in chosen]
    free = jnp.where(limited, 0.0, 1.0).astype(jnp.bfloat16)
    none = jnp.zeros_like(free)
    right = jnp.concatenate(
        [jnp.concatenate(ones + [none], axis=1)] * 3
        + [jnp.concatenate([none] * LIMITED + [free], axis=1)] * 3,
        axis=0,
    )

    def step(picked, sums):
        others = jnp.exp2(picked[:, LIMITED * queries :])
        mass, slope = [], []
        for k in range(LIMITED):
            points = picked[:, k * queries : (k + 1) * queries]
            m, s = box_terms(low_at[k] - points, high_at[k] - points)
            mass.append(m)
            slope.append(s)
        pair = others * mass[0]
        last_two = pair * mass[1]
        whole = last_two * mass[2]
        return whole, (
            sums[0] + whole,
            sums[1] + (others * mass[1]) * (mass[2] * slope[0]),
            sums[2] + pair * (mass[2] * slope[1]),
            sums[3] + last_two * slope[2],
        )

    def piece(start, totals):
        sums, products = totals[:-1], totals[-1]
        some = [blocks_ref[start + b] for b in range(per_piece)]
        x = unit * jnp.concatenate(
            [
                jnp.concatenate([block[:, width * j : width * (j + 1)] for block in some], axis=1)
                for j in range(dims // 8)
            ],
            axis=0,
        )
        full, slope = box_terms(-x, float(GRID) * unit - x)
        ratio = jnp.concatenate(split(slope / full, 2), axis=0)
        left = jnp.concatenate(split(x, 3) + split(jnp.log(0.5 * full) * LOG2_E, 3), axis=0)
        picked = lax.dot_general(
            left, right, (((0,), (0,)), ((), ())), preferred_element_type=jnp.float32
        )
        inside = []
        for at_row in range(0, per_piece * width, 16):
            whole, sums = step(picked[at_row : at_row + 16], sums)
            inside.append(jnp.concatenate(split(whole, 2), axis=1))
        inside = jnp.concatenate(inside, axis=0)
        products = products + jnp.dot(ratio, inside, preferred_element_type=jnp.float32)
        return (*sums, products)

    def pieces(number, totals):
        for start in range(0, group, per_piece):
            totals = piece(number * group + start, totals)
        return totals

    zero = jnp.zeros((16, queries), jnp.float32)
    totals = (zero,) * (1 + LIMITED) + (jnp.zeros((2 * dims, 2 * queries), jnp.float32),)
    if count == group:
        totals = pieces(0, totals)
    else:
        totals = lax.fori_loop(0, count // group, pieces, totals)
    sums = [jnp.sum(s, axis=0, keepdims=True) for s in totals[:-1]]
    products = totals[-1]
    deriv = products[:dims, :queries] + (products[dims:, :queries] + products[:dims, queries:])
    deriv = jnp.where(limited, 0.0, deriv * (SLOPE / 4))
    for mask, s in zip(chosen, sums[1:]):
        deriv = jnp.where(mask, s * (SLOPE / 4), deriv)
    out_ref[:dims, :] = deriv
    out_ref[dims:, :] = jnp.broadcast_to(sums[0] * 0.125, (8, queries))


def finish_kernel(sample_total, query_total, *refs):
    part_refs, (target_ref, log_ref, share_ref) = refs[:-3], refs[-3:]
    whole = tree_sum([ref[...] for ref in part_refs])
    dims, queries = whole.shape[0] - 8, whole.shape[1]
    smoothing = 1.0 / TABLE_ROWS
    estimate = whole[dims : dims + 1] / sample_total
    log_est = jnp.log(estimate + smoothing)
    log_ref[...] = log_est
    weight = 2.0 * (log_est - target_ref[...]) / (query_total * (estimate + smoothing))
    terms = whole[:dims] * (weight / sample_total)
    terms = jnp.concatenate([terms, jnp.zeros((queries - dims, queries), jnp.float32)], axis=0)
    share = jnp.sum(terms.T, axis=0, keepdims=True)
    for peer in range(share_ref.shape[0]):
        share_ref[peer] = share


def last_kernel(shares_ref, held_log_ref, log_ref, gradient_ref):
    total = tree_sum([shares_ref[peer] for peer in range(shares_ref.shape[0])])
    log_ref[...] = held_log_ref[0]
    gradient_ref[...] = total[0, : gradient_ref.shape[0]]


def everyone(x, axis):
    size = lax.axis_size(axis)
    return [x] + [
        lax.ppermute(x, axis, [(i, i ^ offset) for i in range(size)]) for offset in range(1, size)
    ]


def call(kernel, args, outs, scratch=(), placed=pltpu.VMEM):
    single = len(outs) == 1
    return pl.pallas_call(
        kernel,
        out_shape=outs[0] if single else outs,
        in_specs=[pl.BlockSpec(memory_space=placed)] * len(args),
        out_specs=pl.BlockSpec(memory_space=pltpu.VMEM)
        if single
        else [pl.BlockSpec(memory_space=pltpu.VMEM)] * len(outs),
        scratch_shapes=list(scratch),
        compiler_params=pltpu.CompilerParams(vmem_limit_bytes=32 << 20),
    )(*args)


def shape(*sizes):
    return jax.ShapeDtypeStruct(sizes, jnp.float32)


def on_device(samples, bounds, spread, counts):
    dims, width = samples.shape
    queries = bounds.shape[2]
    blocks, copies = lax.axis_size("blk"), lax.axis_size("grp")
    sample_total = width * blocks * copies
    query_total = queries * blocks

    counts_vector = pltpu.VMEM((1, queries), jnp.int32)
    packed, bounds, spread, target = call(
        load_kernel,
        [
            pltpu.with_memory_space_constraint(array, pltpu.HBM)
            for array in (samples, bounds, spread.reshape(1, dims), counts.reshape(1, queries))
        ],
        [
            pltpu.VMEM((blocks, 8, dims * width // 8), jnp.float32),
            pltpu.VMEM(bounds.shape, bounds.dtype),
            pltpu.VMEM((1, dims), jnp.float32),
            pltpu.VMEM((1, queries), jnp.float32),
        ],
        [pltpu.VMEM((dims, width), jnp.float32), counts_vector, pltpu.SemaphoreType.DMA((4,))],
        placed=pl.ANY,
    )
    def exchange(x, turned):
        groups = [
            [b * copies + (c + (b in turned)) % copies for b in reversed(range(blocks))]
            for c in range(copies)
        ]
        return lax.all_to_all(x, ("blk", "grp"), 0, 0, axis_index_groups=groups)

    gathered = exchange(packed, [0])
    part = call(
        functools.partial(terms_kernel, width),
        [gathered, bounds, spread],
        [shape(dims + 8, queries)],
    )
    log_est, share = call(
        functools.partial(finish_kernel, sample_total, query_total),
        everyone(part, "grp") + [target],
        [shape(1, queries), shape(blocks, 1, queries)],
    )
    shares = exchange(share, [0, 1, 2, 4])
    return call(last_kernel, [shares, log_est], [shape(queries), shape(dims)])


def solution(mesh):
    return jax.shard_map(
        on_device,
        mesh=mesh,
        in_specs=(P(None, ("blk", "grp")), P(None, None, "blk"), P(), P("blk")),
        out_specs=(P("blk"), P()),
        check_vma=False,
    )
```

```python
import functools

import jax
import jax.numpy as jnp
from jax import lax
from jax.experimental import pallas as pl
from jax.experimental.pallas import tpu as pltpu
from jax.sharding import PartitionSpec as P

TABLE_ROWS = 1048576
GRID = 256
LIMITED = 3

ROOT_HALF = 0.7071067811865476
LOG2_E = 1.4426950408889634
SLOPE = 0.5641895835477563


def box_terms(low, high):
    low_bell = jnp.exp2((low * low) * -LOG2_E)
    high_bell = jnp.exp2((high * high) * -LOG2_E)
    return lax.erf(high) - lax.erf(low), low * low_bell - high * high_bell


def split(x, parts):
    out = []
    for _ in range(parts - 1):
        head = x.astype(jnp.bfloat16)
        out.append(head)
        x = x - head.astype(jnp.float32)
    return out + [x.astype(jnp.bfloat16)]


def tree_sum(parts):
    while len(parts) > 1:
        parts = [a + b for a, b in zip(parts[::2], parts[1::2])]
    return parts[0]


def load_kernel(
    x_ref, bounds_ref, spread_ref, counts_ref,
    out_ref, held_bounds, held_spread, target_ref,
    held_x, held_counts, sems,
):
    sources = (x_ref, bounds_ref, spread_ref, counts_ref)
    targets = (held_x, held_bounds, held_spread, held_counts)
    copies = [
        pltpu.make_async_copy(source, target, sems.at[i])
        for i, (source, target) in enumerate(zip(sources, targets))
    ]
    for copy in copies:
        copy.start()
    copies[0].wait()
    rows = held_x.shape[0]
    packed = jnp.concatenate([held_x[8 * j : 8 * (j + 1), :] for j in range(rows // 8)], axis=1)
    for peer in range(out_ref.shape[0]):
        out_ref[peer] = packed
    for copy in copies[1:]:
        copy.wait()
    smoothing = 1.0 / TABLE_ROWS
    target_ref[...] = jnp.log(held_counts[...].astype(jnp.float32) / TABLE_ROWS + smoothing)


def terms_kernel(width, blocks_ref, bounds_ref, spread_ref, out_ref):
    dims, queries = bounds_ref.shape[1:]
    count = blocks_ref.shape[0]
    per_piece = 128 // width
    group = min(count, 4 * per_piece)

    low, high = bounds_ref[0], bounds_ref[1]
    limited = (high - low) != GRID
    at = lax.broadcasted_iota(jnp.int32, (dims, queries), 0)
    first = jnp.min(jnp.where(limited, at, dims), axis=0, keepdims=True)
    last = jnp.max(jnp.where(limited, at, -1), axis=0, keepdims=True)
    chosen = [at == first, limited & (at > first) & (at < last), at == last]

    row = lax.broadcasted_iota(jnp.int32, (dims, dims), 0)
    column = lax.broadcasted_iota(jnp.int32, (dims, dims), 1)
    spread = jnp.sum(jnp.where(row == column, spread_ref[...], 0.0), axis=1, keepdims=True)
    unit = ROOT_HALF / spread

    pick = lambda mask, values: jnp.sum(jnp.where(mask, values, 0.0), axis=0, keepdims=True)
    low = low.astype(jnp.float32) * unit
    high = high.astype(jnp.float32) * unit
    low_at = [pick(mask, low) for mask in chosen]
    high_at = [pick(mask, high) for mask in chosen]

    ones = [mask.astype(jnp.float32).astype(jnp.bfloat16) for mask in chosen]
    free = jnp.where(limited, 0.0, 1.0).astype(jnp.bfloat16)
    none = jnp.zeros_like(free)
    right = jnp.concatenate(
        [jnp.concatenate(ones + [none], axis=1)] * 3
        + [jnp.concatenate([none] * LIMITED + [free], axis=1)] * 3,
        axis=0,
    )

    def step(picked, sums):
        others = jnp.exp2(picked[:, LIMITED * queries :])
        mass, slope = [], []
        for k in range(LIMITED):
            points = picked[:, k * queries : (k + 1) * queries]
            m, s = box_terms(low_at[k] - points, high_at[k] - points)
            mass.append(m)
            slope.append(s)
        pair = others * mass[0]
        last_two = pair * mass[1]
        whole = last_two * mass[2]
        return whole, (
            sums[0] + whole,
            sums[1] + (others * mass[1]) * (mass[2] * slope[0]),
            sums[2] + pair * (mass[2] * slope[1]),
            sums[3] + last_two * slope[2],
        )

    def piece(start, totals):
        sums, products = totals[:-1], totals[-1]
        some = [blocks_ref[start + b] for b in range(per_piece)]
        x = unit * jnp.concatenate(
            [
                jnp.concatenate([block[:, width * j : width * (j + 1)] for block in some], axis=1)
                for j in range(dims // 8)
            ],
            axis=0,
        )
        full, slope = box_terms(-x, float(GRID) * unit - x)
        ratio = jnp.concatenate(split(slope / full, 2), axis=0)
        left = jnp.concatenate(split(x, 3) + split(jnp.log(0.5 * full) * LOG2_E, 3), axis=0)
        picked = lax.dot_general(
            left, right, (((0,), (0,)), ((), ())), preferred_element_type=jnp.float32
        )
        inside = []
        for at_row in range(0, per_piece * width, 16):
            whole, sums = step(picked[at_row : at_row + 16], sums)
            inside.append(jnp.concatenate(split(whole, 2), axis=1))
        inside = jnp.concatenate(inside, axis=0)
        products = products + jnp.dot(ratio, inside, preferred_element_type=jnp.float32)
        return (*sums, products)

    def pieces(number, totals):
        for start in range(0, group, per_piece):
            totals = piece(number * group + start, totals)
        return totals

    zero = jnp.zeros((16, queries), jnp.float32)
    totals = (zero,) * (1 + LIMITED) + (jnp.zeros((2 * dims, 2 * queries), jnp.float32),)
    if count == group:
        totals = pieces(0, totals)
    else:
        totals = lax.fori_loop(0, count // group, pieces, totals)
    sums = [jnp.sum(s, axis=0, keepdims=True) for s in totals[:-1]]
    products = totals[-1]
    deriv = products[:dims, :queries] + (products[dims:, :queries] + products[:dims, queries:])
    deriv = jnp.where(limited, 0.0, deriv * (SLOPE / 4))
    for mask, s in zip(chosen, sums[1:]):
        deriv = jnp.where(mask, s * (SLOPE / 4), deriv)
    out_ref[:dims, :] = deriv
    out_ref[dims:, :] = jnp.broadcast_to(sums[0] * 0.125, (8, queries))


def finish_kernel(sample_total, query_total, *refs):
    part_refs, (target_ref, log_ref, share_ref) = refs[:-3], refs[-3:]
    whole = tree_sum([ref[...] for ref in part_refs])
    dims, queries = whole.shape[0] - 8, whole.shape[1]
    smoothing = 1.0 / TABLE_ROWS
    estimate = whole[dims : dims + 1] / sample_total
    log_est = jnp.log(estimate + smoothing)
    log_ref[...] = log_est
    weight = 2.0 * (log_est - target_ref[...]) / (query_total * (estimate + smoothing))
    terms = whole[:dims] * (weight / sample_total)
    terms = jnp.concatenate([terms, jnp.zeros((queries - dims, queries), jnp.float32)], axis=0)
    share = jnp.sum(terms.T, axis=0, keepdims=True)
    for peer in range(share_ref.shape[0]):
        share_ref[peer] = share


def last_kernel(shares_ref, held_log_ref, log_ref, gradient_ref):
    total = tree_sum([shares_ref[peer] for peer in range(shares_ref.shape[0])])
    log_ref[...] = held_log_ref[0]
    gradient_ref[...] = total[0, : gradient_ref.shape[0]]


def everyone(x, axis):
    size = lax.axis_size(axis)
    return [x] + [
        lax.ppermute(x, axis, [(i, i ^ offset) for i in range(size)]) for offset in range(1, size)
    ]


def call(kernel, args, outs, scratch=(), placed=pltpu.VMEM):
    single = len(outs) == 1
    return pl.pallas_call(
        kernel,
        out_shape=outs[0] if single else outs,
        in_specs=[pl.BlockSpec(memory_space=placed)] * len(args),
        out_specs=pl.BlockSpec(memory_space=pltpu.VMEM)
        if single
        else [pl.BlockSpec(memory_space=pltpu.VMEM)] * len(outs),
        scratch_shapes=list(scratch),
        compiler_params=pltpu.CompilerParams(vmem_limit_bytes=32 << 20),
    )(*args)


def shape(*sizes):
    return jax.ShapeDtypeStruct(sizes, jnp.float32)


def on_device(samples, bounds, spread, counts):
    dims, width = samples.shape
    queries = bounds.shape[2]
    blocks, copies = lax.axis_size("blk"), lax.axis_size("grp")
    sample_total = width * blocks * copies
    query_total = queries * blocks

    counts_vector = pltpu.VMEM((1, queries), jnp.int32)
    packed, bounds, spread, target = call(
        load_kernel,
        [
            pltpu.with_memory_space_constraint(array, pltpu.HBM)
            for array in (samples, bounds, spread.reshape(1, dims), counts.reshape(1, queries))
        ],
        [
            pltpu.VMEM((blocks, 8, dims * width // 8), jnp.float32),
            pltpu.VMEM(bounds.shape, bounds.dtype),
            pltpu.VMEM((1, dims), jnp.float32),
            pltpu.VMEM((1, queries), jnp.float32),
        ],
        [pltpu.VMEM((dims, width), jnp.float32), counts_vector, pltpu.SemaphoreType.DMA((4,))],
        placed=pl.ANY,
    )
    def exchange(x, turned):
        groups = [
            [b * copies + (c + (b in turned)) % copies for b in reversed(range(blocks))]
            for c in range(copies)
        ]
        return lax.all_to_all(x, ("blk", "grp"), 0, 0, axis_index_groups=groups)

    gathered = exchange(packed, [0])
    part = call(
        functools.partial(terms_kernel, width),
        [gathered, bounds, spread],
        [shape(dims + 8, queries)],
    )
    log_est, share = call(
        functools.partial(finish_kernel, sample_total, query_total),
        everyone(part, "grp") + [target],
        [shape(1, queries), shape(blocks, 1, queries)],
    )
    shares = exchange(share, [0] + list(range(blocks // 2, blocks)))
    return call(last_kernel, [shares, log_est], [shape(queries), shape(dims)])


def solution(mesh):
    return jax.shard_map(
        on_device,
        mesh=mesh,
        in_specs=(P(None, ("blk", "grp")), P(None, None, "blk"), P(), P("blk")),
        out_specs=(P("blk"), P()),
        check_vma=False,
    )
```

```python
import functools

import jax
import jax.numpy as jnp
from jax import lax
from jax.experimental import pallas as pl
from jax.experimental.pallas import tpu as pltpu
from jax.sharding import PartitionSpec as P

TABLE_ROWS = 1048576
GRID = 256
LIMITED = 3

ROOT_HALF = 0.7071067811865476
LOG2_E = 1.4426950408889634
SLOPE = 0.5641895835477563


def box_terms(low, high):
    low_bell = jnp.exp2((low * low) * -LOG2_E)
    high_bell = jnp.exp2((high * high) * -LOG2_E)
    return lax.erf(high) - lax.erf(low), low * low_bell - high * high_bell


def split(x, parts):
    out = []
    for _ in range(parts - 1):
        head = x.astype(jnp.bfloat16)
        out.append(head)
        x = x - head.astype(jnp.float32)
    return out + [x.astype(jnp.bfloat16)]


def tree_sum(parts):
    while len(parts) > 1:
        parts = [a + b for a, b in zip(parts[::2], parts[1::2])]
    return parts[0]


def load_kernel(x_ref, spread_ref, out_ref, held_spread, held_x, sems):
    copies = [
        pltpu.make_async_copy(x_ref, held_x, sems.at[0]),
        pltpu.make_async_copy(spread_ref, held_spread, sems.at[1]),
    ]
    for copy in copies:
        copy.start()
    copies[0].wait()
    rows = held_x.shape[0]
    packed = jnp.concatenate([held_x[8 * j : 8 * (j + 1), :] for j in range(rows // 8)], axis=1)
    for peer in range(out_ref.shape[0]):
        out_ref[peer] = packed
    copies[1].wait()


def terms_kernel(width, blocks_ref, bounds_ref, spread_ref, out_ref):
    dims, queries = bounds_ref.shape[1:]
    count = blocks_ref.shape[0]
    per_piece = 128 // width
    group = min(count, 4 * per_piece)

    low, high = bounds_ref[0], bounds_ref[1]
    limited = (high - low) != GRID
    at = lax.broadcasted_iota(jnp.int32, (dims, queries), 0)
    first = jnp.min(jnp.where(limited, at, dims), axis=0, keepdims=True)
    last = jnp.max(jnp.where(limited, at, -1), axis=0, keepdims=True)
    chosen = [at == first, limited & (at > first) & (at < last), at == last]

    row = lax.broadcasted_iota(jnp.int32, (dims, dims), 0)
    column = lax.broadcasted_iota(jnp.int32, (dims, dims), 1)
    spread = jnp.sum(jnp.where(row == column, spread_ref[...], 0.0), axis=1, keepdims=True)
    unit = ROOT_HALF / spread

    pick = lambda mask, values: jnp.sum(jnp.where(mask, values, 0.0), axis=0, keepdims=True)
    low = low.astype(jnp.float32) * unit
    high = high.astype(jnp.float32) * unit
    low_at = [pick(mask, low) for mask in chosen]
    high_at = [pick(mask, high) for mask in chosen]

    ones = [mask.astype(jnp.float32).astype(jnp.bfloat16) for mask in chosen]
    free = jnp.where(limited, 0.0, 1.0).astype(jnp.bfloat16)
    none = jnp.zeros_like(free)
    right = jnp.concatenate(
        [jnp.concatenate(ones + [none], axis=1)] * 3
        + [jnp.concatenate([none] * LIMITED + [free], axis=1)] * 3,
        axis=0,
    )

    def step(picked, sums):
        others = jnp.exp2(picked[:, LIMITED * queries :])
        mass, slope = [], []
        for k in range(LIMITED):
            points = picked[:, k * queries : (k + 1) * queries]
            m, s = box_terms(low_at[k] - points, high_at[k] - points)
            mass.append(m)
            slope.append(s)
        pair = others * mass[0]
        last_two = pair * mass[1]
        whole = last_two * mass[2]
        return whole, (
            sums[0] + whole,
            sums[1] + (others * mass[1]) * (mass[2] * slope[0]),
            sums[2] + pair * (mass[2] * slope[1]),
            sums[3] + last_two * slope[2],
        )

    def piece(start, totals):
        sums, products = totals[:-1], totals[-1]
        some = [blocks_ref[start + b] for b in range(per_piece)]
        x = unit * jnp.concatenate(
            [
                jnp.concatenate([block[:, width * j : width * (j + 1)] for block in some], axis=1)
                for j in range(dims // 8)
            ],
            axis=0,
        )
        full, slope = box_terms(-x, float(GRID) * unit - x)
        ratio = jnp.concatenate(split(slope / full, 2), axis=0)
        left = jnp.concatenate(split(x, 3) + split(jnp.log(0.5 * full) * LOG2_E, 3), axis=0)
        picked = lax.dot_general(
            left, right, (((0,), (0,)), ((), ())), preferred_element_type=jnp.float32
        )
        inside = []
        for at_row in range(0, per_piece * width, 16):
            whole, sums = step(picked[at_row : at_row + 16], sums)
            inside.append(jnp.concatenate(split(whole, 2), axis=1))
        inside = jnp.concatenate(inside, axis=0)
        products = products + jnp.dot(ratio, inside, preferred_element_type=jnp.float32)
        return (*sums, products)

    def pieces(number, totals):
        for start in range(0, group, per_piece):
            totals = piece(number * group + start, totals)
        return totals

    zero = jnp.zeros((16, queries), jnp.float32)
    totals = (zero,) * (1 + LIMITED) + (jnp.zeros((2 * dims, 2 * queries), jnp.float32),)
    if count == group:
        totals = pieces(0, totals)
    else:
        totals = lax.fori_loop(0, count // group, pieces, totals)
    sums = [jnp.sum(s, axis=0, keepdims=True) for s in totals[:-1]]
    products = totals[-1]
    deriv = products[:dims, :queries] + (products[dims:, :queries] + products[:dims, queries:])
    deriv = jnp.where(limited, 0.0, deriv * (SLOPE / 4))
    for mask, s in zip(chosen, sums[1:]):
        deriv = jnp.where(mask, s * (SLOPE / 4), deriv)
    out_ref[:dims, :] = deriv
    out_ref[dims:, :] = jnp.broadcast_to(sums[0] * 0.125, (8, queries))


def finish_kernel(sample_total, query_total, *refs):
    part_refs, (counts_ref, log_ref, share_ref) = refs[:-3], refs[-3:]
    whole = tree_sum([ref[...] for ref in part_refs])
    dims, queries = whole.shape[0] - 8, whole.shape[1]
    smoothing = 1.0 / TABLE_ROWS
    estimate = whole[dims : dims + 1] / sample_total
    log_est = jnp.log(estimate + smoothing)
    log_ref[...] = log_est
    target = jnp.log(counts_ref[...].astype(jnp.float32) / TABLE_ROWS + smoothing)
    weight = 2.0 * (log_est - target) / (query_total * (estimate + smoothing))
    terms = whole[:dims] * (weight / sample_total)
    terms = jnp.concatenate([terms, jnp.zeros((queries - dims, queries), jnp.float32)], axis=0)
    share = jnp.sum(terms.T, axis=0, keepdims=True)
    for peer in range(share_ref.shape[0]):
        share_ref[peer] = share


def last_kernel(shares_ref, held_log_ref, log_ref, gradient_ref):
    total = tree_sum([shares_ref[peer] for peer in range(shares_ref.shape[0])])
    log_ref[...] = held_log_ref[0]
    gradient_ref[...] = total[0, : gradient_ref.shape[0]]


def everyone(x, axis):
    size = lax.axis_size(axis)
    return [x] + [
        lax.ppermute(x, axis, [(i, i ^ offset) for i in range(size)]) for offset in range(1, size)
    ]


def call(kernel, args, outs, scratch=(), placed=pltpu.VMEM):
    single = len(outs) == 1
    return pl.pallas_call(
        kernel,
        out_shape=outs[0] if single else outs,
        in_specs=[pl.BlockSpec(memory_space=placed)] * len(args),
        out_specs=pl.BlockSpec(memory_space=pltpu.VMEM)
        if single
        else [pl.BlockSpec(memory_space=pltpu.VMEM)] * len(outs),
        scratch_shapes=list(scratch),
        compiler_params=pltpu.CompilerParams(vmem_limit_bytes=32 << 20),
    )(*args)


def shape(*sizes):
    return jax.ShapeDtypeStruct(sizes, jnp.float32)


def on_device(samples, bounds, spread, counts):
    dims, width = samples.shape
    queries = bounds.shape[2]
    blocks, copies = lax.axis_size("blk"), lax.axis_size("grp")
    sample_total = width * blocks * copies
    query_total = queries * blocks

    packed, spread = call(
        load_kernel,
        [
            pltpu.with_memory_space_constraint(array, pltpu.HBM)
            for array in (samples, spread.reshape(1, dims))
        ],
        [
            pltpu.VMEM((blocks, 8, dims * width // 8), jnp.float32),
            pltpu.VMEM((1, dims), jnp.float32),
        ],
        [pltpu.VMEM((dims, width), jnp.float32), pltpu.SemaphoreType.DMA((2,))],
        placed=pl.ANY,
    )
    turned = [1] + [0] * (blocks - 1)
    groups = [
        [b * copies + (c + turned[b]) % copies for b in reversed(range(blocks))]
        for c in range(copies)
    ]
    exchange = lambda x: lax.all_to_all(x, ("blk", "grp"), 0, 0, axis_index_groups=groups)
    gathered = exchange(packed)
    part = call(
        functools.partial(terms_kernel, width),
        [gathered, bounds, spread],
        [shape(dims + 8, queries)],
    )
    log_est, share = call(
        functools.partial(finish_kernel, sample_total, query_total),
        everyone(part, "grp") + [counts.reshape(1, queries)],
        [shape(1, queries), shape(blocks, 1, queries)],
    )
    shares = exchange(share)
    return call(last_kernel, [shares, log_est], [shape(queries), shape(dims)])


def solution(mesh):
    return jax.shard_map(
        on_device,
        mesh=mesh,
        in_specs=(P(None, ("blk", "grp")), P(None, None, "blk"), P(), P("blk")),
        out_specs=(P("blk"), P()),
        check_vma=False,
    )
```

```python
import functools

import jax
import jax.numpy as jnp
from jax import lax
from jax.experimental import pallas as pl
from jax.experimental.pallas import tpu as pltpu
from jax.sharding import PartitionSpec as P

TABLE_ROWS = 1048576
GRID = 256
LIMITED = 3

ROOT_HALF = 0.7071067811865476
LOG2_E = 1.4426950408889634
SLOPE = 0.5641895835477563


def box_terms(low, high):
    low_bell = jnp.exp2((low * low) * -LOG2_E)
    high_bell = jnp.exp2((high * high) * -LOG2_E)
    return lax.erf(high) - lax.erf(low), low * low_bell - high * high_bell


def split(x, parts):
    out = []
    for _ in range(parts - 1):
        head = x.astype(jnp.bfloat16)
        out.append(head)
        x = x - head.astype(jnp.float32)
    return out + [x.astype(jnp.bfloat16)]


def tree_sum(parts):
    while len(parts) > 1:
        parts = [a + b for a, b in zip(parts[::2], parts[1::2])]
    return parts[0]


def load_kernel(x_ref, spread_ref, out_ref, held_spread, held_x, sems):
    copies = [
        pltpu.make_async_copy(x_ref, held_x, sems.at[0]),
        pltpu.make_async_copy(spread_ref, held_spread, sems.at[1]),
    ]
    for copy in copies:
        copy.start()
    copies[0].wait()
    rows = held_x.shape[0]
    packed = jnp.concatenate([held_x[8 * j : 8 * (j + 1), :] for j in range(rows // 8)], axis=1)
    for peer in range(out_ref.shape[0]):
        out_ref[peer] = packed
    copies[1].wait()


def terms_kernel(width, blocks_ref, bounds_ref, spread_ref, out_ref):
    dims, queries = bounds_ref.shape[1:]
    count = blocks_ref.shape[0]
    per_piece = 128 // width
    group = min(count, 4 * per_piece)

    low, high = bounds_ref[0], bounds_ref[1]
    limited = (high - low) != GRID
    at = lax.broadcasted_iota(jnp.int32, (dims, queries), 0)
    first = jnp.min(jnp.where(limited, at, dims), axis=0, keepdims=True)
    last = jnp.max(jnp.where(limited, at, -1), axis=0, keepdims=True)
    chosen = [at == first, limited & (at > first) & (at < last), at == last]

    row = lax.broadcasted_iota(jnp.int32, (dims, dims), 0)
    column = lax.broadcasted_iota(jnp.int32, (dims, dims), 1)
    spread = jnp.sum(jnp.where(row == column, spread_ref[...], 0.0), axis=1, keepdims=True)
    unit = ROOT_HALF / spread

    pick = lambda mask, values: jnp.sum(jnp.where(mask, values, 0.0), axis=0, keepdims=True)
    low = low.astype(jnp.float32) * unit
    high = high.astype(jnp.float32) * unit
    low_at = [pick(mask, low) for mask in chosen]
    high_at = [pick(mask, high) for mask in chosen]

    ones = [mask.astype(jnp.float32).astype(jnp.bfloat16) for mask in chosen]
    free = jnp.where(limited, 0.0, 1.0).astype(jnp.bfloat16)
    none = jnp.zeros_like(free)
    right = jnp.concatenate(
        [jnp.concatenate(ones + [none], axis=1)] * 3
        + [jnp.concatenate([none] * LIMITED + [free], axis=1)] * 3,
        axis=0,
    )

    def step(picked, sums):
        others = jnp.exp2(picked[:, LIMITED * queries :])
        mass, slope = [], []
        for k in range(LIMITED):
            points = picked[:, k * queries : (k + 1) * queries]
            m, s = box_terms(low_at[k] - points, high_at[k] - points)
            mass.append(m)
            slope.append(s)
        pair = others * mass[0]
        last_two = pair * mass[1]
        whole = last_two * mass[2]
        return whole, (
            sums[0] + whole,
            sums[1] + (others * mass[1]) * (mass[2] * slope[0]),
            sums[2] + pair * (mass[2] * slope[1]),
            sums[3] + last_two * slope[2],
        )

    def piece(start, totals):
        sums, products = totals[:-1], totals[-1]
        some = [blocks_ref[start + b] for b in range(per_piece)]
        x = unit * jnp.concatenate(
            [
                jnp.concatenate([block[:, width * j : width * (j + 1)] for block in some], axis=1)
                for j in range(dims // 8)
            ],
            axis=0,
        )
        full, slope = box_terms(-x, float(GRID) * unit - x)
        ratio = jnp.concatenate(split(slope / full, 2), axis=0)
        left = jnp.concatenate(split(x, 3) + split(jnp.log(0.5 * full) * LOG2_E, 3), axis=0)
        picked = lax.dot_general(
            left, right, (((0,), (0,)), ((), ())), preferred_element_type=jnp.float32
        )
        inside = []
        for at_row in range(0, per_piece * width, 16):
            whole, sums = step(picked[at_row : at_row + 16], sums)
            inside.append(jnp.concatenate(split(whole, 2), axis=1))
        inside = jnp.concatenate(inside, axis=0)
        products = products + jnp.dot(ratio, inside, preferred_element_type=jnp.float32)
        return (*sums, products)

    def pieces(number, totals):
        for start in range(0, group, per_piece):
            totals = piece(number * group + start, totals)
        return totals

    zero = jnp.zeros((16, queries), jnp.float32)
    totals = (zero,) * (1 + LIMITED) + (jnp.zeros((2 * dims, 2 * queries), jnp.float32),)
    if count == group:
        totals = pieces(0, totals)
    else:
        totals = lax.fori_loop(0, count // group, pieces, totals)
    sums = [jnp.sum(s, axis=0, keepdims=True) for s in totals[:-1]]
    products = totals[-1]
    deriv = products[:dims, :queries] + (products[dims:, :queries] + products[:dims, queries:])
    deriv = jnp.where(limited, 0.0, deriv * (SLOPE / 4))
    for mask, s in zip(chosen, sums[1:]):
        deriv = jnp.where(mask, s * (SLOPE / 4), deriv)
    out_ref[:dims, :] = deriv
    out_ref[dims:, :] = jnp.broadcast_to(sums[0] * 0.125, (8, queries))


def finish_kernel(sample_total, query_total, *refs):
    part_refs, (counts_ref, log_ref, share_ref) = refs[:-3], refs[-3:]
    whole = tree_sum([ref[...] for ref in part_refs])
    dims, queries = whole.shape[0] - 8, whole.shape[1]
    smoothing = 1.0 / TABLE_ROWS
    estimate = whole[dims : dims + 1] / sample_total
    log_est = jnp.log(estimate + smoothing)
    log_ref[...] = log_est
    target = jnp.log(counts_ref[...].astype(jnp.float32) / TABLE_ROWS + smoothing)
    weight = 2.0 * (log_est - target) / (query_total * (estimate + smoothing))
    terms = whole[:dims] * (weight / sample_total)
    terms = jnp.concatenate([terms, jnp.zeros((queries - dims, queries), jnp.float32)], axis=0)
    share = jnp.sum(terms.T, axis=0, keepdims=True)
    for peer in range(share_ref.shape[0]):
        share_ref[peer] = share


def last_kernel(shares_ref, held_log_ref, log_ref, gradient_ref):
    total = tree_sum([shares_ref[peer] for peer in range(shares_ref.shape[0])])
    log_ref[...] = held_log_ref[0]
    gradient_ref[...] = total[0, : gradient_ref.shape[0]]


def everyone(x, axis):
    size = lax.axis_size(axis)
    return [x] + [
        lax.ppermute(x, axis, [(i, i ^ offset) for i in range(size)]) for offset in range(1, size)
    ]


def call(kernel, args, outs, scratch=(), placed=pltpu.VMEM):
    single = len(outs) == 1
    return pl.pallas_call(
        kernel,
        out_shape=outs[0] if single else outs,
        in_specs=[pl.BlockSpec(memory_space=placed)] * len(args),
        out_specs=pl.BlockSpec(memory_space=pltpu.VMEM)
        if single
        else [pl.BlockSpec(memory_space=pltpu.VMEM)] * len(outs),
        scratch_shapes=list(scratch),
        compiler_params=pltpu.CompilerParams(vmem_limit_bytes=32 << 20),
    )(*args)


def shape(*sizes):
    return jax.ShapeDtypeStruct(sizes, jnp.float32)


def on_device(samples, bounds, spread, counts):
    dims, width = samples.shape
    queries = bounds.shape[2]
    blocks, copies = lax.axis_size("blk"), lax.axis_size("grp")
    sample_total = width * blocks * copies
    query_total = queries * blocks

    packed, spread = call(
        load_kernel,
        [
            pltpu.with_memory_space_constraint(array, pltpu.HBM)
            for array in (samples, spread.reshape(1, dims))
        ],
        [
            pltpu.VMEM((blocks, 8, dims * width // 8), jnp.float32),
            pltpu.VMEM((1, dims), jnp.float32),
        ],
        [pltpu.VMEM((dims, width), jnp.float32), pltpu.SemaphoreType.DMA((2,))],
        placed=pl.ANY,
    )
    turned = [1] + [0] * (blocks - 1)
    hops = lambda b: (b & 1) + (b >> 1 & 1) + (b >> 2)
    order = sorted(range(blocks), key=lambda b: (-hops(b), -b))
    groups = [
        [b * copies + (c + turned[b]) % copies for b in order]
        for c in range(copies)
    ]
    exchange = lambda x: lax.all_to_all(x, ("blk", "grp"), 0, 0, axis_index_groups=groups)
    gathered = exchange(packed)
    part = call(
        functools.partial(terms_kernel, width),
        [gathered, bounds, spread],
        [shape(dims + 8, queries)],
    )
    log_est, share = call(
        functools.partial(finish_kernel, sample_total, query_total),
        everyone(part, "grp") + [counts.reshape(1, queries)],
        [shape(1, queries), shape(blocks, 1, queries)],
    )
    shares = exchange(share)
    return call(last_kernel, [shares, log_est], [shape(queries), shape(dims)])


def solution(mesh):
    return jax.shard_map(
        on_device,
        mesh=mesh,
        in_specs=(P(None, ("blk", "grp")), P(None, None, "blk"), P(), P("blk")),
        out_specs=(P("blk"), P()),
        check_vma=False,
    )
```

```python
import functools

import jax
import jax.numpy as jnp
from jax import lax
from jax.experimental import pallas as pl
from jax.experimental.pallas import tpu as pltpu
from jax.sharding import PartitionSpec as P

TABLE_ROWS = 1048576
GRID = 256
LIMITED = 3

ROOT_HALF = 0.7071067811865476
LOG2_E = 1.4426950408889634
SLOPE = 0.5641895835477563


def box_terms(low, high):
    low_bell = jnp.exp2((low * low) * -LOG2_E)
    high_bell = jnp.exp2((high * high) * -LOG2_E)
    return lax.erf(high) - lax.erf(low), low * low_bell - high * high_bell


def split(x, parts):
    out = []
    for _ in range(parts - 1):
        head = x.astype(jnp.bfloat16)
        out.append(head)
        x = x - head.astype(jnp.float32)
    return out + [x.astype(jnp.bfloat16)]


def tree_sum(parts):
    while len(parts) > 1:
        parts = [a + b for a, b in zip(parts[::2], parts[1::2])]
    return parts[0]


def load_kernel(x_ref, spread_ref, out_ref, held_spread, held_x, sems):
    copies = [
        pltpu.make_async_copy(x_ref, held_x, sems.at[0]),
        pltpu.make_async_copy(spread_ref, held_spread, sems.at[1]),
    ]
    for copy in copies:
        copy.start()
    copies[0].wait()
    rows = held_x.shape[0]
    packed = jnp.concatenate([held_x[8 * j : 8 * (j + 1), :] for j in range(rows // 8)], axis=1)
    for peer in range(out_ref.shape[0]):
        out_ref[peer] = packed
    copies[1].wait()


def terms_kernel(width, blocks_ref, bounds_ref, spread_ref, out_ref):
    dims, queries = bounds_ref.shape[1:]
    count = blocks_ref.shape[0]
    per_piece = 128 // width
    group = min(count, 4 * per_piece)

    low, high = bounds_ref[0], bounds_ref[1]
    limited = (high - low) != GRID
    at = lax.broadcasted_iota(jnp.int32, (dims, queries), 0)
    first = jnp.min(jnp.where(limited, at, dims), axis=0, keepdims=True)
    last = jnp.max(jnp.where(limited, at, -1), axis=0, keepdims=True)
    chosen = [at == first, limited & (at > first) & (at < last), at == last]

    row = lax.broadcasted_iota(jnp.int32, (dims, dims), 0)
    column = lax.broadcasted_iota(jnp.int32, (dims, dims), 1)
    spread = jnp.sum(jnp.where(row == column, spread_ref[...], 0.0), axis=1, keepdims=True)
    unit = ROOT_HALF / spread

    pick = lambda mask, values: jnp.sum(jnp.where(mask, values, 0.0), axis=0, keepdims=True)
    low = low.astype(jnp.float32) * unit
    high = high.astype(jnp.float32) * unit
    low_at = [pick(mask, low) for mask in chosen]
    high_at = [pick(mask, high) for mask in chosen]

    ones = [mask.astype(jnp.float32).astype(jnp.bfloat16) for mask in chosen]
    free = jnp.where(limited, 0.0, 1.0).astype(jnp.bfloat16)
    none = jnp.zeros_like(free)
    right = jnp.concatenate(
        [jnp.concatenate(ones + [none], axis=1)] * 3
        + [jnp.concatenate([none] * LIMITED + [free], axis=1)] * 3,
        axis=0,
    )

    def step(picked, sums):
        others = jnp.exp2(picked[:, LIMITED * queries :])
        mass, slope = [], []
        for k in range(LIMITED):
            points = picked[:, k * queries : (k + 1) * queries]
            m, s = box_terms(low_at[k] - points, high_at[k] - points)
            mass.append(m)
            slope.append(s)
        pair = others * mass[0]
        last_two = pair * mass[1]
        whole = last_two * mass[2]
        return whole, (
            sums[0] + whole,
            sums[1] + (others * mass[1]) * (mass[2] * slope[0]),
            sums[2] + pair * (mass[2] * slope[1]),
            sums[3] + last_two * slope[2],
        )

    def piece(start, totals):
        sums, products = totals[:-1], totals[-1]
        some = [blocks_ref[start + b] for b in range(per_piece)]
        x = unit * jnp.concatenate(
            [
                jnp.concatenate([block[:, width * j : width * (j + 1)] for block in some], axis=1)
                for j in range(dims // 8)
            ],
            axis=0,
        )
        full, slope = box_terms(-x, float(GRID) * unit - x)
        ratio = jnp.concatenate(split(slope / full, 2), axis=0)
        left = jnp.concatenate(split(x, 3) + split(jnp.log(0.5 * full) * LOG2_E, 3), axis=0)
        picked = lax.dot_general(
            left, right, (((0,), (0,)), ((), ())), preferred_element_type=jnp.float32
        )
        inside = []
        for at_row in range(0, per_piece * width, 16):
            upper, sums = step(picked[at_row : at_row + 8], sums)
            lower, sums = step(picked[at_row + 8 : at_row + 16], sums)
            whole = jnp.concatenate([upper, lower], axis=0)
            inside.append(jnp.concatenate(split(whole, 2), axis=1))
        inside = jnp.concatenate(inside, axis=0)
        products = products + jnp.dot(ratio, inside, preferred_element_type=jnp.float32)
        return (*sums, products)

    def pieces(number, totals):
        for start in range(0, group, per_piece):
            totals = piece(number * group + start, totals)
        return totals

    zero = jnp.zeros((8, queries), jnp.float32)
    totals = (zero,) * (1 + LIMITED) + (jnp.zeros((2 * dims, 2 * queries), jnp.float32),)
    if count == group:
        totals = pieces(0, totals)
    else:
        totals = lax.fori_loop(0, count // group, pieces, totals)
    sums = [jnp.sum(s, axis=0, keepdims=True) for s in totals[:-1]]
    products = totals[-1]
    deriv = products[:dims, :queries] + (products[dims:, :queries] + products[:dims, queries:])
    deriv = jnp.where(limited, 0.0, deriv * (SLOPE / 4))
    for mask, s in zip(chosen, sums[1:]):
        deriv = jnp.where(mask, s * (SLOPE / 4), deriv)
    out_ref[:dims, :] = deriv
    out_ref[dims:, :] = jnp.broadcast_to(sums[0] * 0.125, (8, queries))


def finish_kernel(sample_total, query_total, *refs):
    part_refs, (counts_ref, log_ref, share_ref) = refs[:-3], refs[-3:]
    whole = tree_sum([ref[...] for ref in part_refs])
    dims, queries = whole.shape[0] - 8, whole.shape[1]
    smoothing = 1.0 / TABLE_ROWS
    estimate = whole[dims : dims + 1] / sample_total
    log_est = jnp.log(estimate + smoothing)
    log_ref[...] = log_est
    target = jnp.log(counts_ref[...].astype(jnp.float32) / TABLE_ROWS + smoothing)
    weight = 2.0 * (log_est - target) / (query_total * (estimate + smoothing))
    terms = whole[:dims] * (weight / sample_total)
    terms = jnp.concatenate([terms, jnp.zeros((queries - dims, queries), jnp.float32)], axis=0)
    share = jnp.sum(terms.T, axis=0, keepdims=True)
    for peer in range(share_ref.shape[0]):
        share_ref[peer] = share


def last_kernel(shares_ref, held_log_ref, log_ref, gradient_ref):
    total = tree_sum([shares_ref[peer] for peer in range(shares_ref.shape[0])])
    log_ref[...] = held_log_ref[0]
    gradient_ref[...] = total[0, : gradient_ref.shape[0]]


def everyone(x, axis):
    size = lax.axis_size(axis)
    return [x] + [
        lax.ppermute(x, axis, [(i, i ^ offset) for i in range(size)]) for offset in range(1, size)
    ]


def call(kernel, args, outs, scratch=(), placed=pltpu.VMEM):
    single = len(outs) == 1
    return pl.pallas_call(
        kernel,
        out_shape=outs[0] if single else outs,
        in_specs=[pl.BlockSpec(memory_space=placed)] * len(args),
        out_specs=pl.BlockSpec(memory_space=pltpu.VMEM)
        if single
        else [pl.BlockSpec(memory_space=pltpu.VMEM)] * len(outs),
        scratch_shapes=list(scratch),
        compiler_params=pltpu.CompilerParams(vmem_limit_bytes=32 << 20),
    )(*args)


def shape(*sizes):
    return jax.ShapeDtypeStruct(sizes, jnp.float32)


def on_device(samples, bounds, spread, counts):
    dims, width = samples.shape
    queries = bounds.shape[2]
    blocks, copies = lax.axis_size("blk"), lax.axis_size("grp")
    sample_total = width * blocks * copies
    query_total = queries * blocks

    packed, spread = call(
        load_kernel,
        [
            pltpu.with_memory_space_constraint(array, pltpu.HBM)
            for array in (samples, spread.reshape(1, dims))
        ],
        [
            pltpu.VMEM((blocks, 8, dims * width // 8), jnp.float32),
            pltpu.VMEM((1, dims), jnp.float32),
        ],
        [pltpu.VMEM((dims, width), jnp.float32), pltpu.SemaphoreType.DMA((2,))],
        placed=pl.ANY,
    )
    turned = [1] + [0] * (blocks - 1)
    hops = lambda b: (b & 1) + (b >> 1 & 1) + (b >> 2)
    order = sorted(range(blocks), key=lambda b: (-hops(b), -b))
    groups = [
        [b * copies + (c + turned[b]) % copies for b in order]
        for c in range(copies)
    ]
    exchange = lambda x: lax.all_to_all(x, ("blk", "grp"), 0, 0, axis_index_groups=groups)
    gathered = exchange(packed)
    part = call(
        functools.partial(terms_kernel, width),
        [gathered, bounds, spread],
        [shape(dims + 8, queries)],
    )
    log_est, share = call(
        functools.partial(finish_kernel, sample_total, query_total),
        everyone(part, "grp") + [counts.reshape(1, queries)],
        [shape(1, queries), shape(blocks, 1, queries)],
    )
    shares = exchange(share)
    return call(last_kernel, [shares, log_est], [shape(queries), shape(dims)])


def solution(mesh):
    return jax.shard_map(
        on_device,
        mesh=mesh,
        in_specs=(P(None, ("blk", "grp")), P(None, None, "blk"), P(), P("blk")),
        out_specs=(P("blk"), P()),
        check_vma=False,
    )
```

```python
import functools

import jax
import jax.numpy as jnp
from jax import lax
from jax.experimental import pallas as pl
from jax.experimental.pallas import tpu as pltpu
from jax.sharding import PartitionSpec as P

TABLE_ROWS = 1048576
GRID = 256
LIMITED = 3

ROOT_HALF = 0.7071067811865476
LOG2_E = 1.4426950408889634
SLOPE = 0.5641895835477563


def box_terms(low, high):
    low_bell = jnp.exp2((low * low) * -LOG2_E)
    high_bell = jnp.exp2((high * high) * -LOG2_E)
    return lax.erf(high) - lax.erf(low), low * low_bell - high * high_bell


def split(x, parts):
    out = []
    for _ in range(parts - 1):
        head = x.astype(jnp.bfloat16)
        out.append(head)
        x = x - head.astype(jnp.float32)
    return out + [x.astype(jnp.bfloat16)]


def tree_sum(parts):
    while len(parts) > 1:
        parts = [a + b for a, b in zip(parts[::2], parts[1::2])]
    return parts[0]


def load_kernel(x_ref, spread_ref, out_ref, held_spread, held_x, sems):
    copies = [
        pltpu.make_async_copy(x_ref, held_x, sems.at[0]),
        pltpu.make_async_copy(spread_ref, held_spread, sems.at[1]),
    ]
    for copy in copies:
        copy.start()
    copies[0].wait()
    rows = held_x.shape[0]
    packed = jnp.concatenate([held_x[8 * j : 8 * (j + 1), :] for j in range(rows // 8)], axis=1)
    for peer in range(out_ref.shape[0]):
        out_ref[peer] = packed
    copies[1].wait()


def terms_kernel(width, blocks_ref, bounds_ref, spread_ref, out_ref):
    dims, queries = bounds_ref.shape[1:]
    count = blocks_ref.shape[0]
    per_piece = 128 // width
    group = min(count, 4 * per_piece)

    low, high = bounds_ref[0], bounds_ref[1]
    limited = (high - low) != GRID
    at = lax.broadcasted_iota(jnp.int32, (dims, queries), 0)
    first = jnp.min(jnp.where(limited, at, dims), axis=0, keepdims=True)
    last = jnp.max(jnp.where(limited, at, -1), axis=0, keepdims=True)
    chosen = [at == first, limited & (at > first) & (at < last), at == last]

    row = lax.broadcasted_iota(jnp.int32, (dims, dims), 0)
    column = lax.broadcasted_iota(jnp.int32, (dims, dims), 1)
    spread = jnp.sum(jnp.where(row == column, spread_ref[...], 0.0), axis=1, keepdims=True)
    unit = ROOT_HALF / spread

    pick = lambda mask, values: jnp.sum(jnp.where(mask, values, 0.0), axis=0, keepdims=True)
    low = low.astype(jnp.float32) * unit
    high = high.astype(jnp.float32) * unit
    low_at = [pick(mask, low) for mask in chosen]
    high_at = [pick(mask, high) for mask in chosen]

    ones = [mask.astype(jnp.float32).astype(jnp.bfloat16) for mask in chosen]
    free = jnp.where(limited, 0.0, 1.0).astype(jnp.bfloat16)
    none = jnp.zeros_like(free)
    right = jnp.concatenate(
        [jnp.concatenate(ones + [none], axis=1)] * 3
        + [jnp.concatenate([none] * LIMITED + [free], axis=1)] * 3,
        axis=0,
    )

    def step(picked, sums):
        others = jnp.exp2(picked[:, LIMITED * queries :])
        mass, slope = [], []
        for k in range(LIMITED):
            points = picked[:, k * queries : (k + 1) * queries]
            m, s = box_terms(low_at[k] - points, high_at[k] - points)
            mass.append(m)
            slope.append(s)
        pair = others * mass[0]
        last_two = pair * mass[1]
        whole = last_two * mass[2]
        return whole, (
            sums[0] + whole,
            sums[1] + (others * mass[1]) * (mass[2] * slope[0]),
            sums[2] + pair * (mass[2] * slope[1]),
            sums[3] + last_two * slope[2],
        )

    def piece(start, totals):
        sums, products = totals[:-1], totals[-1]
        some = [blocks_ref[start + b] for b in range(per_piece)]
        x = unit * jnp.concatenate(
            [
                jnp.concatenate([block[:, width * j : width * (j + 1)] for block in some], axis=1)
                for j in range(dims // 8)
            ],
            axis=0,
        )
        full, slope = box_terms(-x, float(GRID) * unit - x)
        ratio = jnp.concatenate(split(slope / full, 2), axis=0)
        left = jnp.concatenate(split(x, 3) + split(jnp.log(0.5 * full) * LOG2_E, 3), axis=0)
        picked = lax.dot_general(
            left, right, (((0,), (0,)), ((), ())), preferred_element_type=jnp.float32
        )
        inside = []
        for at_row in range(0, per_piece * width, 16):
            upper, sums = step(picked[at_row : at_row + 8], sums)
            lower, sums = step(picked[at_row + 8 : at_row + 16], sums)
            whole = jnp.concatenate([upper, lower], axis=0)
            inside.append(jnp.concatenate(split(whole, 2), axis=1))
        inside = jnp.concatenate(inside, axis=0)
        products = products + jnp.dot(ratio, inside, preferred_element_type=jnp.float32)
        return (*sums, products)

    def pieces(number, totals):
        for start in range(0, group, per_piece):
            totals = piece(number * group + start, totals)
        return totals

    zero = jnp.zeros((8, queries), jnp.float32)
    totals = (zero,) * (1 + LIMITED) + (jnp.zeros((2 * dims, 2 * queries), jnp.float32),)
    if count == group:
        totals = pieces(0, totals)
    else:
        totals = lax.fori_loop(0, count // group, pieces, totals)
    sums = [jnp.sum(s, axis=0, keepdims=True) for s in totals[:-1]]
    products = totals[-1]
    deriv = products[:dims, :queries] + (products[dims:, :queries] + products[:dims, queries:])
    deriv = jnp.where(limited, 0.0, deriv * (SLOPE / 4))
    for mask, s in zip(chosen, sums[1:]):
        deriv = jnp.where(mask, s * (SLOPE / 4), deriv)
    out_ref[:dims, :] = deriv
    out_ref[dims:, :] = jnp.broadcast_to(sums[0] * 0.125, (8, queries))


def finish_kernel(sample_total, query_total, *refs):
    part_refs, (counts_ref, log_ref, share_ref) = refs[:-3], refs[-3:]
    whole = tree_sum([ref[...] for ref in part_refs])
    dims, queries = whole.shape[0] - 8, whole.shape[1]
    smoothing = 1.0 / TABLE_ROWS
    estimate = whole[dims : dims + 1] / sample_total
    log_est = jnp.log(estimate + smoothing)
    log_ref[...] = log_est
    target = jnp.log(counts_ref[...].astype(jnp.float32) / TABLE_ROWS + smoothing)
    weight = 2.0 * (log_est - target) / (query_total * (estimate + smoothing))
    terms = whole[:dims] * (weight / sample_total)
    share = jnp.sum(terms.T, axis=0, keepdims=True)
    share = jnp.concatenate([share, jnp.zeros((1, queries - dims), jnp.float32)], axis=1)
    for peer in range(share_ref.shape[0]):
        share_ref[peer] = share


def last_kernel(shares_ref, held_log_ref, log_ref, gradient_ref):
    total = tree_sum([shares_ref[peer] for peer in range(shares_ref.shape[0])])
    log_ref[...] = held_log_ref[0]
    gradient_ref[...] = total[0, : gradient_ref.shape[0]]


def everyone(x, axis):
    size = lax.axis_size(axis)
    return [x] + [
        lax.ppermute(x, axis, [(i, i ^ offset) for i in range(size)]) for offset in range(1, size)
    ]


def call(kernel, args, outs, scratch=(), placed=pltpu.VMEM):
    single = len(outs) == 1
    return pl.pallas_call(
        kernel,
        out_shape=outs[0] if single else outs,
        in_specs=[pl.BlockSpec(memory_space=placed)] * len(args),
        out_specs=pl.BlockSpec(memory_space=pltpu.VMEM)
        if single
        else [pl.BlockSpec(memory_space=pltpu.VMEM)] * len(outs),
        scratch_shapes=list(scratch),
        compiler_params=pltpu.CompilerParams(vmem_limit_bytes=32 << 20),
    )(*args)


def shape(*sizes):
    return jax.ShapeDtypeStruct(sizes, jnp.float32)


def on_device(samples, bounds, spread, counts):
    dims, width = samples.shape
    queries = bounds.shape[2]
    blocks, copies = lax.axis_size("blk"), lax.axis_size("grp")
    sample_total = width * blocks * copies
    query_total = queries * blocks

    packed, spread = call(
        load_kernel,
        [
            pltpu.with_memory_space_constraint(array, pltpu.HBM)
            for array in (samples, spread.reshape(1, dims))
        ],
        [
            pltpu.VMEM((blocks, 8, dims * width // 8), jnp.float32),
            pltpu.VMEM((1, dims), jnp.float32),
        ],
        [pltpu.VMEM((dims, width), jnp.float32), pltpu.SemaphoreType.DMA((2,))],
        placed=pl.ANY,
    )
    turned = [1] + [0] * (blocks - 1)
    hops = lambda b: (b & 1) + (b >> 1 & 1) + (b >> 2)
    order = sorted(range(blocks), key=lambda b: (-hops(b), -b))
    groups = [
        [b * copies + (c + turned[b]) % copies for b in order]
        for c in range(copies)
    ]
    exchange = lambda x: lax.all_to_all(x, ("blk", "grp"), 0, 0, axis_index_groups=groups)
    gathered = exchange(packed)
    part = call(
        functools.partial(terms_kernel, width),
        [gathered, bounds, spread],
        [shape(dims + 8, queries)],
    )
    log_est, share = call(
        functools.partial(finish_kernel, sample_total, query_total),
        everyone(part, "grp") + [counts.reshape(1, queries)],
        [shape(1, queries), shape(blocks, 1, queries)],
    )
    shares = exchange(share)
    return call(last_kernel, [shares, log_est], [shape(queries), shape(dims)])


def solution(mesh):
    return jax.shard_map(
        on_device,
        mesh=mesh,
        in_specs=(P(None, ("blk", "grp")), P(None, None, "blk"), P(), P("blk")),
        out_specs=(P("blk"), P()),
        check_vma=False,
    )
```

```python
import functools

import jax
import jax.numpy as jnp
from jax import lax
from jax.experimental import pallas as pl
from jax.experimental.pallas import tpu as pltpu
from jax.sharding import PartitionSpec as P

TABLE_ROWS = 1048576
GRID = 256
LIMITED = 3

ROOT_HALF = 0.7071067811865476
LOG2_E = 1.4426950408889634
SLOPE = 0.5641895835477563


def box_terms(low, high):
    low_bell = jnp.exp2((low * low) * -LOG2_E)
    high_bell = jnp.exp2((high * high) * -LOG2_E)
    return lax.erf(high) - lax.erf(low), low * low_bell - high * high_bell


def split(x, parts):
    out = []
    for _ in range(parts - 1):
        head = x.astype(jnp.bfloat16)
        out.append(head)
        x = x - head.astype(jnp.float32)
    return out + [x.astype(jnp.bfloat16)]


def tree_sum(parts):
    while len(parts) > 1:
        parts = [a + b for a, b in zip(parts[::2], parts[1::2])]
    return parts[0]


def load_kernel(x_ref, spread_ref, out_ref, held_spread, held_x, sems):
    copies = [
        pltpu.make_async_copy(x_ref, held_x, sems.at[0]),
        pltpu.make_async_copy(spread_ref, held_spread, sems.at[1]),
    ]
    for copy in copies:
        copy.start()
    copies[0].wait()
    rows = held_x.shape[0]
    packed = jnp.concatenate([held_x[8 * j : 8 * (j + 1), :] for j in range(rows // 8)], axis=1)
    for peer in range(out_ref.shape[0]):
        out_ref[peer] = packed
    copies[1].wait()


def terms_kernel(width, blocks_ref, bounds_ref, spread_ref, out_ref):
    dims, queries = bounds_ref.shape[1:]
    count = blocks_ref.shape[0]
    per_piece = 128 // width
    group = min(count, 4 * per_piece)

    low, high = bounds_ref[0], bounds_ref[1]
    limited = (high - low) != GRID
    at = lax.broadcasted_iota(jnp.int32, (dims, queries), 0)
    first = jnp.min(jnp.where(limited, at, dims), axis=0, keepdims=True)
    last = jnp.max(jnp.where(limited, at, -1), axis=0, keepdims=True)
    chosen = [at == first, limited & (at > first) & (at < last), at == last]

    row = lax.broadcasted_iota(jnp.int32, (dims, dims), 0)
    column = lax.broadcasted_iota(jnp.int32, (dims, dims), 1)
    spread = jnp.sum(jnp.where(row == column, spread_ref[...], 0.0), axis=1, keepdims=True)
    unit = ROOT_HALF / spread

    pick = lambda mask, values: jnp.sum(jnp.where(mask, values, 0.0), axis=0, keepdims=True)
    low = low.astype(jnp.float32) * unit
    high = high.astype(jnp.float32) * unit
    low_at = [pick(mask, low) for mask in chosen]
    high_at = [pick(mask, high) for mask in chosen]

    ones = [mask.astype(jnp.float32).astype(jnp.bfloat16) for mask in chosen]
    free = jnp.where(limited, 0.0, 1.0).astype(jnp.bfloat16)
    none = jnp.zeros_like(free)
    right = jnp.concatenate(
        [jnp.concatenate(ones + [none], axis=1)] * 3
        + [jnp.concatenate([none] * LIMITED + [free], axis=1)] * 3,
        axis=0,
    )

    def step(picked, sums):
        others = jnp.exp2(picked[:, LIMITED * queries :])
        mass, slope = [], []
        for k in range(LIMITED):
            points = picked[:, k * queries : (k + 1) * queries]
            m, s = box_terms(low_at[k] - points, high_at[k] - points)
            mass.append(m)
            slope.append(s)
        pair = others * mass[0]
        last_two = pair * mass[1]
        whole = last_two * mass[2]
        return whole, (
            sums[0] + whole,
            sums[1] + (others * mass[1]) * (mass[2] * slope[0]),
            sums[2] + pair * (mass[2] * slope[1]),
            sums[3] + last_two * slope[2],
        )

    def piece(start, totals):
        sums, products = totals[:-1], totals[-1]
        some = [blocks_ref[start + b] for b in range(per_piece)]
        x = unit * jnp.concatenate(
            [
                jnp.concatenate([block[:, width * j : width * (j + 1)] for block in some], axis=1)
                for j in range(dims // 8)
            ],
            axis=0,
        )
        full, slope = box_terms(-x, float(GRID) * unit - x)
        ratio = jnp.concatenate(split(slope / full, 2), axis=0)
        left = jnp.concatenate(split(x, 3) + split(jnp.log(0.5 * full) * LOG2_E, 3), axis=0)
        picked = lax.dot_general(
            left, right, (((0,), (0,)), ((), ())), preferred_element_type=jnp.float32
        )
        inside = []
        for at_row in range(0, per_piece * width, 16):
            whole, sums = step(picked[at_row : at_row + 16], sums)
            inside.append(jnp.concatenate(split(whole, 2), axis=1))
        inside = jnp.concatenate(inside, axis=0)
        products = products + jnp.dot(ratio, inside, preferred_element_type=jnp.float32)
        return (*sums, products)

    def pieces(number, totals):
        for start in range(0, group, per_piece):
            totals = piece(number * group + start, totals)
        return totals

    zero = jnp.zeros((16, queries), jnp.float32)
    totals = (zero,) * (1 + LIMITED) + (jnp.zeros((2 * dims, 2 * queries), jnp.float32),)
    if count == group:
        totals = pieces(0, totals)
    else:
        totals = lax.fori_loop(0, count // group, pieces, totals)
    sums = [jnp.sum(s, axis=0, keepdims=True) for s in totals[:-1]]
    products = totals[-1]
    deriv = products[:dims, :queries] + (products[dims:, :queries] + products[:dims, queries:])
    deriv = jnp.where(limited, 0.0, deriv * (SLOPE / 4))
    for mask, s in zip(chosen, sums[1:]):
        deriv = jnp.where(mask, s * (SLOPE / 4), deriv)
    out_ref[:dims, :] = deriv
    out_ref[dims:, :] = jnp.broadcast_to(sums[0] * 0.125, (8, queries))


def finish_kernel(sample_total, query_total, *refs):
    part_refs, (counts_ref, log_ref, share_ref) = refs[:-3], refs[-3:]
    whole = tree_sum([ref[...] for ref in part_refs])
    dims, queries = whole.shape[0] - 8, whole.shape[1]
    smoothing = 1.0 / TABLE_ROWS
    estimate = whole[dims : dims + 1] / sample_total
    log_est = jnp.log(estimate + smoothing)
    log_ref[...] = log_est
    target = jnp.log(counts_ref[...].astype(jnp.float32) / TABLE_ROWS + smoothing)
    weight = 2.0 * (log_est - target) / (query_total * (estimate + smoothing))
    terms = whole[:dims] * (weight / sample_total)
    terms = jnp.concatenate([terms, jnp.zeros((queries - dims, queries), jnp.float32)], axis=0)
    share = jnp.sum(terms.T, axis=0, keepdims=True)
    for peer in range(share_ref.shape[0]):
        share_ref[peer] = share


def last_kernel(shares_ref, held_log_ref, log_ref, gradient_ref):
    total = tree_sum([shares_ref[peer] for peer in range(shares_ref.shape[0])])
    log_ref[...] = held_log_ref[0]
    gradient_ref[...] = total[0, : gradient_ref.shape[0]]


def everyone(x, axis):
    size = lax.axis_size(axis)
    return [x] + [
        lax.ppermute(x, axis, [(i, i ^ offset) for i in range(size)]) for offset in range(1, size)
    ]


def call(kernel, args, outs, scratch=(), placed=pltpu.VMEM):
    single = len(outs) == 1
    return pl.pallas_call(
        kernel,
        out_shape=outs[0] if single else outs,
        in_specs=[pl.BlockSpec(memory_space=placed)] * len(args),
        out_specs=pl.BlockSpec(memory_space=pltpu.VMEM)
        if single
        else [pl.BlockSpec(memory_space=pltpu.VMEM)] * len(outs),
        scratch_shapes=list(scratch),
        compiler_params=pltpu.CompilerParams(vmem_limit_bytes=32 << 20),
    )(*args)


def shape(*sizes):
    return jax.ShapeDtypeStruct(sizes, jnp.float32)


def on_device(samples, bounds, spread, counts):
    dims, width = samples.shape
    queries = bounds.shape[2]
    blocks, copies = lax.axis_size("blk"), lax.axis_size("grp")
    sample_total = width * blocks * copies
    query_total = queries * blocks

    packed, spread = call(
        load_kernel,
        [
            pltpu.with_memory_space_constraint(array, pltpu.HBM)
            for array in (samples, spread.reshape(1, dims))
        ],
        [
            pltpu.VMEM((blocks, 8, dims * width // 8), jnp.float32),
            pltpu.VMEM((1, dims), jnp.float32),
        ],
        [pltpu.VMEM((dims, width), jnp.float32), pltpu.SemaphoreType.DMA((2,))],
        placed=pl.ANY,
    )
    turned = [1] + [0] * (blocks - 1)
    hops = lambda b: (b & 1) + (b >> 1 & 1) + (b >> 2)
    order = sorted(range(blocks), key=lambda b: (-hops(b), -b))
    def exchange(x, orders):
        groups = [
            [b * copies + (c + turned[b]) % copies for b in orders[c]] for c in range(copies)
        ]
        return lax.all_to_all(x, ("blk", "grp"), 0, 0, axis_index_groups=groups)

    other_way = [b for b in reversed(order) if b != 0] + [0]
    gathered = exchange(packed, [order] * (copies - 1) + [other_way])
    part = call(
        functools.partial(terms_kernel, width),
        [gathered, bounds, spread],
        [shape(dims + 8, queries)],
    )
    log_est, share = call(
        functools.partial(finish_kernel, sample_total, query_total),
        everyone(part, "grp") + [counts.reshape(1, queries)],
        [shape(1, queries), shape(blocks, 1, queries)],
    )
    shares = exchange(share, [order] * copies)
    return call(last_kernel, [shares, log_est], [shape(queries), shape(dims)])


def solution(mesh):
    return jax.shard_map(
        on_device,
        mesh=mesh,
        in_specs=(P(None, ("blk", "grp")), P(None, None, "blk"), P(), P("blk")),
        out_specs=(P("blk"), P()),
        check_vma=False,
    )
```

```python
import functools

import jax
import jax.numpy as jnp
from jax import lax
from jax.experimental import pallas as pl
from jax.experimental.pallas import tpu as pltpu
from jax.sharding import PartitionSpec as P

TABLE_ROWS = 1048576
GRID = 256
LIMITED = 3

ROOT_HALF = 0.7071067811865476
LOG2_E = 1.4426950408889634
SLOPE = 0.5641895835477563


def box_terms(low, high):
    low_bell = jnp.exp2((low * low) * -LOG2_E)
    high_bell = jnp.exp2((high * high) * -LOG2_E)
    return lax.erf(high) - lax.erf(low), low * low_bell - high * high_bell


def split(x, parts):
    out = []
    for _ in range(parts - 1):
        head = x.astype(jnp.bfloat16)
        out.append(head)
        x = x - head.astype(jnp.float32)
    return out + [x.astype(jnp.bfloat16)]


def tree_sum(parts):
    while len(parts) > 1:
        parts = [a + b for a, b in zip(parts[::2], parts[1::2])]
    return parts[0]


def load_kernel(x_ref, spread_ref, out_ref, held_spread, held_x, sems):
    bands = [pl.ds(8 * j, 8) for j in range(held_x.shape[0] // 8)]
    copies = [
        pltpu.make_async_copy(x_ref.at[band], held_x.at[band], sems.at[j])
        for j, band in enumerate(bands)
    ]
    copies.append(pltpu.make_async_copy(spread_ref, held_spread, sems.at[len(bands)]))
    for copy in copies:
        copy.start()
    pieces = []
    for copy, band in zip(copies, bands):
        copy.wait()
        pieces.append(held_x[band, :])
    packed = jnp.concatenate(pieces, axis=1)
    for peer in range(out_ref.shape[0]):
        out_ref[peer] = packed
    copies[-1].wait()


def terms_kernel(width, blocks_ref, bounds_ref, spread_ref, out_ref):
    dims, queries = bounds_ref.shape[1:]
    count = blocks_ref.shape[0]
    per_piece = 128 // width
    group = min(count, 4 * per_piece)

    low, high = bounds_ref[0], bounds_ref[1]
    limited = (high - low) != GRID
    at = lax.broadcasted_iota(jnp.int32, (dims, queries), 0)
    first = jnp.min(jnp.where(limited, at, dims), axis=0, keepdims=True)
    last = jnp.max(jnp.where(limited, at, -1), axis=0, keepdims=True)
    chosen = [at == first, limited & (at > first) & (at < last), at == last]

    row = lax.broadcasted_iota(jnp.int32, (dims, dims), 0)
    column = lax.broadcasted_iota(jnp.int32, (dims, dims), 1)
    spread = jnp.sum(jnp.where(row == column, spread_ref[...], 0.0), axis=1, keepdims=True)
    unit = ROOT_HALF / spread

    pick = lambda mask, values: jnp.sum(jnp.where(mask, values, 0.0), axis=0, keepdims=True)
    low = low.astype(jnp.float32) * unit
    high = high.astype(jnp.float32) * unit
    low_at = [pick(mask, low) for mask in chosen]
    high_at = [pick(mask, high) for mask in chosen]

    ones = [mask.astype(jnp.float32).astype(jnp.bfloat16) for mask in chosen]
    free = jnp.where(limited, 0.0, 1.0).astype(jnp.bfloat16)
    none = jnp.zeros_like(free)
    right = jnp.concatenate(
        [jnp.concatenate(ones + [none], axis=1)] * 3
        + [jnp.concatenate([none] * LIMITED + [free], axis=1)] * 3,
        axis=0,
    )

    def step(picked, sums):
        others = jnp.exp2(picked[:, LIMITED * queries :])
        mass, slope = [], []
        for k in range(LIMITED):
            points = picked[:, k * queries : (k + 1) * queries]
            m, s = box_terms(low_at[k] - points, high_at[k] - points)
            mass.append(m)
            slope.append(s)
        pair = others * mass[0]
        last_two = pair * mass[1]
        whole = last_two * mass[2]
        return whole, (
            sums[0] + whole,
            sums[1] + (others * mass[1]) * (mass[2] * slope[0]),
            sums[2] + pair * (mass[2] * slope[1]),
            sums[3] + last_two * slope[2],
        )

    def piece(start, totals):
        sums, products = totals[:-1], totals[-1]
        some = [blocks_ref[start + b] for b in range(per_piece)]
        x = unit * jnp.concatenate(
            [
                jnp.concatenate([block[:, width * j : width * (j + 1)] for block in some], axis=1)
                for j in range(dims // 8)
            ],
            axis=0,
        )
        full, slope = box_terms(-x, float(GRID) * unit - x)
        ratio = jnp.concatenate(split(slope / full, 2), axis=0)
        left = jnp.concatenate(split(x, 3) + split(jnp.log(0.5 * full) * LOG2_E, 3), axis=0)
        picked = lax.dot_general(
            left, right, (((0,), (0,)), ((), ())), preferred_element_type=jnp.float32
        )
        inside = []
        for at_row in range(0, per_piece * width, 16):
            whole, sums = step(picked[at_row : at_row + 16], sums)
            inside.append(jnp.concatenate(split(whole, 2), axis=1))
        inside = jnp.concatenate(inside, axis=0)
        products = products + jnp.dot(ratio, inside, preferred_element_type=jnp.float32)
        return (*sums, products)

    def pieces(number, totals):
        for start in range(0, group, per_piece):
            totals = piece(number * group + start, totals)
        return totals

    zero = jnp.zeros((16, queries), jnp.float32)
    totals = (zero,) * (1 + LIMITED) + (jnp.zeros((2 * dims, 2 * queries), jnp.float32),)
    if count == group:
        totals = pieces(0, totals)
    else:
        totals = lax.fori_loop(0, count // group, pieces, totals)
    sums = [jnp.sum(s, axis=0, keepdims=True) for s in totals[:-1]]
    products = totals[-1]
    deriv = products[:dims, :queries] + (products[dims:, :queries] + products[:dims, queries:])
    deriv = jnp.where(limited, 0.0, deriv * (SLOPE / 4))
    for mask, s in zip(chosen, sums[1:]):
        deriv = jnp.where(mask, s * (SLOPE / 4), deriv)
    out_ref[:dims, :] = deriv
    out_ref[dims:, :] = jnp.broadcast_to(sums[0] * 0.125, (8, queries))


def finish_kernel(sample_total, query_total, *refs):
    part_refs, (counts_ref, log_ref, share_ref) = refs[:-3], refs[-3:]
    whole = tree_sum([ref[...] for ref in part_refs])
    dims, queries = whole.shape[0] - 8, whole.shape[1]
    smoothing = 1.0 / TABLE_ROWS
    estimate = whole[dims : dims + 1] / sample_total
    log_est = jnp.log(estimate + smoothing)
    log_ref[...] = log_est
    target = jnp.log(counts_ref[...].astype(jnp.float32) / TABLE_ROWS + smoothing)
    weight = 2.0 * (log_est - target) / (query_total * (estimate + smoothing))
    terms = whole[:dims] * (weight / sample_total)
    terms = jnp.concatenate([terms, jnp.zeros((queries - dims, queries), jnp.float32)], axis=0)
    share = jnp.sum(terms.T, axis=0, keepdims=True)
    for peer in range(share_ref.shape[0]):
        share_ref[peer] = share


def last_kernel(shares_ref, held_log_ref, log_ref, gradient_ref):
    total = tree_sum([shares_ref[peer] for peer in range(shares_ref.shape[0])])
    log_ref[...] = held_log_ref[0]
    gradient_ref[...] = total[0, : gradient_ref.shape[0]]


def everyone(x, axis):
    size = lax.axis_size(axis)
    return [x] + [
        lax.ppermute(x, axis, [(i, i ^ offset) for i in range(size)]) for offset in range(1, size)
    ]


def call(kernel, args, outs, scratch=(), placed=pltpu.VMEM):
    single = len(outs) == 1
    return pl.pallas_call(
        kernel,
        out_shape=outs[0] if single else outs,
        in_specs=[pl.BlockSpec(memory_space=placed)] * len(args),
        out_specs=pl.BlockSpec(memory_space=pltpu.VMEM)
        if single
        else [pl.BlockSpec(memory_space=pltpu.VMEM)] * len(outs),
        scratch_shapes=list(scratch),
        compiler_params=pltpu.CompilerParams(vmem_limit_bytes=32 << 20),
    )(*args)


def shape(*sizes):
    return jax.ShapeDtypeStruct(sizes, jnp.float32)


def on_device(samples, bounds, spread, counts):
    dims, width = samples.shape
    queries = bounds.shape[2]
    blocks, copies = lax.axis_size("blk"), lax.axis_size("grp")
    sample_total = width * blocks * copies
    query_total = queries * blocks

    packed, spread = call(
        load_kernel,
        [
            pltpu.with_memory_space_constraint(array, pltpu.HBM)
            for array in (samples, spread.reshape(1, dims))
        ],
        [
            pltpu.VMEM((blocks, 8, dims * width // 8), jnp.float32),
            pltpu.VMEM((1, dims), jnp.float32),
        ],
        [pltpu.VMEM((dims, width), jnp.float32), pltpu.SemaphoreType.DMA((dims // 8 + 1,))],
        placed=pl.ANY,
    )
    turned = [1] + [0] * (blocks - 1)
    hops = lambda b: (b & 1) + (b >> 1 & 1) + (b >> 2)
    order = sorted(range(blocks), key=lambda b: (-hops(b), -b))
    groups = [
        [b * copies + (c + turned[b]) % copies for b in order]
        for c in range(copies)
    ]
    exchange = lambda x: lax.all_to_all(x, ("blk", "grp"), 0, 0, axis_index_groups=groups)
    gathered = exchange(packed)
    part = call(
        functools.partial(terms_kernel, width),
        [gathered, bounds, spread],
        [shape(dims + 8, queries)],
    )
    log_est, share = call(
        functools.partial(finish_kernel, sample_total, query_total),
        everyone(part, "grp") + [counts.reshape(1, queries)],
        [shape(1, queries), shape(blocks, 1, queries)],
    )
    shares = exchange(share)
    return call(last_kernel, [shares, log_est], [shape(queries), shape(dims)])


def solution(mesh):
    return jax.shard_map(
        on_device,
        mesh=mesh,
        in_specs=(P(None, ("blk", "grp")), P(None, None, "blk"), P(), P("blk")),
        out_specs=(P("blk"), P()),
        check_vma=False,
    )
```

```python
import functools

import jax
import jax.numpy as jnp
from jax import lax
from jax.experimental import pallas as pl
from jax.experimental.pallas import tpu as pltpu
from jax.sharding import PartitionSpec as P

TABLE_ROWS = 1048576
GRID = 256
LIMITED = 3

ROOT_HALF = 0.7071067811865476
LOG2_E = 1.4426950408889634
SLOPE = 0.5641895835477563


def box_terms(low, high):
    low_bell = jnp.exp2((low * low) * -LOG2_E)
    high_bell = jnp.exp2((high * high) * -LOG2_E)
    return lax.erf(high) - lax.erf(low), low * low_bell - high * high_bell


def split(x, parts):
    out = []
    for _ in range(parts - 1):
        head = x.astype(jnp.bfloat16)
        out.append(head)
        x = x - head.astype(jnp.float32)
    return out + [x.astype(jnp.bfloat16)]


def tree_sum(parts):
    while len(parts) > 1:
        parts = [a + b for a, b in zip(parts[::2], parts[1::2])]
    return parts[0]


def load_kernel(x_ref, spread_ref, out_ref, held_spread, held_x, sems):
    copies = [
        pltpu.make_async_copy(x_ref, held_x, sems.at[0]),
        pltpu.make_async_copy(spread_ref, held_spread, sems.at[1]),
    ]
    for copy in copies:
        copy.start()
    copies[0].wait()
    rows = held_x.shape[0]
    packed = jnp.concatenate([held_x[8 * j : 8 * (j + 1), :] for j in range(rows // 8)], axis=1)
    for peer in range(out_ref.shape[0]):
        out_ref[peer] = packed
    copies[1].wait()


def unit_kernel(spread_ref, unit_ref):
    dims = spread_ref.shape[1]
    row = lax.broadcasted_iota(jnp.int32, (dims, dims), 0)
    column = lax.broadcasted_iota(jnp.int32, (dims, dims), 1)
    unit = jnp.where(row == column, ROOT_HALF / spread_ref[...], 0.0)
    unit_ref[...] = jnp.broadcast_to(jnp.sum(unit, axis=1, keepdims=True), unit_ref.shape)


def terms_kernel(width, blocks_ref, bounds_ref, unit_ref, out_ref):
    dims, queries = bounds_ref.shape[1:]
    count = blocks_ref.shape[0]
    per_piece = 128 // width
    group = min(count, 4 * per_piece)

    low, high = bounds_ref[0], bounds_ref[1]
    limited = (high - low) != GRID
    at = lax.broadcasted_iota(jnp.int32, (dims, queries), 0)
    first = jnp.min(jnp.where(limited, at, dims), axis=0, keepdims=True)
    last = jnp.max(jnp.where(limited, at, -1), axis=0, keepdims=True)
    chosen = [at == first, limited & (at > first) & (at < last), at == last]

    unit = unit_ref[...]

    pick = lambda mask, values: jnp.sum(jnp.where(mask, values, 0.0), axis=0, keepdims=True)
    low = low.astype(jnp.float32) * unit
    high = high.astype(jnp.float32) * unit
    low_at = [pick(mask, low) for mask in chosen]
    high_at = [pick(mask, high) for mask in chosen]

    ones = [mask.astype(jnp.float32).astype(jnp.bfloat16) for mask in chosen]
    free = jnp.where(limited, 0.0, 1.0).astype(jnp.bfloat16)
    none = jnp.zeros_like(free)
    right = jnp.concatenate(
        [jnp.concatenate(ones + [none], axis=1)] * 3
        + [jnp.concatenate([none] * LIMITED + [free], axis=1)] * 3,
        axis=0,
    )

    def step(picked, sums):
        others = jnp.exp2(picked[:, LIMITED * queries :])
        mass, slope = [], []
        for k in range(LIMITED):
            points = picked[:, k * queries : (k + 1) * queries]
            m, s = box_terms(low_at[k] - points, high_at[k] - points)
            mass.append(m)
            slope.append(s)
        pair = others * mass[0]
        last_two = pair * mass[1]
        whole = last_two * mass[2]
        return whole, (
            sums[0] + whole,
            sums[1] + (others * mass[1]) * (mass[2] * slope[0]),
            sums[2] + pair * (mass[2] * slope[1]),
            sums[3] + last_two * slope[2],
        )

    def piece(start, totals):
        sums, products = totals[:-1], totals[-1]
        some = [blocks_ref[start + b] for b in range(per_piece)]
        x = unit * jnp.concatenate(
            [
                jnp.concatenate([block[:, width * j : width * (j + 1)] for block in some], axis=1)
                for j in range(dims // 8)
            ],
            axis=0,
        )
        full, slope = box_terms(-x, float(GRID) * unit - x)
        ratio = jnp.concatenate(split(slope / full, 2), axis=0)
        left = jnp.concatenate(split(x, 3) + split(jnp.log(0.5 * full) * LOG2_E, 3), axis=0)
        picked = lax.dot_general(
            left, right, (((0,), (0,)), ((), ())), preferred_element_type=jnp.float32
        )
        inside = []
        for at_row in range(0, per_piece * width, 16):
            whole, sums = step(picked[at_row : at_row + 16], sums)
            inside.append(jnp.concatenate(split(whole, 2), axis=1))
        inside = jnp.concatenate(inside, axis=0)
        products = products + jnp.dot(ratio, inside, preferred_element_type=jnp.float32)
        return (*sums, products)

    def pieces(number, totals):
        for start in range(0, group, per_piece):
            totals = piece(number * group + start, totals)
        return totals

    zero = jnp.zeros((16, queries), jnp.float32)
    totals = (zero,) * (1 + LIMITED) + (jnp.zeros((2 * dims, 2 * queries), jnp.float32),)
    if count == group:
        totals = pieces(0, totals)
    else:
        totals = lax.fori_loop(0, count // group, pieces, totals)
    sums = [jnp.sum(s, axis=0, keepdims=True) for s in totals[:-1]]
    products = totals[-1]
    deriv = products[:dims, :queries] + (products[dims:, :queries] + products[:dims, queries:])
    deriv = jnp.where(limited, 0.0, deriv * (SLOPE / 4))
    for mask, s in zip(chosen, sums[1:]):
        deriv = jnp.where(mask, s * (SLOPE / 4), deriv)
    out_ref[:dims, :] = deriv
    out_ref[dims:, :] = jnp.broadcast_to(sums[0] * 0.125, (8, queries))


def finish_kernel(sample_total, query_total, *refs):
    part_refs, (counts_ref, log_ref, share_ref) = refs[:-3], refs[-3:]
    whole = tree_sum([ref[...] for ref in part_refs])
    dims, queries = whole.shape[0] - 8, whole.shape[1]
    smoothing = 1.0 / TABLE_ROWS
    estimate = whole[dims : dims + 1] / sample_total
    log_est = jnp.log(estimate + smoothing)
    log_ref[...] = log_est
    target = jnp.log(counts_ref[...].astype(jnp.float32) / TABLE_ROWS + smoothing)
    weight = 2.0 * (log_est - target) / (query_total * (estimate + smoothing))
    terms = whole[:dims] * (weight / sample_total)
    terms = jnp.concatenate([terms, jnp.zeros((queries - dims, queries), jnp.float32)], axis=0)
    share = jnp.sum(terms.T, axis=0, keepdims=True)
    for peer in range(share_ref.shape[0]):
        share_ref[peer] = share


def last_kernel(shares_ref, held_log_ref, log_ref, gradient_ref):
    total = tree_sum([shares_ref[peer] for peer in range(shares_ref.shape[0])])
    log_ref[...] = held_log_ref[0]
    gradient_ref[...] = total[0, : gradient_ref.shape[0]]


def everyone(x, axis):
    size = lax.axis_size(axis)
    return [x] + [
        lax.ppermute(x, axis, [(i, i ^ offset) for i in range(size)]) for offset in range(1, size)
    ]


def call(kernel, args, outs, scratch=(), placed=pltpu.VMEM):
    single = len(outs) == 1
    return pl.pallas_call(
        kernel,
        out_shape=outs[0] if single else outs,
        in_specs=[pl.BlockSpec(memory_space=placed)] * len(args),
        out_specs=pl.BlockSpec(memory_space=pltpu.VMEM)
        if single
        else [pl.BlockSpec(memory_space=pltpu.VMEM)] * len(outs),
        scratch_shapes=list(scratch),
        compiler_params=pltpu.CompilerParams(vmem_limit_bytes=32 << 20),
    )(*args)


def shape(*sizes):
    return jax.ShapeDtypeStruct(sizes, jnp.float32)


def on_device(samples, bounds, spread, counts):
    dims, width = samples.shape
    queries = bounds.shape[2]
    blocks, copies = lax.axis_size("blk"), lax.axis_size("grp")
    sample_total = width * blocks * copies
    query_total = queries * blocks

    packed, spread = call(
        load_kernel,
        [
            pltpu.with_memory_space_constraint(array, pltpu.HBM)
            for array in (samples, spread.reshape(1, dims))
        ],
        [
            pltpu.VMEM((blocks, 8, dims * width // 8), jnp.float32),
            pltpu.VMEM((1, dims), jnp.float32),
        ],
        [pltpu.VMEM((dims, width), jnp.float32), pltpu.SemaphoreType.DMA((2,))],
        placed=pl.ANY,
    )
    turned = [1] + [0] * (blocks - 1)
    hops = lambda b: (b & 1) + (b >> 1 & 1) + (b >> 2)
    order = sorted(range(blocks), key=lambda b: (-hops(b), -b))
    groups = [
        [b * copies + (c + turned[b]) % copies for b in order]
        for c in range(copies)
    ]
    exchange = lambda x: lax.all_to_all(x, ("blk", "grp"), 0, 0, axis_index_groups=groups)
    gathered = exchange(packed)
    part = call(
        functools.partial(terms_kernel, width),
        [gathered, bounds, call(unit_kernel, [spread], [shape(dims, queries)])],
        [shape(dims + 8, queries)],
    )
    log_est, share = call(
        functools.partial(finish_kernel, sample_total, query_total),
        everyone(part, "grp") + [counts.reshape(1, queries)],
        [shape(1, queries), shape(blocks, 1, queries)],
    )
    shares = exchange(share)
    return call(last_kernel, [shares, log_est], [shape(queries), shape(dims)])


def solution(mesh):
    return jax.shard_map(
        on_device,
        mesh=mesh,
        in_specs=(P(None, ("blk", "grp")), P(None, None, "blk"), P(), P("blk")),
        out_specs=(P("blk"), P()),
        check_vma=False,
    )
```

```python
import functools

import jax
import jax.numpy as jnp
from jax import lax
from jax.experimental import pallas as pl
from jax.experimental.pallas import tpu as pltpu
from jax.sharding import PartitionSpec as P

TABLE_ROWS = 1048576
GRID = 256
LIMITED = 3

ROOT_HALF = 0.7071067811865476
LOG2_E = 1.4426950408889634
SLOPE = 0.5641895835477563


def box_terms(low, high):
    low_bell = jnp.exp2((low * low) * -LOG2_E)
    high_bell = jnp.exp2((high * high) * -LOG2_E)
    return lax.erf(high) - lax.erf(low), low * low_bell - high * high_bell


def split(x, parts):
    out = []
    for _ in range(parts - 1):
        head = x.astype(jnp.bfloat16)
        out.append(head)
        x = x - head.astype(jnp.float32)
    return out + [x.astype(jnp.bfloat16)]


def tree_sum(parts):
    while len(parts) > 1:
        parts = [a + b for a, b in zip(parts[::2], parts[1::2])]
    return parts[0]


def load_kernel(
    x_ref, bounds_ref, spread_ref, counts_ref,
    out_ref, held_bounds, held_spread, target_ref,
    held_x, held_counts, sems,
):
    sources = (x_ref, bounds_ref, spread_ref, counts_ref)
    targets = (held_x, held_bounds, held_spread, held_counts)
    copies = [
        pltpu.make_async_copy(source, target, sems.at[i])
        for i, (source, target) in enumerate(zip(sources, targets))
    ]
    for copy in copies:
        copy.start()
    copies[0].wait()
    rows = held_x.shape[0]
    packed = jnp.concatenate([held_x[8 * j : 8 * (j + 1), :] for j in range(rows // 8)], axis=1)
    for peer in range(out_ref.shape[0]):
        out_ref[peer] = packed
    for copy in copies[1:]:
        copy.wait()
    smoothing = 1.0 / TABLE_ROWS
    target_ref[...] = jnp.log(held_counts[...].astype(jnp.float32) / TABLE_ROWS + smoothing)


def terms_kernel(width, blocks_ref, bounds_ref, spread_ref, out_ref):
    dims, queries = bounds_ref.shape[1:]
    count = blocks_ref.shape[0]
    per_piece = 128 // width
    group = min(count, 4 * per_piece)

    low, high = bounds_ref[0], bounds_ref[1]
    limited = (high - low) != GRID
    at = lax.broadcasted_iota(jnp.int32, (dims, queries), 0)
    first = jnp.min(jnp.where(limited, at, dims), axis=0, keepdims=True)
    last = jnp.max(jnp.where(limited, at, -1), axis=0, keepdims=True)
    chosen = [at == first, limited & (at > first) & (at < last), at == last]

    row = lax.broadcasted_iota(jnp.int32, (dims, dims), 0)
    column = lax.broadcasted_iota(jnp.int32, (dims, dims), 1)
    spread = jnp.sum(jnp.where(row == column, spread_ref[...], 0.0), axis=1, keepdims=True)
    unit = ROOT_HALF / spread

    pick = lambda mask, values: jnp.sum(jnp.where(mask, values, 0.0), axis=0, keepdims=True)
    low = low.astype(jnp.float32) * unit
    high = high.astype(jnp.float32) * unit
    low_at = [pick(mask, low) for mask in chosen]
    high_at = [pick(mask, high) for mask in chosen]

    ones = [mask.astype(jnp.float32).astype(jnp.bfloat16) for mask in chosen]
    free = jnp.where(limited, 0.0, 1.0).astype(jnp.bfloat16)
    none = jnp.zeros_like(free)
    right = jnp.concatenate(
        [jnp.concatenate(ones + [none], axis=1)] * 3
        + [jnp.concatenate([none] * LIMITED + [free], axis=1)] * 3,
        axis=0,
    )

    def step(picked, sums):
        others = jnp.exp2(picked[:, LIMITED * queries :])
        mass, slope = [], []
        for k in range(LIMITED):
            points = picked[:, k * queries : (k + 1) * queries]
            m, s = box_terms(low_at[k] - points, high_at[k] - points)
            mass.append(m)
            slope.append(s)
        pair = others * mass[0]
        last_two = pair * mass[1]
        whole = last_two * mass[2]
        return whole, (
            sums[0] + whole,
            sums[1] + (others * mass[1]) * (mass[2] * slope[0]),
            sums[2] + pair * (mass[2] * slope[1]),
            sums[3] + last_two * slope[2],
        )

    def piece(start, totals):
        sums, products = totals[:-1], totals[-1]
        some = [blocks_ref[start + b] for b in range(per_piece)]
        x = unit * jnp.concatenate(
            [
                jnp.concatenate([block[:, width * j : width * (j + 1)] for block in some], axis=1)
                for j in range(dims // 8)
            ],
            axis=0,
        )
        full, slope = box_terms(-x, float(GRID) * unit - x)
        ratio = jnp.concatenate(split(slope / full, 2), axis=0)
        left = jnp.concatenate(split(x, 3) + split(jnp.log(0.5 * full) * LOG2_E, 3), axis=0)
        picked = lax.dot_general(
            left, right, (((0,), (0,)), ((), ())), preferred_element_type=jnp.float32
        )
        inside = []
        for at_row in range(0, per_piece * width, 16):
            whole, sums = step(picked[at_row : at_row + 16], sums)
            inside.append(jnp.concatenate(split(whole, 2), axis=1))
        inside = jnp.concatenate(inside, axis=0)
        products = products + jnp.dot(ratio, inside, preferred_element_type=jnp.float32)
        return (*sums, products)

    def pieces(number, totals):
        for start in range(0, group, per_piece):
            totals = piece(number * group + start, totals)
        return totals

    zero = jnp.zeros((16, queries), jnp.float32)
    totals = (zero,) * (1 + LIMITED) + (jnp.zeros((2 * dims, 2 * queries), jnp.float32),)
    if count == group:
        totals = pieces(0, totals)
    else:
        totals = lax.fori_loop(0, count // group, pieces, totals)
    sums = [jnp.sum(s, axis=0, keepdims=True) for s in totals[:-1]]
    products = totals[-1]
    deriv = products[:dims, :queries] + (products[dims:, :queries] + products[:dims, queries:])
    deriv = jnp.where(limited, 0.0, deriv * (SLOPE / 4))
    for mask, s in zip(chosen, sums[1:]):
        deriv = jnp.where(mask, s * (SLOPE / 4), deriv)
    out_ref[:dims, :] = deriv
    out_ref[dims:, :] = jnp.broadcast_to(sums[0] * 0.125, (8, queries))


def finish_kernel(sample_total, query_total, *refs):
    part_refs, (target_ref, log_ref, share_ref) = refs[:-3], refs[-3:]
    whole = tree_sum([ref[...] for ref in part_refs])
    dims, queries = whole.shape[0] - 8, whole.shape[1]
    smoothing = 1.0 / TABLE_ROWS
    estimate = whole[dims : dims + 1] / sample_total
    log_est = jnp.log(estimate + smoothing)
    log_ref[...] = log_est
    weight = 2.0 * (log_est - target_ref[...]) / (query_total * (estimate + smoothing))
    terms = whole[:dims] * (weight / sample_total)
    terms = jnp.concatenate([terms, jnp.zeros((queries - dims, queries), jnp.float32)], axis=0)
    share = jnp.sum(terms.T, axis=0, keepdims=True)
    for peer in range(share_ref.shape[0]):
        share_ref[peer] = share


def last_kernel(shares_ref, held_log_ref, log_ref, gradient_ref):
    total = tree_sum([shares_ref[peer] for peer in range(shares_ref.shape[0])])
    log_ref[...] = held_log_ref[0]
    gradient_ref[...] = total[0, : gradient_ref.shape[0]]


def everyone(x, axis):
    size = lax.axis_size(axis)
    return [x] + [
        lax.ppermute(x, axis, [(i, i ^ offset) for i in range(size)]) for offset in range(1, size)
    ]


def call(kernel, args, outs, scratch=(), placed=pltpu.VMEM):
    single = len(outs) == 1
    return pl.pallas_call(
        kernel,
        out_shape=outs[0] if single else outs,
        in_specs=[pl.BlockSpec(memory_space=placed)] * len(args),
        out_specs=pl.BlockSpec(memory_space=pltpu.VMEM)
        if single
        else [pl.BlockSpec(memory_space=pltpu.VMEM)] * len(outs),
        scratch_shapes=list(scratch),
        compiler_params=pltpu.CompilerParams(vmem_limit_bytes=32 << 20),
    )(*args)


def shape(*sizes):
    return jax.ShapeDtypeStruct(sizes, jnp.float32)


def on_device(samples, bounds, spread, counts):
    dims, width = samples.shape
    queries = bounds.shape[2]
    blocks, copies = lax.axis_size("blk"), lax.axis_size("grp")
    sample_total = width * blocks * copies
    query_total = queries * blocks

    counts_vector = pltpu.VMEM((1, queries), jnp.int32)
    packed, bounds, spread, target = call(
        load_kernel,
        [
            pltpu.with_memory_space_constraint(array, pltpu.HBM)
            for array in (samples, bounds, spread.reshape(1, dims), counts.reshape(1, queries))
        ],
        [
            pltpu.VMEM((blocks, 8, dims * width // 8), jnp.float32),
            pltpu.VMEM(bounds.shape, bounds.dtype),
            pltpu.VMEM((1, dims), jnp.float32),
            pltpu.VMEM((1, queries), jnp.float32),
        ],
        [pltpu.VMEM((dims, width), jnp.float32), counts_vector, pltpu.SemaphoreType.DMA((4,))],
        placed=pl.ANY,
    )
    turned = [1] + [0] * (blocks - 1)
    def exchange(x, order):
        groups = [
            [b * copies + (c + turned[b]) % copies for b in order] for c in range(copies)
        ]
        return lax.all_to_all(x, ("blk", "grp"), 0, 0, axis_index_groups=groups)

    falling = range(blocks - 1, -1, -1)
    hops = lambda b: (b & 1) + (b >> 1 & 1) + (b >> 2)
    gathered = exchange(packed, falling)
    part = call(
        functools.partial(terms_kernel, width),
        [gathered, bounds, spread],
        [shape(dims + 8, queries)],
    )
    log_est, share = call(
        functools.partial(finish_kernel, sample_total, query_total),
        everyone(part, "grp") + [target],
        [shape(1, queries), shape(blocks, 1, queries)],
    )
    shares = exchange(share, sorted(falling, key=hops, reverse=True))
    return call(last_kernel, [shares, log_est], [shape(queries), shape(dims)])


def solution(mesh):
    return jax.shard_map(
        on_device,
        mesh=mesh,
        in_specs=(P(None, ("blk", "grp")), P(None, None, "blk"), P(), P("blk")),
        out_specs=(P("blk"), P()),
        check_vma=False,
    )
```

```python
import functools

import jax
import jax.numpy as jnp
from jax import lax
from jax.experimental import pallas as pl
from jax.experimental.pallas import tpu as pltpu
from jax.sharding import PartitionSpec as P

TABLE_ROWS = 1048576
GRID = 256
LIMITED = 3

ROOT_HALF = 0.7071067811865476
LOG2_E = 1.4426950408889634
SLOPE = 0.5641895835477563


def box_terms(low, high):
    low_bell = jnp.exp2((low * low) * -LOG2_E)
    high_bell = jnp.exp2((high * high) * -LOG2_E)
    return lax.erf(high) - lax.erf(low), low * low_bell - high * high_bell


def split(x, parts):
    out = []
    for _ in range(parts - 1):
        head = x.astype(jnp.bfloat16)
        out.append(head)
        x = x - head.astype(jnp.float32)
    return out + [x.astype(jnp.bfloat16)]


def tree_sum(parts):
    while len(parts) > 1:
        parts = [a + b for a, b in zip(parts[::2], parts[1::2])]
    return parts[0]


def load_kernel(
    x_ref, bounds_ref, spread_ref, counts_ref,
    out_ref, held_bounds, held_spread, target_ref,
    held_x, held_counts, sems,
):
    sources = (x_ref, bounds_ref, spread_ref, counts_ref)
    targets = (held_x, held_bounds, held_spread, held_counts)
    copies = [
        pltpu.make_async_copy(source, target, sems.at[i])
        for i, (source, target) in enumerate(zip(sources, targets))
    ]
    for copy in copies:
        copy.start()
    copies[0].wait()
    rows = held_x.shape[0]
    packed = jnp.concatenate([held_x[8 * j : 8 * (j + 1), :] for j in range(rows // 8)], axis=1)
    for peer in range(out_ref.shape[0]):
        out_ref[peer] = packed
    for copy in copies[1:]:
        copy.wait()
    smoothing = 1.0 / TABLE_ROWS
    target_ref[...] = jnp.log(held_counts[...].astype(jnp.float32) / TABLE_ROWS + smoothing)


def terms_kernel(width, blocks_ref, bounds_ref, spread_ref, out_ref):
    dims, queries = bounds_ref.shape[1:]
    count = blocks_ref.shape[0]
    per_piece = 128 // width
    group = min(count, 4 * per_piece)

    low, high = bounds_ref[0], bounds_ref[1]
    limited = (high - low) != GRID
    at = lax.broadcasted_iota(jnp.int32, (dims, queries), 0)
    first = jnp.min(jnp.where(limited, at, dims), axis=0, keepdims=True)
    last = jnp.max(jnp.where(limited, at, -1), axis=0, keepdims=True)
    chosen = [at == first, limited & (at > first) & (at < last), at == last]

    row = lax.broadcasted_iota(jnp.int32, (dims, dims), 0)
    column = lax.broadcasted_iota(jnp.int32, (dims, dims), 1)
    spread = jnp.sum(jnp.where(row == column, spread_ref[...], 0.0), axis=1, keepdims=True)
    unit = ROOT_HALF / spread

    pick = lambda mask, values: jnp.sum(jnp.where(mask, values, 0.0), axis=0, keepdims=True)
    low = low.astype(jnp.float32) * unit
    high = high.astype(jnp.float32) * unit
    low_at = [pick(mask, low) for mask in chosen]
    high_at = [pick(mask, high) for mask in chosen]

    ones = [mask.astype(jnp.float32).astype(jnp.bfloat16) for mask in chosen]
    free = jnp.where(limited, 0.0, 1.0).astype(jnp.bfloat16)
    none = jnp.zeros_like(free)
    right = jnp.concatenate(
        [jnp.concatenate(ones + [none], axis=1)] * 3
        + [jnp.concatenate([none] * LIMITED + [free], axis=1)] * 3,
        axis=0,
    )

    def step(picked, sums):
        others = jnp.exp2(picked[:, LIMITED * queries :])
        mass, slope = [], []
        for k in range(LIMITED):
            points = picked[:, k * queries : (k + 1) * queries]
            m, s = box_terms(low_at[k] - points, high_at[k] - points)
            mass.append(m)
            slope.append(s)
        pair = others * mass[0]
        last_two = pair * mass[1]
        whole = last_two * mass[2]
        return whole, (
            sums[0] + whole,
            sums[1] + (others * mass[1]) * (mass[2] * slope[0]),
            sums[2] + pair * (mass[2] * slope[1]),
            sums[3] + last_two * slope[2],
        )

    def piece(start, totals):
        sums, products = totals[:-1], totals[-1]
        some = [blocks_ref[start + b] for b in range(per_piece)]
        x = unit * jnp.concatenate(
            [
                jnp.concatenate([block[:, width * j : width * (j + 1)] for block in some], axis=1)
                for j in range(dims // 8)
            ],
            axis=0,
        )
        full, slope = box_terms(-x, float(GRID) * unit - x)
        ratio = jnp.concatenate(split(slope / full, 2), axis=0)
        left = jnp.concatenate(split(x, 3) + split(jnp.log(0.5 * full) * LOG2_E, 3), axis=0)
        picked = lax.dot_general(
            left, right, (((0,), (0,)), ((), ())), preferred_element_type=jnp.float32
        )
        inside = []
        for at_row in range(0, per_piece * width, 16):
            upper, sums = step(picked[at_row : at_row + 8], sums)
            lower, sums = step(picked[at_row + 8 : at_row + 16], sums)
            whole = jnp.concatenate([upper, lower], axis=0)
            inside.append(jnp.concatenate(split(whole, 2), axis=1))
        inside = jnp.concatenate(inside, axis=0)
        products = products + jnp.dot(ratio, inside, preferred_element_type=jnp.float32)
        return (*sums, products)

    def pieces(number, totals):
        for start in range(0, group, per_piece):
            totals = piece(number * group + start, totals)
        return totals

    zero = jnp.zeros((8, queries), jnp.float32)
    totals = (zero,) * (1 + LIMITED) + (jnp.zeros((2 * dims, 2 * queries), jnp.float32),)
    if count == group:
        totals = pieces(0, totals)
    else:
        totals = lax.fori_loop(0, count // group, pieces, totals)
    sums = [jnp.sum(s, axis=0, keepdims=True) for s in totals[:-1]]
    products = totals[-1]
    deriv = products[:dims, :queries] + (products[dims:, :queries] + products[:dims, queries:])
    deriv = jnp.where(limited, 0.0, deriv * (SLOPE / 4))
    for mask, s in zip(chosen, sums[1:]):
        deriv = jnp.where(mask, s * (SLOPE / 4), deriv)
    out_ref[:dims, :] = deriv
    out_ref[dims:, :] = jnp.broadcast_to(sums[0] * 0.125, (8, queries))


def finish_kernel(sample_total, query_total, *refs):
    part_refs, (target_ref, log_ref, share_ref) = refs[:-3], refs[-3:]
    whole = tree_sum([ref[...] for ref in part_refs])
    dims, queries = whole.shape[0] - 8, whole.shape[1]
    smoothing = 1.0 / TABLE_ROWS
    estimate = whole[dims : dims + 1] / sample_total
    log_est = jnp.log(estimate + smoothing)
    log_ref[...] = log_est
    weight = 2.0 * (log_est - target_ref[...]) / (query_total * (estimate + smoothing))
    terms = whole[:dims] * (weight / sample_total)
    terms = jnp.concatenate([terms, jnp.zeros((queries - dims, queries), jnp.float32)], axis=0)
    share = jnp.sum(terms.T, axis=0, keepdims=True)
    for peer in range(share_ref.shape[0]):
        share_ref[peer] = share


def last_kernel(shares_ref, held_log_ref, log_ref, gradient_ref):
    total = tree_sum([shares_ref[peer] for peer in range(shares_ref.shape[0])])
    log_ref[...] = held_log_ref[0]
    gradient_ref[...] = total[0, : gradient_ref.shape[0]]


def everyone(x, axis):
    size = lax.axis_size(axis)
    return [x] + [
        lax.ppermute(x, axis, [(i, i ^ offset) for i in range(size)]) for offset in range(1, size)
    ]


def call(kernel, args, outs, scratch=(), placed=pltpu.VMEM):
    single = len(outs) == 1
    return pl.pallas_call(
        kernel,
        out_shape=outs[0] if single else outs,
        in_specs=[pl.BlockSpec(memory_space=placed)] * len(args),
        out_specs=pl.BlockSpec(memory_space=pltpu.VMEM)
        if single
        else [pl.BlockSpec(memory_space=pltpu.VMEM)] * len(outs),
        scratch_shapes=list(scratch),
        compiler_params=pltpu.CompilerParams(vmem_limit_bytes=32 << 20),
    )(*args)


def shape(*sizes):
    return jax.ShapeDtypeStruct(sizes, jnp.float32)


def on_device(samples, bounds, spread, counts):
    dims, width = samples.shape
    queries = bounds.shape[2]
    blocks, copies = lax.axis_size("blk"), lax.axis_size("grp")
    sample_total = width * blocks * copies
    query_total = queries * blocks

    counts_vector = pltpu.VMEM((1, queries), jnp.int32)
    packed, bounds, spread, target = call(
        load_kernel,
        [
            pltpu.with_memory_space_constraint(array, pltpu.HBM)
            for array in (samples, bounds, spread.reshape(1, dims), counts.reshape(1, queries))
        ],
        [
            pltpu.VMEM((blocks, 8, dims * width // 8), jnp.float32),
            pltpu.VMEM(bounds.shape, bounds.dtype),
            pltpu.VMEM((1, dims), jnp.float32),
            pltpu.VMEM((1, queries), jnp.float32),
        ],
        [pltpu.VMEM((dims, width), jnp.float32), counts_vector, pltpu.SemaphoreType.DMA((4,))],
        placed=pl.ANY,
    )
    turned = [1] + [0] * (blocks - 1)
    groups = [
        [b * copies + (c + turned[b]) % copies for b in reversed(range(blocks))]
        for c in range(copies)
    ]
    exchange = lambda x: lax.all_to_all(x, ("blk", "grp"), 0, 0, axis_index_groups=groups)
    gathered = exchange(packed)
    part = call(
        functools.partial(terms_kernel, width),
        [gathered, bounds, spread],
        [shape(dims + 8, queries)],
    )
    log_est, share = call(
        functools.partial(finish_kernel, sample_total, query_total),
        everyone(part, "grp") + [target],
        [shape(1, queries), shape(blocks, 1, queries)],
    )
    shares = exchange(share)
    return call(last_kernel, [shares, log_est], [shape(queries), shape(dims)])


def solution(mesh):
    return jax.shard_map(
        on_device,
        mesh=mesh,
        in_specs=(P(None, ("blk", "grp")), P(None, None, "blk"), P(), P("blk")),
        out_specs=(P("blk"), P()),
        check_vma=False,
    )
```
